32 devices in a mesh: dp: 4 (over y, x), seq: 8 (over z, core).
Axes of the slice: x: 2, y: 2, z: 4, core: 2. Of those that a mesh axis runs over, the one named last changes fastest.
Arguments:
- inputs: bfloat16 [8, 1024, 768], P('dp', 'seq'), may hold values from -6 to 6
- segments: int32 [8, 1024], P('dp', 'seq'), may hold values from 0 to 10, as said below
- cotangent: bfloat16 [8, 1024, 768], P('dp', 'seq'), may hold values from -6 to 6
- ln1_gain: bfloat16 [768], P(('dp', 'seq')), may hold values from 0.5 to 1.5
- ln1_bias: bfloat16 [768], P(('dp', 'seq')), may hold values from -3 to 3
- w_qkv: bfloat16 [1769472], P(('dp', 'seq')), may hold values from -0.3125 to 0.3125
- b_qv: bfloat16 [1536], P(('dp', 'seq')), may hold values from -3 to 3
- w_out: bfloat16 [589824], P(('dp', 'seq')), may hold values from -1.75 to 1.75
- b_out: bfloat16 [768], P(('dp', 'seq')), may hold values from -3 to 3
- ln2_gain: bfloat16 [768], P(('dp', 'seq')), may hold values from 0.5 to 1.5
- ln2_bias: bfloat16 [768], P(('dp', 'seq')), may hold values from -3 to 3
- w_fc: bfloat16 [2359296], P(('dp', 'seq')), may hold values from -0.21875 to 0.21875
- b_fc: bfloat16 [3072], P(('dp', 'seq')), may hold values from -3 to 3
- w_proj: bfloat16 [2359296], P(('dp', 'seq')), may hold values from -0.15625 to 0.15625
- b_proj: bfloat16 [768], P(('dp', 'seq')), may hold values from -3 to 3
Outputs:
- outputs: bfloat16 [8, 1024, 768], P('dp', 'seq')
- grad_inputs: bfloat16 [8, 1024, 768], P('dp', 'seq')
- grad_ln1_gain: float32 [768], P(('dp', 'seq'))
- grad_ln1_bias: float32 [768], P(('dp', 'seq'))
- grad_w_qkv: float32 [1769472], P(('dp', 'seq'))
- grad_b_qv: float32 [1536], P(('dp', 'seq'))
- grad_w_out: float32 [589824], P(('dp', 'seq'))
- grad_b_out: float32 [768], P(('dp', 'seq'))
- grad_ln2_gain: float32 [768], P(('dp', 'seq'))
- grad_ln2_bias: float32 [768], P(('dp', 'seq'))
- grad_w_fc: float32 [2359296], P(('dp', 'seq'))
- grad_b_fc: float32 [3072], P(('dp', 'seq'))
- grad_w_proj: float32 [2359296], P(('dp', 'seq'))
- grad_b_proj: float32 [768], P(('dp', 'seq'))
The draws below stay inside these ranges and needn't reach their ends.
Inputs may be any that keep to these rules, and one draw needn't show every extreme that they name: `segments`: along each sequence the document numbers start at 0 and rise by one from each document to the next; documents are consecutive runs of tokens. Every document has 102 tokens or more, except possibly the first or the last of a sequence.
All inputs are finite; a program needn't handle non-finite values.
Results may differ from the reference program's by a relative error of at most 0.014.
Values may be sent and summed in bfloat16 or wider, within the bound.
No kernel may reach another device: no remote copies, remote signals or barrier semaphores. Data moves between devices by JAX's collectives and lax.ppermute only.
A program may use at most 192 MiB of HBM per device.

```python
import math
import jax
import jax.numpy as jnp
from jax import lax

D = 768
HEADS = 12
FF = 3072
SEQS_DEV = 2
BLK = 128
SEQ_LEN = 1024
SEQS = 8


def draw_segments(key, part):
    key = jax.random.fold_in(key, 7)
    key_sizes, key_lead, key_pick = jax.random.split(key, 3)
    shortest = max(SEQ_LEN // 10, 1)
    count = SEQ_LEN // shortest + 2
    sizes = jax.random.randint(key_sizes, (SEQS, count), shortest, SEQ_LEN)
    leading = jax.random.randint(key_lead, (SEQS,), 1, BLK)
    picked = jax.random.randint(key_pick, (SEQS // SEQS_DEV,), 0, SEQS_DEV)
    member = jnp.arange(SEQS) % SEQS_DEV
    chosen = member == jnp.repeat(picked, SEQS_DEV)
    packed = (member == (picked[0] + 1) % SEQS_DEV) & (jnp.arange(SEQS) < SEQS_DEV)
    sizes = jnp.where(packed[:, None], shortest, sizes)
    first_size = jnp.where(chosen, leading, sizes[:, 0])
    second_size = jnp.where(chosen, SEQ_LEN, sizes[:, 1])
    sizes = jnp.concatenate([first_size[:, None], second_size[:, None], sizes[:, 2:]], axis=1)
    ends = jnp.cumsum(sizes, axis=1)
    positions = jnp.arange(SEQ_LEN)
    return jnp.sum((ends[:, None, :] <= positions[None, :, None]).astype(jnp.int32), axis=2)


def block_scale(stream_key, shape, pieces, low, largest):
    level = 1.0
    for position, parts in pieces:
        draws = jax.random.uniform(jax.random.fold_in(jax.random.fold_in(stream_key, 6), position), (parts,), jnp.float32, low / len(pieces), largest / len(pieces))
        level = level * jnp.repeat(jnp.exp(draws), shape[position] // parts).reshape((-1,) + (1,) * (len(shape) - 1 - position))
    return level


def gaussian(stream_key, dims, scale, limit, pieces=(), kind=jnp.bfloat16):
    array = jax.random.normal(stream_key, dims, jnp.float32) * scale
    if len(pieces) > 0:
        array = block_scale(stream_key, dims, pieces, -0.22, 0.18) * array
    return jnp.clip(array, min=-limit, max=limit).astype(kind)


def setup_inputs(seed: int = 0) -> dict:
    splits = jax.random.split(jax.random.key(seed), 16)
    inputs = gaussian(splits[0], (SEQS, SEQ_LEN, D), 1.0, 6.0, ((0, 4), (1, 8)))
    segments = draw_segments(jax.random.fold_in(splits[15], 71), 0)
    cotangent = gaussian(splits[2], (SEQS, SEQ_LEN, D), 1.0, 6.0, ((0, 4), (1, 8)))
    ln1_gain = jnp.clip(1.0 + 0.1 * jax.random.normal(splits[3], (D,), jnp.float32), 0.5, 1.5).astype(jnp.bfloat16)
    ln1_bias = gaussian(splits[4], (D,), 0.3, 3.0, ((0, 32),))
    w_qkv = gaussian(splits[5], (3 * D * D,), (D // 2) ** -0.5, 0.3125, ((0, 32),))
    b_qv = gaussian(splits[6], (2 * D,), 0.3, 3.0, ((0, 32),))
    w_out = gaussian(splits[7], (D * D,), (D // 64) ** -0.5, 1.75, ((0, 32),))
    b_out = gaussian(splits[8], (D,), 0.3, 3.0, ((0, 32),))
    ln2_gain = jnp.clip(1.0 + 0.1 * jax.random.normal(splits[9], (D,), jnp.float32), 0.5, 1.5).astype(jnp.bfloat16)
    ln2_bias = gaussian(splits[10], (D,), 0.3, 3.0, ((0, 32),))
    w_fc = gaussian(splits[11], (D * FF,), D ** -0.5, 0.21875, ((0, 32),))
    b_fc = gaussian(splits[12], (FF,), 0.3, 3.0, ((0, 32),))
    w_proj = gaussian(splits[13], (FF * D,), (FF // 2) ** -0.5, 0.15625, ((0, 32),))
    b_proj = gaussian(splits[14], (D,), 0.3, 3.0, ((0, 32),))
    return dict(inputs=inputs, segments=segments, cotangent=cotangent, ln1_gain=ln1_gain, ln1_bias=ln1_bias, w_qkv=w_qkv, b_qv=b_qv, w_out=w_out, b_out=b_out, ln2_gain=ln2_gain, ln2_bias=ln2_bias, w_fc=w_fc, b_fc=b_fc, w_proj=w_proj, b_proj=b_proj)


HIGH = lax.Precision.HIGHEST
EPSILON = 1e-05
MASKED = -1e+30

@jax.custom_vjp
def low(v):
    return lax.optimization_barrier(v.astype(jnp.bfloat16)).astype(jnp.float32)

@jax.custom_vjp
def low_back(v):
    return v

def low_keep(v):
    return (low(v), None)

def low_pass(kept, grad):
    return (grad,)

def back_keep(v):
    return (v, None)

def back_low(kept, grad):
    return (low(grad),)
low.defvjp(low_keep, low_pass)
low_back.defvjp(back_keep, back_low)

def norm_affine(values, gain, bias):
    center = lax.optimization_barrier(jnp.mean(values, -1, keepdims=True))
    centered = values - center
    variance = lax.optimization_barrier(jnp.mean(centered * centered, -1, keepdims=True))
    return centered * lax.rsqrt(variance + EPSILON) * gain + bias

def layer_forward(inputs, doc_ids, gain1, bias1, wqkv, bqv, wout, bout, gain2, bias2, wfc, bfc, wproj, bproj):
    group, length, width = inputs.shape
    head_size = width // HEADS
    factor = head_size ** (-0.5)
    normed1 = low(norm_affine(inputs, gain1, bias1))
    qkv_bias = jnp.concatenate([bqv[:width], jnp.zeros((width,), jnp.float32), bqv[width:]])
    qkv = low_back(low(jnp.einsum('gtd,de->gte', normed1, wqkv, precision=HIGH) + qkv_bias))
    split = qkv.reshape(group, length, 3, HEADS, head_size)
    queries = split[:, :, 0]
    keys = split[:, :, 1]
    values = split[:, :, 2]
    rows_step = math.gcd(length, 512)
    positions = jnp.arange(length, dtype=jnp.int32)

    def one_block(start):
        query_block = lax.dynamic_slice_in_dim(queries, start, rows_step, 1)
        query_ids = lax.dynamic_slice_in_dim(doc_ids, start, rows_step, 1)
        query_pos = start + jnp.arange(rows_step, dtype=jnp.int32)
        scores = low_back(jnp.einsum('gqhd,gkhd->ghqk', query_block, keys, precision=HIGH) * factor)
        causal = positions[None, :] <= query_pos[:, None]
        same_doc = query_ids[:, :, None] == doc_ids[:, None, :]
        allowed = (causal[None] & same_doc)[:, None]
        probs = jax.nn.softmax(jnp.where(allowed, scores, MASKED), axis=-1)
        return jnp.einsum('ghqk,gkhd->gqhd', low(probs), values, precision=HIGH)
    starts = (jnp.arange(length // rows_step, dtype=jnp.int32) * rows_step).astype(jnp.int32)
    blocks = lax.map(jax.checkpoint(one_block), starts)
    attended = low_back(low(jnp.moveaxis(blocks, 0, 1).reshape(group, length, width)))
    middle = inputs + low_back(jnp.einsum('gtd,de->gte', attended, wout, precision=HIGH) + bout)
    normed2 = low(norm_affine(middle, gain2, bias2))
    hidden_pre = low_back(jnp.einsum('gtd,df->gtf', normed2, wfc, precision=HIGH) + bfc)
    hidden = low(jax.nn.gelu(hidden_pre, approximate=True))
    return middle + low_back(jnp.einsum('gtf,fd->gtd', hidden, wproj, precision=HIGH) + bproj)

def reference(inputs, segments, cotangent, ln1_gain, ln1_bias, w_qkv, b_qv, w_out, b_out, ln2_gain, ln2_bias, w_fc, b_fc, w_proj, b_proj):
    width = D
    units = FF
    params = (ln1_gain.astype(jnp.float32), ln1_bias.astype(jnp.float32), w_qkv.astype(jnp.float32).reshape(width, 3 * width), b_qv.astype(jnp.float32), w_out.astype(jnp.float32).reshape(width, width), b_out.astype(jnp.float32), ln2_gain.astype(jnp.float32), ln2_bias.astype(jnp.float32), w_fc.astype(jnp.float32).reshape(width, units), b_fc.astype(jnp.float32), w_proj.astype(jnp.float32).reshape(units, width), b_proj.astype(jnp.float32))
    group = math.gcd(SEQS, max(1, 4096 // SEQ_LEN))
    turns = SEQS // group
    inputs_all = inputs.astype(jnp.float32).reshape(turns, group, SEQ_LEN, width)
    ids_all = segments.reshape(turns, group, SEQ_LEN)
    cotangent_all = cotangent.astype(jnp.float32).reshape(turns, group, SEQ_LEN, width)

    def one_step(totals, item):
        input_group, id_group, grad_group = item

        def forward(input_value, *weights):
            return layer_forward(input_value, id_group, *weights)
        result, backward = jax.vjp(forward, input_group, *params)
        grads = backward(grad_group)
        totals = tuple((total + grad for total, grad in zip(totals, grads[1:])))
        return (totals, (result.astype(jnp.bfloat16), grads[0].astype(jnp.bfloat16)))
    zeros = tuple((jnp.zeros(weight.shape, jnp.float32) for weight in params))
    totals, (results, grad_in) = lax.scan(one_step, zeros, (inputs_all, ids_all, cotangent_all))
    shape = (SEQS, SEQ_LEN, width)
    flat = tuple((total.reshape(-1) for total in totals))
    return (results.reshape(shape), grad_in.reshape(shape), flat[0], flat[1], flat[2], flat[3], flat[4], flat[5], flat[6], flat[7], flat[8], flat[9], flat[10], flat[11])
```

```python
import functools

import jax
import jax.numpy as jnp
from jax import lax
from jax.experimental import pallas as pl
from jax.experimental.pallas import tpu as pltpu
from jax.sharding import PartitionSpec as P

HEADS = 12
CORES = 2


EPSILON = 1e-05
MASKED = -1e30
F32 = jnp.float32
BF16 = jnp.bfloat16


def norm_affine(values, gain, bias):
    center = jnp.mean(values, -1, keepdims=True)
    centered = values - center
    variance = jnp.mean(centered * centered, -1, keepdims=True)
    return centered * lax.rsqrt(variance + EPSILON) * gain + bias


def shift_seq(value, step):
    size = lax.axis_size("seq")
    return lax.ppermute(value, "seq", [(i, (i + step) % size) for i in range(size)])


def shift_z(value, step):
    size = lax.axis_size("seq")
    return lax.ppermute(value, "seq", [(i, (i + CORES * step) % size) for i in range(size)])


def swap_core(value):
    size = lax.axis_size("seq")
    return lax.ppermute(value, "seq", [(i, i ^ 1) for i in range(size)])


def swap_dp(value, bit):
    size = lax.axis_size("dp")
    return lax.ppermute(value, "dp", [(i, i ^ bit) for i in range(size)])


def ordered(flag, mine, other, axis):
    first = jnp.where(flag == 0, mine, other)
    second = jnp.where(flag == 0, other, mine)
    return jnp.stack([first, second], axis)


def roll_blocks(pieces, place):
    count = len(pieces)
    stacked = jnp.stack(pieces)
    twice = jnp.concatenate([stacked, stacked])
    return lax.dynamic_slice_in_dim(twice, lax.rem(count - place, count), count, 0)


def gather_rows(shard):
    rows, columns = shard.shape
    heights = lax.axis_size("seq") // CORES
    place = lax.axis_index("seq")
    level, core = place // CORES, place % CORES
    pieces = [shard] + [shift_z(shard, -step) for step in range(1, heights)]
    tower = roll_blocks(pieces, level)
    if lax.axis_size("dp") == 4:
        plane = lax.axis_index("dp")
        y, x = plane // 2, plane % 2
        low, high = tower[: heights // 2], tower[heights // 2 :]
        low_x = ordered(x, low, swap_dp(low, 1), 0)
        high_y = ordered(y, high, swap_dp(high, 2), 0)
        low_all = ordered(y, low_x, swap_dp(low_x, 2), 0)
        high_all = ordered(x, high_y, swap_dp(high_y, 1), 1)
        half = jnp.concatenate([low_all, high_all], 2)
    else:
        half = lax.all_gather(tower, "dp", axis=0, tiled=False)
    half = half.reshape(-1, rows, columns)
    return ordered(core, half, swap_core(half), 1).reshape(-1, columns)


def scatter_rows(total):
    kind = total.dtype
    columns = total.shape[-1]
    size, planes = lax.axis_size("seq"), lax.axis_size("dp")
    heights = size // CORES
    rows = total.shape[0] // (size * planes)
    place = lax.axis_index("seq")
    level, core = place // CORES, place % CORES

    def pick(value, index, axis):
        return lax.dynamic_index_in_dim(value, index, axis, keepdims=False)

    def add(mine, other):
        return (mine.astype(F32) + other.astype(F32)).astype(kind)

    split = total.reshape(planes * heights, CORES, rows, columns)
    split = add(pick(split, core, 1), swap_core(pick(split, 1 - core, 1)))
    if planes == 4:
        plane = lax.axis_index("dp")
        y, x = plane // 2, plane % 2
        split = split.reshape(2, 2, heights, rows, columns)
        low, high = split[:, :, : heights // 2], split[:, :, heights // 2 :]
        low = add(pick(low, y, 0), swap_dp(pick(low, 1 - y, 0), 2))
        high = add(pick(high, x, 1), swap_dp(pick(high, 1 - x, 1), 1))
        low = add(pick(low, x, 0), swap_dp(pick(low, 1 - x, 0), 1))
        high = add(pick(high, y, 0), swap_dp(pick(high, 1 - y, 0), 2))
        tower = jnp.concatenate([low, high], 0)
    else:
        split = split.reshape(planes, heights, rows, columns)
        tower = lax.psum_scatter(split, "dp", scatter_dimension=0, tiled=False)
    mine = pick(tower, level, 0).astype(F32)
    for step in range(1, heights):
        mine += shift_z(pick(tower, lax.rem(level + step, heights), 0), step).astype(F32)
    return mine


def masked_scores(keys, queries, id_column, id_row, first, last):
    scores = lax.dot_general(keys, queries, (((1,), (1,)), ((), ())), preferred_element_type=F32)
    key_pos = lax.broadcasted_iota(jnp.int32, scores.shape, 0)
    query_pos = lax.broadcasted_iota(jnp.int32, scores.shape, 1) + first
    allowed = (key_pos <= query_pos) & (id_column == id_row)
    return jnp.where(allowed, scores, MASKED)


def load_sequence(place, blocks, whole):
    count = len(blocks)
    rows = blocks[0].shape[0]
    for step, block in enumerate(blocks):
        source = lax.rem(place + (count - step), count)
        whole[pl.ds(pl.multiple_of(source * rows, rows), rows), :] = block[...]


def read_ids(whole):
    width = whole.shape[1]
    tail = whole[:, width - 128 :].astype(F32)
    return tail[:, 127:128], tail.T[127:128, :]


def forward_kernel(count, heads, head_size, step_rows, place_ref, *refs):
    blocks, outs = refs[:count], refs[count : 2 * count]
    stats, whole, result = refs[2 * count :]
    place = place_ref[0]
    load_sequence(place, blocks, whole)
    length = whole.shape[0]
    group = heads * head_size
    id_column, id_row = read_ids(whole)
    values_t = whole[:, 2 * group : 3 * group].astype(F32).T.astype(BF16)
    for first in range(0, length, step_rows):
        last = first + step_rows
        tops = []
        for head in range(heads):
            lo = head * head_size
            queries = whole[first:last, lo : lo + head_size] * BF16(head_size**-0.5)
            keys = whole[:last, group + lo : group + lo + head_size]
            scores = masked_scores(
                keys, queries, id_column[:last], id_row[:, first:last], first, last
            )
            highest = jnp.max(scores, 0, keepdims=True)
            weights = jnp.exp(scores - highest)
            total = jnp.sum(weights, 0, keepdims=True)
            probs = (weights * (1.0 / total)).astype(BF16)
            tops.append(
                jnp.dot(
                    values_t[lo : lo + head_size, :last], probs, preferred_element_type=F32
                )
            )
            stats[head : head + 1, first:last] = highest + jnp.log(total)
        result[first:last, :] = jnp.concatenate(tops, 0).T.astype(BF16)
    half = outs[0].shape[0]
    for step, out in enumerate(outs):
        source = lax.rem(place + (count - step), count)
        start = pl.multiple_of(source * 2 * half, 2 * half)
        out[:, :group] = result[pl.ds(start, half), :]
        out[:, group:] = result[pl.ds(start + half, half), :]


def backward_kernel(count, heads, head_size, step_rows, place_ref, *refs):
    blocks, grads, stats = refs[:count], refs[count : 2 * count], refs[2 * count]
    outs = refs[2 * count + 1 : 3 * count + 1]
    whole, grad_out, grad_query, grad_key, grad_value = refs[3 * count + 1 :]
    place = place_ref[0]
    load_sequence(place, blocks, whole)
    length = whole.shape[0]
    group = heads * head_size
    half = grads[0].shape[0]
    for step, grad in enumerate(grads):
        source = lax.rem(place + (count - step), count)
        start = pl.multiple_of(source * 2 * half, 2 * half)
        grad_out[pl.ds(start, half), :] = grad[:, :group]
        grad_out[pl.ds(start + half, half), :] = grad[:, group:]
    id_column, id_row = read_ids(whole)
    keys_t = whole[:, group : 2 * group].astype(F32).T.astype(BF16)
    factor = head_size**-0.5
    grad_key[...] = jnp.zeros_like(grad_key)
    grad_value[...] = jnp.zeros_like(grad_value)
    for first in range(0, length, step_rows):
        last = first + step_rows
        tops = []
        for head in range(heads):
            lo = head * head_size
            queries = whole[first:last, lo : lo + head_size] * BF16(factor)
            keys = whole[:last, group + lo : group + lo + head_size]
            values = whole[:last, 2 * group + lo : 2 * group + lo + head_size]
            grad = grad_out[first:last, lo : lo + head_size]
            scores = masked_scores(
                keys, queries, id_column[:last], id_row[:, first:last], first, last
            )
            probs = jnp.exp(scores - stats[head : head + 1, first:last])
            grad_probs = lax.dot_general(
                values, grad, (((1,), (1,)), ((), ())), preferred_element_type=F32
            )
            delta = jnp.sum(probs * grad_probs, 0, keepdims=True)
            grad_scores = (probs * (grad_probs - delta)).astype(BF16)
            tops.append(
                jnp.dot(
                    keys_t[lo : lo + head_size, :last], grad_scores, preferred_element_type=F32
                )
                * factor
            )
            grad_key[head, :last, :] += jnp.dot(
                grad_scores, queries, preferred_element_type=F32
            )
            grad_value[head, :last, :] += jnp.dot(
                probs.astype(BF16), grad, preferred_element_type=F32
            )
        grad_query[first:last, :] = jnp.concatenate(tops, 0).T.astype(BF16)
    rows = outs[0].shape[0]
    for step, out in enumerate(outs):
        source = lax.rem(place + (count - step), count)
        start = pl.multiple_of(source * rows, rows)
        out[:, :group] = grad_query[pl.ds(start, rows), :]
        for head in range(heads):
            lo = head * head_size
            out[:, group + lo : group + lo + head_size] = grad_key[
                head, pl.ds(start, rows), :
            ].astype(BF16)
            out[:, 2 * group + lo : 2 * group + lo + head_size] = grad_value[
                head, pl.ds(start, rows), :
            ].astype(BF16)


def vmem_specs(count):
    return [pl.BlockSpec(memory_space=pltpu.VMEM) for _ in range(count)]


def attend_forward(place, blocks, heads, head_size):
    count = len(blocks)
    rows, width = blocks[0].shape
    length = rows * count
    group = heads * head_size
    pairs = length * length // 2 * heads
    return pl.pallas_call(
        functools.partial(forward_kernel, count, heads, head_size, min(256, length)),
        out_shape=[jax.ShapeDtypeStruct((rows // 2, 2 * group), BF16)] * count
        + [jax.ShapeDtypeStruct((heads, length), F32)],
        in_specs=[pl.BlockSpec(memory_space=pltpu.SMEM)] + vmem_specs(count),
        out_specs=vmem_specs(count + 1),
        scratch_shapes=[pltpu.VMEM((length, width), BF16), pltpu.VMEM((length, group), BF16)],
        compiler_params=pltpu.CompilerParams(vmem_limit_bytes=48 * 2**20),
        cost_estimate=pl.CostEstimate(
            flops=pairs * head_size * 4, bytes_accessed=length * width * 3, transcendentals=pairs
        ),
    )(place, *blocks)


def attend_backward(place, blocks, grads, stats, heads, head_size):
    count = len(blocks)
    rows, width = blocks[0].shape
    length = rows * count
    group = heads * head_size
    pairs = length * length // 2 * heads
    return pl.pallas_call(
        functools.partial(backward_kernel, count, heads, head_size, min(256, length)),
        out_shape=[jax.ShapeDtypeStruct((rows, 3 * group), BF16)] * count,
        in_specs=[pl.BlockSpec(memory_space=pltpu.SMEM)] + vmem_specs(2 * count + 1),
        out_specs=vmem_specs(count),
        scratch_shapes=[
            pltpu.VMEM((length, width), BF16),
            pltpu.VMEM((length, group), BF16),
            pltpu.VMEM((length, group), BF16),
            pltpu.VMEM((heads, length, head_size), F32),
            pltpu.VMEM((heads, length, head_size), F32),
        ],
        compiler_params=pltpu.CompilerParams(vmem_limit_bytes=48 * 2**20),
        cost_estimate=pl.CostEstimate(
            flops=pairs * head_size * 10, bytes_accessed=length * width * 6, transcendentals=pairs
        ),
    )(place, *blocks, *grads, stats)


def on_device(
    inputs,
    segments,
    cotangent,
    ln1_gain,
    ln1_bias,
    w_qkv,
    b_qv,
    w_out,
    b_out,
    ln2_gain,
    ln2_bias,
    w_fc,
    b_fc,
    w_proj,
    b_proj,
):
    seq_count, block, width = inputs.shape
    head_size = width // HEADS
    tokens = seq_count * block
    count = lax.axis_size("seq")
    devices = count * lax.axis_size("dp")
    place = lax.axis_index("seq")
    place_ref = place.reshape(1).astype(jnp.int32)
    groups = count // seq_count
    heads = -(-HEADS // groups)
    spare = groups * heads - HEADS
    group = heads * head_size

    vectors = (ln1_gain, ln1_bias, b_qv, b_out, ln2_gain, ln2_bias, b_fc, b_proj)
    sizes = [vector.shape[0] for vector in vectors]
    starts = [sum(sizes[:i]) for i in range(len(sizes))]
    small = gather_rows(jnp.concatenate(vectors).reshape(1, -1)).astype(F32)
    gain1, bias1, bqv, bout, gain2, bias2, bfc, bproj = [
        small[:, start : start + size].reshape(-1) for start, size in zip(starts, sizes)
    ]
    units = bfc.shape[0]
    wqkv = gather_rows(w_qkv.reshape(-1, 3 * width))
    wout = gather_rows(w_out.reshape(-1, width))
    wfc = gather_rows(w_fc.reshape(-1, units))
    wproj = gather_rows(w_proj.reshape(-1, width))

    def by_group(value, parts):
        value = value.reshape(seq_count, block, parts, HEADS, head_size)
        if spare:
            value = jnp.pad(value, ((0, 0), (0, 0), (0, 0), (0, spare), (0, 0)))
        value = value.reshape(seq_count, block, parts, groups, group)
        return value.transpose(0, 3, 1, 2, 4).reshape(count, block, parts * group)

    def from_group(value, parts):
        value = value.reshape(seq_count, groups, block, parts, group).transpose(0, 2, 3, 1, 4)
        value = value.reshape(tokens, parts, groups * heads, head_size)
        return value[:, :, :HEADS].reshape(tokens, parts * width)

    def pack(value):
        value = value.reshape(value.shape[0], 2, block // 2, group).transpose(0, 2, 1, 3)
        return value.reshape(-1, block // 2, 2 * group)

    def unpack(value):
        value = value.reshape(value.shape[0], block // 2, 2, group).transpose(0, 2, 1, 3)
        return value.reshape(-1, block, group)

    def send_out(blocks):
        picked = [
            lax.dynamic_index_in_dim(blocks, lax.rem(place + step, count), 0, keepdims=False)
            for step in range(count)
        ]
        return [picked[0]] + [shift_seq(picked[step], step) for step in range(1, count)]

    def send_back(blocks):
        moved = [blocks[0]] + [shift_seq(blocks[step], -step) for step in range(1, count)]
        return roll_blocks(moved, place)

    rows = inputs.astype(F32).reshape(tokens, width)
    normed1 = norm_affine(rows, gain1, bias1).astype(BF16)
    qkv_bias = jnp.concatenate([bqv[:width], jnp.zeros((width,), F32), bqv[width:]])
    qkv = (jnp.dot(normed1, wqkv, preferred_element_type=F32) + qkv_bias).astype(BF16)
    fill = -(3 * group) % 128 or 128
    ids = jnp.broadcast_to(
        segments.astype(BF16)[:, None, :, None], (seq_count, groups, block, fill)
    )
    blocks = jnp.concatenate([by_group(qkv, 3), ids.reshape(count, block, fill)], -1)
    blocks = send_out(blocks)
    *attended, stats = attend_forward(place_ref, blocks, heads, head_size)
    attended_rows = from_group(unpack(send_back(attended)), 1)

    middle = rows + (jnp.dot(attended_rows, wout, preferred_element_type=F32) + bout)
    normed2 = norm_affine(middle, gain2, bias2).astype(BF16)
    hidden_pre = jnp.dot(normed2, wfc, preferred_element_type=F32) + bfc
    hidden = jax.nn.gelu(hidden_pre, approximate=True).astype(BF16)
    result_rows = middle + (jnp.dot(hidden, wproj, preferred_element_type=F32) + bproj)
    outputs = result_rows.astype(BF16).reshape(inputs.shape)

    grad_rows = cotangent.astype(F32).reshape(tokens, width)
    grad_branch = cotangent.reshape(tokens, width)
    grad_bproj = jnp.sum(grad_branch, 0, dtype=F32)
    grad_wproj = jnp.einsum("tf,td->fd", hidden, grad_branch, preferred_element_type=F32)
    grad_hidden = jnp.einsum("td,fd->tf", grad_branch, wproj, preferred_element_type=F32)
    _, gelu_back = jax.vjp(lambda value: jax.nn.gelu(value, approximate=True), hidden_pre)
    grad_pre = gelu_back(grad_hidden)[0].astype(BF16)
    grad_bfc = jnp.sum(grad_pre, 0, dtype=F32)
    grad_wfc = jnp.einsum("td,tf->df", normed2, grad_pre, preferred_element_type=F32)
    grad_normed2 = jnp.einsum("tf,df->td", grad_pre, wfc, preferred_element_type=F32)
    _, norm2_back = jax.vjp(norm_affine, middle, gain2, bias2)
    grad_mid_part, grad_gain2, grad_bias2 = norm2_back(grad_normed2)
    grad_middle = grad_rows + grad_mid_part
    grad_attn_out = grad_middle.astype(BF16)
    grad_bout = jnp.sum(grad_attn_out, 0, dtype=F32)
    grad_wout = jnp.einsum("td,te->de", attended_rows, grad_attn_out, preferred_element_type=F32)
    grad_attended = jnp.einsum("te,de->td", grad_attn_out, wout, preferred_element_type=F32)
    grad_blocks = send_out(pack(by_group(grad_attended.astype(BF16), 1)))
    own_wproj = scatter_rows(grad_wproj.astype(BF16))
    own_wfc = scatter_rows(grad_wfc.astype(BF16))
    own_wout = scatter_rows(grad_wout.astype(BF16))

    grad_back = attend_backward(place_ref, blocks, grad_blocks, stats, heads, head_size)
    grad_qkv = from_group(send_back(grad_back), 3)
    grad_bqv = jnp.concatenate(
        [
            jnp.sum(grad_qkv[:, :width], 0, dtype=F32),
            jnp.sum(grad_qkv[:, 2 * width :], 0, dtype=F32),
        ]
    )
    grad_wqkv = jnp.einsum("td,te->de", normed1, grad_qkv, preferred_element_type=F32)
    own_wqkv = scatter_rows(grad_wqkv.astype(BF16))
    grad_normed1 = jnp.einsum("te,de->td", grad_qkv, wqkv, preferred_element_type=F32)
    _, norm1_back = jax.vjp(norm_affine, rows, gain1, bias1)
    grad_in_part, grad_gain1, grad_bias1 = norm1_back(grad_normed1)
    grad_inputs = (grad_middle + grad_in_part).astype(BF16).reshape(inputs.shape)
    grads = (
        grad_gain1,
        grad_bias1,
        grad_bqv,
        grad_bout,
        grad_gain2,
        grad_bias2,
        grad_bfc,
        grad_bproj,
    )
    own_small = scatter_rows(
        jnp.concatenate([grad.reshape(devices, -1) for grad in grads], 1)
    ).reshape(-1)
    own = [own_small[start : start + size] for start, size in zip(starts, sizes)]
    return (
        outputs,
        grad_inputs,
        own[0],
        own[1],
        own_wqkv.reshape(-1),
        own[2],
        own_wout.reshape(-1),
        own[3],
        own[4],
        own[5],
        own_wfc.reshape(-1),
        own[6],
        own_wproj.reshape(-1),
        own[7],
    )


def solution(mesh):
    token_spec = P("dp", "seq", None)
    flat_spec = P(("dp", "seq"))
    in_specs = (token_spec, P("dp", "seq"), token_spec) + (flat_spec,) * 12
    out_specs = (token_spec, token_spec) + (flat_spec,) * 12
    return jax.shard_map(
        on_device, mesh=mesh, in_specs=in_specs, out_specs=out_specs, check_vma=False
    )
```

```python
import functools

import jax
import jax.numpy as jnp
from jax import lax
from jax.experimental import pallas as pl
from jax.experimental.pallas import tpu as pltpu
from jax.sharding import PartitionSpec as P

HEADS = 12
CORES = 2


EPSILON = 1e-05
MASKED = -1e30
F32 = jnp.float32
BF16 = jnp.bfloat16


def norm_affine(values, gain, bias):
    center = jnp.mean(values, -1, keepdims=True)
    centered = values - center
    variance = jnp.mean(centered * centered, -1, keepdims=True)
    return centered * lax.rsqrt(variance + EPSILON) * gain + bias


def shift_z(value, step):
    size = lax.axis_size("seq")
    return lax.ppermute(value, "seq", [(i, (i + CORES * step) % size) for i in range(size)])


def swap_core(value):
    size = lax.axis_size("seq")
    return lax.ppermute(value, "seq", [(i, i ^ 1) for i in range(size)])


def swap_dp(value, bit):
    size = lax.axis_size("dp")
    return lax.ppermute(value, "dp", [(i, i ^ bit) for i in range(size)])


def ordered(flag, mine, other, axis):
    first = jnp.where(flag == 0, mine, other)
    second = jnp.where(flag == 0, other, mine)
    return jnp.stack([first, second], axis)


def roll_blocks(pieces, place):
    count = len(pieces)
    stacked = jnp.stack(pieces)
    twice = jnp.concatenate([stacked, stacked])
    return lax.dynamic_slice_in_dim(twice, lax.rem(count - place, count), count, 0)


def gather_z(shard):
    heights = lax.axis_size("seq") // CORES
    level = lax.axis_index("seq") // CORES
    pieces = [shard] + [shift_z(shard, -step) for step in range(1, heights)]
    return roll_blocks(pieces, level)


def gather_plane(tower):
    heights = tower.shape[0]
    shard = tower.shape[1:]
    core = lax.axis_index("seq") % CORES
    if lax.axis_size("dp") == 4:
        plane = lax.axis_index("dp")
        y, x = plane // 2, plane % 2
        low, high = tower[: heights // 2], tower[heights // 2 :]
        low_x = ordered(x, low, swap_dp(low, 1), 0)
        high_y = ordered(y, high, swap_dp(high, 2), 0)
        low_all = ordered(y, low_x, swap_dp(low_x, 2), 0)
        high_all = ordered(x, high_y, swap_dp(high_y, 1), 1)
        half = jnp.concatenate([low_all, high_all], 2)
    else:
        half = lax.all_gather(tower, "dp", axis=0, tiled=False)
    half = half.reshape(-1, *shard)
    return ordered(core, half, swap_core(half), 1).reshape(-1, *shard)


def pick(value, index, axis):
    return lax.dynamic_index_in_dim(value, index, axis, keepdims=False)


def split_cores(parts):
    core = lax.axis_index("seq") % CORES
    parts = [part.reshape(-1, CORES, *part.shape[1:]) for part in parts]
    send = jnp.concatenate([pick(part, 1 - core, 1) for part in parts], 1)
    keep = jnp.concatenate([pick(part, core, 1) for part in parts], 1)
    return send, keep


def scatter_sum(send, keep):
    kind = send.dtype
    rows, columns = send.shape[1:]
    planes = lax.axis_size("dp")
    heights = lax.axis_size("seq") // CORES
    level = lax.axis_index("seq") // CORES

    def add(mine, other):
        return (mine.astype(F32) + other.astype(F32)).astype(kind)

    split = add(keep, swap_core(send))
    if planes == 4:
        plane = lax.axis_index("dp")
        y, x = plane // 2, plane % 2
        split = split.reshape(2, 2, heights, rows, columns)
        low, high = split[:, :, : heights // 2], split[:, :, heights // 2 :]
        low = add(pick(low, y, 0), swap_dp(pick(low, 1 - y, 0), 2))
        high = add(pick(high, x, 1), swap_dp(pick(high, 1 - x, 1), 1))
        low = add(pick(low, x, 0), swap_dp(pick(low, 1 - x, 0), 1))
        high = add(pick(high, y, 0), swap_dp(pick(high, 1 - y, 0), 2))
        tower = jnp.concatenate([low, high], 0)
    else:
        split = split.reshape(planes, heights, rows, columns)
        tower = lax.psum_scatter(split, "dp", scatter_dimension=0, tiled=False)
    mine = pick(tower, level, 0).astype(F32)
    for step in range(1, heights):
        mine += shift_z(pick(tower, lax.rem(level + step, heights), 0), step).astype(F32)
    return mine


def exchange(blocks):
    return lax.all_to_all(blocks, "seq", split_axis=0, concat_axis=0, tiled=True)


ROWS = 8
LANES = 128


def vmem_specs(count):
    return [pl.BlockSpec(memory_space=pltpu.VMEM) for _ in range(count)]


def place_lanes(size, total):
    source = lax.broadcasted_iota(jnp.int32, (LANES, total), 0)
    target = lax.rem(lax.broadcasted_iota(jnp.int32, (LANES, total), 1), size)
    return jnp.where(source == target, 1.0, 0.0).astype(BF16)


def owned_lanes(devices, size):
    device = lax.broadcasted_iota(jnp.int32, (devices, devices * size), 0)
    lane = lax.broadcasted_iota(jnp.int32, (devices, devices * size), 1)
    offset = lane - device * size
    return (offset >= 0) & (offset < size)


def unpack_kernel(sizes, small_ref, *outs):
    devices = small_ref.shape[0]
    small = small_ref[...].astype(F32)
    for i, (size, out) in enumerate(zip(sizes, outs)):
        spread = jnp.dot(
            small[:, i, :].astype(BF16),
            place_lanes(size, devices * size),
            preferred_element_type=F32,
        )
        out[...] = jnp.sum(jnp.where(owned_lanes(devices, size), spread, 0.0), 0, keepdims=True)


def unpack_small(small, sizes):
    devices = small.shape[0]
    return pl.pallas_call(
        functools.partial(unpack_kernel, sizes),
        out_shape=[jax.ShapeDtypeStruct((1, devices * size), F32) for size in sizes],
        in_specs=vmem_specs(1),
        out_specs=vmem_specs(len(sizes)),
        compiler_params=pltpu.CompilerParams(vmem_limit_bytes=32 * 2**20),
    )(small)


def pack_kernel(sizes, *refs):
    grads, packed, rows = refs[: len(sizes)], refs[len(sizes)], refs[len(sizes) + 1]
    devices = packed.shape[0]
    for i, (size, grad) in enumerate(zip(sizes, grads)):
        owned = jnp.where(owned_lanes(devices, size), grad[...], 0.0).astype(BF16)
        rows[:, i, :] = lax.dot_general(
            owned,
            place_lanes(size, devices * size),
            (((1,), (1,)), ((), ())),
            preferred_element_type=F32,
        )
    packed[...] = rows[...].astype(BF16)


def pack_small(grads, sizes, devices):
    return pl.pallas_call(
        functools.partial(pack_kernel, sizes),
        out_shape=jax.ShapeDtypeStruct((devices, ROWS, LANES), BF16),
        in_specs=vmem_specs(len(sizes)),
        out_specs=vmem_specs(1)[0],
        scratch_shapes=[pltpu.VMEM((devices, ROWS, LANES), F32)],
        compiler_params=pltpu.CompilerParams(vmem_limit_bytes=32 * 2**20),
    )(*grads)


def stack_kernel(out_ref, fc_ref, proj_ref, after_ref, stacked):
    width = out_ref.shape[1]
    stacked[0] = out_ref[...]
    parts = fc_ref.shape[1] // width
    for i in range(parts):
        stacked[1 + i] = fc_ref[:, i * width : (i + 1) * width]
    for i in range(parts):
        stacked[1 + parts + i] = proj_ref[i]


def stack_weights(w_out, w_fc, w_proj, after):
    rows, width = w_out.shape
    parts = w_fc.shape[1] // width
    return pl.pallas_call(
        stack_kernel,
        out_shape=jax.ShapeDtypeStruct((1 + 2 * parts, rows, width), BF16),
        in_specs=vmem_specs(3) + [pl.BlockSpec(memory_space=pl.ANY)],
        out_specs=vmem_specs(1)[0],
    )(w_out, w_fc, w_proj, after)


def masked_scores(keys, queries, id_column, id_row, first, last):
    scores = lax.dot_general(keys, queries, (((1,), (1,)), ((), ())), preferred_element_type=F32)
    key_pos = lax.broadcasted_iota(jnp.int32, scores.shape, 0)
    query_pos = lax.broadcasted_iota(jnp.int32, scores.shape, 1) + first
    allowed = (key_pos <= query_pos) & (id_column == id_row)
    return jnp.where(allowed, scores, MASKED)


def read_ids(whole):
    width = whole.shape[1]
    tail = whole[:, width - 128 :].astype(F32)
    return tail[:, 127:128], tail.T[127:128, :]


def forward_kernel(heads, head_size, step_rows, block, whole, out, stats, result):
    length = whole.shape[0]
    group = heads * head_size
    id_column, id_row = read_ids(whole)
    values_t = whole[:, 2 * group : 3 * group].astype(F32).T.astype(BF16)
    for first in range(0, length, step_rows):
        last = first + step_rows
        tops = []
        for head in range(heads):
            lo = head * head_size
            queries = whole[first:last, lo : lo + head_size] * BF16(head_size**-0.5)
            keys = whole[:last, group + lo : group + lo + head_size]
            scores = masked_scores(
                keys, queries, id_column[:last], id_row[:, first:last], first, last
            )
            highest = jnp.max(scores, 0, keepdims=True)
            weights = jnp.exp(scores - highest)
            total = jnp.sum(weights, 0, keepdims=True)
            probs = (weights * (1.0 / total)).astype(BF16)
            tops.append(
                jnp.dot(
                    values_t[lo : lo + head_size, :last], probs, preferred_element_type=F32
                )
            )
            stats[head : head + 1, first:last] = highest + jnp.log(total)
        result[first:last, :] = jnp.concatenate(tops, 0).T.astype(BF16)
    half = block // 2
    for start in range(0, length, block):
        out[start // 2 : start // 2 + half, :group] = result[start : start + half, :]
        out[start // 2 : start // 2 + half, group:] = result[start + half : start + block, :]


def backward_kernel(
    heads,
    head_size,
    step_rows,
    block,
    whole,
    grads,
    stats,
    out,
    grad_out,
    grad_query,
    grad_key,
    grad_value,
):
    length = whole.shape[0]
    group = heads * head_size
    half = block // 2
    for start in range(0, length, block):
        packed = grads[start // 2 : start // 2 + half, :]
        grad_out[start : start + half, :] = packed[:, :group]
        grad_out[start + half : start + block, :] = packed[:, group:]
    id_column, id_row = read_ids(whole)
    keys_t = whole[:, group : 2 * group].astype(F32).T.astype(BF16)
    factor = head_size**-0.5
    grad_key[...] = jnp.zeros_like(grad_key)
    grad_value[...] = jnp.zeros_like(grad_value)
    for first in range(0, length, step_rows):
        last = first + step_rows
        tops = []
        for head in range(heads):
            lo = head * head_size
            queries = whole[first:last, lo : lo + head_size] * BF16(factor)
            keys = whole[:last, group + lo : group + lo + head_size]
            values = whole[:last, 2 * group + lo : 2 * group + lo + head_size]
            grad = grad_out[first:last, lo : lo + head_size]
            scores = masked_scores(
                keys, queries, id_column[:last], id_row[:, first:last], first, last
            )
            probs = jnp.exp(scores - stats[head : head + 1, first:last])
            grad_probs = lax.dot_general(
                values, grad, (((1,), (1,)), ((), ())), preferred_element_type=F32
            )
            delta = jnp.sum(probs * grad_probs, 0, keepdims=True)
            grad_scores = (probs * (grad_probs - delta)).astype(BF16)
            tops.append(
                jnp.dot(
                    keys_t[lo : lo + head_size, :last], grad_scores, preferred_element_type=F32
                )
                * factor
            )
            grad_key[head, :last, :] += jnp.dot(
                grad_scores, queries, preferred_element_type=F32
            )
            grad_value[head, :last, :] += jnp.dot(
                probs.astype(BF16), grad, preferred_element_type=F32
            )
        grad_query[first:last, :] = jnp.concatenate(tops, 0).T.astype(BF16)
    out[:, :group] = grad_query[...]
    for head in range(heads):
        lo = head * head_size
        out[:, group + lo : group + lo + head_size] = grad_key[head].astype(BF16)
        out[:, 2 * group + lo : 2 * group + lo + head_size] = grad_value[head].astype(BF16)


def attend_forward(whole, heads, head_size, block):
    length, width = whole.shape
    group = heads * head_size
    pairs = length * length // 2 * heads
    return pl.pallas_call(
        functools.partial(forward_kernel, heads, head_size, min(256, length), block),
        out_shape=[
            jax.ShapeDtypeStruct((length // 2, 2 * group), BF16),
            jax.ShapeDtypeStruct((heads, length), F32),
        ],
        in_specs=vmem_specs(1),
        out_specs=vmem_specs(2),
        scratch_shapes=[pltpu.VMEM((length, group), BF16)],
        compiler_params=pltpu.CompilerParams(vmem_limit_bytes=48 * 2**20),
        cost_estimate=pl.CostEstimate(
            flops=pairs * head_size * 4, bytes_accessed=length * width * 3, transcendentals=pairs
        ),
    )(whole)


def attend_backward(whole, grads, stats, heads, head_size, block):
    length, width = whole.shape
    group = heads * head_size
    pairs = length * length // 2 * heads
    return pl.pallas_call(
        functools.partial(backward_kernel, heads, head_size, min(256, length), block),
        out_shape=jax.ShapeDtypeStruct((length, 3 * group), BF16),
        in_specs=vmem_specs(3),
        out_specs=vmem_specs(1)[0],
        scratch_shapes=[
            pltpu.VMEM((length, group), BF16),
            pltpu.VMEM((length, group), BF16),
            pltpu.VMEM((heads, length, head_size), F32),
            pltpu.VMEM((heads, length, head_size), F32),
        ],
        compiler_params=pltpu.CompilerParams(vmem_limit_bytes=48 * 2**20),
        cost_estimate=pl.CostEstimate(
            flops=pairs * head_size * 10, bytes_accessed=length * width * 6, transcendentals=pairs
        ),
    )(whole, grads, stats)


def on_device(
    inputs,
    segments,
    cotangent,
    ln1_gain,
    ln1_bias,
    w_qkv,
    b_qv,
    w_out,
    b_out,
    ln2_gain,
    ln2_bias,
    w_fc,
    b_fc,
    w_proj,
    b_proj,
):
    seq_count, block, width = inputs.shape
    head_size = width // HEADS
    tokens = seq_count * block
    count = lax.axis_size("seq")
    devices = count * lax.axis_size("dp")
    groups = count // seq_count
    heads = -(-HEADS // groups)
    spare = groups * heads - HEADS
    group = heads * head_size

    vectors = (ln1_gain, ln1_bias, b_qv, b_out, ln2_gain, ln2_bias, b_fc, b_proj)
    sizes = tuple(vector.shape[0] for vector in vectors)
    shard_rows = w_out.shape[0] // width
    parts = w_fc.shape[0] // w_out.shape[0]
    small = [jnp.pad(vector[None], ((0, 0), (0, width - vector.shape[0]))) for vector in vectors]
    thirds = w_qkv.reshape(shard_rows, 3, width).transpose(1, 0, 2).reshape(-1, width)
    tower_a = gather_z(jnp.concatenate([thirds] + small, 0))
    stacked = stack_weights(
        w_out.reshape(-1, width),
        w_fc.reshape(-1, parts * width),
        w_proj.reshape(parts, -1, width),
        tower_a,
    )
    tower_b = gather_z(stacked)
    whole_a = gather_plane(tower_a)
    whole_b = gather_plane(tower_b)
    gain1, bias1, bqv, bout, gain2, bias2, bfc, bproj = unpack_small(
        whole_a[:, 3 * shard_rows :, :LANES], sizes
    )
    wqkv = jnp.concatenate(
        [whole_a[:, i * shard_rows : (i + 1) * shard_rows] for i in range(3)], -1
    ).reshape(width, 3 * width)
    wout = whole_b[:, 0].reshape(width, width)
    wfc = whole_b[:, 1 : 1 + parts].transpose(0, 2, 1, 3).reshape(width, parts * width)
    wproj = whole_b[:, 1 + parts :].reshape(parts * width, width)

    def by_group(value, parts):
        value = value.reshape(seq_count, block, parts, HEADS, head_size)
        if spare:
            value = jnp.pad(value, ((0, 0), (0, 0), (0, 0), (0, spare), (0, 0)))
        value = value.reshape(seq_count, block, parts, groups, group)
        return value.transpose(0, 3, 1, 2, 4).reshape(count, block, parts * group)

    def from_group(value, parts):
        value = value.reshape(seq_count, groups, block, parts, group).transpose(0, 2, 3, 1, 4)
        value = value.reshape(tokens, parts, groups * heads, head_size)
        return value[:, :, :HEADS].reshape(tokens, parts * width)

    def pack(value):
        value = value.reshape(value.shape[0], 2, block // 2, group).transpose(0, 2, 1, 3)
        return value.reshape(-1, block // 2, 2 * group)

    def unpack(value):
        value = value.reshape(value.shape[0], block // 2, 2, group).transpose(0, 2, 1, 3)
        return value.reshape(-1, block, group)

    rows = inputs.astype(F32).reshape(tokens, width)
    normed1 = norm_affine(rows, gain1, bias1).astype(BF16)
    qkv_bias = jnp.concatenate(
        [bqv[:, :width], jnp.zeros((1, width), F32), bqv[:, width:]], axis=1
    )
    qkv = (jnp.dot(normed1, wqkv, preferred_element_type=F32) + qkv_bias).astype(BF16)
    fill = -(3 * group) % 128 or 128
    ids = jnp.broadcast_to(
        segments.astype(BF16)[:, None, :, None], (seq_count, groups, block, fill)
    )
    blocks = jnp.concatenate([by_group(qkv, 3), ids.reshape(count, block, fill)], -1)
    whole = exchange(blocks).reshape(count * block, 3 * group + fill)
    attended, stats = attend_forward(whole, heads, head_size, block)
    attended = exchange(attended.reshape(count, block // 2, 2 * group))
    attended_rows = from_group(unpack(attended), 1)

    middle = rows + (jnp.dot(attended_rows, wout, preferred_element_type=F32) + bout)
    normed2 = norm_affine(middle, gain2, bias2).astype(BF16)
    hidden_pre = jnp.dot(normed2, wfc, preferred_element_type=F32) + bfc
    hidden = jax.nn.gelu(hidden_pre, approximate=True).astype(BF16)
    result_rows = middle + (jnp.dot(hidden, wproj, preferred_element_type=F32) + bproj)
    outputs = result_rows.astype(BF16).reshape(inputs.shape)

    grad_rows = cotangent.astype(F32).reshape(tokens, width)
    grad_branch = cotangent.reshape(tokens, width)
    grad_bproj = jnp.sum(grad_branch, 0, dtype=F32)
    grad_wproj = jnp.einsum("tf,td->fd", hidden, grad_branch, preferred_element_type=F32)
    grad_hidden = jnp.einsum("td,fd->tf", grad_branch, wproj, preferred_element_type=F32)
    _, gelu_back = jax.vjp(lambda value: jax.nn.gelu(value, approximate=True), hidden_pre)
    grad_pre = gelu_back(grad_hidden)[0].astype(BF16)
    grad_bfc = jnp.sum(grad_pre, 0, dtype=F32)
    grad_wfc = jnp.einsum("td,tf->df", normed2, grad_pre, preferred_element_type=F32)
    grad_normed2 = jnp.einsum("tf,df->td", grad_pre, wfc, preferred_element_type=F32)
    _, norm2_back = jax.vjp(norm_affine, middle, gain2, bias2)
    grad_mid_part, grad_gain2, grad_bias2 = norm2_back(grad_normed2)
    grad_middle = grad_rows + grad_mid_part
    grad_attn_out = grad_middle.astype(BF16)
    grad_bout = jnp.sum(grad_attn_out, 0, dtype=F32)
    grad_wout = jnp.einsum("td,te->de", attended_rows, grad_attn_out, preferred_element_type=F32)
    grad_attended = jnp.einsum("te,de->td", grad_attn_out, wout, preferred_element_type=F32)
    grad_blocks = exchange(pack(by_group(grad_attended.astype(BF16), 1)))
    by_part = grad_wfc.astype(BF16).reshape(devices, shard_rows, parts, width)
    send_b, keep_b = split_cores(
        [
            grad_wout.astype(BF16).reshape(devices, -1, width),
            by_part.transpose(0, 2, 1, 3).reshape(devices, -1, width),
            grad_wproj.astype(BF16).reshape(devices, -1, width),
        ]
    )
    own_b = scatter_sum(send_b, keep_b)

    grad_back = attend_backward(
        whole, grad_blocks.reshape(-1, 2 * group), stats, heads, head_size, block
    )
    grad_qkv = from_group(exchange(grad_back.reshape(count, block, 3 * group)), 3)
    grad_bqv = jnp.concatenate(
        [
            jnp.sum(grad_qkv[:, :width], 0, dtype=F32),
            jnp.sum(grad_qkv[:, 2 * width :], 0, dtype=F32),
        ]
    )
    grad_wqkv = jnp.einsum("td,te->de", normed1, grad_qkv, preferred_element_type=F32)
    grad_normed1 = jnp.einsum("te,de->td", grad_qkv, wqkv, preferred_element_type=F32)
    _, norm1_back = jax.vjp(norm_affine, rows, gain1, bias1)
    grad_in_part, grad_gain1, grad_bias1 = norm1_back(grad_normed1)
    grad_inputs = (grad_middle + grad_in_part).astype(BF16).reshape(inputs.shape)
    grads = (
        grad_gain1,
        grad_bias1,
        grad_bqv,
        grad_bout,
        grad_gain2,
        grad_bias2,
        grad_bfc,
        grad_bproj,
    )
    small_grads = pack_small([grad.reshape(1, -1) for grad in grads], sizes, devices)
    by_part = grad_wqkv.astype(BF16).reshape(devices, shard_rows, 3, width)
    send_a, keep_a = split_cores(
        [
            by_part.transpose(0, 2, 1, 3).reshape(devices, -1, width),
            jnp.pad(small_grads, ((0, 0), (0, 0), (0, width - LANES))),
        ]
    )
    own_a = scatter_sum(send_a, keep_a)
    own_small = own_a[3 * shard_rows :]
    own = [own_small[i, :size] for i, size in enumerate(sizes)]

    def by_row(value, parts):
        return value.reshape(parts, shard_rows, width).transpose(1, 0, 2).reshape(-1)

    own_fc = own_b[shard_rows : (1 + parts) * shard_rows]
    return (
        outputs,
        grad_inputs,
        own[0],
        own[1],
        by_row(own_a[: 3 * shard_rows], 3),
        own[2],
        own_b[:shard_rows].reshape(-1),
        own[3],
        own[4],
        own[5],
        by_row(own_fc, parts),
        own[6],
        own_b[(1 + parts) * shard_rows :].reshape(-1),
        own[7],
    )


def solution(mesh):
    token_spec = P("dp", "seq", None)
    flat_spec = P(("dp", "seq"))
    in_specs = (token_spec, P("dp", "seq"), token_spec) + (flat_spec,) * 12
    out_specs = (token_spec, token_spec) + (flat_spec,) * 12
    return jax.shard_map(
        on_device, mesh=mesh, in_specs=in_specs, out_specs=out_specs, check_vma=False
    )
```

```python
import functools

import jax
import jax.numpy as jnp
from jax import lax
from jax.experimental import pallas as pl
from jax.experimental.pallas import tpu as pltpu
from jax.sharding import PartitionSpec as P

HEADS = 12
CORES = 2


EPSILON = 1e-05
MASKED = -1e30
F32 = jnp.float32
BF16 = jnp.bfloat16


def norm_affine(values, gain, bias):
    center = jnp.mean(values, -1, keepdims=True)
    centered = values - center
    variance = jnp.mean(centered * centered, -1, keepdims=True)
    return centered * lax.rsqrt(variance + EPSILON) * gain + bias


def shift_z(value, step):
    size = lax.axis_size("seq")
    return lax.ppermute(value, "seq", [(i, (i + CORES * step) % size) for i in range(size)])


def swap_core(value):
    size = lax.axis_size("seq")
    return lax.ppermute(value, "seq", [(i, i ^ 1) for i in range(size)])


def swap_dp(value, bit):
    size = lax.axis_size("dp")
    return lax.ppermute(value, "dp", [(i, i ^ bit) for i in range(size)])


def ordered(flag, mine, other, axis):
    first = jnp.where(flag == 0, mine, other)
    second = jnp.where(flag == 0, other, mine)
    return jnp.stack([first, second], axis)


def roll_blocks(pieces, place):
    count = len(pieces)
    stacked = jnp.stack(pieces)
    twice = jnp.concatenate([stacked, stacked])
    return lax.dynamic_slice_in_dim(twice, lax.rem(count - place, count), count, 0)


def gather_z(shard):
    heights = lax.axis_size("seq") // CORES
    level = lax.axis_index("seq") // CORES
    pieces = [shard] + [shift_z(shard, -step) for step in range(1, heights)]
    return roll_blocks(pieces, level)


def swap_z(value, bit):
    size = lax.axis_size("seq")
    return lax.ppermute(value, "seq", [(i, i ^ (CORES * bit)) for i in range(size)])


def gather_plane(tower):
    heights = tower.shape[0]
    shard = tower.shape[1:]
    if lax.axis_size("dp") == 4:
        plane = lax.axis_index("dp")
        y, x = plane // 2, plane % 2
        low, high = tower[: heights // 2], tower[heights // 2 :]
        low_x = ordered(x, low, swap_dp(low, 1), 0)
        high_y = ordered(y, high, swap_dp(high, 2), 0)
        low_all = ordered(y, low_x, swap_dp(low_x, 2), 0)
        high_all = ordered(x, high_y, swap_dp(high_y, 1), 1)
        half = jnp.concatenate([low_all, high_all], 2)
    else:
        half = lax.all_gather(tower, "dp", axis=0, tiled=False)
    return half.reshape(-1, *shard)


def pick(value, index, axis):
    return lax.dynamic_index_in_dim(value, index, axis, keepdims=False)


def split_cores(parts):
    core = lax.axis_index("seq") % CORES
    parts = [part.reshape(-1, CORES, *part.shape[1:]) for part in parts]
    send = jnp.concatenate([pick(part, 1 - core, 1) for part in parts], 1)
    keep = jnp.concatenate([pick(part, core, 1) for part in parts], 1)
    return send, keep


def add(mine, other):
    return (mine.astype(F32) + other.astype(F32)).astype(mine.dtype)


def scatter_plane(split):
    rows, columns = split.shape[1:]
    planes = lax.axis_size("dp")
    heights = lax.axis_size("seq") // CORES
    if planes == 4:
        plane = lax.axis_index("dp")
        y, x = plane // 2, plane % 2
        split = split.reshape(2, 2, heights, rows, columns)
        low, high = split[:, :, : heights // 2], split[:, :, heights // 2 :]
        low = add(pick(low, y, 0), swap_dp(pick(low, 1 - y, 0), 2))
        high = add(pick(high, x, 1), swap_dp(pick(high, 1 - x, 1), 1))
        low = add(pick(low, x, 0), swap_dp(pick(low, 1 - x, 0), 1))
        high = add(pick(high, y, 0), swap_dp(pick(high, 1 - y, 0), 2))
        return jnp.concatenate([low, high], 0)
    split = split.reshape(planes, heights, rows, columns)
    return lax.psum_scatter(split, "dp", scatter_dimension=0, tiled=False)


def scatter_z(tower):
    heights = tower.shape[0]
    level = lax.axis_index("seq") // CORES
    mine = pick(tower, level, 0).astype(F32)
    for step in range(1, heights):
        mine += shift_z(pick(tower, lax.rem(level + step, heights), 0), step).astype(F32)
    return mine


def z_bits():
    heights = lax.axis_size("seq") // CORES
    level = lax.axis_index("seq") // CORES
    top = heights // 2
    return level, top, level // top


def gather_sequence(blocks):
    level, top, half = z_bits()
    core = lax.axis_index("seq") % CORES
    held = ordered(half, pick(blocks, half, 0), swap_z(pick(blocks, 1 - half, 0), top), 0)
    axis, bit = 1, top // 2
    while bit:
        held = ordered(level // bit % 2, held, swap_z(held, bit), axis)
        axis, bit = axis + 1, bit // 2
    return ordered(core, held, swap_core(held), axis).reshape(-1, *blocks.shape[1:])


def scatter_sequence(partial):
    level, top, half = z_bits()
    core = lax.axis_index("seq") % CORES
    shape = partial.shape[1:]
    count = top.bit_length()
    held = partial.reshape(*[2] * (count + 1), *shape)
    held = add(pick(held, core, count), swap_core(pick(held, 1 - core, count)))
    axis, bit = count - 1, 1
    while bit < top:
        flag = level // bit % 2
        held = add(pick(held, flag, axis), swap_z(pick(held, 1 - flag, axis), bit))
        axis, bit = axis - 1, bit * 2
    return ordered(half, pick(held, half, 0), swap_z(pick(held, 1 - half, 0), top), 0)


def gather_columns(blocks):
    level, top, half = z_bits()
    shape = blocks.shape[1:]
    count = top.bit_length() - 1
    held = blocks.reshape(*[2] * count, *shape)
    bit = top // 2
    while bit:
        flag = level // bit % 2
        got = swap_z(pick(held, 1 - flag, 0), bit)
        held = ordered(flag, pick(held, flag, 0), got, count - 1)
        bit //= 2
    return ordered(half, held, swap_z(held, top), 0).reshape(-1, *shape)


def scatter_columns(tower):
    level, top, half = z_bits()
    shape = tower.shape[1:]
    count = top.bit_length() - 1
    held = tower.reshape(*[2] * (count + 1), *shape)
    held = add(pick(held, half, 0), swap_z(pick(held, 1 - half, 0), top))
    bit = 1
    while bit < top:
        flag = level // bit % 2
        got = swap_z(pick(held, 1 - flag, count - 1), bit)
        held = ordered(flag, pick(held, flag, count - 1), got, 0)
        bit *= 2
    return held.reshape(-1, *shape).astype(F32)


def exchange(blocks):
    return lax.all_to_all(blocks, "seq", split_axis=0, concat_axis=0, tiled=True)


ROWS = 8
LANES = 128


def vmem_specs(count):
    return [pl.BlockSpec(memory_space=pltpu.VMEM) for _ in range(count)]


def place_lanes(size, total):
    source = lax.broadcasted_iota(jnp.int32, (LANES, total), 0)
    target = lax.rem(lax.broadcasted_iota(jnp.int32, (LANES, total), 1), size)
    return jnp.where(source == target, 1.0, 0.0).astype(BF16)


def owned_lanes(devices, size):
    device = lax.broadcasted_iota(jnp.int32, (devices, devices * size), 0)
    lane = lax.broadcasted_iota(jnp.int32, (devices, devices * size), 1)
    offset = lane - device * size
    return (offset >= 0) & (offset < size)


def unpack_kernel(sizes, small_ref, *outs):
    devices = small_ref.shape[0]
    small = small_ref[...].astype(F32)
    for i, (size, out) in enumerate(zip(sizes, outs)):
        spread = jnp.dot(
            small[:, i, :].astype(BF16),
            place_lanes(size, devices * size),
            preferred_element_type=F32,
        )
        out[...] = jnp.sum(jnp.where(owned_lanes(devices, size), spread, 0.0), 0, keepdims=True)


def unpack_small(small, sizes):
    devices = small.shape[0]
    return pl.pallas_call(
        functools.partial(unpack_kernel, sizes),
        out_shape=[jax.ShapeDtypeStruct((1, devices * size), F32) for size in sizes],
        in_specs=vmem_specs(1),
        out_specs=vmem_specs(len(sizes)),
        compiler_params=pltpu.CompilerParams(vmem_limit_bytes=32 * 2**20),
    )(small)


def pack_kernel(sizes, *refs):
    grads, packed, rows = refs[: len(sizes)], refs[len(sizes)], refs[len(sizes) + 1]
    devices = packed.shape[0]
    for i, (size, grad) in enumerate(zip(sizes, grads)):
        owned = jnp.where(owned_lanes(devices, size), grad[...], 0.0).astype(BF16)
        rows[:, i, :] = lax.dot_general(
            owned,
            place_lanes(size, devices * size),
            (((1,), (1,)), ((), ())),
            preferred_element_type=F32,
        )
    packed[...] = rows[...].astype(BF16)


def pack_small(grads, sizes, devices):
    return pl.pallas_call(
        functools.partial(pack_kernel, sizes),
        out_shape=jax.ShapeDtypeStruct((devices, ROWS, LANES), BF16),
        in_specs=vmem_specs(len(sizes)),
        out_specs=vmem_specs(1)[0],
        scratch_shapes=[pltpu.VMEM((devices, ROWS, LANES), F32)],
        compiler_params=pltpu.CompilerParams(vmem_limit_bytes=32 * 2**20),
    )(*grads)


def stack_kernel(out_ref, fc_ref, proj_ref, after_ref, stacked):
    width = out_ref.shape[1]
    stacked[0] = out_ref[...]
    parts = fc_ref.shape[1] // width
    for i in range(parts):
        stacked[1 + i] = fc_ref[:, i * width : (i + 1) * width]
    for i in range(parts):
        stacked[1 + parts + i] = proj_ref[i]


def stack_weights(w_out, w_fc, w_proj, after):
    rows, width = w_out.shape
    parts = w_fc.shape[1] // width
    return pl.pallas_call(
        stack_kernel,
        out_shape=jax.ShapeDtypeStruct((1 + 2 * parts, rows, width), BF16),
        in_specs=vmem_specs(3) + [pl.BlockSpec(memory_space=pl.ANY)],
        out_specs=vmem_specs(1)[0],
    )(w_out, w_fc, w_proj, after)


def spread_kernel(parts, half, other, out_ref, fc_ref, proj_ref, sems):
    core = lax.rem(lax.axis_index("seq"), CORES)
    copies = []
    for source, place in ((half, core), (other, 1 - core)):
        pairs = [(source.at[:, 0], out_ref.at[:, place])]
        pairs += [(source.at[:, 1 + i], fc_ref.at[i, :, place]) for i in range(parts)]
        pairs += [(source.at[:, pl.ds(1 + parts, parts)], proj_ref.at[:, place])]
        for pair in pairs:
            copies.append(pltpu.make_async_copy(*pair, sems.at[len(copies)]))
    for copy in copies:
        copy.start()
    for copy in copies:
        copy.wait()


def spread_weights(half, other):
    chips, kinds, rows, width = half.shape
    parts = (kinds - 1) // 2
    anywhere = pl.BlockSpec(memory_space=pl.ANY)
    wout, wfc, wproj = pl.pallas_call(
        functools.partial(spread_kernel, parts),
        out_shape=[
            jax.ShapeDtypeStruct((chips, CORES, rows, width), BF16),
            jax.ShapeDtypeStruct((parts, chips, CORES, rows, width), BF16),
            jax.ShapeDtypeStruct((chips, CORES, parts, rows, width), BF16),
        ],
        in_specs=[anywhere] * 2,
        out_specs=[anywhere] * 3,
        scratch_shapes=[pltpu.SemaphoreType.DMA((2 * (parts + 2),))],
    )(half, other)
    return (
        wout.reshape(width, width),
        wfc.reshape(parts, width, width),
        wproj.reshape(parts, width, width),
    )


def masked_scores(keys, queries, id_column, id_row, first):
    scores = lax.dot_general(keys, queries, (((1,), (1,)), ((), ())), preferred_element_type=F32)
    key_pos = lax.broadcasted_iota(jnp.int32, scores.shape, 0)
    query_pos = lax.broadcasted_iota(jnp.int32, scores.shape, 1) + first
    allowed = (key_pos <= query_pos) & (id_column == id_row)
    return jnp.where(allowed, scores, MASKED)


def column_of(id_row):
    length = id_row.shape[1]
    return jnp.broadcast_to(id_row, (LANES, length)).T[:, :1]


def forward_kernel(
    heads,
    head_size,
    step_rows,
    block,
    rows_ref,
    weight,
    gain,
    bias,
    qkv_bias,
    out,
    stats,
    whole,
    normed,
    ids,
    result,
):
    length = whole.shape[0]
    group = heads * head_size
    for i in range(length // block):
        rows = norm_affine(rows_ref[i, :block, :].astype(F32), gain[...], bias[...])
        normed[i * block : (i + 1) * block, :] = rows.astype(BF16)
    id_rows = [rows_ref[i, block:, :block].astype(F32)[:1] for i in range(length // block)]
    id_row = jnp.concatenate(id_rows, 1)
    ids[...] = id_row
    id_column = column_of(id_row)
    for first in range(0, length, step_rows):
        last = first + step_rows
        product = jnp.dot(normed[first:last, :], weight[...], preferred_element_type=F32)
        whole[first:last, :] = (product + qkv_bias[...]).astype(BF16)
    values_t = whole[:, 2 * group : 3 * group].astype(F32).T.astype(BF16)
    for first in range(0, length, step_rows):
        last = first + step_rows
        tops = []
        for head in range(heads):
            lo = head * head_size
            queries = whole[first:last, lo : lo + head_size] * BF16(head_size**-0.5)
            keys = whole[:last, group + lo : group + lo + head_size]
            scores = masked_scores(keys, queries, id_column[:last], id_row[:, first:last], first)
            highest = jnp.max(scores, 0, keepdims=True)
            weights = jnp.exp(scores - highest)
            total = jnp.sum(weights, 0, keepdims=True)
            probs = (weights * (1.0 / total)).astype(BF16)
            tops.append(
                jnp.dot(
                    values_t[lo : lo + head_size, :last], probs, preferred_element_type=F32
                )
            )
            stats[head : head + 1, first:last] = highest + jnp.log(total)
        result[first:last, :] = jnp.concatenate(tops, 0).T.astype(BF16)
    half = block // 2
    for start in range(0, length, block):
        out[start // 2 : start // 2 + half, :group] = result[start : start + half, :]
        out[start // 2 : start // 2 + half, group:] = result[start + half : start + block, :]


def backward_kernel(
    heads,
    head_size,
    step_rows,
    block,
    whole,
    grads,
    stats,
    ids,
    out,
    grad_out,
    grad_query,
    grad_key,
    grad_value,
):
    length = whole.shape[0]
    group = heads * head_size
    half = block // 2
    for start in range(0, length, block):
        packed = grads[start // 2 : start // 2 + half, :]
        grad_out[start : start + half, :] = packed[:, :group]
        grad_out[start + half : start + block, :] = packed[:, group:]
    id_row = ids[...]
    id_column = column_of(id_row)
    keys_t = whole[:, group : 2 * group].astype(F32).T.astype(BF16)
    factor = head_size**-0.5
    grad_key[...] = jnp.zeros_like(grad_key)
    grad_value[...] = jnp.zeros_like(grad_value)
    for first in range(0, length, step_rows):
        last = first + step_rows
        tops = []
        for head in range(heads):
            lo = head * head_size
            queries = whole[first:last, lo : lo + head_size] * BF16(factor)
            keys = whole[:last, group + lo : group + lo + head_size]
            values = whole[:last, 2 * group + lo : 2 * group + lo + head_size]
            grad = grad_out[first:last, lo : lo + head_size]
            scores = masked_scores(keys, queries, id_column[:last], id_row[:, first:last], first)
            probs = jnp.exp(scores - stats[head : head + 1, first:last])
            grad_probs = lax.dot_general(
                values, grad, (((1,), (1,)), ((), ())), preferred_element_type=F32
            )
            delta = jnp.sum(probs * grad_probs, 0, keepdims=True)
            grad_scores = (probs * (grad_probs - delta)).astype(BF16)
            tops.append(
                jnp.dot(
                    keys_t[lo : lo + head_size, :last], grad_scores, preferred_element_type=F32
                )
                * factor
            )
            grad_key[head, :last, :] += jnp.dot(
                grad_scores, queries, preferred_element_type=F32
            )
            grad_value[head, :last, :] += jnp.dot(
                probs.astype(BF16), grad, preferred_element_type=F32
            )
        grad_query[first:last, :] = jnp.concatenate(tops, 0).T.astype(BF16)
    out[:, :group] = grad_query[...]
    for head in range(heads):
        lo = head * head_size
        out[:, group + lo : group + lo + head_size] = grad_key[head].astype(BF16)
        out[:, 2 * group + lo : 2 * group + lo + head_size] = grad_value[head].astype(BF16)


def attend_forward(rows, weight, gain, bias, qkv_bias, heads, head_size, block):
    length = rows.shape[0] * block
    width = rows.shape[2]
    group = heads * head_size
    pairs = length * length // 2 * heads
    return pl.pallas_call(
        functools.partial(forward_kernel, heads, head_size, min(256, length), block),
        out_shape=[
            jax.ShapeDtypeStruct((length // 2, 2 * group), BF16),
            jax.ShapeDtypeStruct((heads, length), F32),
            jax.ShapeDtypeStruct((length, 3 * group), BF16),
            jax.ShapeDtypeStruct((length, width), BF16),
            jax.ShapeDtypeStruct((1, length), F32),
        ],
        in_specs=vmem_specs(5),
        out_specs=vmem_specs(5),
        scratch_shapes=[pltpu.VMEM((length, group), BF16)],
        compiler_params=pltpu.CompilerParams(vmem_limit_bytes=48 * 2**20),
        cost_estimate=pl.CostEstimate(
            flops=pairs * head_size * 4 + length * width * group * 6,
            bytes_accessed=length * width * 8,
            transcendentals=pairs,
        ),
    )(rows, weight, gain, bias, qkv_bias)


def attend_backward(whole, grads, stats, ids, heads, head_size, block):
    length, width = whole.shape
    group = heads * head_size
    pairs = length * length // 2 * heads
    return pl.pallas_call(
        functools.partial(backward_kernel, heads, head_size, min(256, length), block),
        out_shape=jax.ShapeDtypeStruct((length, 3 * group), BF16),
        in_specs=vmem_specs(4),
        out_specs=vmem_specs(1)[0],
        scratch_shapes=[
            pltpu.VMEM((length, group), BF16),
            pltpu.VMEM((length, group), BF16),
            pltpu.VMEM((heads, length, head_size), F32),
            pltpu.VMEM((heads, length, head_size), F32),
        ],
        compiler_params=pltpu.CompilerParams(vmem_limit_bytes=48 * 2**20),
        cost_estimate=pl.CostEstimate(
            flops=pairs * head_size * 10, bytes_accessed=length * width * 6, transcendentals=pairs
        ),
    )(whole, grads, stats, ids)


def on_device(
    inputs,
    segments,
    cotangent,
    ln1_gain,
    ln1_bias,
    w_qkv,
    b_qv,
    w_out,
    b_out,
    ln2_gain,
    ln2_bias,
    w_fc,
    b_fc,
    w_proj,
    b_proj,
):
    seq_count, block, width = inputs.shape
    head_size = width // HEADS
    tokens = seq_count * block
    count = lax.axis_size("seq")
    devices = count * lax.axis_size("dp")
    groups = count // seq_count
    heads = -(-HEADS // groups)
    spare = groups * heads - HEADS
    group = heads * head_size

    vectors = (ln1_gain, ln1_bias, b_qv, b_out, ln2_gain, ln2_bias, b_fc, b_proj)
    sizes = tuple(vector.shape[0] for vector in vectors)
    shard_rows = w_out.shape[0] // width
    parts = w_fc.shape[0] // w_out.shape[0]
    small = jnp.concatenate(
        [jnp.pad(vector[None], ((0, 0), (0, 3 * group - vector.shape[0]))) for vector in vectors]
    )
    classes = groups // CORES
    place = lax.axis_index("seq")
    core = place % CORES
    group_index = place % groups

    def by_head(value, axis):
        if not spare:
            return value
        pads = [(0, 0)] * value.ndim
        pads[axis] = (0, spare)
        return jnp.pad(value, pads)

    marks = jnp.pad(segments.astype(BF16)[:, None], ((0, 0), (0, 15), (0, width - block)))
    sequence = gather_sequence(jnp.concatenate([inputs, marks], 1))

    columns = by_head(w_qkv.reshape(shard_rows, 3, HEADS, head_size), 2)
    columns = columns.reshape(shard_rows, 3, classes, CORES, group).transpose(2, 0, 3, 1, 4)
    columns = columns.reshape(classes, shard_rows, CORES * 3 * group)
    extra = jnp.broadcast_to(jnp.concatenate([small] * CORES, 1), (classes, ROWS, 6 * group))
    tower_a = gather_columns(jnp.concatenate([columns, extra], 1))
    stacked = stack_weights(
        w_out.reshape(-1, width),
        w_fc.reshape(-1, parts * width),
        w_proj.reshape(parts, -1, width),
        tower_a,
    )
    tower_b = gather_z(stacked)
    half_a = gather_plane(tower_a)
    left, right = half_a[..., : 3 * group], half_a[..., 3 * group :]
    mine_a = jnp.where(core == 0, left, right)
    whole_a = ordered(core, mine_a, swap_core(jnp.where(core == 0, right, left)), 1)
    whole_a = whole_a.reshape(devices, shard_rows + ROWS, 3 * group)
    wqkv = whole_a[:, :shard_rows].reshape(width, 3 * group)
    gain1, bias1, bqv, bout, gain2, bias2, bfc, bproj = unpack_small(
        whole_a[:, shard_rows:, :LANES], sizes
    )
    half_b = gather_plane(tower_b)
    wout, wfc, wproj = spread_weights(half_b, swap_core(half_b))

    both = by_head(bqv.reshape(2, HEADS, head_size), 1).reshape(2, groups, group)
    both = pick(both, group_index, 1)
    qkv_bias = jnp.concatenate([both[0], jnp.zeros((group,), F32), both[1]]).reshape(1, -1)
    attended, stats, qkv, normed1, ids = attend_forward(
        sequence, wqkv, gain1, bias1, qkv_bias, heads, head_size, block
    )
    attended = exchange(attended.reshape(count, block // 2, 2 * group))
    attended = attended.reshape(seq_count, groups, block // 2, 2, heads, head_size)
    attended = attended.transpose(0, 3, 2, 1, 4, 5).reshape(tokens, groups * heads, head_size)
    attended_rows = attended[:, :HEADS].reshape(tokens, width)

    rows = inputs.astype(F32).reshape(tokens, width)
    middle = rows + (jnp.dot(attended_rows, wout, preferred_element_type=F32) + bout)
    normed2 = norm_affine(middle, gain2, bias2).astype(BF16)
    bfc_parts = bfc.reshape(parts, 1, width)
    hidden_pre = jnp.einsum("td,qde->qte", normed2, wfc, preferred_element_type=F32) + bfc_parts
    hidden = jax.nn.gelu(hidden_pre, approximate=True).astype(BF16)
    projected = jnp.einsum("qte,qed->td", hidden, wproj, preferred_element_type=F32)
    outputs = (middle + (projected + bproj)).astype(BF16).reshape(inputs.shape)

    grad_rows = cotangent.astype(F32).reshape(tokens, width)
    grad_branch = cotangent.reshape(tokens, width)
    grad_bproj = jnp.sum(grad_branch, 0, dtype=F32)
    grad_wproj = jnp.einsum("qte,td->qed", hidden, grad_branch, preferred_element_type=F32)
    grad_hidden = jnp.einsum("td,qed->qte", grad_branch, wproj, preferred_element_type=F32)
    _, gelu_back = jax.vjp(lambda value: jax.nn.gelu(value, approximate=True), hidden_pre)
    grad_pre = gelu_back(grad_hidden)[0].astype(BF16)
    grad_bfc = jnp.sum(grad_pre, 1, dtype=F32)
    grad_wfc = jnp.einsum("td,qte->qde", normed2, grad_pre, preferred_element_type=F32)
    grad_normed2 = jnp.einsum("qte,qde->td", grad_pre, wfc, preferred_element_type=F32)
    _, norm2_back = jax.vjp(norm_affine, middle, gain2, bias2)
    grad_mid_part, grad_gain2, grad_bias2 = norm2_back(grad_normed2)
    grad_middle = grad_rows + grad_mid_part
    grad_attn_out = grad_middle.astype(BF16)
    grad_bout = jnp.sum(grad_attn_out, 0, dtype=F32)
    grad_wout = jnp.einsum("td,te->de", attended_rows, grad_attn_out, preferred_element_type=F32)
    grad_attended = jnp.einsum("te,de->td", grad_attn_out, wout, preferred_element_type=F32)
    grad_attended = by_head(
        grad_attended.astype(BF16).reshape(seq_count, 2, block // 2, HEADS, head_size), 3
    )
    grad_blocks = grad_attended.reshape(seq_count, 2, block // 2, groups, group)
    grad_blocks = grad_blocks.transpose(0, 3, 2, 1, 4).reshape(count, block // 2, 2 * group)
    grad_blocks = exchange(grad_blocks).reshape(-1, 2 * group)

    def blocks_of(value, rows):
        return value.astype(BF16).reshape(devices, rows, -1)

    send_b, keep_b = split_cores(
        [blocks_of(grad_wout, shard_rows)]
        + [blocks_of(grad_wfc[i], shard_rows) for i in range(parts)]
        + [blocks_of(grad_wproj, parts * shard_rows)]
    )
    tower_b = scatter_plane(add(keep_b, swap_core(send_b)))
    own_b = scatter_z(tower_b)

    grad_qkv = attend_backward(qkv, grad_blocks, stats, ids, heads, head_size, block)
    grad_normed1 = lax.dot_general(
        grad_qkv, wqkv, (((1,), (1,)), ((), ())), preferred_element_type=F32
    )
    own_normed1 = scatter_sequence(grad_normed1.astype(BF16).reshape(count, block, width))
    _, norm1_back = jax.vjp(lambda value: norm_affine(value, gain1, bias1), rows)
    (grad_in_part,) = norm1_back(own_normed1.astype(F32).reshape(tokens, width))
    grad_inputs = (grad_middle + grad_in_part).astype(BF16).reshape(inputs.shape)

    long_rows = sequence[:, :block].astype(F32).reshape(count * block, width)
    _, norm1_long_back = jax.vjp(lambda g, b: norm_affine(long_rows, g, b), gain1, bias1)
    grad_gain1, grad_bias1 = norm1_long_back(grad_normed1)
    grad_wqkv = lax.dot_general(
        normed1, grad_qkv, (((0,), (0,)), ((), ())), preferred_element_type=F32
    )
    sums = jnp.sum(grad_qkv, 0, dtype=F32).reshape(3, group)
    here = (jnp.arange(groups) == group_index)[None, :, None]
    grad_bqv = jnp.where(here, jnp.stack([sums[0], sums[2]])[:, None], 0.0)
    grad_bqv = grad_bqv.reshape(2, groups * heads, head_size)[:, :HEADS]
    grads = (
        grad_gain1,
        grad_bias1,
        grad_bqv,
        grad_bout,
        grad_gain2,
        grad_bias2,
        grad_bfc,
        grad_bproj,
    )
    small_grads = pack_small([grad.reshape(1, -1) for grad in grads], sizes, devices)
    small_grads = jnp.pad(small_grads, ((0, 0), (0, 0), (0, 3 * group - LANES)))
    send_a, keep_a = split_cores([blocks_of(grad_wqkv, shard_rows), small_grads])
    got_a = swap_core(send_a)
    pair_a = jnp.concatenate(
        [jnp.where(core == 0, keep_a, got_a), jnp.where(core == 0, got_a, keep_a)], -1
    )
    own_a = scatter_columns(scatter_plane(pair_a))
    own_small = jnp.sum(
        own_a[:, shard_rows:].reshape(classes, ROWS, CORES, 3 * group)[..., :LANES], (0, 2)
    )
    own = [own_small[i, :size] for i, size in enumerate(sizes)]
    own_qkv = own_a[:, :shard_rows].reshape(classes, shard_rows, CORES, 3, group)
    own_qkv = own_qkv.transpose(1, 3, 0, 2, 4).reshape(shard_rows, 3, groups * heads, head_size)
    own_qkv = own_qkv[:, :, :HEADS].reshape(-1)
    own_fc = own_b[shard_rows : (1 + parts) * shard_rows].reshape(parts, shard_rows, width)
    return (
        outputs,
        grad_inputs,
        own[0],
        own[1],
        own_qkv,
        own[2],
        own_b[:shard_rows].reshape(-1),
        own[3],
        own[4],
        own[5],
        own_fc.transpose(1, 0, 2).reshape(-1),
        own[6],
        own_b[(1 + parts) * shard_rows :].reshape(-1),
        own[7],
    )


def solution(mesh):
    token_spec = P("dp", "seq", None)
    flat_spec = P(("dp", "seq"))
    in_specs = (token_spec, P("dp", "seq"), token_spec) + (flat_spec,) * 12
    out_specs = (token_spec, token_spec) + (flat_spec,) * 12
    return jax.shard_map(
        on_device, mesh=mesh, in_specs=in_specs, out_specs=out_specs, check_vma=False
    )
```

```python
import functools
import math

import jax
import jax.numpy as jnp
from jax import lax
from jax.experimental import pallas as pl
from jax.experimental.pallas import tpu as pltpu
from jax.sharding import PartitionSpec as P

HEADS = 12
CORES = 2


EPSILON = 1e-05
MASKED = -1e30
F32 = jnp.float32
BF16 = jnp.bfloat16


def norm_affine(values, gain, bias):
    center = jnp.mean(values, -1, keepdims=True)
    centered = values - center
    variance = jnp.mean(centered * centered, -1, keepdims=True)
    return centered * lax.rsqrt(variance + EPSILON) * gain + bias


def shift_z(value, step):
    size = lax.axis_size("seq")
    return lax.ppermute(value, "seq", [(i, (i + CORES * step) % size) for i in range(size)])


def swap_core(value):
    size = lax.axis_size("seq")
    return lax.ppermute(value, "seq", [(i, i ^ 1) for i in range(size)])


def swap_dp(value, bit):
    size = lax.axis_size("dp")
    return lax.ppermute(value, "dp", [(i, i ^ bit) for i in range(size)])


def ordered(flag, mine, other, axis):
    first = jnp.where(flag == 0, mine, other)
    second = jnp.where(flag == 0, other, mine)
    return jnp.stack([first, second], axis)


def roll_blocks(pieces, place):
    count = len(pieces)
    stacked = jnp.stack(pieces)
    twice = jnp.concatenate([stacked, stacked])
    return lax.dynamic_slice_in_dim(twice, lax.rem(count - place, count), count, 0)


def z_pieces(shard):
    heights = lax.axis_size("seq") // CORES
    return [shard] + [shift_z(shard, -step) for step in range(1, heights)]


def swap_z(value, bit):
    size = lax.axis_size("seq")
    return lax.ppermute(value, "seq", [(i, i ^ (CORES * bit)) for i in range(size)])


def gather_plane(low, high, axis):
    if lax.axis_size("dp") == 4:
        plane = lax.axis_index("dp")
        y, x = plane // 2, plane % 2
        low_x = ordered(x, low, swap_dp(low, 1), axis)
        high_y = ordered(y, high, swap_dp(high, 2), axis)
        low_all = ordered(y, low_x, swap_dp(low_x, 2), axis)
        high_all = ordered(x, high_y, swap_dp(high_y, 1), axis + 1)
        half = jnp.concatenate([low_all, high_all], axis + 2)
        count = 4 * half.shape[axis + 2]
    else:
        tower = jnp.concatenate([low, high], axis)
        half = lax.all_gather(tower, "dp", axis=axis, tiled=True)
        return half
    return half.reshape(*low.shape[:axis], count, *low.shape[axis + 1 :])


def pick(value, index, axis):
    return lax.dynamic_index_in_dim(value, index, axis, keepdims=False)


def add(mine, other):
    return (mine.astype(F32) + other.astype(F32)).astype(mine.dtype)


def scatter_plane(split, axis):
    planes = lax.axis_size("dp")
    heights = lax.axis_size("seq") // CORES
    if planes == 4:
        plane = lax.axis_index("dp")
        y, x = plane // 2, plane % 2
        split = split.reshape(
            *split.shape[:axis], 2, 2, heights, *split.shape[axis + 1 :]
        )
        low = lax.slice_in_dim(split, 0, heights // 2, axis=axis + 2)
        high = lax.slice_in_dim(split, heights // 2, heights, axis=axis + 2)
        low = add(pick(low, y, axis), swap_dp(pick(low, 1 - y, axis), 2))
        high = add(pick(high, x, axis + 1), swap_dp(pick(high, 1 - x, axis + 1), 1))
        low = add(pick(low, x, axis), swap_dp(pick(low, 1 - x, axis), 1))
        high = add(pick(high, y, axis), swap_dp(pick(high, 1 - y, axis), 2))
        return jnp.concatenate([low, high], axis)
    return lax.psum_scatter(split, "dp", scatter_dimension=axis, tiled=True)


def scatter_z(tower, axis):
    heights = lax.axis_size("seq") // CORES
    level = lax.axis_index("seq") // CORES
    mine = pick(tower, level, axis).astype(F32)
    for step in range(1, heights):
        mine += shift_z(pick(tower, lax.rem(level + step, heights), axis), step).astype(F32)
    return mine


def z_bits():
    heights = lax.axis_size("seq") // CORES
    level = lax.axis_index("seq") // CORES
    top = heights // 2
    return level, top, level // top


def gather_sequence(blocks):
    level, top, half = z_bits()
    core = lax.axis_index("seq") % CORES
    held = ordered(half, pick(blocks, half, 0), swap_z(pick(blocks, 1 - half, 0), top), 0)
    early = held
    axis, bit = 1, top // 2
    while bit:
        held = ordered(level // bit % 2, held, swap_z(held, bit), axis)
        axis, bit = axis + 1, bit // 2
    return early, ordered(core, held, swap_core(held), axis).reshape(-1, *blocks.shape[1:])


def scatter_sequence(partial):
    level, top, half = z_bits()
    core = lax.axis_index("seq") % CORES
    shape = partial.shape[1:]
    count = top.bit_length()
    held = partial.reshape(*[2] * (count + 1), *shape)
    held = add(pick(held, core, count), swap_core(pick(held, 1 - core, count)))
    axis, bit = count - 1, 1
    while bit < top:
        flag = level // bit % 2
        held = add(pick(held, flag, axis), swap_z(pick(held, 1 - flag, axis), bit))
        axis, bit = axis - 1, bit * 2
    return ordered(half, pick(held, half, 0), swap_z(pick(held, 1 - half, 0), top), 0)


def gather_columns(blocks):
    level, top, half = z_bits()
    shape = blocks.shape[1:]
    count = top.bit_length() - 1
    held = blocks.reshape(*[2] * count, *shape)
    bit = top // 2
    while bit:
        flag = level // bit % 2
        got = swap_z(pick(held, 1 - flag, 0), bit)
        held = ordered(flag, pick(held, flag, 0), got, count - 1)
        bit //= 2
    return ordered(half, held, swap_z(held, top), 0).reshape(-1, *shape)


def scatter_columns(tower):
    level, top, half = z_bits()
    shape = tower.shape[1:]
    count = top.bit_length() - 1
    held = tower.reshape(*[2] * (count + 1), *shape)
    held = add(pick(held, half, 0), swap_z(pick(held, 1 - half, 0), top))
    bit = 1
    while bit < top:
        flag = level // bit % 2
        got = swap_z(pick(held, 1 - flag, count - 1), bit)
        held = ordered(flag, pick(held, flag, count - 1), got, 0)
        bit *= 2
    return held.reshape(-1, *shape).astype(F32)


def exchange(blocks):
    return lax.all_to_all(blocks, "seq", split_axis=0, concat_axis=0, tiled=True)


ROWS = 8
LANES = 128


def vmem_specs(count):
    return [pl.BlockSpec(memory_space=pltpu.VMEM) for _ in range(count)]


def place_lanes(size, total):
    source = lax.broadcasted_iota(jnp.int32, (LANES, total), 0)
    target = lax.rem(lax.broadcasted_iota(jnp.int32, (LANES, total), 1), size)
    return jnp.where(source == target, 1.0, 0.0).astype(BF16)


def owned_lanes(devices, size):
    device = lax.broadcasted_iota(jnp.int32, (devices, devices * size), 0)
    lane = lax.broadcasted_iota(jnp.int32, (devices, devices * size), 1)
    offset = lane - device * size
    return (offset >= 0) & (offset < size)


def unpack_kernel(sizes, small_ref, *outs):
    devices = small_ref.shape[0]
    small = small_ref[...].astype(F32)
    for i, (size, out) in enumerate(zip(sizes, outs)):
        spread = jnp.dot(
            small[:, i, :].astype(BF16),
            place_lanes(size, devices * size),
            preferred_element_type=F32,
        )
        out[...] = jnp.sum(jnp.where(owned_lanes(devices, size), spread, 0.0), 0, keepdims=True)


def unpack_small(small, sizes):
    devices = small.shape[0]
    return pl.pallas_call(
        functools.partial(unpack_kernel, sizes),
        out_shape=[jax.ShapeDtypeStruct((1, devices * size), F32) for size in sizes],
        in_specs=vmem_specs(1),
        out_specs=vmem_specs(len(sizes)),
        compiler_params=pltpu.CompilerParams(vmem_limit_bytes=32 * 2**20),
    )(small)


def pack_kernel(sizes, *refs):
    grads, packed, rows = refs[: len(sizes)], refs[len(sizes)], refs[len(sizes) + 1]
    devices = packed.shape[0]
    for i, (size, grad) in enumerate(zip(sizes, grads)):
        owned = jnp.where(owned_lanes(devices, size), grad[...], 0.0).astype(BF16)
        rows[:, i, :] = lax.dot_general(
            owned,
            place_lanes(size, devices * size),
            (((1,), (1,)), ((), ())),
            preferred_element_type=F32,
        )
    packed[...] = rows[...].astype(BF16)


def pack_small(grads, sizes, devices):
    return pl.pallas_call(
        functools.partial(pack_kernel, sizes),
        out_shape=jax.ShapeDtypeStruct((devices, ROWS, LANES), BF16),
        in_specs=vmem_specs(len(sizes)),
        out_specs=vmem_specs(1)[0],
        scratch_shapes=[pltpu.VMEM((devices, ROWS, LANES), F32)],
        compiler_params=pltpu.CompilerParams(vmem_limit_bytes=32 * 2**20),
    )(*grads)


ANYWHERE = pl.BlockSpec(memory_space=pl.ANY)


def first_kernel(group, weight, rows, marks, *refs):
    vectors, (columns, blocks, lines, extra) = refs[:-4], refs[-4:]
    classes, _, width_pair = columns.shape
    shard_rows, width = weight.shape[0], weight.shape[1] // 3
    lines[...] = jnp.zeros_like(lines)
    for i, vector in enumerate(vectors):
        for start in range(0, width_pair, 3 * group):
            at = shard_rows + i
            lines[at : at + 1, start : start + vector.shape[1]] = vector[...].astype(F32)
    for kind in range(classes):
        for core in range(CORES):
            lo = (kind * CORES + core) * group
            for part in range(3):
                start = (core * 3 + part) * group
                if lo < width:
                    piece = weight[:, part * width + lo : part * width + lo + group].astype(F32)
                else:
                    piece = jnp.zeros((shard_rows, group), F32)
                lines[:shard_rows, start : start + group] = piece
        columns[kind] = lines[...].astype(BF16)
    block = rows.shape[1]
    extra[...] = jnp.zeros_like(extra)
    for i in range(rows.shape[0]):
        blocks[i, :block, :] = rows[i]
        extra[:1, :block] = marks[i : i + 1, :].astype(F32)
        blocks[i, block:, :] = extra[...].astype(BF16)


def first_blocks(weight, rows, marks, vectors, classes, group):
    shard_rows = weight.shape[0]
    count, block, width = rows.shape
    return pl.pallas_call(
        functools.partial(first_kernel, group),
        out_shape=[
            jax.ShapeDtypeStruct((classes, shard_rows + ROWS, CORES * 3 * group), BF16),
            jax.ShapeDtypeStruct((count, block + 16, width), BF16),
        ],
        in_specs=vmem_specs(3 + len(vectors)),
        out_specs=vmem_specs(2),
        scratch_shapes=[
            pltpu.VMEM((shard_rows + ROWS, CORES * 3 * group), F32),
            pltpu.VMEM((16, width), F32),
        ],
    )(weight, rows, marks, *vectors)


def stack_kernel(out_ref, fc_ref, after, stacked):
    width = out_ref.shape[1]
    stacked[0] = out_ref[...]
    for i in range(fc_ref.shape[1] // width):
        stacked[1 + i] = fc_ref[:, i * width : (i + 1) * width]


def stack_weights(w_out, w_fc, after):
    rows, width = w_out.shape
    return pl.pallas_call(
        stack_kernel,
        out_shape=jax.ShapeDtypeStruct((1 + w_fc.shape[1] // width, rows, width), BF16),
        in_specs=vmem_specs(2) + [ANYWHERE],
        out_specs=vmem_specs(1)[0],
    )(w_out, w_fc, after)


def tower_kernel(axis, count, *refs):
    pieces, low, high = refs[:count], refs[-2], refs[-1]
    level = lax.axis_index("seq") // CORES
    for step, piece in enumerate(pieces):
        place = lax.rem(level + step, count)
        for half, start in ((low, 0), (high, count // 2)):

            @pl.when((place >= start) & (place < start + count // 2))
            def _():
                if axis == 1:
                    half[:, place - start] = piece[...]
                else:
                    half[place - start] = piece[...]


def build_tower(pieces, axis, after):
    count = len(pieces)
    shape = pieces[0].shape
    shape = (*shape[:axis], count // 2, *shape[axis:])
    return pl.pallas_call(
        functools.partial(tower_kernel, axis, count),
        out_shape=[jax.ShapeDtypeStruct(shape, BF16)] * 2,
        in_specs=vmem_specs(count) + [ANYWHERE] * len(after),
        out_specs=vmem_specs(2),
        compiler_params=pltpu.CompilerParams(vmem_limit_bytes=32 * 2**20),
    )(*pieces, *after)


def one_hot_order(order_ref):
    width = order_ref.shape[1]
    features = lax.broadcasted_iota(jnp.int32, (width, width), 0)
    return jnp.where(features == order_ref[...], 1.0, 0.0).astype(BF16)


def contract_last(left, right):
    return lax.dot_general(left, right, (((1,), (1,)), ((), ())), preferred_element_type=F32)


def middle_kernel(
    groups,
    half1,
    other1,
    half2,
    other2,
    attended,
    inputs,
    cotangent,
    order_ref,
    bout,
    gain,
    bias,
    bfc,
    bproj,
    outputs,
    grad_middle,
    grad_blocks,
    placed_a,
    placed_n,
    hidden,
    grad_pre,
    grad_out,
    sum_out,
    sum_gain,
    sum_bias,
    sum_fc,
    sum_proj,
    weights1,
    weights2,
    attended_rows,
    slopes,
    permuted,
    sems,
):
    parts = weights1.shape[0] - 1
    width = weights1.shape[2]
    side = width // CORES
    seq_count, block, _ = inputs.shape
    tokens = seq_count * block
    core = lax.rem(lax.axis_index("seq"), CORES)
    chips, rows2 = half2.shape[:2]
    copies = []
    for kind in range(parts + 1):
        for index, source in enumerate((half1, other1)):
            copies.append(
                pltpu.make_async_copy(
                    source.at[kind],
                    weights1.at[kind, pl.ds(index * side, side)],
                    sems.at[len(copies)],
                )
            )
    ready1 = len(copies)
    if chips == 1:
        copies.append(pltpu.make_async_copy(half2.at[0], weights2, sems.at[len(copies)]))
    for index, source in enumerate((half2, other2) if chips > 1 else ()):
        place = core if index == 0 else 1 - core
        for chip in range(chips):
            start = pl.multiple_of((chip * CORES + place) * rows2, rows2)
            copies.append(
                pltpu.make_async_copy(
                    source.at[chip], weights2.at[pl.ds(start, rows2)], sems.at[len(copies)]
                )
            )
    for copy in copies:
        copy.start()
    order = one_hot_order(order_ref)

    half_block = block // 2
    group = attended.shape[2] // 2
    for i in range(seq_count):
        for g in range(groups):
            for part in range(2):
                start = i * block + part * half_block
                attended_rows[start : start + half_block, g * group : (g + 1) * group] = attended[
                    i * groups + g, :, part * group : (part + 1) * group
                ]
    placed = jnp.dot(attended_rows[:, :width], order, preferred_element_type=F32).astype(BF16)
    placed_a[...] = placed
    for copy in copies[:2]:
        copy.wait()
    rows = inputs[...].astype(F32).reshape(tokens, width)
    middle = rows + (jnp.dot(placed, weights1[0], preferred_element_type=F32) + bout[...])
    center = jnp.mean(middle, -1, keepdims=True)
    centered = middle - center
    scale = lax.rsqrt(jnp.mean(centered * centered, -1, keepdims=True) + EPSILON)
    unit = centered * scale
    normed = (unit * gain[...] + bias[...]).astype(BF16)
    placed = jnp.dot(normed, order, preferred_element_type=F32).astype(BF16)
    placed_n[...] = placed
    for copy in copies[2:ready1]:
        copy.wait()
    curve = math.sqrt(2.0 / math.pi)
    for q in range(parts):
        lo = q * width
        pre = jnp.dot(placed, weights1[1 + q], preferred_element_type=F32)
        pre = pre + bfc[:, lo : lo + width]
        square = pre * pre
        tanh = jnp.tanh(curve * (pre + 0.044715 * (pre * square)))
        hidden[:, lo : lo + width] = (0.5 * pre * (1.0 + tanh)).astype(BF16)
        slopes[:, lo : lo + width] = 0.5 * (1.0 + tanh) + 0.5 * pre * (1.0 - tanh * tanh) * (
            curve * (1.0 + 3 * 0.044715 * square)
        )
    for copy in copies[ready1:]:
        copy.wait()
    result = middle + bproj[...]
    for q in range(parts):
        lo = q * width
        result += jnp.dot(
            hidden[:, lo : lo + width], weights2[lo : lo + width], preferred_element_type=F32
        )
    outputs[...] = result.astype(BF16).reshape(seq_count, block, width)

    branch = cotangent[...].reshape(tokens, width)
    grad_rows = branch.astype(F32)
    sum_proj[...] = jnp.sum(grad_rows, 0, keepdims=True)
    grad_placed = jnp.zeros((tokens, width), F32)
    for q in range(parts):
        lo = q * width
        grad = contract_last(branch, weights2[lo : lo + width]) * slopes[:, lo : lo + width]
        grad = grad.astype(BF16)
        grad_pre[:, lo : lo + width] = grad
        sum_fc[:, lo : lo + width] = jnp.sum(grad.astype(F32), 0, keepdims=True)
        grad_placed += contract_last(grad, weights1[1 + q])
    high = grad_placed.astype(BF16)
    rest = grad_placed - high.astype(F32)
    mid = rest.astype(BF16)
    low = (rest - mid.astype(F32)).astype(BF16)
    grad_normed = contract_last(high, order) + (contract_last(mid, order) + contract_last(low, order))
    sum_bias[...] = jnp.sum(grad_normed, 0, keepdims=True)
    sum_gain[...] = jnp.sum(grad_normed * unit, 0, keepdims=True)
    grad_unit = grad_normed * gain[...]
    part = jnp.mean(grad_unit, -1, keepdims=True)
    cross = jnp.mean(grad_unit * unit, -1, keepdims=True)
    grad_mid = grad_rows + scale * (grad_unit - part - unit * cross)
    grad_middle[...] = grad_mid
    grad_attn = grad_mid.astype(BF16)
    grad_out[...] = grad_attn
    sum_out[...] = jnp.sum(grad_attn.astype(F32), 0, keepdims=True)
    back = contract_last(grad_attn, weights1[0]).astype(BF16)
    if permuted.shape[1] > width:
        permuted[...] = jnp.zeros_like(permuted)
    permuted[:, :width] = contract_last(back, order).astype(BF16)
    for i in range(seq_count):
        for g in range(groups):
            for part in range(2):
                start = i * block + part * half_block
                grad_blocks[i * groups + g, :, part * group : (part + 1) * group] = permuted[
                    start : start + half_block, g * group : (g + 1) * group
                ]


def middle_block(half1, other1, half2, other2, attended, inputs, cotangent, order, vectors, groups):
    kinds, side, width = half1.shape
    parts = kinds - 1
    chips = half2.shape[0]
    seq_count, block, _ = inputs.shape
    tokens = seq_count * block
    wide = groups * attended.shape[2] // 2

    def shape(*dims, kind=BF16):
        return jax.ShapeDtypeStruct(dims, kind)

    return pl.pallas_call(
        functools.partial(middle_kernel, groups),
        out_shape=[
            shape(seq_count, block, width),
            shape(tokens, width, kind=F32),
            shape(*attended.shape),
            shape(tokens, width),
            shape(tokens, width),
            shape(tokens, parts * width),
            shape(tokens, parts * width),
            shape(tokens, width),
            shape(1, width, kind=F32),
            shape(1, width, kind=F32),
            shape(1, width, kind=F32),
            shape(1, parts * width, kind=F32),
            shape(1, width, kind=F32),
        ],
        in_specs=[ANYWHERE] * 4 + vmem_specs(9),
        out_specs=vmem_specs(13),
        scratch_shapes=[
            pltpu.VMEM((kinds, width, width), BF16),
            pltpu.VMEM((parts * width, width), BF16),
            pltpu.VMEM((tokens, wide), BF16),
            pltpu.VMEM((tokens, parts * width), F32),
            pltpu.VMEM((tokens, wide), BF16),
            pltpu.SemaphoreType.DMA((2 * kinds + 2 * chips,)),
        ],
        compiler_params=pltpu.CompilerParams(vmem_limit_bytes=50 * 2**20),
        cost_estimate=pl.CostEstimate(
            flops=tokens * width * width * 44, bytes_accessed=2**24, transcendentals=2**20
        ),
    )(half1, other1, half2, other2, attended, inputs, cotangent, order, *vectors)


def gradient_kernel(
    placed_a, placed_n, hidden, grad_pre, grad_out, cotangent, send1, keep1, send2, keep2, turned, some
):
    width = placed_a.shape[1]
    side = width // CORES
    parts = send1.shape[0] - 1
    chips, rows2 = send2.shape[:2]
    core = lax.rem(lax.axis_index("seq"), CORES)
    for start in range(0, turned.shape[0], width):
        turned[start : start + width, :] = (
            hidden[:, start : start + width].astype(F32).T.astype(BF16)
        )
    branch = cotangent[...].reshape(-1, width)
    for target, place in ((send2, 1 - core), (keep2, core)):
        if rows2 % 16:
            target[...] = jnp.zeros_like(target)
            continue
        for chip in range(chips):
            start = pl.multiple_of((chip * CORES + place) * rows2, rows2)
            some[chip * rows2 : (chip + 1) * rows2, :] = turned[pl.ds(start, rows2), :]
        step = max(1, 4 * 96 // rows2)
        for chip in range(0, chips, step):
            product = jnp.dot(
                some[chip * rows2 : (chip + step) * rows2, :], branch, preferred_element_type=F32
            )
            target[chip : chip + step] = product.astype(BF16).reshape(step, rows2, width)
    turned_a = placed_a[...].astype(F32).T.astype(BF16)
    turned_n = placed_n[...].astype(F32).T.astype(BF16)
    for target, start in ((send1, side), (keep1, 0)):
        target[0] = jnp.dot(
            turned_a[start : start + side], grad_out[...], preferred_element_type=F32
        ).astype(BF16)
        for q in range(parts):
            target[1 + q] = jnp.dot(
                turned_n[start : start + side],
                grad_pre[:, q * width : (q + 1) * width],
                preferred_element_type=F32,
            ).astype(BF16)


def weight_gradients(placed_a, placed_n, hidden, grad_pre, grad_out, cotangent, chips):
    tokens, width = placed_a.shape
    parts = hidden.shape[1] // width
    shape1 = jax.ShapeDtypeStruct((1 + parts, width // CORES, width), BF16)
    rows2 = parts * width // (chips * CORES)
    shape2 = jax.ShapeDtypeStruct((chips, rows2, width), BF16)
    return pl.pallas_call(
        gradient_kernel,
        out_shape=[shape1, shape1, shape2, shape2],
        in_specs=vmem_specs(6),
        out_specs=vmem_specs(4),
        scratch_shapes=[
            pltpu.VMEM((parts * width, tokens), BF16),
            pltpu.VMEM((parts * width // CORES, tokens), BF16),
        ],
        compiler_params=pltpu.CompilerParams(vmem_limit_bytes=50 * 2**20),
        cost_estimate=pl.CostEstimate(
            flops=tokens * width * width * 18, bytes_accessed=2**24, transcendentals=0
        ),
    )(placed_a, placed_n, hidden, grad_pre, grad_out, cotangent)


def masked_scores(keys, queries, id_column, id_row, first):
    scores = lax.dot_general(keys, queries, (((1,), (1,)), ((), ())), preferred_element_type=F32)
    key_pos = lax.broadcasted_iota(jnp.int32, scores.shape, 0)
    query_pos = lax.broadcasted_iota(jnp.int32, scores.shape, 1) + first
    allowed = (key_pos <= query_pos) & (id_column == id_row)
    return jnp.where(allowed, scores, MASKED)


def column_of(id_row):
    length = id_row.shape[1]
    return jnp.broadcast_to(id_row, (LANES, length)).T[:, :1]


def forward_kernel(
    seq_count,
    heads,
    head_size,
    step_rows,
    block,
    rows_ref,
    weight,
    gain,
    bias,
    bqv,
    after,
    out,
    stats,
    whole,
    normed,
    ids,
    result,
    qkv_bias,
):
    length = whole.shape[0]
    group = heads * head_size
    width = weight.shape[0]
    index = lax.rem(lax.axis_index("seq"), lax.axis_size("seq") // seq_count)
    qkv_bias[...] = jnp.zeros_like(qkv_bias)
    for lo in range(0, width, group):
        here = index == lo // group
        for base, start in ((0, 0), (width, 2 * group)):
            piece = jnp.where(here, bqv[:, base + lo : base + lo + group], 0.0)
            qkv_bias[:, start : start + group] += piece
    for i in range(length // block):
        rows = norm_affine(rows_ref[i, :block, :].astype(F32), gain[...], bias[...])
        normed[i * block : (i + 1) * block, :] = rows.astype(BF16)
    id_rows = [rows_ref[i, block:, :block].astype(F32)[:1] for i in range(length // block)]
    id_row = jnp.concatenate(id_rows, 1)
    ids[...] = id_row
    id_column = column_of(id_row)
    for first in range(0, length, step_rows):
        last = first + step_rows
        product = jnp.dot(normed[first:last, :], weight[...], preferred_element_type=F32)
        whole[first:last, :] = (product + qkv_bias[...]).astype(BF16)
    values_t = whole[:, 2 * group : 3 * group].astype(F32).T.astype(BF16)
    for first in range(0, length, step_rows):
        last = first + step_rows
        tops = []
        for head in range(heads):
            lo = head * head_size
            queries = whole[first:last, lo : lo + head_size] * BF16(head_size**-0.5)
            keys = whole[:last, group + lo : group + lo + head_size]
            scores = masked_scores(keys, queries, id_column[:last], id_row[:, first:last], first)
            highest = jnp.max(scores, 0, keepdims=True)
            weights = jnp.exp(scores - highest)
            total = jnp.sum(weights, 0, keepdims=True)
            probs = (weights * (1.0 / total)).astype(BF16)
            tops.append(
                jnp.dot(
                    values_t[lo : lo + head_size, :last], probs, preferred_element_type=F32
                )
            )
            stats[head : head + 1, first:last] = highest + jnp.log(total)
        result[first:last, :] = jnp.concatenate(tops, 0).T.astype(BF16)
    half = block // 2
    for start in range(0, length, block):
        out[start // 2 : start // 2 + half, :group] = result[start : start + half, :]
        out[start // 2 : start // 2 + half, group:] = result[start + half : start + block, :]


def backward_kernel(
    heads,
    head_size,
    step_rows,
    block,
    whole,
    grads,
    stats,
    ids,
    after,
    out,
    grad_out,
    grad_query,
    grad_key,
    grad_value,
):
    length = whole.shape[0]
    group = heads * head_size
    half = block // 2
    for start in range(0, length, block):
        packed = grads[start // 2 : start // 2 + half, :]
        grad_out[start : start + half, :] = packed[:, :group]
        grad_out[start + half : start + block, :] = packed[:, group:]
    id_row = ids[...]
    id_column = column_of(id_row)
    keys_t = whole[:, group : 2 * group].astype(F32).T.astype(BF16)
    factor = head_size**-0.5
    grad_key[...] = jnp.zeros_like(grad_key)
    grad_value[...] = jnp.zeros_like(grad_value)
    for first in range(0, length, step_rows):
        last = first + step_rows
        tops = []
        for head in range(heads):
            lo = head * head_size
            queries = whole[first:last, lo : lo + head_size] * BF16(factor)
            keys = whole[:last, group + lo : group + lo + head_size]
            values = whole[:last, 2 * group + lo : 2 * group + lo + head_size]
            grad = grad_out[first:last, lo : lo + head_size]
            scores = masked_scores(keys, queries, id_column[:last], id_row[:, first:last], first)
            probs = jnp.exp(scores - stats[head : head + 1, first:last])
            grad_probs = lax.dot_general(
                values, grad, (((1,), (1,)), ((), ())), preferred_element_type=F32
            )
            delta = jnp.sum(probs * grad_probs, 0, keepdims=True)
            grad_scores = (probs * (grad_probs - delta)).astype(BF16)
            tops.append(
                jnp.dot(
                    keys_t[lo : lo + head_size, :last], grad_scores, preferred_element_type=F32
                )
                * factor
            )
            grad_key[head, :last, :] += jnp.dot(
                grad_scores, queries, preferred_element_type=F32
            )
            grad_value[head, :last, :] += jnp.dot(
                probs.astype(BF16), grad, preferred_element_type=F32
            )
        grad_query[first:last, :] = jnp.concatenate(tops, 0).T.astype(BF16)
    out[:, :group] = grad_query[...]
    for head in range(heads):
        lo = head * head_size
        out[:, group + lo : group + lo + head_size] = grad_key[head].astype(BF16)
        out[:, 2 * group + lo : 2 * group + lo + head_size] = grad_value[head].astype(BF16)


def attend_forward(rows, weight, gain, bias, bqv, after, seq_count, heads, head_size, block):
    length = rows.shape[0] * block
    width = rows.shape[2]
    group = heads * head_size
    pairs = length * length // 2 * heads
    return pl.pallas_call(
        functools.partial(forward_kernel, seq_count, heads, head_size, min(256, length), block),
        out_shape=[
            jax.ShapeDtypeStruct((length // 2, 2 * group), BF16),
            jax.ShapeDtypeStruct((heads, length), F32),
            jax.ShapeDtypeStruct((length, 3 * group), BF16),
            jax.ShapeDtypeStruct((length, width), BF16),
            jax.ShapeDtypeStruct((1, length), F32),
        ],
        in_specs=vmem_specs(5) + [ANYWHERE],
        out_specs=vmem_specs(5),
        scratch_shapes=[pltpu.VMEM((length, group), BF16), pltpu.VMEM((1, 3 * group), F32)],
        compiler_params=pltpu.CompilerParams(vmem_limit_bytes=48 * 2**20),
        cost_estimate=pl.CostEstimate(
            flops=pairs * head_size * 4 + length * width * group * 6,
            bytes_accessed=length * width * 8,
            transcendentals=pairs,
        ),
    )(rows, weight, gain, bias, bqv, after)


def attend_backward(whole, grads, stats, ids, after, heads, head_size, block):
    length, width = whole.shape
    group = heads * head_size
    pairs = length * length // 2 * heads
    return pl.pallas_call(
        functools.partial(backward_kernel, heads, head_size, min(256, length), block),
        out_shape=jax.ShapeDtypeStruct((length, 3 * group), BF16),
        in_specs=vmem_specs(4) + [ANYWHERE],
        out_specs=vmem_specs(1)[0],
        scratch_shapes=[
            pltpu.VMEM((length, group), BF16),
            pltpu.VMEM((length, group), BF16),
            pltpu.VMEM((heads, length, head_size), F32),
            pltpu.VMEM((heads, length, head_size), F32),
        ],
        compiler_params=pltpu.CompilerParams(vmem_limit_bytes=48 * 2**20),
        cost_estimate=pl.CostEstimate(
            flops=pairs * head_size * 10, bytes_accessed=length * width * 6, transcendentals=pairs
        ),
    )(whole, grads, stats, ids, after)


def on_device(
    inputs,
    segments,
    cotangent,
    ln1_gain,
    ln1_bias,
    w_qkv,
    b_qv,
    w_out,
    b_out,
    ln2_gain,
    ln2_bias,
    w_fc,
    b_fc,
    w_proj,
    b_proj,
):
    seq_count, block, width = inputs.shape
    head_size = width // HEADS
    tokens = seq_count * block
    count = lax.axis_size("seq")
    devices = count * lax.axis_size("dp")
    groups = count // seq_count
    heads = -(-HEADS // groups)
    spare = groups * heads - HEADS
    group = heads * head_size

    vectors = (ln1_gain, ln1_bias, b_qv, b_out, ln2_gain, ln2_bias, b_fc, b_proj)
    sizes = tuple(vector.shape[0] for vector in vectors)
    shard_rows = w_out.shape[0] // width
    parts = w_fc.shape[0] // w_out.shape[0]
    classes = groups // CORES
    chips = devices // CORES
    place = lax.axis_index("seq")
    core = place % CORES
    group_index = place % groups

    columns, blocks = first_blocks(
        w_qkv.reshape(shard_rows, 3 * width),
        inputs,
        segments,
        [vector.reshape(1, -1) for vector in vectors],
        classes,
        group,
    )
    early, sequence = gather_sequence(blocks)
    tower_a = gather_columns(columns)
    heights = tower_a.shape[0]
    half_a = gather_plane(tower_a[: heights // 2], tower_a[heights // 2 :], 0)
    left, right = half_a[..., : 3 * group], half_a[..., 3 * group :]
    mine_a = jnp.where(core == 0, left, right)
    whole_a = ordered(core, mine_a, swap_core(jnp.where(core == 0, right, left)), 1)
    whole_a = whole_a.reshape(devices, shard_rows + ROWS, 3 * group)
    wqkv = whole_a[:, :shard_rows].reshape(width, 3 * group)
    gain1, bias1, bqv, bout, gain2, bias2, bfc, bproj = unpack_small(
        whole_a[:, shard_rows:, :LANES], sizes
    )

    stacked = stack_weights(w_out.reshape(-1, width), w_fc.reshape(-1, parts * width), tower_a)
    low1, high1 = build_tower(z_pieces(stacked), 1, [half_a, early])
    low2, high2 = build_tower(z_pieces(w_proj.reshape(-1, width)), 0, [low1])
    half1 = gather_plane(low1, high1, 1).reshape(1 + parts, -1, width)
    half2 = gather_plane(low2, high2, 0)
    other1 = swap_core(half1)
    other2 = swap_core(half2)
    aligned = half2.shape[1] % 16 == 0
    if not aligned:
        half2 = ordered(core, half2, other2, 1).reshape(1, parts * width, width)

    attended, stats, qkv, normed1, ids = attend_forward(
        sequence, wqkv, gain1, bias1, bqv, low1, seq_count, heads, head_size, block
    )
    attended = exchange(attended.reshape(count, block // 2, 2 * group))

    spot = jnp.arange(width, dtype=jnp.int32)
    side = width // CORES
    own_core = (core + spot // side) % CORES
    order = (spot % side // shard_rows * CORES + own_core) * shard_rows + spot % shard_rows
    (
        outputs,
        grad_middle,
        grad_blocks,
        placed_a,
        placed_n,
        hidden,
        grad_pre,
        grad_out,
        grad_bout,
        grad_gain2,
        grad_bias2,
        grad_bfc,
        grad_bproj,
    ) = middle_block(
        half1,
        other1,
        half2,
        other2,
        attended,
        inputs,
        cotangent,
        order.reshape(1, width),
        (bout, gain2, bias2, bfc, bproj),
        groups,
    )
    grad_blocks = exchange(grad_blocks).reshape(-1, 2 * group)
    send1, keep1, send2, keep2 = weight_gradients(
        placed_a, placed_n, hidden, grad_pre, grad_out, cotangent, chips
    )
    if not aligned:
        grad_wproj = lax.dot_general(
            hidden,
            cotangent.reshape(tokens, width),
            (((0,), (0,)), ((), ())),
            preferred_element_type=F32,
        )
        grad_wproj = grad_wproj.astype(BF16).reshape(chips, CORES, -1, width)
        send2, keep2 = pick(grad_wproj, 1 - core, 1), pick(grad_wproj, core, 1)
    half1 = add(keep1, swap_core(send1))
    half2 = add(keep2, swap_core(send2))
    half1 = half1.reshape(1 + parts, chips, shard_rows, width)
    own1 = scatter_z(scatter_plane(half1, 1), 1)
    own2 = scatter_z(scatter_plane(half2, 0), 0)

    def blocks_of(value, rows):
        return value.astype(BF16).reshape(chips, CORES, rows, -1)

    rows = inputs.astype(F32).reshape(tokens, width)
    grad_qkv = attend_backward(
        qkv, grad_blocks, stats, ids, half1, heads, head_size, block
    )
    grad_normed1 = lax.dot_general(
        grad_qkv, wqkv, (((1,), (1,)), ((), ())), preferred_element_type=F32
    )
    own_normed1 = scatter_sequence(grad_normed1.astype(BF16).reshape(count, block, width))
    _, norm1_back = jax.vjp(lambda value: norm_affine(value, gain1, bias1), rows)
    (grad_in_part,) = norm1_back(own_normed1.astype(F32).reshape(tokens, width))
    grad_inputs = (grad_middle + grad_in_part).astype(BF16).reshape(inputs.shape)

    long_rows = sequence[:, :block].astype(F32).reshape(count * block, width)
    _, norm1_long_back = jax.vjp(lambda g, b: norm_affine(long_rows, g, b), gain1, bias1)
    grad_gain1, grad_bias1 = norm1_long_back(grad_normed1)
    grad_wqkv = lax.dot_general(
        normed1, grad_qkv, (((0,), (0,)), ((), ())), preferred_element_type=F32
    )
    sums = jnp.sum(grad_qkv, 0, dtype=F32).reshape(3, group)
    here = (jnp.arange(groups) == group_index)[None, :, None]
    grad_bqv = jnp.where(here, jnp.stack([sums[0], sums[2]])[:, None], 0.0)
    grad_bqv = grad_bqv.reshape(2, groups * heads, head_size)[:, :HEADS]
    grads = (
        grad_gain1,
        grad_bias1,
        grad_bqv,
        grad_bout,
        grad_gain2,
        grad_bias2,
        grad_bfc,
        grad_bproj,
    )
    small_grads = pack_small([grad.reshape(1, -1) for grad in grads], sizes, devices)
    small_grads = jnp.pad(small_grads, ((0, 0), (0, 0), (0, 3 * group - LANES)))
    block_a = jnp.concatenate(
        [blocks_of(grad_wqkv, shard_rows), small_grads.reshape(chips, CORES, ROWS, -1)], 2
    )
    send_a, keep_a = pick(block_a, 1 - core, 1), pick(block_a, core, 1)
    got_a = swap_core(send_a)
    pair_a = jnp.concatenate(
        [jnp.where(core == 0, keep_a, got_a), jnp.where(core == 0, got_a, keep_a)], -1
    )
    own_a = scatter_columns(scatter_plane(pair_a, 0))
    own_small = jnp.sum(
        own_a[:, shard_rows:].reshape(classes, ROWS, CORES, 3 * group)[..., :LANES], (0, 2)
    )
    own = [own_small[i, :size] for i, size in enumerate(sizes)]
    own_qkv = own_a[:, :shard_rows].reshape(classes, shard_rows, CORES, 3, group)
    own_qkv = own_qkv.transpose(1, 3, 0, 2, 4).reshape(shard_rows, 3, groups * heads, head_size)
    own_qkv = own_qkv[:, :, :HEADS].reshape(-1)
    return (
        outputs,
        grad_inputs,
        own[0],
        own[1],
        own_qkv,
        own[2],
        own1[0].reshape(-1),
        own[3],
        own[4],
        own[5],
        own1[1:].transpose(1, 0, 2).reshape(-1),
        own[6],
        own2.reshape(-1),
        own[7],
    )


def solution(mesh):
    token_spec = P("dp", "seq", None)
    flat_spec = P(("dp", "seq"))
    in_specs = (token_spec, P("dp", "seq"), token_spec) + (flat_spec,) * 12
    out_specs = (token_spec, token_spec) + (flat_spec,) * 12
    return jax.shard_map(
        on_device, mesh=mesh, in_specs=in_specs, out_specs=out_specs, check_vma=False
    )
```

```python
import functools
import math

import jax
import jax.numpy as jnp
from jax import lax
from jax.experimental import pallas as pl
from jax.experimental.pallas import tpu as pltpu
from jax.sharding import PartitionSpec as P

HEADS = 12
CORES = 2


EPSILON = 1e-05
MASKED = -1e30
F32 = jnp.float32
BF16 = jnp.bfloat16


def norm_affine(values, gain, bias):
    center = jnp.mean(values, -1, keepdims=True)
    centered = values - center
    variance = jnp.mean(centered * centered, -1, keepdims=True)
    return centered * lax.rsqrt(variance + EPSILON) * gain + bias


ANYWHERE = pl.BlockSpec(memory_space=pl.ANY)


def shift_z(value, step):
    size = lax.axis_size("seq")
    return lax.ppermute(value, "seq", [(i, (i + CORES * step) % size) for i in range(size)])


def swap_core(value):
    size = lax.axis_size("seq")
    return lax.ppermute(value, "seq", [(i, i ^ 1) for i in range(size)])


def swap_dp(value, bit):
    size = lax.axis_size("dp")
    return lax.ppermute(value, "dp", [(i, i ^ bit) for i in range(size)])


def ordered(flag, mine, other, axis):
    first = jnp.where(flag == 0, mine, other)
    second = jnp.where(flag == 0, other, mine)
    return jnp.stack([first, second], axis)


def roll_blocks(pieces, place):
    count = len(pieces)
    stacked = jnp.stack(pieces)
    twice = jnp.concatenate([stacked, stacked])
    return lax.dynamic_slice_in_dim(twice, lax.rem(count - place, count), count, 0)


def z_pieces(shard):
    heights = lax.axis_size("seq") // CORES
    return [shard] + [shift_z(shard, -step) for step in range(1, heights)]


def swap_z(value, bit):
    size = lax.axis_size("seq")
    return lax.ppermute(value, "seq", [(i, i ^ (CORES * bit)) for i in range(size)])


def gather_plane(low, high, axis):
    if lax.axis_size("dp") == 4:
        plane = lax.axis_index("dp")
        y, x = plane // 2, plane % 2
        low_x = ordered(x, low, swap_dp(low, 1), axis)
        high_y = ordered(y, high, swap_dp(high, 2), axis)
        low_all = ordered(y, low_x, swap_dp(low_x, 2), axis)
        high_all = ordered(x, high_y, swap_dp(high_y, 1), axis + 1)
        half = jnp.concatenate([low_all, high_all], axis + 2)
        count = 4 * half.shape[axis + 2]
    else:
        tower = jnp.concatenate([low, high], axis)
        half = lax.all_gather(tower, "dp", axis=axis, tiled=True)
        return half
    return half.reshape(*low.shape[:axis], count, *low.shape[axis + 1 :])


def pick(value, index, axis):
    return lax.dynamic_index_in_dim(value, index, axis, keepdims=False)


def add(mine, other):
    return (mine.astype(F32) + other.astype(F32)).astype(mine.dtype)


def scatter_plane(split, axis, between=None):
    planes = lax.axis_size("dp")
    heights = lax.axis_size("seq") // CORES
    if planes != 4:
        if between is not None:
            between(split, split)
        return lax.psum_scatter(split, "dp", scatter_dimension=axis, tiled=True)
    plane = lax.axis_index("dp")
    y, x = plane // 2, plane % 2
    split = split.reshape(*split.shape[:axis], 2, 2, heights, *split.shape[axis + 1 :])
    low = lax.slice_in_dim(split, 0, heights // 2, axis=axis + 2)
    high = lax.slice_in_dim(split, heights // 2, heights, axis=axis + 2)
    low_send, high_send = pick(low, 1 - y, axis), pick(high, 1 - x, axis + 1)
    low_got, high_got = swap_dp(low_send, 2), swap_dp(high_send, 1)
    if between is not None:
        after = between(low_send, high_send)
        low_got, high_got = gate(low_got, after), gate(high_got, after)
    low = add(pick(low, y, axis), low_got)
    high = add(pick(high, x, axis + 1), high_got)
    low = add(pick(low, x, axis), swap_dp(pick(low, 1 - x, axis), 1))
    high = add(pick(high, y, axis), swap_dp(pick(high, 1 - y, axis), 2))
    return jnp.concatenate([low, high], axis)


def scatter_z(tower, axis):
    heights = lax.axis_size("seq") // CORES
    level = lax.axis_index("seq") // CORES
    mine = pick(tower, level, axis).astype(F32)
    for step in range(1, heights):
        mine += shift_z(pick(tower, lax.rem(level + step, heights), axis), step).astype(F32)
    return mine


def z_bits():
    heights = lax.axis_size("seq") // CORES
    level = lax.axis_index("seq") // CORES
    top = heights // 2
    return level, top, level // top


def gather_sequence(blocks):
    level, top, half = z_bits()
    core = lax.axis_index("seq") % CORES
    held = ordered(half, pick(blocks, half, 0), swap_z(pick(blocks, 1 - half, 0), top), 0)
    axis, bit = 1, top // 2
    while bit:
        held = ordered(level // bit % 2, held, swap_z(held, bit), axis)
        axis, bit = axis + 1, bit // 2
    return held, ordered(core, held, swap_core(held), axis).reshape(-1, *blocks.shape[1:])


def scatter_sequence(partial):
    level, top, half = z_bits()
    core = lax.axis_index("seq") % CORES
    shape = partial.shape[1:]
    count = top.bit_length()
    held = partial.reshape(*[2] * (count + 1), *shape)
    held = add(pick(held, core, count), swap_core(pick(held, 1 - core, count)))
    axis, bit = count - 1, 1
    while bit < top:
        flag = level // bit % 2
        held = add(pick(held, flag, axis), swap_z(pick(held, 1 - flag, axis), bit))
        axis, bit = axis - 1, bit * 2
    return ordered(half, pick(held, half, 0), swap_z(pick(held, 1 - half, 0), top), 0)


def gather_columns(blocks):
    level, top, half = z_bits()
    shape = blocks.shape[1:]
    count = top.bit_length() - 1
    held = blocks.reshape(*[2] * count, *shape)
    bit = top // 2
    while bit:
        flag = level // bit % 2
        got = swap_z(pick(held, 1 - flag, 0), bit)
        held = ordered(flag, pick(held, flag, 0), got, count - 1)
        bit //= 2
    return ordered(half, held, swap_z(held, top), 0).reshape(-1, *shape)


def scatter_columns(tower):
    level, top, half = z_bits()
    shape = tower.shape[1:]
    count = top.bit_length() - 1
    held = tower.reshape(*[2] * (count + 1), *shape)
    held = add(pick(held, half, 0), swap_z(pick(held, 1 - half, 0), top))
    bit = 1
    while bit < top:
        flag = level // bit % 2
        got = swap_z(pick(held, 1 - flag, count - 1), bit)
        held = ordered(flag, pick(held, flag, count - 1), got, 0)
        bit *= 2
    return held.reshape(-1, *shape).astype(F32)


def exchange(blocks):
    return lax.all_to_all(blocks, "seq", split_axis=0, concat_axis=0, tiled=True)


ROWS = 8
LANES = 128


def vmem_specs(count):
    return [pl.BlockSpec(memory_space=pltpu.VMEM) for _ in range(count)]


def place_lanes(size, total):
    source = lax.broadcasted_iota(jnp.int32, (LANES, total), 0)
    target = lax.rem(lax.broadcasted_iota(jnp.int32, (LANES, total), 1), size)
    return jnp.where(source == target, 1.0, 0.0).astype(BF16)


def owned_lanes(devices, size):
    device = lax.broadcasted_iota(jnp.int32, (devices, devices * size), 0)
    lane = lax.broadcasted_iota(jnp.int32, (devices, devices * size), 1)
    offset = lane - device * size
    return (offset >= 0) & (offset < size)


def unpack_kernel(sizes, small_ref, *outs):
    devices = small_ref.shape[0]
    small = small_ref[...].astype(F32)
    for i, (size, out) in enumerate(zip(sizes, outs)):
        spread = jnp.dot(
            small[:, i, :].astype(BF16),
            place_lanes(size, devices * size),
            preferred_element_type=F32,
        )
        out[...] = jnp.sum(jnp.where(owned_lanes(devices, size), spread, 0.0), 0, keepdims=True)


def unpack_small(small, sizes):
    devices = small.shape[0]
    return pl.pallas_call(
        functools.partial(unpack_kernel, sizes),
        out_shape=[jax.ShapeDtypeStruct((1, devices * size), F32) for size in sizes],
        in_specs=vmem_specs(1),
        out_specs=vmem_specs(len(sizes)),
        compiler_params=pltpu.CompilerParams(vmem_limit_bytes=32 * 2**20),
    )(small)


def pack_kernel(sizes, *refs):
    grads, packed, rows = refs[: len(sizes)], refs[len(sizes)], refs[len(sizes) + 1]
    devices = packed.shape[0]
    for i, (size, grad) in enumerate(zip(sizes, grads)):
        owned = jnp.where(owned_lanes(devices, size), grad[...], 0.0).astype(BF16)
        rows[:, i, :] = lax.dot_general(
            owned,
            place_lanes(size, devices * size),
            (((1,), (1,)), ((), ())),
            preferred_element_type=F32,
        )
    packed[...] = rows[...].astype(BF16)


def pack_small(grads, sizes, devices):
    return pl.pallas_call(
        functools.partial(pack_kernel, sizes),
        out_shape=jax.ShapeDtypeStruct((devices, ROWS, LANES), BF16),
        in_specs=vmem_specs(len(sizes)),
        out_specs=vmem_specs(1)[0],
        scratch_shapes=[pltpu.VMEM((devices, ROWS, LANES), F32)],
        compiler_params=pltpu.CompilerParams(vmem_limit_bytes=32 * 2**20),
    )(*grads)


def gate(value, *after):
    def kernel(*refs):
        pass

    return pl.pallas_call(
        kernel,
        out_shape=jax.ShapeDtypeStruct(value.shape, value.dtype),
        in_specs=[ANYWHERE] * (1 + len(after)),
        out_specs=ANYWHERE,
        input_output_aliases={0: 0},
    )(value, *after)


def first_kernel(group, weight, rows, marks, *refs):
    vectors, (columns, blocks, lines, extra) = refs[:-4], refs[-4:]
    classes, _, width_pair = columns.shape
    shard_rows, width = weight.shape[0], weight.shape[1] // 3
    lines[...] = jnp.zeros_like(lines)
    for i, vector in enumerate(vectors):
        for start in range(0, width_pair, 3 * group):
            at = shard_rows + i
            lines[at : at + 1, start : start + vector.shape[1]] = vector[...].astype(F32)
    for kind in range(classes):
        for core in range(CORES):
            lo = (kind * CORES + core) * group
            for part in range(3):
                start = (core * 3 + part) * group
                if lo < width:
                    piece = weight[:, part * width + lo : part * width + lo + group].astype(F32)
                else:
                    piece = jnp.zeros((shard_rows, group), F32)
                lines[:shard_rows, start : start + group] = piece
        columns[kind] = lines[...].astype(BF16)
    block = rows.shape[1]
    extra[...] = jnp.zeros_like(extra)
    for i in range(rows.shape[0]):
        blocks[i, :block, :] = rows[i]
        extra[:1, :block] = marks[i : i + 1, :].astype(F32)
        blocks[i, block:, :] = extra[...].astype(BF16)


def first_blocks(weight, rows, marks, vectors, classes, group):
    shard_rows = weight.shape[0]
    count, block, width = rows.shape
    return pl.pallas_call(
        functools.partial(first_kernel, group),
        out_shape=[
            jax.ShapeDtypeStruct((classes, shard_rows + ROWS, CORES * 3 * group), BF16),
            jax.ShapeDtypeStruct((count, block + 16, width), BF16),
        ],
        in_specs=vmem_specs(3 + len(vectors)),
        out_specs=vmem_specs(2),
        scratch_shapes=[
            pltpu.VMEM((shard_rows + ROWS, CORES * 3 * group), F32),
            pltpu.VMEM((16, width), F32),
        ],
    )(weight, rows, marks, *vectors)


def stack_kernel(out_ref, fc_ref, after, stacked):
    width = out_ref.shape[1]
    stacked[0] = out_ref[...]
    for i in range(fc_ref.shape[1] // width):
        stacked[1 + i] = fc_ref[:, i * width : (i + 1) * width]


def stack_weights(w_out, w_fc, after):
    rows, width = w_out.shape
    return pl.pallas_call(
        stack_kernel,
        out_shape=jax.ShapeDtypeStruct((1 + w_fc.shape[1] // width, rows, width), BF16),
        in_specs=vmem_specs(2) + [ANYWHERE],
        out_specs=vmem_specs(1)[0],
    )(w_out, w_fc, after)


def tower_kernel(axis, count, *refs):
    pieces, low, high = refs[:count], refs[-2], refs[-1]
    level = lax.axis_index("seq") // CORES
    for step, piece in enumerate(pieces):
        place = lax.rem(level + step, count)
        for half, start in ((low, 0), (high, count // 2)):

            @pl.when((place >= start) & (place < start + count // 2))
            def _():
                if axis == 1:
                    half[:, place - start] = piece[...]
                else:
                    half[place - start] = piece[...]


def build_tower(pieces, axis, after):
    count = len(pieces)
    shape = pieces[0].shape
    shape = (*shape[:axis], count // 2, *shape[axis:])
    return pl.pallas_call(
        functools.partial(tower_kernel, axis, count),
        out_shape=[jax.ShapeDtypeStruct(shape, BF16)] * 2,
        in_specs=vmem_specs(count) + [ANYWHERE] * len(after),
        out_specs=vmem_specs(2),
        compiler_params=pltpu.CompilerParams(vmem_limit_bytes=32 * 2**20),
    )(*pieces, *after)


def one_hot_order(order_ref):
    width = order_ref.shape[1]
    features = lax.broadcasted_iota(jnp.int32, (width, width), 0)
    return jnp.where(features == order_ref[...], 1.0, 0.0).astype(BF16)


def contract_last(left, right):
    return lax.dot_general(left, right, (((1,), (1,)), ((), ())), preferred_element_type=F32)


def middle_kernel(
    groups,
    half1,
    other1,
    half2,
    other2,
    attended,
    inputs,
    cotangent,
    order_ref,
    bout,
    gain,
    bias,
    bfc,
    bproj,
    outputs,
    grad_middle,
    grad_blocks,
    placed_a,
    placed_n,
    hidden,
    grad_pre,
    grad_out,
    sum_out,
    sum_gain,
    sum_bias,
    sum_fc,
    sum_proj,
    weights1,
    weights2,
    attended_rows,
    slopes,
    permuted,
    sems,
):
    parts = weights1.shape[0] - 1
    width = weights1.shape[2]
    side = width // CORES
    seq_count, block, _ = inputs.shape
    tokens = seq_count * block
    core = lax.rem(lax.axis_index("seq"), CORES)
    chips, rows2 = half2.shape[:2]
    copies = []
    for kind in range(parts + 1):
        for index, source in enumerate((half1, other1)):
            copies.append(
                pltpu.make_async_copy(
                    source.at[kind],
                    weights1.at[kind, pl.ds(index * side, side)],
                    sems.at[len(copies)],
                )
            )
    ready1 = len(copies)
    if chips == 1:
        copies.append(pltpu.make_async_copy(half2.at[0], weights2, sems.at[len(copies)]))
    for index, source in enumerate((half2, other2) if chips > 1 else ()):
        place = core if index == 0 else 1 - core
        for chip in range(chips):
            start = pl.multiple_of((chip * CORES + place) * rows2, rows2)
            copies.append(
                pltpu.make_async_copy(
                    source.at[chip], weights2.at[pl.ds(start, rows2)], sems.at[len(copies)]
                )
            )
    for copy in copies:
        copy.start()
    order = one_hot_order(order_ref)

    half_block = block // 2
    group = attended.shape[2] // 2
    for i in range(seq_count):
        for g in range(groups):
            for part in range(2):
                start = i * block + part * half_block
                attended_rows[start : start + half_block, g * group : (g + 1) * group] = attended[
                    i * groups + g, :, part * group : (part + 1) * group
                ]
    placed = jnp.dot(attended_rows[:, :width], order, preferred_element_type=F32).astype(BF16)
    placed_a[...] = placed
    for copy in copies[:2]:
        copy.wait()
    rows = inputs[...].astype(F32).reshape(tokens, width)
    middle = rows + (jnp.dot(placed, weights1[0], preferred_element_type=F32) + bout[...])
    center = jnp.mean(middle, -1, keepdims=True)
    centered = middle - center
    scale = lax.rsqrt(jnp.mean(centered * centered, -1, keepdims=True) + EPSILON)
    unit = centered * scale
    normed = (unit * gain[...] + bias[...]).astype(BF16)
    placed = jnp.dot(normed, order, preferred_element_type=F32).astype(BF16)
    placed_n[...] = placed
    for copy in copies[2:ready1]:
        copy.wait()
    curve = math.sqrt(2.0 / math.pi)
    for q in range(parts):
        lo = q * width
        pre = jnp.dot(placed, weights1[1 + q], preferred_element_type=F32)
        pre = pre + bfc[:, lo : lo + width]
        square = pre * pre
        tanh = jnp.tanh(curve * (pre + 0.044715 * (pre * square)))
        hidden[:, lo : lo + width] = (0.5 * pre * (1.0 + tanh)).astype(BF16)
        slopes[:, lo : lo + width] = 0.5 * (1.0 + tanh) + 0.5 * pre * (1.0 - tanh * tanh) * (
            curve * (1.0 + 3 * 0.044715 * square)
        )
    for copy in copies[ready1:]:
        copy.wait()
    result = middle + bproj[...]
    for q in range(parts):
        lo = q * width
        result += jnp.dot(
            hidden[:, lo : lo + width], weights2[lo : lo + width], preferred_element_type=F32
        )
    outputs[...] = result.astype(BF16).reshape(seq_count, block, width)

    branch = cotangent[...].reshape(tokens, width)
    grad_rows = branch.astype(F32)
    sum_proj[...] = jnp.sum(grad_rows, 0, keepdims=True)
    grad_placed = jnp.zeros((tokens, width), F32)
    for q in range(parts):
        lo = q * width
        grad = contract_last(branch, weights2[lo : lo + width]) * slopes[:, lo : lo + width]
        grad = grad.astype(BF16)
        grad_pre[:, lo : lo + width] = grad
        sum_fc[:, lo : lo + width] = jnp.sum(grad.astype(F32), 0, keepdims=True)
        grad_placed += contract_last(grad, weights1[1 + q])
    high = grad_placed.astype(BF16)
    rest = grad_placed - high.astype(F32)
    mid = rest.astype(BF16)
    low = (rest - mid.astype(F32)).astype(BF16)
    grad_normed = contract_last(high, order) + (contract_last(mid, order) + contract_last(low, order))
    sum_bias[...] = jnp.sum(grad_normed, 0, keepdims=True)
    sum_gain[...] = jnp.sum(grad_normed * unit, 0, keepdims=True)
    grad_unit = grad_normed * gain[...]
    part = jnp.mean(grad_unit, -1, keepdims=True)
    cross = jnp.mean(grad_unit * unit, -1, keepdims=True)
    grad_mid = grad_rows + scale * (grad_unit - part - unit * cross)
    grad_middle[...] = grad_mid
    grad_attn = grad_mid.astype(BF16)
    grad_out[...] = grad_attn
    sum_out[...] = jnp.sum(grad_attn.astype(F32), 0, keepdims=True)
    back = contract_last(grad_attn, weights1[0]).astype(BF16)
    if permuted.shape[1] > width:
        permuted[...] = jnp.zeros_like(permuted)
    permuted[:, :width] = contract_last(back, order).astype(BF16)
    for i in range(seq_count):
        for g in range(groups):
            for part in range(2):
                start = i * block + part * half_block
                grad_blocks[i * groups + g, :, part * group : (part + 1) * group] = permuted[
                    start : start + half_block, g * group : (g + 1) * group
                ]


def middle_block(half1, other1, half2, other2, attended, inputs, cotangent, order, vectors, groups):
    kinds, side, width = half1.shape
    parts = kinds - 1
    chips = half2.shape[0]
    seq_count, block, _ = inputs.shape
    tokens = seq_count * block
    wide = groups * attended.shape[2] // 2

    def shape(*dims, kind=BF16):
        return jax.ShapeDtypeStruct(dims, kind)

    return pl.pallas_call(
        functools.partial(middle_kernel, groups),
        out_shape=[
            shape(seq_count, block, width),
            shape(tokens, width, kind=F32),
            shape(*attended.shape),
            shape(tokens, width),
            shape(tokens, width),
            shape(tokens, parts * width),
            shape(tokens, parts * width),
            shape(tokens, width),
            shape(1, width, kind=F32),
            shape(1, width, kind=F32),
            shape(1, width, kind=F32),
            shape(1, parts * width, kind=F32),
            shape(1, width, kind=F32),
        ],
        in_specs=[ANYWHERE] * 4 + vmem_specs(9),
        out_specs=vmem_specs(13),
        scratch_shapes=[
            pltpu.VMEM((kinds, width, width), BF16),
            pltpu.VMEM((parts * width, width), BF16),
            pltpu.VMEM((tokens, wide), BF16),
            pltpu.VMEM((tokens, parts * width), F32),
            pltpu.VMEM((tokens, wide), BF16),
            pltpu.SemaphoreType.DMA((2 * kinds + 2 * chips,)),
        ],
        compiler_params=pltpu.CompilerParams(vmem_limit_bytes=50 * 2**20),
        cost_estimate=pl.CostEstimate(
            flops=tokens * width * width * 44, bytes_accessed=2**24, transcendentals=2**20
        ),
    )(half1, other1, half2, other2, attended, inputs, cotangent, order, *vectors)


def gradient_kernel(
    shard_rows, placed_a, placed_n, hidden, grad_pre, grad_out, cotangent, send, keep, turned, some
):
    width = placed_a.shape[1]
    side = width // CORES
    parts = hidden.shape[1] // width
    chips = side // shard_rows
    core = lax.rem(lax.axis_index("seq"), CORES)
    branch = cotangent[...].reshape(-1, width)
    if send.shape[0] > 1 + parts:
        for start in range(0, turned.shape[0], width):
            turned[start : start + width, :] = hidden[:, start : start + width].astype(F32).T
        for target, place in ((send, 1 - core), (keep, core)):
            for chip in range(chips):
                for i in range(parts):
                    start = ((chip * CORES + place) * parts + i) * shard_rows
                    start = pl.multiple_of(start, shard_rows)
                    to = i * side + chip * shard_rows
                    some[to : to + shard_rows, :] = turned[pl.ds(start, shard_rows), :]
            for i in range(parts):
                target[1 + parts + i] = jnp.dot(
                    some[i * side : (i + 1) * side, :].astype(BF16),
                    branch,
                    preferred_element_type=F32,
                ).astype(BF16)
    turned_a = placed_a[...].astype(F32).T.astype(BF16)
    turned_n = placed_n[...].astype(F32).T.astype(BF16)
    for target, start in ((send, side), (keep, 0)):
        target[0] = jnp.dot(
            turned_a[start : start + side], grad_out[...], preferred_element_type=F32
        ).astype(BF16)
        for q in range(parts):
            target[1 + q] = jnp.dot(
                turned_n[start : start + side],
                grad_pre[:, q * width : (q + 1) * width],
                preferred_element_type=F32,
            ).astype(BF16)


def weight_gradients(placed_a, placed_n, hidden, grad_pre, grad_out, cotangent, shard_rows):
    tokens, width = placed_a.shape
    parts = hidden.shape[1] // width
    kinds = 1 + parts * (1 if shard_rows % 8 else 2)
    shape = jax.ShapeDtypeStruct((kinds, width // CORES, width), BF16)
    return pl.pallas_call(
        functools.partial(gradient_kernel, shard_rows),
        out_shape=[shape, shape],
        in_specs=vmem_specs(6),
        out_specs=vmem_specs(2),
        scratch_shapes=[
            pltpu.VMEM((parts * width, tokens), F32),
            pltpu.VMEM((parts * width // CORES, tokens), F32),
        ],
        compiler_params=pltpu.CompilerParams(vmem_limit_bytes=50 * 2**20),
        cost_estimate=pl.CostEstimate(
            flops=tokens * width * width * 18, bytes_accessed=2**24, transcendentals=0
        ),
    )(placed_a, placed_n, hidden, grad_pre, grad_out, cotangent)


def masked_scores(keys, queries, id_column, id_row, first):
    scores = lax.dot_general(keys, queries, (((1,), (1,)), ((), ())), preferred_element_type=F32)
    key_pos = lax.broadcasted_iota(jnp.int32, scores.shape, 0)
    query_pos = lax.broadcasted_iota(jnp.int32, scores.shape, 1) + first
    allowed = (key_pos <= query_pos) & (id_column == id_row)
    return jnp.where(allowed, scores, MASKED)


def column_of(id_row):
    length = id_row.shape[1]
    return jnp.broadcast_to(id_row, (LANES, length)).T[:, :1]


def forward_kernel(
    seq_count,
    heads,
    head_size,
    step_rows,
    block,
    rows_ref,
    weight,
    gain,
    bias,
    bqv,
    after,
    out,
    stats,
    whole,
    normed,
    ids,
    result,
    qkv_bias,
):
    length = whole.shape[0]
    group = heads * head_size
    width = weight.shape[0]
    index = lax.rem(lax.axis_index("seq"), lax.axis_size("seq") // seq_count)
    qkv_bias[...] = jnp.zeros_like(qkv_bias)
    for lo in range(0, width, group):
        here = index == lo // group
        for base, start in ((0, 0), (width, 2 * group)):
            piece = jnp.where(here, bqv[:, base + lo : base + lo + group], 0.0)
            qkv_bias[:, start : start + group] += piece
    for i in range(length // block):
        rows = norm_affine(rows_ref[i, :block, :].astype(F32), gain[...], bias[...])
        normed[i * block : (i + 1) * block, :] = rows.astype(BF16)
    id_rows = [rows_ref[i, block:, :block].astype(F32)[:1] for i in range(length // block)]
    id_row = jnp.concatenate(id_rows, 1)
    ids[...] = id_row
    id_column = column_of(id_row)
    for first in range(0, length, step_rows):
        last = first + step_rows
        product = jnp.dot(normed[first:last, :], weight[...], preferred_element_type=F32)
        whole[first:last, :] = (product + qkv_bias[...]).astype(BF16)
    values_t = whole[:, 2 * group : 3 * group].astype(F32).T.astype(BF16)
    for first in range(0, length, step_rows):
        last = first + step_rows
        tops = []
        for head in range(heads):
            lo = head * head_size
            queries = whole[first:last, lo : lo + head_size] * BF16(head_size**-0.5)
            keys = whole[:last, group + lo : group + lo + head_size]
            scores = masked_scores(keys, queries, id_column[:last], id_row[:, first:last], first)
            highest = jnp.max(scores, 0, keepdims=True)
            weights = jnp.exp(scores - highest)
            total = jnp.sum(weights, 0, keepdims=True)
            probs = (weights * (1.0 / total)).astype(BF16)
            tops.append(
                jnp.dot(
                    values_t[lo : lo + head_size, :last], probs, preferred_element_type=F32
                )
            )
            stats[head : head + 1, first:last] = highest + jnp.log(total)
        result[first:last, :] = jnp.concatenate(tops, 0).T.astype(BF16)
    half = block // 2
    for start in range(0, length, block):
        out[start // 2 : start // 2 + half, :group] = result[start : start + half, :]
        out[start // 2 : start // 2 + half, group:] = result[start + half : start + block, :]


def backward_kernel(
    heads,
    head_size,
    step_rows,
    block,
    whole,
    grads,
    stats,
    ids,
    after1,
    after2,
    out,
    grad_out,
    grad_query,
    grad_key,
    grad_value,
):
    length = whole.shape[0]
    group = heads * head_size
    half = block // 2
    for start in range(0, length, block):
        packed = grads[start // 2 : start // 2 + half, :]
        grad_out[start : start + half, :] = packed[:, :group]
        grad_out[start + half : start + block, :] = packed[:, group:]
    id_row = ids[...]
    id_column = column_of(id_row)
    keys_t = whole[:, group : 2 * group].astype(F32).T.astype(BF16)
    factor = head_size**-0.5
    grad_key[...] = jnp.zeros_like(grad_key)
    grad_value[...] = jnp.zeros_like(grad_value)
    for first in range(0, length, step_rows):
        last = first + step_rows
        tops = []
        for head in range(heads):
            lo = head * head_size
            queries = whole[first:last, lo : lo + head_size] * BF16(factor)
            keys = whole[:last, group + lo : group + lo + head_size]
            values = whole[:last, 2 * group + lo : 2 * group + lo + head_size]
            grad = grad_out[first:last, lo : lo + head_size]
            scores = masked_scores(keys, queries, id_column[:last], id_row[:, first:last], first)
            probs = jnp.exp(scores - stats[head : head + 1, first:last])
            grad_probs = lax.dot_general(
                values, grad, (((1,), (1,)), ((), ())), preferred_element_type=F32
            )
            delta = jnp.sum(probs * grad_probs, 0, keepdims=True)
            grad_scores = (probs * (grad_probs - delta)).astype(BF16)
            tops.append(
                jnp.dot(
                    keys_t[lo : lo + head_size, :last], grad_scores, preferred_element_type=F32
                )
                * factor
            )
            grad_key[head, :last, :] += jnp.dot(
                grad_scores, queries, preferred_element_type=F32
            )
            grad_value[head, :last, :] += jnp.dot(
                probs.astype(BF16), grad, preferred_element_type=F32
            )
        grad_query[first:last, :] = jnp.concatenate(tops, 0).T.astype(BF16)
    out[:, :group] = grad_query[...]
    for head in range(heads):
        lo = head * head_size
        out[:, group + lo : group + lo + head_size] = grad_key[head].astype(BF16)
        out[:, 2 * group + lo : 2 * group + lo + head_size] = grad_value[head].astype(BF16)


def attend_forward(rows, weight, gain, bias, bqv, after, seq_count, heads, head_size, block):
    length = rows.shape[0] * block
    width = rows.shape[2]
    group = heads * head_size
    pairs = length * length // 2 * heads
    return pl.pallas_call(
        functools.partial(forward_kernel, seq_count, heads, head_size, min(256, length), block),
        out_shape=[
            jax.ShapeDtypeStruct((length // 2, 2 * group), BF16),
            jax.ShapeDtypeStruct((heads, length), F32),
            jax.ShapeDtypeStruct((length, 3 * group), BF16),
            jax.ShapeDtypeStruct((length, width), BF16),
            jax.ShapeDtypeStruct((1, length), F32),
        ],
        in_specs=vmem_specs(5) + [ANYWHERE],
        out_specs=vmem_specs(5),
        scratch_shapes=[pltpu.VMEM((length, group), BF16), pltpu.VMEM((1, 3 * group), F32)],
        compiler_params=pltpu.CompilerParams(vmem_limit_bytes=48 * 2**20),
        cost_estimate=pl.CostEstimate(
            flops=pairs * head_size * 4 + length * width * group * 6,
            bytes_accessed=length * width * 8,
            transcendentals=pairs,
        ),
    )(rows, weight, gain, bias, bqv, after)


def attend_backward(whole, grads, stats, ids, after, heads, head_size, block):
    length, width = whole.shape
    group = heads * head_size
    pairs = length * length // 2 * heads
    return pl.pallas_call(
        functools.partial(backward_kernel, heads, head_size, min(256, length), block),
        out_shape=jax.ShapeDtypeStruct((length, 3 * group), BF16),
        in_specs=vmem_specs(4) + [ANYWHERE] * 2,
        out_specs=vmem_specs(1)[0],
        scratch_shapes=[
            pltpu.VMEM((length, group), BF16),
            pltpu.VMEM((length, group), BF16),
            pltpu.VMEM((heads, length, head_size), F32),
            pltpu.VMEM((heads, length, head_size), F32),
        ],
        compiler_params=pltpu.CompilerParams(vmem_limit_bytes=48 * 2**20),
        cost_estimate=pl.CostEstimate(
            flops=pairs * head_size * 10, bytes_accessed=length * width * 6, transcendentals=pairs
        ),
    )(whole, grads, stats, ids, *after)


def on_device(
    inputs,
    segments,
    cotangent,
    ln1_gain,
    ln1_bias,
    w_qkv,
    b_qv,
    w_out,
    b_out,
    ln2_gain,
    ln2_bias,
    w_fc,
    b_fc,
    w_proj,
    b_proj,
):
    seq_count, block, width = inputs.shape
    head_size = width // HEADS
    tokens = seq_count * block
    count = lax.axis_size("seq")
    devices = count * lax.axis_size("dp")
    groups = count // seq_count
    heads = -(-HEADS // groups)
    spare = groups * heads - HEADS
    group = heads * head_size

    vectors = (ln1_gain, ln1_bias, b_qv, b_out, ln2_gain, ln2_bias, b_fc, b_proj)
    sizes = tuple(vector.shape[0] for vector in vectors)
    shard_rows = w_out.shape[0] // width
    parts = w_fc.shape[0] // w_out.shape[0]
    classes = groups // CORES
    chips = devices // CORES
    place = lax.axis_index("seq")
    core = place % CORES
    group_index = place % groups

    columns, blocks = first_blocks(
        w_qkv.reshape(shard_rows, 3 * width),
        inputs,
        segments,
        [vector.reshape(1, -1) for vector in vectors],
        classes,
        group,
    )
    lines, sequence = gather_sequence(blocks)
    tower_a = gather_columns(columns)
    heights = tower_a.shape[0]
    half_a = gather_plane(tower_a[: heights // 2], tower_a[heights // 2 :], 0)
    left, right = half_a[..., : 3 * group], half_a[..., 3 * group :]
    mine_a = jnp.where(core == 0, left, right)
    whole_a = ordered(core, mine_a, swap_core(jnp.where(core == 0, right, left)), 1)
    whole_a = whole_a.reshape(devices, shard_rows + ROWS, 3 * group)
    wqkv = whole_a[:, :shard_rows].reshape(width, 3 * group)
    gain1, bias1, bqv, bout, gain2, bias2, bfc, bproj = unpack_small(
        whole_a[:, shard_rows:, :LANES], sizes
    )

    stacked = stack_weights(w_out.reshape(-1, width), w_fc.reshape(-1, parts * width), tower_a)
    low1, high1 = build_tower(z_pieces(stacked), 1, [whole_a, lines])
    attended, stats, qkv, normed1, ids = attend_forward(
        sequence, wqkv, gain1, bias1, bqv, low1, seq_count, heads, head_size, block
    )
    pieces2 = z_pieces(gate(w_proj.reshape(-1, width), lines))
    low2, high2 = build_tower(pieces2, 0, [attended])
    attended = exchange(attended.reshape(count, block // 2, 2 * group))
    half1 = gather_plane(low1, high1, 1).reshape(1 + parts, -1, width)
    half2 = gather_plane(low2, high2, 0)
    other1 = swap_core(half1)
    other2 = swap_core(half2)
    aligned = half2.shape[1] % 16 == 0
    if not aligned:
        half2 = ordered(core, half2, other2, 1).reshape(1, parts * width, width)

    spot = jnp.arange(width, dtype=jnp.int32)
    side = width // CORES
    own_core = (core + spot // side) % CORES
    order = (spot % side // shard_rows * CORES + own_core) * shard_rows + spot % shard_rows
    (
        outputs,
        grad_middle,
        grad_blocks,
        placed_a,
        placed_n,
        hidden,
        grad_pre,
        grad_out,
        grad_bout,
        grad_gain2,
        grad_bias2,
        grad_bfc,
        grad_bproj,
    ) = middle_block(
        half1,
        other1,
        half2,
        other2,
        attended,
        inputs,
        cotangent,
        order.reshape(1, width),
        (bout, gain2, bias2, bfc, bproj),
        groups,
    )
    grad_blocks = exchange(grad_blocks).reshape(-1, 2 * group)
    send_b, keep_b = weight_gradients(
        placed_a, placed_n, hidden, grad_pre, grad_out, cotangent, shard_rows
    )
    if send_b.shape[0] == 1 + parts:
        grad_wproj = lax.dot_general(
            hidden,
            cotangent.reshape(tokens, width),
            (((0,), (0,)), ((), ())),
            preferred_element_type=F32,
        )
        grad_wproj = grad_wproj.astype(BF16).reshape(chips, CORES, parts, shard_rows, width)
        grad_wproj = grad_wproj.transpose(1, 2, 0, 3, 4).reshape(CORES, parts, -1, width)
        send_b = jnp.concatenate([send_b, pick(grad_wproj, 1 - core, 0)], 0)
        keep_b = jnp.concatenate([keep_b, pick(grad_wproj, core, 0)], 0)
    sum_b = add(keep_b, swap_core(send_b)).reshape(-1, chips, shard_rows, width)
    attention_grads = []

    def between(*after):
        attention_grads.append(
            attend_backward(qkv, grad_blocks, stats, ids, after, heads, head_size, block)
        )
        return attention_grads[0]

    own_b = scatter_z(scatter_plane(sum_b, 1, between), 1)
    grad_qkv = attention_grads[0]

    def blocks_of(value, rows):
        return value.astype(BF16).reshape(chips, CORES, rows, -1)

    rows = inputs.astype(F32).reshape(tokens, width)
    grad_normed1 = lax.dot_general(
        grad_qkv, wqkv, (((1,), (1,)), ((), ())), preferred_element_type=F32
    )
    own_normed1 = scatter_sequence(grad_normed1.astype(BF16).reshape(count, block, width))
    _, norm1_back = jax.vjp(lambda value: norm_affine(value, gain1, bias1), rows)
    (grad_in_part,) = norm1_back(own_normed1.astype(F32).reshape(tokens, width))
    grad_inputs = (grad_middle + grad_in_part).astype(BF16).reshape(inputs.shape)

    long_rows = sequence[:, :block].astype(F32).reshape(count * block, width)
    _, norm1_long_back = jax.vjp(lambda g, b: norm_affine(long_rows, g, b), gain1, bias1)
    grad_gain1, grad_bias1 = norm1_long_back(grad_normed1)
    grad_wqkv = lax.dot_general(
        normed1, grad_qkv, (((0,), (0,)), ((), ())), preferred_element_type=F32
    )
    sums = jnp.sum(grad_qkv, 0, dtype=F32).reshape(3, group)
    here = (jnp.arange(groups) == group_index)[None, :, None]
    grad_bqv = jnp.where(here, jnp.stack([sums[0], sums[2]])[:, None], 0.0)
    grad_bqv = grad_bqv.reshape(2, groups * heads, head_size)[:, :HEADS]
    grads = (
        grad_gain1,
        grad_bias1,
        grad_bqv,
        grad_bout,
        grad_gain2,
        grad_bias2,
        grad_bfc,
        grad_bproj,
    )
    small_grads = pack_small([grad.reshape(1, -1) for grad in grads], sizes, devices)
    small_grads = jnp.pad(small_grads, ((0, 0), (0, 0), (0, 3 * group - LANES)))
    block_a = jnp.concatenate(
        [blocks_of(grad_wqkv, shard_rows), small_grads.reshape(chips, CORES, ROWS, -1)], 2
    )
    send_a, keep_a = pick(block_a, 1 - core, 1), pick(block_a, core, 1)
    got_a = swap_core(send_a)
    pair_a = jnp.concatenate(
        [jnp.where(core == 0, keep_a, got_a), jnp.where(core == 0, got_a, keep_a)], -1
    )
    own_a = scatter_columns(scatter_plane(pair_a, 0))
    own_small = jnp.sum(
        own_a[:, shard_rows:].reshape(classes, ROWS, CORES, 3 * group)[..., :LANES], (0, 2)
    )
    own = [own_small[i, :size] for i, size in enumerate(sizes)]
    own_qkv = own_a[:, :shard_rows].reshape(classes, shard_rows, CORES, 3, group)
    own_qkv = own_qkv.transpose(1, 3, 0, 2, 4).reshape(shard_rows, 3, groups * heads, head_size)
    own_qkv = own_qkv[:, :, :HEADS].reshape(-1)
    return (
        outputs,
        grad_inputs,
        own[0],
        own[1],
        own_qkv,
        own[2],
        own_b[0].reshape(-1),
        own[3],
        own[4],
        own[5],
        own_b[1 : 1 + parts].transpose(1, 0, 2).reshape(-1),
        own[6],
        own_b[1 + parts :].reshape(-1),
        own[7],
    )


def solution(mesh):
    token_spec = P("dp", "seq", None)
    flat_spec = P(("dp", "seq"))
    in_specs = (token_spec, P("dp", "seq"), token_spec) + (flat_spec,) * 12
    out_specs = (token_spec, token_spec) + (flat_spec,) * 12
    return jax.shard_map(
        on_device, mesh=mesh, in_specs=in_specs, out_specs=out_specs, check_vma=False
    )
```

```python
import functools
import math

import jax
import jax.numpy as jnp
from jax import lax
from jax.experimental import pallas as pl
from jax.experimental.pallas import tpu as pltpu
from jax.sharding import PartitionSpec as P

HEADS = 12
CORES = 2


EPSILON = 1e-05
MASKED = -1e30
F32 = jnp.float32
BF16 = jnp.bfloat16


def norm_affine(values, gain, bias):
    center = jnp.mean(values, -1, keepdims=True)
    centered = values - center
    variance = jnp.mean(centered * centered, -1, keepdims=True)
    return centered * lax.rsqrt(variance + EPSILON) * gain + bias


ANYWHERE = pl.BlockSpec(memory_space=pl.ANY)
LIGHT = pl.CostEstimate(flops=1, bytes_accessed=1, transcendentals=0)


def shift_z(value, step):
    size = lax.axis_size("seq")
    return lax.ppermute(value, "seq", [(i, (i + CORES * step) % size) for i in range(size)])


def swap_core(value):
    size = lax.axis_size("seq")
    return lax.ppermute(value, "seq", [(i, i ^ 1) for i in range(size)])


def swap_dp(value, bit):
    size = lax.axis_size("dp")
    return lax.ppermute(value, "dp", [(i, i ^ bit) for i in range(size)])


def ordered(flag, mine, other, axis):
    first = jnp.where(flag == 0, mine, other)
    second = jnp.where(flag == 0, other, mine)
    return jnp.stack([first, second], axis)


def roll_blocks(pieces, place):
    count = len(pieces)
    stacked = jnp.stack(pieces)
    twice = jnp.concatenate([stacked, stacked])
    return lax.dynamic_slice_in_dim(twice, lax.rem(count - place, count), count, 0)


def z_pieces(shard):
    heights = lax.axis_size("seq") // CORES
    return [shard] + [shift_z(shard, -step) for step in range(1, heights)]


def swap_z(value, bit):
    size = lax.axis_size("seq")
    return lax.ppermute(value, "seq", [(i, i ^ (CORES * bit)) for i in range(size)])


def gather_plane(low, high, axis, first=None, second=None):
    def move(value, bit, after):
        moved = swap_dp(value, bit)
        return moved if after is None else gate(moved, after)

    if lax.axis_size("dp") == 4:
        plane = lax.axis_index("dp")
        y, x = plane // 2, plane % 2
        low_x = ordered(x, low, move(low, 1, first), axis)
        high_y = ordered(y, high, move(high, 2, first), axis)
        low_all = ordered(y, low_x, move(low_x, 2, second), axis)
        high_all = ordered(x, high_y, move(high_y, 1, second), axis + 1)
        half = jnp.concatenate([low_all, high_all], axis + 2)
        count = 4 * half.shape[axis + 2]
    else:
        tower = jnp.concatenate([low, high], axis)
        half = lax.all_gather(tower, "dp", axis=axis, tiled=True)
        return half
    return half.reshape(*low.shape[:axis], count, *low.shape[axis + 1 :])


def pick(value, index, axis):
    return lax.dynamic_index_in_dim(value, index, axis, keepdims=False)


def add(mine, other):
    return (mine.astype(F32) + other.astype(F32)).astype(mine.dtype)


def scatter_plane(split, axis, between=None):
    planes = lax.axis_size("dp")
    heights = lax.axis_size("seq") // CORES
    if planes != 4:
        if between is not None:
            between(split, split)
            between(split, split)
        return lax.psum_scatter(split, "dp", scatter_dimension=axis, tiled=True)
    plane = lax.axis_index("dp")
    y, x = plane // 2, plane % 2
    split = split.reshape(*split.shape[:axis], 2, 2, heights, *split.shape[axis + 1 :])
    low = lax.slice_in_dim(split, 0, heights // 2, axis=axis + 2)
    high = lax.slice_in_dim(split, heights // 2, heights, axis=axis + 2)
    low_send, high_send = pick(low, 1 - y, axis), pick(high, 1 - x, axis + 1)
    low_got, high_got = swap_dp(low_send, 2), swap_dp(high_send, 1)
    if between is not None:
        after = between(low_send, high_send)
        low_got, high_got = gate(low_got, after), gate(high_got, after)
    low = add(pick(low, y, axis), low_got)
    high = add(pick(high, x, axis + 1), high_got)
    if between is not None:
        between(low, high)
    low = add(pick(low, x, axis), swap_dp(pick(low, 1 - x, axis), 1))
    high = add(pick(high, y, axis), swap_dp(pick(high, 1 - y, axis), 2))
    return jnp.concatenate([low, high], axis)


def scatter_z(tower, axis):
    heights = lax.axis_size("seq") // CORES
    level = lax.axis_index("seq") // CORES
    mine = pick(tower, level, axis).astype(F32)
    for step in range(1, heights):
        mine += shift_z(pick(tower, lax.rem(level + step, heights), axis), step).astype(F32)
    return mine


def z_bits():
    heights = lax.axis_size("seq") // CORES
    level = lax.axis_index("seq") // CORES
    top = heights // 2
    return level, top, level // top


def gather_sequence(blocks):
    level, top, half = z_bits()
    core = lax.axis_index("seq") % CORES
    held = ordered(half, pick(blocks, half, 0), swap_z(pick(blocks, 1 - half, 0), top), 0)
    axis, bit = 1, top // 2
    while bit:
        held = ordered(level // bit % 2, held, swap_z(held, bit), axis)
        axis, bit = axis + 1, bit // 2
    return held, ordered(core, held, swap_core(held), axis).reshape(-1, *blocks.shape[1:])


def scatter_sequence(partial):
    level, top, half = z_bits()
    core = lax.axis_index("seq") % CORES
    shape = partial.shape[1:]
    count = top.bit_length()
    held = partial.reshape(*[2] * (count + 1), *shape)
    held = add(pick(held, core, count), swap_core(pick(held, 1 - core, count)))
    axis, bit = count - 1, 1
    while bit < top:
        flag = level // bit % 2
        held = add(pick(held, flag, axis), swap_z(pick(held, 1 - flag, axis), bit))
        axis, bit = axis - 1, bit * 2
    return ordered(half, pick(held, half, 0), swap_z(pick(held, 1 - half, 0), top), 0)


def gather_columns(blocks):
    level, top, half = z_bits()
    shape = blocks.shape[1:]
    count = top.bit_length() - 1
    held = blocks.reshape(*[2] * count, *shape)
    bit = top // 2
    while bit:
        flag = level // bit % 2
        got = swap_z(pick(held, 1 - flag, 0), bit)
        held = ordered(flag, pick(held, flag, 0), got, count - 1)
        bit //= 2
    return held, ordered(half, held, swap_z(held, top), 0).reshape(-1, *shape)


def scatter_columns(tower, after):
    level, top, half = z_bits()
    shape = tower.shape[1:]
    count = top.bit_length() - 1
    held = tower.reshape(*[2] * (count + 1), *shape)
    got = gate(swap_z(pick(held, 1 - half, 0), top), after)
    held = add(pick(held, half, 0), got)
    bit = 1
    while bit < top:
        flag = level // bit % 2
        got = swap_z(pick(held, 1 - flag, count - 1), bit)
        held = ordered(flag, pick(held, flag, count - 1), got, 0)
        bit *= 2
    return held.reshape(-1, *shape).astype(F32)


def exchange(blocks):
    return lax.all_to_all(blocks, "seq", split_axis=0, concat_axis=0, tiled=True)


ROWS = 8
LANES = 128


def vmem_specs(count):
    return [pl.BlockSpec(memory_space=pltpu.VMEM) for _ in range(count)]


def place_lanes(size, total):
    source = lax.broadcasted_iota(jnp.int32, (LANES, total), 0)
    target = lax.rem(lax.broadcasted_iota(jnp.int32, (LANES, total), 1), size)
    return jnp.where(source == target, 1.0, 0.0).astype(BF16)


def owned_lanes(devices, size):
    device = lax.broadcasted_iota(jnp.int32, (devices, devices * size), 0)
    lane = lax.broadcasted_iota(jnp.int32, (devices, devices * size), 1)
    offset = lane - device * size
    return (offset >= 0) & (offset < size)


def unpack_kernel(sizes, small_ref, *outs):
    devices = small_ref.shape[0]
    small = small_ref[...].astype(F32)
    for i, (size, out) in enumerate(zip(sizes, outs)):
        spread = jnp.dot(
            small[:, i, :].astype(BF16),
            place_lanes(size, devices * size),
            preferred_element_type=F32,
        )
        out[...] = jnp.sum(jnp.where(owned_lanes(devices, size), spread, 0.0), 0, keepdims=True)


def unpack_small(small, sizes):
    devices = small.shape[0]
    return pl.pallas_call(
        functools.partial(unpack_kernel, sizes),
        out_shape=[jax.ShapeDtypeStruct((1, devices * size), F32) for size in sizes],
        in_specs=vmem_specs(1),
        out_specs=vmem_specs(len(sizes)),
        compiler_params=pltpu.CompilerParams(vmem_limit_bytes=32 * 2**20),
        cost_estimate=LIGHT,
    )(small)


def pack_kernel(sizes, *refs):
    grads, packed, rows = refs[: len(sizes)], refs[len(sizes)], refs[len(sizes) + 1]
    devices = packed.shape[0]
    for i, (size, grad) in enumerate(zip(sizes, grads)):
        owned = jnp.where(owned_lanes(devices, size), grad[...], 0.0).astype(BF16)
        rows[:, i, :] = lax.dot_general(
            owned,
            place_lanes(size, devices * size),
            (((1,), (1,)), ((), ())),
            preferred_element_type=F32,
        )
    packed[...] = rows[...].astype(BF16)


def pack_small(grads, sizes, devices):
    return pl.pallas_call(
        functools.partial(pack_kernel, sizes),
        out_shape=jax.ShapeDtypeStruct((devices, ROWS, LANES), BF16),
        in_specs=vmem_specs(len(sizes)),
        out_specs=vmem_specs(1)[0],
        scratch_shapes=[pltpu.VMEM((devices, ROWS, LANES), F32)],
        compiler_params=pltpu.CompilerParams(vmem_limit_bytes=32 * 2**20),
        cost_estimate=LIGHT,
    )(*grads)


def gate(value, *after):
    def kernel(*refs):
        pass

    return pl.pallas_call(
        kernel,
        out_shape=jax.ShapeDtypeStruct(value.shape, value.dtype),
        in_specs=[ANYWHERE] * (1 + len(after)),
        out_specs=ANYWHERE,
        input_output_aliases={0: 0},
        cost_estimate=LIGHT,
    )(value, *after)


def first_kernel(group, weight, rows, marks, *refs):
    vectors, (columns, blocks, lines, extra) = refs[:-4], refs[-4:]
    classes, _, width_pair = columns.shape
    shard_rows, width = weight.shape[0], weight.shape[1] // 3
    lines[...] = jnp.zeros_like(lines)
    for i, vector in enumerate(vectors):
        for start in range(0, width_pair, 3 * group):
            at = shard_rows + i
            lines[at : at + 1, start : start + vector.shape[1]] = vector[...].astype(F32)
    for kind in range(classes):
        for core in range(CORES):
            lo = (kind * CORES + core) * group
            for part in range(3):
                start = (core * 3 + part) * group
                if lo < width:
                    piece = weight[:, part * width + lo : part * width + lo + group].astype(F32)
                else:
                    piece = jnp.zeros((shard_rows, group), F32)
                lines[:shard_rows, start : start + group] = piece
        columns[kind] = lines[...].astype(BF16)
    block = rows.shape[1]
    extra[...] = jnp.zeros_like(extra)
    for i in range(rows.shape[0]):
        blocks[i, :block, :] = rows[i]
        extra[:1, :block] = marks[i : i + 1, :].astype(F32)
        blocks[i, block:, :] = extra[...].astype(BF16)


def first_blocks(weight, rows, marks, vectors, classes, group):
    shard_rows = weight.shape[0]
    count, block, width = rows.shape
    return pl.pallas_call(
        functools.partial(first_kernel, group),
        out_shape=[
            jax.ShapeDtypeStruct((classes, shard_rows + ROWS, CORES * 3 * group), BF16),
            jax.ShapeDtypeStruct((count, block + 16, width), BF16),
        ],
        in_specs=vmem_specs(3 + len(vectors)),
        out_specs=vmem_specs(2),
        scratch_shapes=[
            pltpu.VMEM((shard_rows + ROWS, CORES * 3 * group), F32),
            pltpu.VMEM((16, width), F32),
        ],
    )(weight, rows, marks, *vectors)


def stack_kernel(out_ref, fc_ref, after, stacked):
    width = out_ref.shape[1]
    stacked[0] = out_ref[...]
    for i in range(fc_ref.shape[1] // width):
        stacked[1 + i] = fc_ref[:, i * width : (i + 1) * width]


def stack_weights(w_out, w_fc, after):
    rows, width = w_out.shape
    return pl.pallas_call(
        stack_kernel,
        out_shape=jax.ShapeDtypeStruct((1 + w_fc.shape[1] // width, rows, width), BF16),
        in_specs=vmem_specs(2) + [ANYWHERE],
        out_specs=vmem_specs(1)[0],
        cost_estimate=LIGHT,
    )(w_out, w_fc, after)


def tower_kernel(axis, count, *refs):
    pieces, low, high = refs[:count], refs[-2], refs[-1]
    level = lax.axis_index("seq") // CORES
    for step, piece in enumerate(pieces):
        place = lax.rem(level + step, count)
        for half, start in ((low, 0), (high, count // 2)):

            @pl.when((place >= start) & (place < start + count // 2))
            def _():
                if axis == 1:
                    half[:, place - start] = piece[...]
                else:
                    half[place - start] = piece[...]


def build_tower(pieces, axis, after):
    count = len(pieces)
    shape = pieces[0].shape
    shape = (*shape[:axis], count // 2, *shape[axis:])
    return pl.pallas_call(
        functools.partial(tower_kernel, axis, count),
        out_shape=[jax.ShapeDtypeStruct(shape, BF16)] * 2,
        in_specs=vmem_specs(count) + [ANYWHERE] * len(after),
        out_specs=vmem_specs(2),
        compiler_params=pltpu.CompilerParams(vmem_limit_bytes=32 * 2**20),
        cost_estimate=LIGHT,
    )(*pieces, *after)


def one_hot_order(order_ref):
    width = order_ref.shape[1]
    features = lax.broadcasted_iota(jnp.int32, (width, width), 0)
    return jnp.where(features == order_ref[...], 1.0, 0.0).astype(BF16)


def contract_last(left, right):
    return lax.dot_general(left, right, (((1,), (1,)), ((), ())), preferred_element_type=F32)


def middle_kernel(
    groups,
    half1,
    other1,
    half2,
    other2,
    attended,
    inputs,
    cotangent,
    order_ref,
    bout,
    gain,
    bias,
    bfc,
    bproj,
    outputs,
    grad_middle,
    grad_blocks,
    placed_a,
    placed_n,
    hidden,
    grad_pre,
    grad_out,
    sum_out,
    sum_gain,
    sum_bias,
    sum_fc,
    sum_proj,
    weights1,
    weights2,
    attended_rows,
    slopes,
    permuted,
    sems,
):
    parts = weights1.shape[0] - 1
    width = weights1.shape[2]
    side = width // CORES
    seq_count, block, _ = inputs.shape
    tokens = seq_count * block
    core = lax.rem(lax.axis_index("seq"), CORES)
    chips, rows2 = half2.shape[:2]
    copies = []
    for kind in range(parts + 1):
        for index, source in enumerate((half1, other1)):
            copies.append(
                pltpu.make_async_copy(
                    source.at[kind],
                    weights1.at[kind, pl.ds(index * side, side)],
                    sems.at[len(copies)],
                )
            )
    ready1 = len(copies)
    if chips == 1:
        copies.append(pltpu.make_async_copy(half2.at[0], weights2, sems.at[len(copies)]))
    for index, source in enumerate((half2, other2) if chips > 1 else ()):
        place = core if index == 0 else 1 - core
        for chip in range(chips):
            start = pl.multiple_of((chip * CORES + place) * rows2, rows2)
            copies.append(
                pltpu.make_async_copy(
                    source.at[chip], weights2.at[pl.ds(start, rows2)], sems.at[len(copies)]
                )
            )
    for copy in copies:
        copy.start()
    order = one_hot_order(order_ref)

    half_block = block // 2
    group = attended.shape[2] // 2
    for i in range(seq_count):
        for g in range(groups):
            for part in range(2):
                start = i * block + part * half_block
                attended_rows[start : start + half_block, g * group : (g + 1) * group] = attended[
                    i * groups + g, :, part * group : (part + 1) * group
                ]
    placed = jnp.dot(attended_rows[:, :width], order, preferred_element_type=F32).astype(BF16)
    placed_a[...] = placed
    for copy in copies[:2]:
        copy.wait()
    rows = inputs[...].astype(F32).reshape(tokens, width)
    middle = rows + (jnp.dot(placed, weights1[0], preferred_element_type=F32) + bout[...])
    center = jnp.mean(middle, -1, keepdims=True)
    centered = middle - center
    scale = lax.rsqrt(jnp.mean(centered * centered, -1, keepdims=True) + EPSILON)
    unit = centered * scale
    normed = (unit * gain[...] + bias[...]).astype(BF16)
    placed = jnp.dot(normed, order, preferred_element_type=F32).astype(BF16)
    placed_n[...] = placed
    for copy in copies[2:ready1]:
        copy.wait()
    curve = math.sqrt(2.0 / math.pi)
    for q in range(parts):
        lo = q * width
        pre = jnp.dot(placed, weights1[1 + q], preferred_element_type=F32)
        pre = pre + bfc[:, lo : lo + width]
        square = pre * pre
        tanh = jnp.tanh(curve * (pre + 0.044715 * (pre * square)))
        hidden[:, lo : lo + width] = (0.5 * pre * (1.0 + tanh)).astype(BF16)
        slopes[:, lo : lo + width] = 0.5 * (1.0 + tanh) + 0.5 * pre * (1.0 - tanh * tanh) * (
            curve * (1.0 + 3 * 0.044715 * square)
        )
    for copy in copies[ready1:]:
        copy.wait()
    result = middle + bproj[...]
    for q in range(parts):
        lo = q * width
        result += jnp.dot(
            hidden[:, lo : lo + width], weights2[lo : lo + width], preferred_element_type=F32
        )
    outputs[...] = result.astype(BF16).reshape(seq_count, block, width)

    branch = cotangent[...].reshape(tokens, width)
    grad_rows = branch.astype(F32)
    sum_proj[...] = jnp.sum(grad_rows, 0, keepdims=True)
    grad_placed = jnp.zeros((tokens, width), F32)
    for q in range(parts):
        lo = q * width
        grad = contract_last(branch, weights2[lo : lo + width]) * slopes[:, lo : lo + width]
        grad = grad.astype(BF16)
        grad_pre[:, lo : lo + width] = grad
        sum_fc[:, lo : lo + width] = jnp.sum(grad.astype(F32), 0, keepdims=True)
        grad_placed += contract_last(grad, weights1[1 + q])
    high = grad_placed.astype(BF16)
    rest = grad_placed - high.astype(F32)
    mid = rest.astype(BF16)
    low = (rest - mid.astype(F32)).astype(BF16)
    grad_normed = contract_last(high, order) + (contract_last(mid, order) + contract_last(low, order))
    sum_bias[...] = jnp.sum(grad_normed, 0, keepdims=True)
    sum_gain[...] = jnp.sum(grad_normed * unit, 0, keepdims=True)
    grad_unit = grad_normed * gain[...]
    part = jnp.mean(grad_unit, -1, keepdims=True)
    cross = jnp.mean(grad_unit * unit, -1, keepdims=True)
    grad_mid = grad_rows + scale * (grad_unit - part - unit * cross)
    grad_middle[...] = grad_mid
    grad_attn = grad_mid.astype(BF16)
    grad_out[...] = grad_attn
    sum_out[...] = jnp.sum(grad_attn.astype(F32), 0, keepdims=True)
    back = contract_last(grad_attn, weights1[0]).astype(BF16)
    if permuted.shape[1] > width:
        permuted[...] = jnp.zeros_like(permuted)
    permuted[:, :width] = contract_last(back, order).astype(BF16)
    for i in range(seq_count):
        for g in range(groups):
            for part in range(2):
                start = i * block + part * half_block
                grad_blocks[i * groups + g, :, part * group : (part + 1) * group] = permuted[
                    start : start + half_block, g * group : (g + 1) * group
                ]


def middle_block(half1, other1, half2, other2, attended, inputs, cotangent, order, vectors, groups):
    kinds, side, width = half1.shape
    parts = kinds - 1
    chips = half2.shape[0]
    seq_count, block, _ = inputs.shape
    tokens = seq_count * block
    wide = groups * attended.shape[2] // 2

    def shape(*dims, kind=BF16):
        return jax.ShapeDtypeStruct(dims, kind)

    return pl.pallas_call(
        functools.partial(middle_kernel, groups),
        out_shape=[
            shape(seq_count, block, width),
            shape(tokens, width, kind=F32),
            shape(*attended.shape),
            shape(tokens, width),
            shape(tokens, width),
            shape(tokens, parts * width),
            shape(tokens, parts * width),
            shape(tokens, width),
            shape(1, width, kind=F32),
            shape(1, width, kind=F32),
            shape(1, width, kind=F32),
            shape(1, parts * width, kind=F32),
            shape(1, width, kind=F32),
        ],
        in_specs=[ANYWHERE] * 4 + vmem_specs(9),
        out_specs=vmem_specs(13),
        scratch_shapes=[
            pltpu.VMEM((kinds, width, width), BF16),
            pltpu.VMEM((parts * width, width), BF16),
            pltpu.VMEM((tokens, wide), BF16),
            pltpu.VMEM((tokens, parts * width), F32),
            pltpu.VMEM((tokens, wide), BF16),
            pltpu.SemaphoreType.DMA((2 * kinds + 2 * chips,)),
        ],
        compiler_params=pltpu.CompilerParams(vmem_limit_bytes=50 * 2**20),
        cost_estimate=LIGHT,
    )(half1, other1, half2, other2, attended, inputs, cotangent, order, *vectors)


def gradient_kernel(
    shard_rows, placed_a, placed_n, hidden, grad_pre, grad_out, cotangent, send, keep, turned, some
):
    width = placed_a.shape[1]
    side = width // CORES
    parts = hidden.shape[1] // width
    chips = side // shard_rows
    core = lax.rem(lax.axis_index("seq"), CORES)
    branch = cotangent[...].reshape(-1, width)
    if send.shape[0] > 1 + parts:
        for start in range(0, turned.shape[0], width):
            turned[start : start + width, :] = hidden[:, start : start + width].astype(F32).T
        for target, place in ((send, 1 - core), (keep, core)):
            for chip in range(chips):
                for i in range(parts):
                    start = ((chip * CORES + place) * parts + i) * shard_rows
                    start = pl.multiple_of(start, shard_rows)
                    to = i * side + chip * shard_rows
                    some[to : to + shard_rows, :] = turned[pl.ds(start, shard_rows), :]
            for i in range(parts):
                target[1 + parts + i] = jnp.dot(
                    some[i * side : (i + 1) * side, :].astype(BF16),
                    branch,
                    preferred_element_type=F32,
                ).astype(BF16)
    turned_a = placed_a[...].astype(F32).T.astype(BF16)
    turned_n = placed_n[...].astype(F32).T.astype(BF16)
    for target, start in ((send, side), (keep, 0)):
        target[0] = jnp.dot(
            turned_a[start : start + side], grad_out[...], preferred_element_type=F32
        ).astype(BF16)
        for q in range(parts):
            target[1 + q] = jnp.dot(
                turned_n[start : start + side],
                grad_pre[:, q * width : (q + 1) * width],
                preferred_element_type=F32,
            ).astype(BF16)


def weight_gradients(placed_a, placed_n, hidden, grad_pre, grad_out, cotangent, shard_rows):
    tokens, width = placed_a.shape
    parts = hidden.shape[1] // width
    kinds = 1 + parts * (1 if shard_rows % 8 else 2)
    shape = jax.ShapeDtypeStruct((kinds, width // CORES, width), BF16)
    return pl.pallas_call(
        functools.partial(gradient_kernel, shard_rows),
        out_shape=[shape, shape],
        in_specs=vmem_specs(6),
        out_specs=vmem_specs(2),
        scratch_shapes=[
            pltpu.VMEM((parts * width, tokens), F32),
            pltpu.VMEM((parts * width // CORES, tokens), F32),
        ],
        compiler_params=pltpu.CompilerParams(vmem_limit_bytes=50 * 2**20),
        cost_estimate=LIGHT,
    )(placed_a, placed_n, hidden, grad_pre, grad_out, cotangent)


def masked_scores(keys, queries, id_column, id_row, first):
    scores = lax.dot_general(keys, queries, (((1,), (1,)), ((), ())), preferred_element_type=F32)
    key_pos = lax.broadcasted_iota(jnp.int32, scores.shape, 0)
    query_pos = lax.broadcasted_iota(jnp.int32, scores.shape, 1) + first
    allowed = (key_pos <= query_pos) & (id_column == id_row)
    return jnp.where(allowed, scores, MASKED)


def column_of(id_row):
    length = id_row.shape[1]
    return jnp.broadcast_to(id_row, (LANES, length)).T[:, :1]


def forward_kernel(
    seq_count,
    heads,
    head_size,
    step_rows,
    block,
    rows_ref,
    weight,
    gain,
    bias,
    bqv,
    after,
    out,
    stats,
    whole,
    normed,
    ids,
    result,
    qkv_bias,
):
    length = whole.shape[0]
    group = heads * head_size
    width = weight.shape[0]
    index = lax.rem(lax.axis_index("seq"), lax.axis_size("seq") // seq_count)
    qkv_bias[...] = jnp.zeros_like(qkv_bias)
    for lo in range(0, width, group):
        here = index == lo // group
        for base, start in ((0, 0), (width, 2 * group)):
            piece = jnp.where(here, bqv[:, base + lo : base + lo + group], 0.0)
            qkv_bias[:, start : start + group] += piece
    for i in range(length // block):
        rows = norm_affine(rows_ref[i, :block, :].astype(F32), gain[...], bias[...])
        normed[i * block : (i + 1) * block, :] = rows.astype(BF16)
    id_rows = [rows_ref[i, block:, :block].astype(F32)[:1] for i in range(length // block)]
    id_row = jnp.concatenate(id_rows, 1)
    ids[...] = id_row
    id_column = column_of(id_row)
    for first in range(0, length, step_rows):
        last = first + step_rows
        product = jnp.dot(normed[first:last, :], weight[...], preferred_element_type=F32)
        whole[first:last, :] = (product + qkv_bias[...]).astype(BF16)
    values_t = whole[:, 2 * group : 3 * group].astype(F32).T.astype(BF16)
    for first in range(0, length, step_rows):
        last = first + step_rows
        tops = []
        for head in range(heads):
            lo = head * head_size
            queries = whole[first:last, lo : lo + head_size] * BF16(head_size**-0.5)
            keys = whole[:last, group + lo : group + lo + head_size]
            scores = masked_scores(keys, queries, id_column[:last], id_row[:, first:last], first)
            highest = jnp.max(scores, 0, keepdims=True)
            weights = jnp.exp(scores - highest)
            total = jnp.sum(weights, 0, keepdims=True)
            probs = (weights * (1.0 / total)).astype(BF16)
            tops.append(
                jnp.dot(
                    values_t[lo : lo + head_size, :last], probs, preferred_element_type=F32
                )
            )
            stats[head : head + 1, first:last] = highest + jnp.log(total)
        result[first:last, :] = jnp.concatenate(tops, 0).T.astype(BF16)
    half = block // 2
    for start in range(0, length, block):
        out[start // 2 : start // 2 + half, :group] = result[start : start + half, :]
        out[start // 2 : start // 2 + half, group:] = result[start + half : start + block, :]


def backward_kernel(
    heads,
    head_size,
    step_rows,
    block,
    whole,
    grads,
    stats,
    ids,
    after1,
    after2,
    out,
    grad_out,
    grad_query,
    grad_key,
    grad_value,
):
    length = whole.shape[0]
    group = heads * head_size
    half = block // 2
    for start in range(0, length, block):
        packed = grads[start // 2 : start // 2 + half, :]
        grad_out[start : start + half, :] = packed[:, :group]
        grad_out[start + half : start + block, :] = packed[:, group:]
    id_row = ids[...]
    id_column = column_of(id_row)
    keys_t = whole[:, group : 2 * group].astype(F32).T.astype(BF16)
    factor = head_size**-0.5
    grad_key[...] = jnp.zeros_like(grad_key)
    grad_value[...] = jnp.zeros_like(grad_value)
    for first in range(0, length, step_rows):
        last = first + step_rows
        tops = []
        for head in range(heads):
            lo = head * head_size
            queries = whole[first:last, lo : lo + head_size] * BF16(factor)
            keys = whole[:last, group + lo : group + lo + head_size]
            values = whole[:last, 2 * group + lo : 2 * group + lo + head_size]
            grad = grad_out[first:last, lo : lo + head_size]
            scores = masked_scores(keys, queries, id_column[:last], id_row[:, first:last], first)
            probs = jnp.exp(scores - stats[head : head + 1, first:last])
            grad_probs = lax.dot_general(
                values, grad, (((1,), (1,)), ((), ())), preferred_element_type=F32
            )
            delta = jnp.sum(probs * grad_probs, 0, keepdims=True)
            grad_scores = (probs * (grad_probs - delta)).astype(BF16)
            tops.append(
                jnp.dot(
                    keys_t[lo : lo + head_size, :last], grad_scores, preferred_element_type=F32
                )
                * factor
            )
            grad_key[head, :last, :] += jnp.dot(
                grad_scores, queries, preferred_element_type=F32
            )
            grad_value[head, :last, :] += jnp.dot(
                probs.astype(BF16), grad, preferred_element_type=F32
            )
        grad_query[first:last, :] = jnp.concatenate(tops, 0).T.astype(BF16)
    out[:, :group] = grad_query[...]
    for head in range(heads):
        lo = head * head_size
        out[:, group + lo : group + lo + head_size] = grad_key[head].astype(BF16)
        out[:, 2 * group + lo : 2 * group + lo + head_size] = grad_value[head].astype(BF16)


def attend_forward(rows, weight, gain, bias, bqv, after, seq_count, heads, head_size, block):
    length = rows.shape[0] * block
    width = rows.shape[2]
    group = heads * head_size
    return pl.pallas_call(
        functools.partial(forward_kernel, seq_count, heads, head_size, min(256, length), block),
        out_shape=[
            jax.ShapeDtypeStruct((length // 2, 2 * group), BF16),
            jax.ShapeDtypeStruct((heads, length), F32),
            jax.ShapeDtypeStruct((length, 3 * group), BF16),
            jax.ShapeDtypeStruct((length, width), BF16),
            jax.ShapeDtypeStruct((1, length), F32),
        ],
        in_specs=vmem_specs(5) + [ANYWHERE],
        out_specs=vmem_specs(5),
        scratch_shapes=[pltpu.VMEM((length, group), BF16), pltpu.VMEM((1, 3 * group), F32)],
        compiler_params=pltpu.CompilerParams(vmem_limit_bytes=48 * 2**20),
        cost_estimate=LIGHT,
    )(rows, weight, gain, bias, bqv, after)


def attend_backward(whole, grads, stats, ids, after, heads, head_size, block):
    length, width = whole.shape
    group = heads * head_size
    return pl.pallas_call(
        functools.partial(backward_kernel, heads, head_size, min(256, length), block),
        out_shape=jax.ShapeDtypeStruct((length, 3 * group), BF16),
        in_specs=vmem_specs(4) + [ANYWHERE] * 2,
        out_specs=vmem_specs(1)[0],
        scratch_shapes=[
            pltpu.VMEM((length, group), BF16),
            pltpu.VMEM((length, group), BF16),
            pltpu.VMEM((heads, length, head_size), F32),
            pltpu.VMEM((heads, length, head_size), F32),
        ],
        compiler_params=pltpu.CompilerParams(vmem_limit_bytes=48 * 2**20),
        cost_estimate=LIGHT,
    )(whole, grads, stats, ids, *after)


def on_device(
    inputs,
    segments,
    cotangent,
    ln1_gain,
    ln1_bias,
    w_qkv,
    b_qv,
    w_out,
    b_out,
    ln2_gain,
    ln2_bias,
    w_fc,
    b_fc,
    w_proj,
    b_proj,
):
    seq_count, block, width = inputs.shape
    head_size = width // HEADS
    tokens = seq_count * block
    count = lax.axis_size("seq")
    devices = count * lax.axis_size("dp")
    groups = count // seq_count
    heads = -(-HEADS // groups)
    spare = groups * heads - HEADS
    group = heads * head_size

    vectors = (ln1_gain, ln1_bias, b_qv, b_out, ln2_gain, ln2_bias, b_fc, b_proj)
    sizes = tuple(vector.shape[0] for vector in vectors)
    shard_rows = w_out.shape[0] // width
    parts = w_fc.shape[0] // w_out.shape[0]
    classes = groups // CORES
    chips = devices // CORES
    place = lax.axis_index("seq")
    core = place % CORES
    group_index = place % groups

    columns, blocks = first_blocks(
        w_qkv.reshape(shard_rows, 3 * width),
        inputs,
        segments,
        [vector.reshape(1, -1) for vector in vectors],
        classes,
        group,
    )
    lines, sequence = gather_sequence(blocks)
    early_a, tower_a = gather_columns(columns)
    stacked = stack_weights(w_out.reshape(-1, width), w_fc.reshape(-1, parts * width), early_a)
    low1, high1 = build_tower(z_pieces(stacked), 1, [])
    tower_a = gate(tower_a, stacked)
    heights = tower_a.shape[0]
    half_a = gather_plane(tower_a[: heights // 2], tower_a[heights // 2 :], 0, None, low1)
    left, right = half_a[..., : 3 * group], half_a[..., 3 * group :]
    mine_a = jnp.where(core == 0, left, right)
    whole_a = ordered(core, mine_a, swap_core(jnp.where(core == 0, right, left)), 1)
    whole_a = whole_a.reshape(devices, shard_rows + ROWS, 3 * group)
    wqkv = whole_a[:, :shard_rows].reshape(width, 3 * group)
    gain1, bias1, bqv, bout, gain2, bias2, bfc, bproj = unpack_small(
        whole_a[:, shard_rows:, :LANES], sizes
    )

    raw, stats, qkv, normed1, ids = attend_forward(
        sequence, wqkv, gain1, bias1, bqv, low1, seq_count, heads, head_size, block
    )
    pieces2 = z_pieces(gate(w_proj.reshape(-1, width), lines))
    low2, high2 = build_tower(pieces2, 0, [raw])
    attended = exchange(raw.reshape(count, block // 2, 2 * group))
    half1 = gather_plane(low1, high1, 1, raw, attended).reshape(1 + parts, -1, width)
    half2 = gather_plane(low2, high2, 0, attended)
    other1 = swap_core(half1)
    other2 = swap_core(half2)
    aligned = half2.shape[1] % 16 == 0
    if not aligned:
        half2 = ordered(core, half2, other2, 1).reshape(1, parts * width, width)

    spot = jnp.arange(width, dtype=jnp.int32)
    side = width // CORES
    own_core = (core + spot // side) % CORES
    order = (spot % side // shard_rows * CORES + own_core) * shard_rows + spot % shard_rows
    (
        outputs,
        grad_middle,
        grad_blocks,
        placed_a,
        placed_n,
        hidden,
        grad_pre,
        grad_out,
        grad_bout,
        grad_gain2,
        grad_bias2,
        grad_bfc,
        grad_bproj,
    ) = middle_block(
        half1,
        other1,
        half2,
        other2,
        attended,
        inputs,
        cotangent,
        order.reshape(1, width),
        (bout, gain2, bias2, bfc, bproj),
        groups,
    )
    grad_blocks = exchange(grad_blocks).reshape(-1, 2 * group)
    send_b, keep_b = weight_gradients(
        placed_a, placed_n, hidden, grad_pre, grad_out, cotangent, shard_rows
    )
    if send_b.shape[0] == 1 + parts:
        grad_wproj = lax.dot_general(
            hidden,
            cotangent.reshape(tokens, width),
            (((0,), (0,)), ((), ())),
            preferred_element_type=F32,
        )
        grad_wproj = grad_wproj.astype(BF16).reshape(chips, CORES, parts, shard_rows, width)
        grad_wproj = grad_wproj.transpose(1, 2, 0, 3, 4).reshape(CORES, parts, -1, width)
        send_b = jnp.concatenate([send_b, pick(grad_wproj, 1 - core, 0)], 0)
        keep_b = jnp.concatenate([keep_b, pick(grad_wproj, core, 0)], 0)
    sum_b = add(keep_b, swap_core(send_b)).reshape(-1, chips, shard_rows, width)
    steps = []

    def between(*after):
        if steps:
            steps.append(after[0])
        else:
            steps.append(
                attend_backward(qkv, grad_blocks, stats, ids, after, heads, head_size, block)
            )
        return steps[0]

    tower_b = scatter_plane(sum_b, 1, between)
    own_b = scatter_z(tower_b, 1)
    grad_qkv, first_sums = steps

    def blocks_of(value, rows):
        return value.astype(BF16).reshape(chips, CORES, rows, -1)

    rows = inputs.astype(F32).reshape(tokens, width)
    grad_normed1 = lax.dot_general(
        grad_qkv, wqkv, (((1,), (1,)), ((), ())), preferred_element_type=F32
    )
    own_normed1 = scatter_sequence(grad_normed1.astype(BF16).reshape(count, block, width))
    _, norm1_back = jax.vjp(lambda value: norm_affine(value, gain1, bias1), rows)
    (grad_in_part,) = norm1_back(own_normed1.astype(F32).reshape(tokens, width))
    grad_inputs = (grad_middle + grad_in_part).astype(BF16).reshape(inputs.shape)

    long_rows = sequence[:, :block].astype(F32).reshape(count * block, width)
    _, norm1_long_back = jax.vjp(lambda g, b: norm_affine(long_rows, g, b), gain1, bias1)
    grad_gain1, grad_bias1 = norm1_long_back(grad_normed1)
    grad_wqkv = lax.dot_general(
        normed1, grad_qkv, (((0,), (0,)), ((), ())), preferred_element_type=F32
    )
    sums = jnp.sum(grad_qkv, 0, dtype=F32).reshape(3, group)
    here = (jnp.arange(groups) == group_index)[None, :, None]
    grad_bqv = jnp.where(here, jnp.stack([sums[0], sums[2]])[:, None], 0.0)
    grad_bqv = grad_bqv.reshape(2, groups * heads, head_size)[:, :HEADS]
    grads = (
        grad_gain1,
        grad_bias1,
        grad_bqv,
        grad_bout,
        grad_gain2,
        grad_bias2,
        grad_bfc,
        grad_bproj,
    )
    small_grads = pack_small([grad.reshape(1, -1) for grad in grads], sizes, devices)
    small_grads = jnp.pad(small_grads, ((0, 0), (0, 0), (0, 3 * group - LANES)))
    block_a = jnp.concatenate(
        [blocks_of(grad_wqkv, shard_rows), small_grads.reshape(chips, CORES, ROWS, -1)], 2
    )
    send_a, keep_a = pick(block_a, 1 - core, 1), pick(block_a, core, 1)
    got_a = swap_core(send_a)
    pair_a = jnp.concatenate(
        [jnp.where(core == 0, keep_a, got_a), jnp.where(core == 0, got_a, keep_a)], -1
    )
    pair_a = gate(pair_a, first_sums)
    tower_a = scatter_plane(pair_a, 0, lambda *_: tower_b)
    own_a = scatter_columns(tower_a, own_b)
    own_small = jnp.sum(
        own_a[:, shard_rows:].reshape(classes, ROWS, CORES, 3 * group)[..., :LANES], (0, 2)
    )
    own = [own_small[i, :size] for i, size in enumerate(sizes)]
    own_qkv = own_a[:, :shard_rows].reshape(classes, shard_rows, CORES, 3, group)
    own_qkv = own_qkv.transpose(1, 3, 0, 2, 4).reshape(shard_rows, 3, groups * heads, head_size)
    own_qkv = own_qkv[:, :, :HEADS].reshape(-1)
    return (
        outputs,
        grad_inputs,
        own[0],
        own[1],
        own_qkv,
        own[2],
        own_b[0].reshape(-1),
        own[3],
        own[4],
        own[5],
        own_b[1 : 1 + parts].transpose(1, 0, 2).reshape(-1),
        own[6],
        own_b[1 + parts :].reshape(-1),
        own[7],
    )


def solution(mesh):
    token_spec = P("dp", "seq", None)
    flat_spec = P(("dp", "seq"))
    in_specs = (token_spec, P("dp", "seq"), token_spec) + (flat_spec,) * 12
    out_specs = (token_spec, token_spec) + (flat_spec,) * 12
    return jax.shard_map(
        on_device, mesh=mesh, in_specs=in_specs, out_specs=out_specs, check_vma=False
    )
```

```python
import functools
import math

import jax
import jax.numpy as jnp
from jax import lax
from jax.experimental import pallas as pl
from jax.experimental.pallas import tpu as pltpu
from jax.sharding import PartitionSpec as P

HEADS = 12
CORES = 2


EPSILON = 1e-05
MASKED = -1e30
F32 = jnp.float32
BF16 = jnp.bfloat16


def norm_affine(values, gain, bias):
    center = jnp.mean(values, -1, keepdims=True)
    centered = values - center
    variance = jnp.mean(centered * centered, -1, keepdims=True)
    return centered * lax.rsqrt(variance + EPSILON) * gain + bias


ANYWHERE = pl.BlockSpec(memory_space=pl.ANY)
LIGHT = pl.CostEstimate(flops=1, bytes_accessed=1, transcendentals=0)


def shift_z(value, step):
    size = lax.axis_size("seq")
    return lax.ppermute(value, "seq", [(i, (i + CORES * step) % size) for i in range(size)])


def swap_core(value):
    size = lax.axis_size("seq")
    return lax.ppermute(value, "seq", [(i, i ^ 1) for i in range(size)])


def swap_dp(value, bit):
    size = lax.axis_size("dp")
    return lax.ppermute(value, "dp", [(i, i ^ bit) for i in range(size)])


def ordered(flag, mine, other, axis):
    first = jnp.where(flag == 0, mine, other)
    second = jnp.where(flag == 0, other, mine)
    return jnp.stack([first, second], axis)


def roll_blocks(pieces, place):
    count = len(pieces)
    stacked = jnp.stack(pieces)
    twice = jnp.concatenate([stacked, stacked])
    return lax.dynamic_slice_in_dim(twice, lax.rem(count - place, count), count, 0)


def z_pieces(shard):
    heights = lax.axis_size("seq") // CORES
    return [shard] + [shift_z(shard, -step) for step in range(1, heights)]


def swap_z(value, bit):
    size = lax.axis_size("seq")
    return lax.ppermute(value, "seq", [(i, i ^ (CORES * bit)) for i in range(size)])


def gather_plane(low, high, axis, first=None, second=None):
    def move(value, bit, after):
        moved = swap_dp(value, bit)
        return moved if after is None else gate(moved, after)

    if lax.axis_size("dp") == 4:
        plane = lax.axis_index("dp")
        y, x = plane // 2, plane % 2
        low_x = ordered(x, low, move(low, 1, first), axis)
        high_y = ordered(y, high, move(high, 2, first), axis)
        low_all = ordered(y, low_x, move(low_x, 2, second), axis)
        high_all = ordered(x, high_y, move(high_y, 1, second), axis + 1)
        half = jnp.concatenate([low_all, high_all], axis + 2)
        count = 4 * half.shape[axis + 2]
    else:
        tower = jnp.concatenate([low, high], axis)
        half = lax.all_gather(tower, "dp", axis=axis, tiled=True)
        return half
    return half.reshape(*low.shape[:axis], count, *low.shape[axis + 1 :])


def plane_pieces(low, high, first, second):
    low_x, low_y = swap_dp(low, 1), swap_dp(low, 2)
    high_x, high_y = swap_dp(high, 1), swap_dp(high, 2)
    low_x, high_y = gate_both(low_x, high_y, first)
    low_y, high_x = gate_both(low_y, high_x, first)
    low_far, high_far = gate_both(swap_dp(low_x, 2), swap_dp(high_y, 1), second)
    return [low, high, low_x, high_x, low_y, high_y, low_far, high_far]


def far_place(order):
    heights = lax.axis_size("seq") // CORES
    if lax.axis_size("dp") != 4:
        return order
    plane = lax.axis_index("dp")
    y = lax.rem(plane // 2 + order // (2 * heights), 2)
    x = lax.rem(plane + order // heights, 2)
    return (y * 2 + x) * heights + order % heights


def scatter_near(split, between):
    planes = lax.axis_size("dp")
    heights = lax.axis_size("seq") // CORES
    if planes != 4:
        between(split, split)
        between(split, split)
        return lax.psum_scatter(split, "dp", scatter_dimension=1, tiled=True)
    split = split.reshape(split.shape[0], 2, 2, 2, heights // 2, *split.shape[2:])
    low_send, high_send = split[:, 1, :, 0], split[:, :, 1, 1]
    low_got, high_got = swap_dp(low_send, 2), swap_dp(high_send, 1)
    low_got, high_got = gate_both(low_got, high_got, between(low_send, high_send))
    low = add(split[:, 0, :, 0], low_got)
    high = add(split[:, :, 0, 1], high_got)
    between(low, high)
    low = add(low[:, 0], swap_dp(low[:, 1], 1))
    high = add(high[:, 0], swap_dp(high[:, 1], 2))
    return jnp.concatenate([low, high], 1)


def pick(value, index, axis):
    return lax.dynamic_index_in_dim(value, index, axis, keepdims=False)


def add(mine, other):
    return (mine.astype(F32) + other.astype(F32)).astype(mine.dtype)


def scatter_plane(split, axis, between=None):
    planes = lax.axis_size("dp")
    heights = lax.axis_size("seq") // CORES
    if planes != 4:
        if between is not None:
            between(split, split)
            between(split, split)
        return lax.psum_scatter(split, "dp", scatter_dimension=axis, tiled=True)
    plane = lax.axis_index("dp")
    y, x = plane // 2, plane % 2
    split = split.reshape(*split.shape[:axis], 2, 2, heights, *split.shape[axis + 1 :])
    low = lax.slice_in_dim(split, 0, heights // 2, axis=axis + 2)
    high = lax.slice_in_dim(split, heights // 2, heights, axis=axis + 2)
    low_send, high_send = pick(low, 1 - y, axis), pick(high, 1 - x, axis + 1)
    low_got, high_got = swap_dp(low_send, 2), swap_dp(high_send, 1)
    if between is not None:
        after = between(low_send, high_send)
        low_got, high_got = gate(low_got, after), gate(high_got, after)
    low = add(pick(low, y, axis), low_got)
    high = add(pick(high, x, axis + 1), high_got)
    if between is not None:
        between(low, high)
    low = add(pick(low, x, axis), swap_dp(pick(low, 1 - x, axis), 1))
    high = add(pick(high, y, axis), swap_dp(pick(high, 1 - y, axis), 2))
    return jnp.concatenate([low, high], axis)


def scatter_z(tower, axis):
    heights = lax.axis_size("seq") // CORES
    level = lax.axis_index("seq") // CORES
    mine = pick(tower, level, axis).astype(F32)
    for step in range(1, heights):
        mine += shift_z(pick(tower, lax.rem(level + step, heights), axis), step).astype(F32)
    return mine


def z_bits():
    heights = lax.axis_size("seq") // CORES
    level = lax.axis_index("seq") // CORES
    top = heights // 2
    return level, top, level // top


def gather_sequence(blocks):
    level, top, half = z_bits()
    core = lax.axis_index("seq") % CORES
    held = ordered(half, pick(blocks, half, 0), swap_z(pick(blocks, 1 - half, 0), top), 0)
    axis, bit = 1, top // 2
    while bit:
        held = ordered(level // bit % 2, held, swap_z(held, bit), axis)
        axis, bit = axis + 1, bit // 2
    return held, ordered(core, held, swap_core(held), axis).reshape(-1, *blocks.shape[1:])


def scatter_sequence(partial, after):
    level, top, half = z_bits()
    core = lax.axis_index("seq") % CORES
    shape = partial.shape[1:]
    count = top.bit_length()
    held = partial.reshape(*[2] * (count + 1), *shape)
    got = gate(swap_core(pick(held, 1 - core, count)), after)
    held = add(pick(held, core, count), got)
    axis, bit = count - 1, 1
    while bit < top:
        flag = level // bit % 2
        held = add(pick(held, flag, axis), swap_z(pick(held, 1 - flag, axis), bit))
        axis, bit = axis - 1, bit * 2
    return ordered(half, pick(held, half, 0), swap_z(pick(held, 1 - half, 0), top), 0)


def gather_columns(blocks):
    level, top, half = z_bits()
    shape = blocks.shape[1:]
    count = top.bit_length() - 1
    held = blocks.reshape(*[2] * count, *shape)
    bit = top // 2
    while bit:
        flag = level // bit % 2
        got = swap_z(pick(held, 1 - flag, 0), bit)
        held = ordered(flag, pick(held, flag, 0), got, count - 1)
        bit //= 2
    return ordered(half, held, swap_z(held, top), 0).reshape(-1, *shape)


def scatter_columns(tower, after):
    level, top, half = z_bits()
    shape = tower.shape[1:]
    count = top.bit_length() - 1
    held = tower.reshape(*[2] * (count + 1), *shape)
    got = gate(swap_z(pick(held, 1 - half, 0), top), after)
    held = add(pick(held, half, 0), got)
    bit = 1
    while bit < top:
        flag = level // bit % 2
        got = swap_z(pick(held, 1 - flag, count - 1), bit)
        held = ordered(flag, pick(held, flag, count - 1), got, 0)
        bit *= 2
    return held.reshape(-1, *shape).astype(F32)


def exchange(blocks):
    return lax.all_to_all(blocks, "seq", split_axis=0, concat_axis=0, tiled=True)


ROWS = 8
LANES = 128


def vmem_specs(count):
    return [pl.BlockSpec(memory_space=pltpu.VMEM) for _ in range(count)]


def place_lanes(size, total):
    source = lax.broadcasted_iota(jnp.int32, (LANES, total), 0)
    target = lax.rem(lax.broadcasted_iota(jnp.int32, (LANES, total), 1), size)
    return jnp.where(source == target, 1.0, 0.0).astype(BF16)


def owned_lanes(devices, size):
    device = lax.broadcasted_iota(jnp.int32, (devices, devices * size), 0)
    lane = lax.broadcasted_iota(jnp.int32, (devices, devices * size), 1)
    offset = lane - device * size
    return (offset >= 0) & (offset < size)


def unpack_kernel(sizes, small_ref, *outs):
    devices = small_ref.shape[0]
    small = small_ref[...].astype(F32)
    for i, (size, out) in enumerate(zip(sizes, outs)):
        spread = jnp.dot(
            small[:, i, :].astype(BF16),
            place_lanes(size, devices * size),
            preferred_element_type=F32,
        )
        out[...] = jnp.sum(jnp.where(owned_lanes(devices, size), spread, 0.0), 0, keepdims=True)


def unpack_small(small, sizes):
    devices = small.shape[0]
    return pl.pallas_call(
        functools.partial(unpack_kernel, sizes),
        out_shape=[jax.ShapeDtypeStruct((1, devices * size), F32) for size in sizes],
        in_specs=vmem_specs(1),
        out_specs=vmem_specs(len(sizes)),
        compiler_params=pltpu.CompilerParams(vmem_limit_bytes=32 * 2**20),
        cost_estimate=LIGHT,
    )(small)


def pack_kernel(sizes, *refs):
    grads, packed, rows = refs[: len(sizes)], refs[len(sizes)], refs[len(sizes) + 1]
    devices = packed.shape[0]
    for i, (size, grad) in enumerate(zip(sizes, grads)):
        owned = jnp.where(owned_lanes(devices, size), grad[...], 0.0).astype(BF16)
        rows[:, i, :] = lax.dot_general(
            owned,
            place_lanes(size, devices * size),
            (((1,), (1,)), ((), ())),
            preferred_element_type=F32,
        )
    packed[...] = rows[...].astype(BF16)


def pack_small(grads, sizes, devices):
    return pl.pallas_call(
        functools.partial(pack_kernel, sizes),
        out_shape=jax.ShapeDtypeStruct((devices, ROWS, LANES), BF16),
        in_specs=vmem_specs(len(sizes)),
        out_specs=vmem_specs(1)[0],
        scratch_shapes=[pltpu.VMEM((devices, ROWS, LANES), F32)],
        compiler_params=pltpu.CompilerParams(vmem_limit_bytes=32 * 2**20),
        cost_estimate=LIGHT,
    )(*grads)


def gate(value, *after):
    def kernel(*refs):
        pass

    return pl.pallas_call(
        kernel,
        out_shape=jax.ShapeDtypeStruct(value.shape, value.dtype),
        in_specs=[ANYWHERE] * (1 + len(after)),
        out_specs=ANYWHERE,
        input_output_aliases={0: 0},
        cost_estimate=LIGHT,
    )(value, *after)


def gate_both(one, two, *after):
    def kernel(*refs):
        pass

    return pl.pallas_call(
        kernel,
        out_shape=[jax.ShapeDtypeStruct(value.shape, value.dtype) for value in (one, two)],
        in_specs=[ANYWHERE] * (2 + len(after)),
        out_specs=[ANYWHERE] * 2,
        input_output_aliases={0: 0, 1: 1},
        cost_estimate=LIGHT,
    )(one, two, *after)


def first_kernel(group, weight, rows, marks, *refs):
    vectors, (columns, blocks, lines, extra) = refs[:-4], refs[-4:]
    classes, _, width_pair = columns.shape
    shard_rows, width = weight.shape[0], weight.shape[1] // 3
    lines[...] = jnp.zeros_like(lines)
    for i, vector in enumerate(vectors):
        for start in range(0, width_pair, 3 * group):
            at = shard_rows + i
            lines[at : at + 1, start : start + vector.shape[1]] = vector[...].astype(F32)
    for kind in range(classes):
        for core in range(CORES):
            lo = (kind * CORES + core) * group
            for part in range(3):
                start = (core * 3 + part) * group
                if lo < width:
                    piece = weight[:, part * width + lo : part * width + lo + group].astype(F32)
                else:
                    piece = jnp.zeros((shard_rows, group), F32)
                lines[:shard_rows, start : start + group] = piece
        columns[kind] = lines[...].astype(BF16)
    block = rows.shape[1]
    extra[...] = jnp.zeros_like(extra)
    for i in range(rows.shape[0]):
        blocks[i, :block, :] = rows[i]
        extra[:1, :block] = marks[i : i + 1, :].astype(F32)
        blocks[i, block:, :] = extra[...].astype(BF16)


def first_blocks(weight, rows, marks, vectors, classes, group):
    shard_rows = weight.shape[0]
    count, block, width = rows.shape
    return pl.pallas_call(
        functools.partial(first_kernel, group),
        out_shape=[
            jax.ShapeDtypeStruct((classes, shard_rows + ROWS, CORES * 3 * group), BF16),
            jax.ShapeDtypeStruct((count, block + 16, width), BF16),
        ],
        in_specs=vmem_specs(3 + len(vectors)),
        out_specs=vmem_specs(2),
        scratch_shapes=[
            pltpu.VMEM((shard_rows + ROWS, CORES * 3 * group), F32),
            pltpu.VMEM((16, width), F32),
        ],
    )(weight, rows, marks, *vectors)


def stack_kernel(out_ref, fc_ref, after, stacked):
    width = out_ref.shape[1]
    stacked[0] = out_ref[...]
    for i in range(fc_ref.shape[1] // width):
        stacked[1 + i] = fc_ref[:, i * width : (i + 1) * width]


def stack_weights(w_out, w_fc, after):
    rows, width = w_out.shape
    return pl.pallas_call(
        stack_kernel,
        out_shape=jax.ShapeDtypeStruct((1 + w_fc.shape[1] // width, rows, width), BF16),
        in_specs=vmem_specs(2) + [ANYWHERE],
        out_specs=vmem_specs(1)[0],
        cost_estimate=LIGHT,
    )(w_out, w_fc, after)


def tower_kernel(axis, count, *refs):
    pieces, low, high = refs[:count], refs[-2], refs[-1]
    level = lax.axis_index("seq") // CORES
    for step, piece in enumerate(pieces):
        place = lax.rem(level + step, count)
        for half, start in ((low, 0), (high, count // 2)):

            @pl.when((place >= start) & (place < start + count // 2))
            def _():
                if axis == 1:
                    half[:, place - start] = piece[...]
                else:
                    half[place - start] = piece[...]


def build_tower(pieces, axis, after):
    count = len(pieces)
    shape = pieces[0].shape
    shape = (*shape[:axis], count // 2, *shape[axis:])
    return pl.pallas_call(
        functools.partial(tower_kernel, axis, count),
        out_shape=[jax.ShapeDtypeStruct(shape, BF16)] * 2,
        in_specs=vmem_specs(count) + [ANYWHERE] * len(after),
        out_specs=vmem_specs(2),
        compiler_params=pltpu.CompilerParams(vmem_limit_bytes=32 * 2**20),
        cost_estimate=LIGHT,
    )(*pieces, *after)


def one_hot_order(order_ref):
    width = order_ref.shape[1]
    features = lax.broadcasted_iota(jnp.int32, (width, width), 0)
    return jnp.where(features == order_ref[...], 1.0, 0.0).astype(BF16)


def contract_last(left, right):
    return lax.dot_general(left, right, (((1,), (1,)), ((), ())), preferred_element_type=F32)


def middle_kernel(count1, count2, groups, *refs):
    sources1, sources2 = refs[:count1], refs[count1 : count1 + count2]
    (
        attended,
        inputs,
        cotangent,
        order_ref,
        bout,
        gain,
        bias,
        bfc,
        bproj,
        outputs,
        grad_middle,
        grad_blocks,
        placed_a,
        placed_n,
        hidden,
        grad_pre,
        grad_out,
        sum_out,
        sum_gain,
        sum_bias,
        sum_fc,
        sum_proj,
        weights1,
        weights2,
        attended_rows,
        slopes,
        permuted,
        sems,
    ) = refs[count1 + count2 :]
    parts = weights1.shape[0] - 1
    width = weights1.shape[2]
    seq_count, block, _ = inputs.shape
    tokens = seq_count * block
    core = lax.rem(lax.axis_index("seq"), CORES)
    copies = []
    rows1 = width // count1
    for i, source in enumerate(sources1):
        target = weights1.at[:, pl.ds(i * rows1, rows1)]
        copies.append(pltpu.make_async_copy(source, target, sems.at[len(copies)]))
    if count2 == 1:
        copies.append(pltpu.make_async_copy(sources2[0].at[0], weights2, sems.at[len(copies)]))
    for i, source in enumerate(sources2 if count2 > 1 else ()):
        lines, rows2 = source.shape[:2]
        place = core if i < count2 // 2 else 1 - core
        for line in range(lines):
            chip = far_place(i % (count2 // 2) * lines + line)
            start = pl.multiple_of((chip * CORES + place) * rows2, rows2)
            copies.append(
                pltpu.make_async_copy(
                    source.at[line], weights2.at[pl.ds(start, rows2)], sems.at[len(copies)]
                )
            )
    for copy in copies:
        copy.start()
    order = one_hot_order(order_ref)

    half_block = block // 2
    group = attended.shape[2] // 2
    for i in range(seq_count):
        for g in range(groups):
            for part in range(2):
                start = i * block + part * half_block
                attended_rows[start : start + half_block, g * group : (g + 1) * group] = attended[
                    i * groups + g, :, part * group : (part + 1) * group
                ]
    placed = jnp.dot(attended_rows[:, :width], order, preferred_element_type=F32).astype(BF16)
    placed_a[...] = placed
    for copy in copies[:count1]:
        copy.wait()
    rows = inputs[...].astype(F32).reshape(tokens, width)
    middle = rows + (jnp.dot(placed, weights1[0], preferred_element_type=F32) + bout[...])
    center = jnp.mean(middle, -1, keepdims=True)
    centered = middle - center
    scale = lax.rsqrt(jnp.mean(centered * centered, -1, keepdims=True) + EPSILON)
    unit = centered * scale
    normed = (unit * gain[...] + bias[...]).astype(BF16)
    placed = jnp.dot(normed, order, preferred_element_type=F32).astype(BF16)
    placed_n[...] = placed
    curve = math.sqrt(2.0 / math.pi)
    for q in range(parts):
        lo = q * width
        pre = jnp.dot(placed, weights1[1 + q], preferred_element_type=F32)
        pre = pre + bfc[:, lo : lo + width]
        square = pre * pre
        tanh = jnp.tanh(curve * (pre + 0.044715 * (pre * square)))
        hidden[:, lo : lo + width] = (0.5 * pre * (1.0 + tanh)).astype(BF16)
        slopes[:, lo : lo + width] = 0.5 * (1.0 + tanh) + 0.5 * pre * (1.0 - tanh * tanh) * (
            curve * (1.0 + 3 * 0.044715 * square)
        )
    for copy in copies[count1:]:
        copy.wait()
    result = middle + bproj[...]
    for q in range(parts):
        lo = q * width
        result += jnp.dot(
            hidden[:, lo : lo + width], weights2[lo : lo + width], preferred_element_type=F32
        )
    outputs[...] = result.astype(BF16).reshape(seq_count, block, width)

    branch = cotangent[...].reshape(tokens, width)
    grad_rows = branch.astype(F32)
    sum_proj[...] = jnp.sum(grad_rows, 0, keepdims=True)
    grad_placed = jnp.zeros((tokens, width), F32)
    for q in range(parts):
        lo = q * width
        grad = contract_last(branch, weights2[lo : lo + width]) * slopes[:, lo : lo + width]
        grad = grad.astype(BF16)
        grad_pre[:, lo : lo + width] = grad
        sum_fc[:, lo : lo + width] = jnp.sum(grad.astype(F32), 0, keepdims=True)
        grad_placed += contract_last(grad, weights1[1 + q])
    high = grad_placed.astype(BF16)
    rest = grad_placed - high.astype(F32)
    mid = rest.astype(BF16)
    low = (rest - mid.astype(F32)).astype(BF16)
    grad_normed = contract_last(high, order) + (contract_last(mid, order) + contract_last(low, order))
    sum_bias[...] = jnp.sum(grad_normed, 0, keepdims=True)
    sum_gain[...] = jnp.sum(grad_normed * unit, 0, keepdims=True)
    grad_unit = grad_normed * gain[...]
    part = jnp.mean(grad_unit, -1, keepdims=True)
    cross = jnp.mean(grad_unit * unit, -1, keepdims=True)
    grad_mid = grad_rows + scale * (grad_unit - part - unit * cross)
    grad_middle[...] = grad_mid
    grad_attn = grad_mid.astype(BF16)
    grad_out[...] = grad_attn
    sum_out[...] = jnp.sum(grad_attn.astype(F32), 0, keepdims=True)
    back = contract_last(grad_attn, weights1[0]).astype(BF16)
    if permuted.shape[1] > width:
        permuted[...] = jnp.zeros_like(permuted)
    permuted[:, :width] = contract_last(back, order).astype(BF16)
    for i in range(seq_count):
        for g in range(groups):
            for part in range(2):
                start = i * block + part * half_block
                grad_blocks[i * groups + g, :, part * group : (part + 1) * group] = permuted[
                    start : start + half_block, g * group : (g + 1) * group
                ]


def middle_block(pieces1, pieces2, attended, inputs, cotangent, order, vectors, groups):
    kinds, _, width = pieces1[0].shape
    parts = kinds - 1
    count1, count2 = len(pieces1), len(pieces2)
    seq_count, block, _ = inputs.shape
    tokens = seq_count * block
    wide = groups * attended.shape[2] // 2

    def shape(*dims, kind=BF16):
        return jax.ShapeDtypeStruct(dims, kind)

    return pl.pallas_call(
        functools.partial(middle_kernel, count1, count2, groups),
        out_shape=[
            shape(seq_count, block, width),
            shape(tokens, width, kind=F32),
            shape(*attended.shape),
            shape(tokens, width),
            shape(tokens, width),
            shape(tokens, parts * width),
            shape(tokens, parts * width),
            shape(tokens, width),
            shape(1, width, kind=F32),
            shape(1, width, kind=F32),
            shape(1, width, kind=F32),
            shape(1, parts * width, kind=F32),
            shape(1, width, kind=F32),
        ],
        in_specs=[ANYWHERE] * (count1 + count2) + vmem_specs(9),
        out_specs=vmem_specs(13),
        scratch_shapes=[
            pltpu.VMEM((kinds, width, width), BF16),
            pltpu.VMEM((parts * width, width), BF16),
            pltpu.VMEM((tokens, wide), BF16),
            pltpu.VMEM((tokens, parts * width), F32),
            pltpu.VMEM((tokens, wide), BF16),
            pltpu.SemaphoreType.DMA((count1 + count2 * pieces2[0].shape[0],)),
        ],
        compiler_params=pltpu.CompilerParams(vmem_limit_bytes=50 * 2**20),
        cost_estimate=LIGHT,
    )(*pieces1, *pieces2, attended, inputs, cotangent, order, *vectors)


def gradient_kernel(
    shard_rows, placed_a, placed_n, hidden, grad_pre, grad_out, cotangent, send, keep, turned, some
):
    width = placed_a.shape[1]
    side = width // CORES
    parts = hidden.shape[1] // width
    chips = side // shard_rows
    core = lax.rem(lax.axis_index("seq"), CORES)
    branch = cotangent[...].reshape(-1, width)
    if send.shape[0] > 1 + parts:
        for start in range(0, turned.shape[0], width):
            turned[start : start + width, :] = hidden[:, start : start + width].astype(F32).T
        for target, place in ((send, 1 - core), (keep, core)):
            for chip in range(chips):
                for i in range(parts):
                    start = ((far_place(chip) * CORES + place) * parts + i) * shard_rows
                    start = pl.multiple_of(start, shard_rows)
                    to = i * side + chip * shard_rows
                    some[to : to + shard_rows, :] = turned[pl.ds(start, shard_rows), :]
            for i in range(parts):
                target[1 + parts + i] = jnp.dot(
                    some[i * side : (i + 1) * side, :].astype(BF16),
                    branch,
                    preferred_element_type=F32,
                ).astype(BF16)
    turned_a = placed_a[...].astype(F32).T.astype(BF16)
    turned_n = placed_n[...].astype(F32).T.astype(BF16)
    for target, start in ((send, side), (keep, 0)):
        target[0] = jnp.dot(
            turned_a[start : start + side], grad_out[...], preferred_element_type=F32
        ).astype(BF16)
        for q in range(parts):
            target[1 + q] = jnp.dot(
                turned_n[start : start + side],
                grad_pre[:, q * width : (q + 1) * width],
                preferred_element_type=F32,
            ).astype(BF16)


def weight_gradients(placed_a, placed_n, hidden, grad_pre, grad_out, cotangent, shard_rows):
    tokens, width = placed_a.shape
    parts = hidden.shape[1] // width
    kinds = 1 + parts * (1 if shard_rows % 8 else 2)
    shape = jax.ShapeDtypeStruct((kinds, width // CORES, width), BF16)
    return pl.pallas_call(
        functools.partial(gradient_kernel, shard_rows),
        out_shape=[shape, shape],
        in_specs=vmem_specs(6),
        out_specs=vmem_specs(2),
        scratch_shapes=[
            pltpu.VMEM((parts * width, tokens), F32),
            pltpu.VMEM((parts * width // CORES, tokens), F32),
        ],
        compiler_params=pltpu.CompilerParams(vmem_limit_bytes=50 * 2**20),
        cost_estimate=LIGHT,
    )(placed_a, placed_n, hidden, grad_pre, grad_out, cotangent)


def masked_scores(keys, queries, id_column, id_row, first):
    scores = lax.dot_general(keys, queries, (((1,), (1,)), ((), ())), preferred_element_type=F32)
    key_pos = lax.broadcasted_iota(jnp.int32, scores.shape, 0)
    query_pos = lax.broadcasted_iota(jnp.int32, scores.shape, 1) + first
    allowed = (key_pos <= query_pos) & (id_column == id_row)
    return jnp.where(allowed, scores, MASKED)


def column_of(id_row):
    length = id_row.shape[1]
    return jnp.broadcast_to(id_row, (LANES, length)).T[:, :1]


def forward_kernel(
    seq_count,
    heads,
    head_size,
    step_rows,
    block,
    rows_ref,
    weight,
    gain,
    bias,
    bqv,
    after,
    out,
    stats,
    whole,
    normed,
    ids,
    result,
    qkv_bias,
):
    length = whole.shape[0]
    group = heads * head_size
    width = weight.shape[0]
    index = lax.rem(lax.axis_index("seq"), lax.axis_size("seq") // seq_count)
    qkv_bias[...] = jnp.zeros_like(qkv_bias)
    for lo in range(0, width, group):
        here = index == lo // group
        for base, start in ((0, 0), (width, 2 * group)):
            piece = jnp.where(here, bqv[:, base + lo : base + lo + group], 0.0)
            qkv_bias[:, start : start + group] += piece
    for i in range(length // block):
        rows = norm_affine(rows_ref[i, :block, :].astype(F32), gain[...], bias[...])
        normed[i * block : (i + 1) * block, :] = rows.astype(BF16)
    id_rows = [rows_ref[i, block:, :block].astype(F32)[:1] for i in range(length // block)]
    id_row = jnp.concatenate(id_rows, 1)
    ids[...] = id_row
    id_column = column_of(id_row)
    for first in range(0, length, step_rows):
        last = first + step_rows
        product = jnp.dot(normed[first:last, :], weight[...], preferred_element_type=F32)
        whole[first:last, :] = (product + qkv_bias[...]).astype(BF16)
    values_t = whole[:, 2 * group : 3 * group].astype(F32).T.astype(BF16)
    for first in range(0, length, step_rows):
        last = first + step_rows
        tops = []
        for head in range(heads):
            lo = head * head_size
            queries = whole[first:last, lo : lo + head_size] * BF16(head_size**-0.5)
            keys = whole[:last, group + lo : group + lo + head_size]
            scores = masked_scores(keys, queries, id_column[:last], id_row[:, first:last], first)
            highest = jnp.max(scores, 0, keepdims=True)
            weights = jnp.exp(scores - highest)
            total = jnp.sum(weights, 0, keepdims=True)
            probs = (weights * (1.0 / total)).astype(BF16)
            tops.append(
                jnp.dot(
                    values_t[lo : lo + head_size, :last], probs, preferred_element_type=F32
                )
            )
            stats[head : head + 1, first:last] = highest + jnp.log(total)
        result[first:last, :] = jnp.concatenate(tops, 0).T.astype(BF16)
    half = block // 2
    for start in range(0, length, block):
        out[start // 2 : start // 2 + half, :group] = result[start : start + half, :]
        out[start // 2 : start // 2 + half, group:] = result[start + half : start + block, :]


def backward_kernel(
    heads,
    head_size,
    step_rows,
    block,
    whole,
    grads,
    stats,
    ids,
    after1,
    after2,
    out,
    grad_out,
    grad_query,
    grad_key,
    grad_value,
):
    length = whole.shape[0]
    group = heads * head_size
    half = block // 2
    for start in range(0, length, block):
        packed = grads[start // 2 : start // 2 + half, :]
        grad_out[start : start + half, :] = packed[:, :group]
        grad_out[start + half : start + block, :] = packed[:, group:]
    id_row = ids[...]
    id_column = column_of(id_row)
    keys_t = whole[:, group : 2 * group].astype(F32).T.astype(BF16)
    factor = head_size**-0.5
    grad_key[...] = jnp.zeros_like(grad_key)
    grad_value[...] = jnp.zeros_like(grad_value)
    for first in range(0, length, step_rows):
        last = first + step_rows
        tops = []
        for head in range(heads):
            lo = head * head_size
            queries = whole[first:last, lo : lo + head_size] * BF16(factor)
            keys = whole[:last, group + lo : group + lo + head_size]
            values = whole[:last, 2 * group + lo : 2 * group + lo + head_size]
            grad = grad_out[first:last, lo : lo + head_size]
            scores = masked_scores(keys, queries, id_column[:last], id_row[:, first:last], first)
            probs = jnp.exp(scores - stats[head : head + 1, first:last])
            grad_probs = lax.dot_general(
                values, grad, (((1,), (1,)), ((), ())), preferred_element_type=F32
            )
            delta = jnp.sum(probs * grad_probs, 0, keepdims=True)
            grad_scores = (probs * (grad_probs - delta)).astype(BF16)
            tops.append(
                jnp.dot(
                    keys_t[lo : lo + head_size, :last], grad_scores, preferred_element_type=F32
                )
                * factor
            )
            grad_key[head, :last, :] += jnp.dot(
                grad_scores, queries, preferred_element_type=F32
            )
            grad_value[head, :last, :] += jnp.dot(
                probs.astype(BF16), grad, preferred_element_type=F32
            )
        grad_query[first:last, :] = jnp.concatenate(tops, 0).T.astype(BF16)
    out[:, :group] = grad_query[...]
    for head in range(heads):
        lo = head * head_size
        out[:, group + lo : group + lo + head_size] = grad_key[head].astype(BF16)
        out[:, 2 * group + lo : 2 * group + lo + head_size] = grad_value[head].astype(BF16)


def attend_forward(rows, weight, gain, bias, bqv, after, seq_count, heads, head_size, block):
    length = rows.shape[0] * block
    width = rows.shape[2]
    group = heads * head_size
    return pl.pallas_call(
        functools.partial(forward_kernel, seq_count, heads, head_size, min(256, length), block),
        out_shape=[
            jax.ShapeDtypeStruct((length // 2, 2 * group), BF16),
            jax.ShapeDtypeStruct((heads, length), F32),
            jax.ShapeDtypeStruct((length, 3 * group), BF16),
            jax.ShapeDtypeStruct((length, width), BF16),
            jax.ShapeDtypeStruct((1, length), F32),
        ],
        in_specs=vmem_specs(5) + [ANYWHERE],
        out_specs=vmem_specs(5),
        scratch_shapes=[pltpu.VMEM((length, group), BF16), pltpu.VMEM((1, 3 * group), F32)],
        compiler_params=pltpu.CompilerParams(vmem_limit_bytes=48 * 2**20),
        cost_estimate=LIGHT,
    )(rows, weight, gain, bias, bqv, after)


def attend_backward(whole, grads, stats, ids, after, heads, head_size, block):
    length, width = whole.shape
    group = heads * head_size
    return pl.pallas_call(
        functools.partial(backward_kernel, heads, head_size, min(256, length), block),
        out_shape=jax.ShapeDtypeStruct((length, 3 * group), BF16),
        in_specs=vmem_specs(4) + [ANYWHERE] * 2,
        out_specs=vmem_specs(1)[0],
        scratch_shapes=[
            pltpu.VMEM((length, group), BF16),
            pltpu.VMEM((length, group), BF16),
            pltpu.VMEM((heads, length, head_size), F32),
            pltpu.VMEM((heads, length, head_size), F32),
        ],
        compiler_params=pltpu.CompilerParams(vmem_limit_bytes=48 * 2**20),
        cost_estimate=LIGHT,
    )(whole, grads, stats, ids, *after)


def on_device(
    inputs,
    segments,
    cotangent,
    ln1_gain,
    ln1_bias,
    w_qkv,
    b_qv,
    w_out,
    b_out,
    ln2_gain,
    ln2_bias,
    w_fc,
    b_fc,
    w_proj,
    b_proj,
):
    seq_count, block, width = inputs.shape
    head_size = width // HEADS
    tokens = seq_count * block
    count = lax.axis_size("seq")
    devices = count * lax.axis_size("dp")
    groups = count // seq_count
    heads = -(-HEADS // groups)
    spare = groups * heads - HEADS
    group = heads * head_size

    vectors = (ln1_gain, ln1_bias, b_qv, b_out, ln2_gain, ln2_bias, b_fc, b_proj)
    sizes = tuple(vector.shape[0] for vector in vectors)
    shard_rows = w_out.shape[0] // width
    parts = w_fc.shape[0] // w_out.shape[0]
    classes = groups // CORES
    chips = devices // CORES
    place = lax.axis_index("seq")
    core = place % CORES
    group_index = place % groups

    columns, blocks = first_blocks(
        w_qkv.reshape(shard_rows, 3 * width),
        inputs,
        segments,
        [vector.reshape(1, -1) for vector in vectors],
        classes,
        group,
    )
    lines, sequence = gather_sequence(blocks)
    tower_a = gather_columns(columns)
    stacked = stack_weights(w_out.reshape(-1, width), w_fc.reshape(-1, parts * width), columns)
    low1, high1 = build_tower(z_pieces(stacked), 1, [])
    tower_a = gate(tower_a, stacked)
    heights = tower_a.shape[0]
    half_a = gather_plane(tower_a[: heights // 2], tower_a[heights // 2 :], 0, low1, lines)
    left, right = half_a[..., : 3 * group], half_a[..., 3 * group :]
    mine_a = jnp.where(core == 0, left, right)
    whole_a = ordered(core, mine_a, swap_core(jnp.where(core == 0, right, left)), 1)
    whole_a = whole_a.reshape(devices, shard_rows + ROWS, 3 * group)
    wqkv = whole_a[:, :shard_rows].reshape(width, 3 * group)
    gain1, bias1, bqv, bout, gain2, bias2, bfc, bproj = unpack_small(
        whole_a[:, shard_rows:, :LANES], sizes
    )

    raw, stats, qkv, normed1, ids = attend_forward(
        sequence, wqkv, gain1, bias1, bqv, low1, seq_count, heads, head_size, block
    )
    pieces2 = z_pieces(gate(w_proj.reshape(-1, width), lines))
    low2, high2 = build_tower(pieces2, 0, [raw])
    attended = exchange(raw.reshape(count, block // 2, 2 * group))
    aligned = w_proj.shape[0] // width % 16 == 0
    if lax.axis_size("dp") == 4:
        pieces1 = plane_pieces(low1, high1, attended, attended)
        pieces2 = plane_pieces(low2, high2, attended, attended)
    else:
        pieces1 = [gather_plane(low1, high1, 1)]
        pieces2 = [gather_plane(low2, high2, 0)]
    pieces1 += [swap_core(piece) for piece in pieces1]
    pieces1 = [piece.reshape(1 + parts, -1, width) for piece in pieces1]
    pieces2 += [swap_core(piece) for piece in pieces2]
    if not aligned:
        pieces2 = [ordered(core, *pieces2, 1).reshape(1, parts * width, width)]

    spot = jnp.arange(width, dtype=jnp.int32)
    side = width // CORES
    own_core = (core + spot // side) % CORES
    order = far_place(spot % side // shard_rows) * CORES + own_core
    order = order * shard_rows + spot % shard_rows
    (
        outputs,
        grad_middle,
        grad_blocks,
        placed_a,
        placed_n,
        hidden,
        grad_pre,
        grad_out,
        grad_bout,
        grad_gain2,
        grad_bias2,
        grad_bfc,
        grad_bproj,
    ) = middle_block(
        pieces1,
        pieces2,
        attended,
        inputs,
        cotangent,
        order.reshape(1, width),
        (bout, gain2, bias2, bfc, bproj),
        groups,
    )
    grad_blocks = exchange(grad_blocks).reshape(-1, 2 * group)
    send_b, keep_b = weight_gradients(
        placed_a, placed_n, hidden, grad_pre, grad_out, cotangent, shard_rows
    )
    if send_b.shape[0] == 1 + parts:
        grad_wproj = lax.dot_general(
            hidden,
            cotangent.reshape(tokens, width),
            (((0,), (0,)), ((), ())),
            preferred_element_type=F32,
        )
        grad_wproj = grad_wproj.astype(BF16).reshape(chips, CORES, parts, shard_rows, width)
        grad_wproj = grad_wproj.transpose(1, 2, 0, 3, 4).reshape(CORES, parts, -1, width)
        send_b = jnp.concatenate([send_b, pick(grad_wproj, 1 - core, 0)], 0)
        keep_b = jnp.concatenate([keep_b, pick(grad_wproj, core, 0)], 0)
    sum_b = add(keep_b, swap_core(send_b)).reshape(-1, chips, shard_rows, width)
    steps = []

    def between(*after):
        if steps:
            steps.append(after[0])
        else:
            steps.append(
                attend_backward(qkv, grad_blocks, stats, ids, after, heads, head_size, block)
            )
        return steps[0]

    tower_b = scatter_near(sum_b, between)
    own_b = scatter_z(tower_b, 1)
    grad_qkv, first_sums = steps

    def blocks_of(value, rows):
        return value.astype(BF16).reshape(chips, CORES, rows, -1)

    rows = inputs.astype(F32).reshape(tokens, width)
    grad_normed1 = lax.dot_general(
        grad_qkv, wqkv, (((1,), (1,)), ((), ())), preferred_element_type=F32
    )
    own_normed1 = scatter_sequence(
        grad_normed1.astype(BF16).reshape(count, block, width), first_sums
    )
    _, norm1_back = jax.vjp(lambda value: norm_affine(value, gain1, bias1), rows)
    (grad_in_part,) = norm1_back(own_normed1.astype(F32).reshape(tokens, width))
    grad_inputs = (grad_middle + grad_in_part).astype(BF16).reshape(inputs.shape)

    grad_qkv = gate(grad_qkv, first_sums)
    long_rows = sequence[:, :block].astype(F32).reshape(count * block, width)
    _, norm1_long_back = jax.vjp(lambda g, b: norm_affine(long_rows, g, b), gain1, bias1)
    grad_gain1, grad_bias1 = norm1_long_back(grad_normed1)
    grad_wqkv = lax.dot_general(
        normed1, grad_qkv, (((0,), (0,)), ((), ())), preferred_element_type=F32
    )
    sums = jnp.sum(grad_qkv, 0, dtype=F32).reshape(3, group)
    here = (jnp.arange(groups) == group_index)[None, :, None]
    grad_bqv = jnp.where(here, jnp.stack([sums[0], sums[2]])[:, None], 0.0)
    grad_bqv = grad_bqv.reshape(2, groups * heads, head_size)[:, :HEADS]
    grads = (
        grad_gain1,
        grad_bias1,
        grad_bqv,
        grad_bout,
        grad_gain2,
        grad_bias2,
        grad_bfc,
        grad_bproj,
    )
    small_grads = pack_small([grad.reshape(1, -1) for grad in grads], sizes, devices)
    small_grads = jnp.pad(small_grads, ((0, 0), (0, 0), (0, 3 * group - LANES)))
    block_a = jnp.concatenate(
        [blocks_of(grad_wqkv, shard_rows), small_grads.reshape(chips, CORES, ROWS, -1)], 2
    )
    send_a, keep_a = pick(block_a, 1 - core, 1), pick(block_a, core, 1)
    got_a = swap_core(send_a)
    pair_a = jnp.concatenate(
        [jnp.where(core == 0, keep_a, got_a), jnp.where(core == 0, got_a, keep_a)], -1
    )
    tower_a = scatter_plane(pair_a, 0, lambda *_: tower_b)
    own_a = scatter_columns(tower_a, own_b)
    own_small = jnp.sum(
        own_a[:, shard_rows:].reshape(classes, ROWS, CORES, 3 * group)[..., :LANES], (0, 2)
    )
    own = [own_small[i, :size] for i, size in enumerate(sizes)]
    own_qkv = own_a[:, :shard_rows].reshape(classes, shard_rows, CORES, 3, group)
    own_qkv = own_qkv.transpose(1, 3, 0, 2, 4).reshape(shard_rows, 3, groups * heads, head_size)
    own_qkv = own_qkv[:, :, :HEADS].reshape(-1)
    return (
        outputs,
        grad_inputs,
        own[0],
        own[1],
        own_qkv,
        own[2],
        own_b[0].reshape(-1),
        own[3],
        own[4],
        own[5],
        own_b[1 : 1 + parts].transpose(1, 0, 2).reshape(-1),
        own[6],
        own_b[1 + parts :].reshape(-1),
        own[7],
    )


def solution(mesh):
    token_spec = P("dp", "seq", None)
    flat_spec = P(("dp", "seq"))
    in_specs = (token_spec, P("dp", "seq"), token_spec) + (flat_spec,) * 12
    out_specs = (token_spec, token_spec) + (flat_spec,) * 12
    return jax.shard_map(
        on_device, mesh=mesh, in_specs=in_specs, out_specs=out_specs, check_vma=False
    )
```

```python
import functools
import math

import jax
import jax.numpy as jnp
from jax import lax
from jax.experimental import pallas as pl
from jax.experimental.pallas import tpu as pltpu
from jax.sharding import PartitionSpec as P

HEADS = 12
CORES = 2


EPSILON = 1e-05
MASKED = -1e30
F32 = jnp.float32
BF16 = jnp.bfloat16


def norm_affine(values, gain, bias):
    center = jnp.mean(values, -1, keepdims=True)
    centered = values - center
    variance = jnp.mean(centered * centered, -1, keepdims=True)
    return centered * lax.rsqrt(variance + EPSILON) * gain + bias


ANYWHERE = pl.BlockSpec(memory_space=pl.ANY)
LIGHT = pl.CostEstimate(flops=1, bytes_accessed=1, transcendentals=0)


def shift_z(value, step):
    size = lax.axis_size("seq")
    return lax.ppermute(value, "seq", [(i, (i + CORES * step) % size) for i in range(size)])


def swap_core(value):
    size = lax.axis_size("seq")
    return lax.ppermute(value, "seq", [(i, i ^ 1) for i in range(size)])


def swap_dp(value, bit):
    size = lax.axis_size("dp")
    return lax.ppermute(value, "dp", [(i, i ^ bit) for i in range(size)])


def ordered(flag, mine, other, axis):
    first = jnp.where(flag == 0, mine, other)
    second = jnp.where(flag == 0, other, mine)
    return jnp.stack([first, second], axis)


def roll_blocks(pieces, place):
    count = len(pieces)
    stacked = jnp.stack(pieces)
    twice = jnp.concatenate([stacked, stacked])
    return lax.dynamic_slice_in_dim(twice, lax.rem(count - place, count), count, 0)


def z_pieces(shard):
    heights = lax.axis_size("seq") // CORES
    return [shard] + [shift_z(shard, -step) for step in range(1, heights)]


def swap_z(value, bit):
    size = lax.axis_size("seq")
    return lax.ppermute(value, "seq", [(i, i ^ (CORES * bit)) for i in range(size)])


def gather_plane(low, high, axis, first=None, second=None):
    def move(value, bit, after):
        moved = swap_dp(value, bit)
        return moved if after is None else gate(moved, after)

    if lax.axis_size("dp") == 4:
        plane = lax.axis_index("dp")
        y, x = plane // 2, plane % 2
        low_x = ordered(x, low, move(low, 1, first), axis)
        high_y = ordered(y, high, move(high, 2, first), axis)
        low_all = ordered(y, low_x, move(low_x, 2, second), axis)
        high_all = ordered(x, high_y, move(high_y, 1, second), axis + 1)
        half = jnp.concatenate([low_all, high_all], axis + 2)
        count = 4 * half.shape[axis + 2]
    else:
        tower = jnp.concatenate([low, high], axis)
        half = lax.all_gather(tower, "dp", axis=axis, tiled=True)
        return half
    return half.reshape(*low.shape[:axis], count, *low.shape[axis + 1 :])


def pick(value, index, axis):
    return lax.dynamic_index_in_dim(value, index, axis, keepdims=False)


def add(mine, other):
    return (mine.astype(F32) + other.astype(F32)).astype(mine.dtype)


def scatter_plane(split, axis, between=None):
    planes = lax.axis_size("dp")
    heights = lax.axis_size("seq") // CORES
    if planes != 4:
        if between is not None:
            between(split, split)
            between(split, split)
        return lax.psum_scatter(split, "dp", scatter_dimension=axis, tiled=True)
    plane = lax.axis_index("dp")
    y, x = plane // 2, plane % 2
    split = split.reshape(*split.shape[:axis], 2, 2, heights, *split.shape[axis + 1 :])
    low = lax.slice_in_dim(split, 0, heights // 2, axis=axis + 2)
    high = lax.slice_in_dim(split, heights // 2, heights, axis=axis + 2)
    low_send, high_send = pick(low, 1 - y, axis), pick(high, 1 - x, axis + 1)
    low_got, high_got = swap_dp(low_send, 2), swap_dp(high_send, 1)
    if between is not None:
        after = between(low_send, high_send)
        low_got, high_got = gate_both(low_got, high_got, after)
    low = add(pick(low, y, axis), low_got)
    high = add(pick(high, x, axis + 1), high_got)
    if between is not None:
        between(low, high)
    low = add(pick(low, x, axis), swap_dp(pick(low, 1 - x, axis), 1))
    high = add(pick(high, y, axis), swap_dp(pick(high, 1 - y, axis), 2))
    return jnp.concatenate([low, high], axis)


def scatter_z(tower, axis):
    heights = lax.axis_size("seq") // CORES
    level = lax.axis_index("seq") // CORES
    mine = pick(tower, level, axis).astype(F32)
    for step in range(1, heights):
        mine += shift_z(pick(tower, lax.rem(level + step, heights), axis), step).astype(F32)
    return mine


def z_bits():
    heights = lax.axis_size("seq") // CORES
    level = lax.axis_index("seq") // CORES
    top = heights // 2
    return level, top, level // top


def gather_sequence(blocks, after):
    level, top, half = z_bits()
    core = lax.axis_index("seq") % CORES
    got = gate(swap_z(pick(blocks, 1 - half, 0), top), after)
    held = ordered(half, pick(blocks, half, 0), got, 0)
    axis, bit = 1, top // 2
    while bit:
        held = ordered(level // bit % 2, held, swap_z(held, bit), axis)
        axis, bit = axis + 1, bit // 2
    return held, ordered(core, held, swap_core(held), axis).reshape(-1, *blocks.shape[1:])


def scatter_sequence(partial, first, second):
    level, top, half = z_bits()
    core = lax.axis_index("seq") % CORES
    shape = partial.shape[1:]
    count = top.bit_length()
    held = partial.reshape(*[2] * (count + 1), *shape)
    got = gate(swap_core(pick(held, 1 - core, count)), first)
    held = add(pick(held, core, count), got)
    axis, bit = count - 1, 1
    while bit < top:
        flag = level // bit % 2
        got = gate(swap_z(pick(held, 1 - flag, axis), bit), second)
        held = add(pick(held, flag, axis), got)
        axis, bit = axis - 1, bit * 2
    return ordered(half, pick(held, half, 0), swap_z(pick(held, 1 - half, 0), top), 0)


def class_of(level):
    return level % (lax.axis_size("seq") // CORES // 2)


def gather_columns(blocks):
    heights = lax.axis_size("seq") // CORES
    level = lax.axis_index("seq") // CORES
    moved = [
        swap_z(pick(blocks, class_of(level ^ mask), 0), mask) for mask in range(1, heights)
    ]
    return [pick(blocks, class_of(level), 0)] + moved


def scatter_columns(tower, after):
    heights = tower.shape[0]
    level = lax.axis_index("seq") // CORES
    kinds = jnp.arange(heights // 2)[:, None, None]
    total = jnp.where(kinds == class_of(level), pick(tower, level, 0).astype(F32)[None], 0.0)
    for mask in range(1, heights):
        got = gate(swap_z(pick(tower, level ^ mask, 0), mask), after)
        total += jnp.where(kinds == class_of(level ^ mask), got.astype(F32)[None], 0.0)
    return total


def scatter_plane_direct(split, after):
    planes = lax.axis_size("dp")
    if planes != 4:
        return lax.psum_scatter(split, "dp", scatter_dimension=0, tiled=True)
    plane = lax.axis_index("dp")
    split = split.reshape(planes, -1, *split.shape[1:])
    total = pick(split, plane, 0).astype(F32)
    for mask in range(1, planes):
        total += gate(swap_dp(pick(split, plane ^ mask, 0), mask), after).astype(F32)
    return total.astype(split.dtype)


def exchange(blocks):
    return lax.all_to_all(blocks, "seq", split_axis=0, concat_axis=0, tiled=True)


ROWS = 8
LANES = 128


def vmem_specs(count):
    return [pl.BlockSpec(memory_space=pltpu.VMEM) for _ in range(count)]


def place_lanes(size, total):
    source = lax.broadcasted_iota(jnp.int32, (LANES, total), 0)
    target = lax.rem(lax.broadcasted_iota(jnp.int32, (LANES, total), 1), size)
    return jnp.where(source == target, 1.0, 0.0).astype(BF16)


def owned_lanes(devices, size):
    device = lax.broadcasted_iota(jnp.int32, (devices, devices * size), 0)
    lane = lax.broadcasted_iota(jnp.int32, (devices, devices * size), 1)
    offset = lane - device * size
    return (offset >= 0) & (offset < size)


def line_kernel(*refs):
    pieces, tower = refs[:-1], refs[-1]
    level = lax.axis_index("seq") // CORES
    for mask, piece in enumerate(pieces):
        tower[level ^ mask] = piece[...]


def build_line(pieces):
    return pl.pallas_call(
        line_kernel,
        out_shape=jax.ShapeDtypeStruct((len(pieces), *pieces[0].shape), BF16),
        in_specs=vmem_specs(len(pieces)),
        out_specs=vmem_specs(1)[0],
        cost_estimate=LIGHT,
    )(*pieces)


def halves_kernel(count, *refs):
    towers, (keep, send) = refs[:count], refs[-2:]
    heights, _, columns = towers[0].shape
    half = columns // CORES
    core = lax.rem(lax.axis_index("seq"), CORES)
    plane = lax.axis_index("dp")
    for own in range(CORES):

        @pl.when(core == own)
        def _():
            for mask, tower in enumerate(towers):
                base = (plane ^ mask) * heights if count > 1 else 0
                for i in range(heights):
                    line = tower[i]
                    keep[base + i] = line[:, own * half : (own + 1) * half]
                    send[base + i] = line[:, (1 - own) * half : (2 - own) * half]


def split_halves(towers, after):
    heights, rows, columns = towers[0].shape
    shape = jax.ShapeDtypeStruct((len(towers) * heights, rows, columns // CORES), BF16)
    return pl.pallas_call(
        functools.partial(halves_kernel, len(towers)),
        out_shape=[shape, shape],
        in_specs=vmem_specs(len(towers)) + [ANYWHERE] * len(after),
        out_specs=vmem_specs(2),
        compiler_params=pltpu.CompilerParams(vmem_limit_bytes=40 * 2**20),
        cost_estimate=LIGHT,
    )(*towers, *after)


def unpack_kernel(sizes, keep, got, weight, *refs):
    outs, (lines, small) = refs[:-2], refs[-2:]
    chips, rows = keep.shape[:2]
    shard = rows - ROWS
    core = lax.rem(lax.axis_index("seq"), CORES)
    for own in range(CORES):

        @pl.when(core == own)
        def _():
            for source, place in ((keep, own), (got, 1 - own)):
                for chip in range(chips):
                    device = chip * CORES + place
                    line = source[chip].astype(F32)
                    lines[device * shard : (device + 1) * shard, :] = line[:shard]
                    small[device] = line[shard:, :LANES]

    weight[...] = lines[...].astype(BF16)
    devices = chips * CORES
    for i, (size, out) in enumerate(zip(sizes, outs)):
        spread = jnp.dot(
            small[:, i, :].astype(BF16),
            place_lanes(size, devices * size),
            preferred_element_type=F32,
        )
        out[...] = jnp.sum(jnp.where(owned_lanes(devices, size), spread, 0.0), 0, keepdims=True)


def unpack_first(keep, got, sizes):
    chips, rows, columns = keep.shape
    devices = chips * CORES
    width = devices * (rows - ROWS)
    return pl.pallas_call(
        functools.partial(unpack_kernel, sizes),
        out_shape=[jax.ShapeDtypeStruct((width, columns), BF16)]
        + [jax.ShapeDtypeStruct((1, devices * size), F32) for size in sizes],
        in_specs=vmem_specs(2),
        out_specs=vmem_specs(1 + len(sizes)),
        scratch_shapes=[
            pltpu.VMEM((width, columns), F32),
            pltpu.VMEM((devices, ROWS, LANES), F32),
        ],
        compiler_params=pltpu.CompilerParams(vmem_limit_bytes=40 * 2**20),
        cost_estimate=LIGHT,
    )(keep, got)


def pack_kernel(sizes, *refs):
    grads, packed, rows = refs[: len(sizes)], refs[len(sizes)], refs[len(sizes) + 1]
    devices = packed.shape[0]
    for i, (size, grad) in enumerate(zip(sizes, grads)):
        owned = jnp.where(owned_lanes(devices, size), grad[...], 0.0).astype(BF16)
        rows[:, i, :] = lax.dot_general(
            owned,
            place_lanes(size, devices * size),
            (((1,), (1,)), ((), ())),
            preferred_element_type=F32,
        )
    packed[...] = rows[...].astype(BF16)


def pack_small(grads, sizes, devices):
    return pl.pallas_call(
        functools.partial(pack_kernel, sizes),
        out_shape=jax.ShapeDtypeStruct((devices, ROWS, LANES), BF16),
        in_specs=vmem_specs(len(sizes)),
        out_specs=vmem_specs(1)[0],
        scratch_shapes=[pltpu.VMEM((devices, ROWS, LANES), F32)],
        compiler_params=pltpu.CompilerParams(vmem_limit_bytes=32 * 2**20),
        cost_estimate=LIGHT,
    )(*grads)


def gate(value, *after):
    def kernel(*refs):
        pass

    return pl.pallas_call(
        kernel,
        out_shape=jax.ShapeDtypeStruct(value.shape, value.dtype),
        in_specs=[ANYWHERE] * (1 + len(after)),
        out_specs=ANYWHERE,
        input_output_aliases={0: 0},
        cost_estimate=LIGHT,
    )(value, *after)


def gate_both(one, two, *after):
    def kernel(*refs):
        pass

    return pl.pallas_call(
        kernel,
        out_shape=[jax.ShapeDtypeStruct(value.shape, value.dtype) for value in (one, two)],
        in_specs=[ANYWHERE] * (2 + len(after)),
        out_specs=[ANYWHERE] * 2,
        input_output_aliases={0: 0, 1: 1},
        cost_estimate=LIGHT,
    )(one, two, *after)


def first_kernel(group, weight, rows, marks, *refs):
    vectors, (columns, blocks, lines, extra) = refs[:-4], refs[-4:]
    classes, _, width_pair = columns.shape
    shard_rows, width = weight.shape[0], weight.shape[1] // 3
    lines[...] = jnp.zeros_like(lines)
    for i, vector in enumerate(vectors):
        for start in range(0, width_pair, 3 * group):
            at = shard_rows + i
            lines[at : at + 1, start : start + vector.shape[1]] = vector[...].astype(F32)
    for kind in range(classes):
        for core in range(CORES):
            lo = (kind * CORES + core) * group
            for part in range(3):
                start = (core * 3 + part) * group
                if lo < width:
                    piece = weight[:, part * width + lo : part * width + lo + group].astype(F32)
                else:
                    piece = jnp.zeros((shard_rows, group), F32)
                lines[:shard_rows, start : start + group] = piece
        columns[kind] = lines[...].astype(BF16)
    block = rows.shape[1]
    extra[...] = jnp.zeros_like(extra)
    for i in range(rows.shape[0]):
        blocks[i, :block, :] = rows[i]
        extra[:1, :block] = marks[i : i + 1, :].astype(F32)
        blocks[i, block:, :] = extra[...].astype(BF16)


def first_blocks(weight, rows, marks, vectors, classes, group):
    shard_rows = weight.shape[0]
    count, block, width = rows.shape
    return pl.pallas_call(
        functools.partial(first_kernel, group),
        out_shape=[
            jax.ShapeDtypeStruct((classes, shard_rows + ROWS, CORES * 3 * group), BF16),
            jax.ShapeDtypeStruct((count, block + 16, width), BF16),
        ],
        in_specs=vmem_specs(3 + len(vectors)),
        out_specs=vmem_specs(2),
        scratch_shapes=[
            pltpu.VMEM((shard_rows + ROWS, CORES * 3 * group), F32),
            pltpu.VMEM((16, width), F32),
        ],
    )(weight, rows, marks, *vectors)


def stack_kernel(out_ref, fc_ref, after, stacked):
    width = out_ref.shape[1]
    stacked[0] = out_ref[...]
    for i in range(fc_ref.shape[1] // width):
        stacked[1 + i] = fc_ref[:, i * width : (i + 1) * width]


def stack_weights(w_out, w_fc, after):
    rows, width = w_out.shape
    return pl.pallas_call(
        stack_kernel,
        out_shape=jax.ShapeDtypeStruct((1 + w_fc.shape[1] // width, rows, width), BF16),
        in_specs=vmem_specs(2) + [ANYWHERE],
        out_specs=vmem_specs(1)[0],
        cost_estimate=LIGHT,
    )(w_out, w_fc, after)


def tower_kernel(axis, count, *refs):
    pieces, low, high = refs[:count], refs[-2], refs[-1]
    level = lax.axis_index("seq") // CORES
    for step, piece in enumerate(pieces):
        place = lax.rem(level + step, count)
        for half, start in ((low, 0), (high, count // 2)):

            @pl.when((place >= start) & (place < start + count // 2))
            def _():
                if axis == 1:
                    half[:, place - start] = piece[...]
                else:
                    half[place - start] = piece[...]


def build_tower(pieces, axis, after):
    count = len(pieces)
    shape = pieces[0].shape
    shape = (*shape[:axis], count // 2, *shape[axis:])
    return pl.pallas_call(
        functools.partial(tower_kernel, axis, count),
        out_shape=[jax.ShapeDtypeStruct(shape, BF16)] * 2,
        in_specs=vmem_specs(count) + [ANYWHERE] * len(after),
        out_specs=vmem_specs(2),
        compiler_params=pltpu.CompilerParams(vmem_limit_bytes=32 * 2**20),
        cost_estimate=LIGHT,
    )(*pieces, *after)


def one_hot_order(order_ref):
    width = order_ref.shape[1]
    features = lax.broadcasted_iota(jnp.int32, (width, width), 0)
    return jnp.where(features == order_ref[...], 1.0, 0.0).astype(BF16)


def contract_last(left, right):
    return lax.dot_general(left, right, (((1,), (1,)), ((), ())), preferred_element_type=F32)


def middle_kernel(
    groups,
    half1,
    other1,
    half2,
    other2,
    attended,
    inputs,
    cotangent,
    order_ref,
    bout,
    gain,
    bias,
    bfc,
    bproj,
    outputs,
    grad_middle,
    grad_blocks,
    placed_a,
    placed_n,
    hidden,
    grad_pre,
    grad_out,
    sum_out,
    sum_gain,
    sum_bias,
    sum_fc,
    sum_proj,
    weights1,
    weights2,
    attended_rows,
    slopes,
    permuted,
    sems,
):
    parts = weights1.shape[0] - 1
    width = weights1.shape[2]
    side = width // CORES
    seq_count, block, _ = inputs.shape
    tokens = seq_count * block
    core = lax.rem(lax.axis_index("seq"), CORES)
    chips, rows2 = half2.shape[:2]
    copies = []
    for kind in range(parts + 1):
        for index, source in enumerate((half1, other1)):
            copies.append(
                pltpu.make_async_copy(
                    source.at[kind],
                    weights1.at[kind, pl.ds(index * side, side)],
                    sems.at[len(copies)],
                )
            )
    ready1 = len(copies)
    if chips == 1:
        copies.append(pltpu.make_async_copy(half2.at[0], weights2, sems.at[len(copies)]))
    for index, source in enumerate((half2, other2) if chips > 1 else ()):
        place = core if index == 0 else 1 - core
        for chip in range(chips):
            start = pl.multiple_of((chip * CORES + place) * rows2, rows2)
            copies.append(
                pltpu.make_async_copy(
                    source.at[chip], weights2.at[pl.ds(start, rows2)], sems.at[len(copies)]
                )
            )
    for copy in copies:
        copy.start()
    order = one_hot_order(order_ref)

    half_block = block // 2
    group = attended.shape[2] // 2
    for i in range(seq_count):
        for g in range(groups):
            for part in range(2):
                start = i * block + part * half_block
                attended_rows[start : start + half_block, g * group : (g + 1) * group] = attended[
                    i * groups + g, :, part * group : (part + 1) * group
                ]
    placed = jnp.dot(attended_rows[:, :width], order, preferred_element_type=F32).astype(BF16)
    placed_a[...] = placed
    for copy in copies[:2]:
        copy.wait()
    rows = inputs[...].astype(F32).reshape(tokens, width)
    middle = rows + (jnp.dot(placed, weights1[0], preferred_element_type=F32) + bout[...])
    center = jnp.mean(middle, -1, keepdims=True)
    centered = middle - center
    scale = lax.rsqrt(jnp.mean(centered * centered, -1, keepdims=True) + EPSILON)
    unit = centered * scale
    normed = (unit * gain[...] + bias[...]).astype(BF16)
    placed = jnp.dot(normed, order, preferred_element_type=F32).astype(BF16)
    placed_n[...] = placed
    for copy in copies[2:ready1]:
        copy.wait()
    curve = math.sqrt(2.0 / math.pi)
    for q in range(parts):
        lo = q * width
        pre = jnp.dot(placed, weights1[1 + q], preferred_element_type=F32)
        pre = pre + bfc[:, lo : lo + width]
        square = pre * pre
        tanh = jnp.tanh(curve * (pre + 0.044715 * (pre * square)))
        hidden[:, lo : lo + width] = (0.5 * pre * (1.0 + tanh)).astype(BF16)
        slopes[:, lo : lo + width] = 0.5 * (1.0 + tanh) + 0.5 * pre * (1.0 - tanh * tanh) * (
            curve * (1.0 + 3 * 0.044715 * square)
        )
    for copy in copies[ready1:]:
        copy.wait()
    result = middle + bproj[...]
    for q in range(parts):
        lo = q * width
        result += jnp.dot(
            hidden[:, lo : lo + width], weights2[lo : lo + width], preferred_element_type=F32
        )
    outputs[...] = result.astype(BF16).reshape(seq_count, block, width)

    branch = cotangent[...].reshape(tokens, width)
    grad_rows = branch.astype(F32)
    sum_proj[...] = jnp.sum(grad_rows, 0, keepdims=True)
    grad_placed = jnp.zeros((tokens, width), F32)
    for q in range(parts):
        lo = q * width
        grad = contract_last(branch, weights2[lo : lo + width]) * slopes[:, lo : lo + width]
        grad = grad.astype(BF16)
        grad_pre[:, lo : lo + width] = grad
        sum_fc[:, lo : lo + width] = jnp.sum(grad.astype(F32), 0, keepdims=True)
        grad_placed += contract_last(grad, weights1[1 + q])
    high = grad_placed.astype(BF16)
    rest = grad_placed - high.astype(F32)
    mid = rest.astype(BF16)
    low = (rest - mid.astype(F32)).astype(BF16)
    grad_normed = contract_last(high, order) + (contract_last(mid, order) + contract_last(low, order))
    sum_bias[...] = jnp.sum(grad_normed, 0, keepdims=True)
    sum_gain[...] = jnp.sum(grad_normed * unit, 0, keepdims=True)
    grad_unit = grad_normed * gain[...]
    part = jnp.mean(grad_unit, -1, keepdims=True)
    cross = jnp.mean(grad_unit * unit, -1, keepdims=True)
    grad_mid = grad_rows + scale * (grad_unit - part - unit * cross)
    grad_middle[...] = grad_mid
    grad_attn = grad_mid.astype(BF16)
    grad_out[...] = grad_attn
    sum_out[...] = jnp.sum(grad_attn.astype(F32), 0, keepdims=True)
    back = contract_last(grad_attn, weights1[0]).astype(BF16)
    if permuted.shape[1] > width:
        permuted[...] = jnp.zeros_like(permuted)
    permuted[:, :width] = contract_last(back, order).astype(BF16)
    for i in range(seq_count):
        for g in range(groups):
            for part in range(2):
                start = i * block + part * half_block
                grad_blocks[i * groups + g, :, part * group : (part + 1) * group] = permuted[
                    start : start + half_block, g * group : (g + 1) * group
                ]


def middle_block(half1, other1, half2, other2, attended, inputs, cotangent, order, vectors, groups):
    kinds, side, width = half1.shape
    parts = kinds - 1
    chips = half2.shape[0]
    seq_count, block, _ = inputs.shape
    tokens = seq_count * block
    wide = groups * attended.shape[2] // 2

    def shape(*dims, kind=BF16):
        return jax.ShapeDtypeStruct(dims, kind)

    return pl.pallas_call(
        functools.partial(middle_kernel, groups),
        out_shape=[
            shape(seq_count, block, width),
            shape(tokens, width, kind=F32),
            shape(*attended.shape),
            shape(tokens, width),
            shape(tokens, width),
            shape(tokens, parts * width),
            shape(tokens, parts * width),
            shape(tokens, width),
            shape(1, width, kind=F32),
            shape(1, width, kind=F32),
            shape(1, width, kind=F32),
            shape(1, parts * width, kind=F32),
            shape(1, width, kind=F32),
        ],
        in_specs=[ANYWHERE] * 4 + vmem_specs(9),
        out_specs=vmem_specs(13),
        scratch_shapes=[
            pltpu.VMEM((kinds, width, width), BF16),
            pltpu.VMEM((parts * width, width), BF16),
            pltpu.VMEM((tokens, wide), BF16),
            pltpu.VMEM((tokens, parts * width), F32),
            pltpu.VMEM((tokens, wide), BF16),
            pltpu.SemaphoreType.DMA((2 * kinds + 2 * chips,)),
        ],
        compiler_params=pltpu.CompilerParams(vmem_limit_bytes=50 * 2**20),
        cost_estimate=LIGHT,
    )(half1, other1, half2, other2, attended, inputs, cotangent, order, *vectors)


def gradient_kernel(
    shard_rows, placed_a, placed_n, hidden, grad_pre, grad_out, cotangent, send, keep, turned, some
):
    width = placed_a.shape[1]
    side = width // CORES
    parts = hidden.shape[1] // width
    chips = side // shard_rows
    core = lax.rem(lax.axis_index("seq"), CORES)
    branch = cotangent[...].reshape(-1, width)
    if send.shape[0] > 1 + parts:
        for start in range(0, turned.shape[0], width):
            turned[start : start + width, :] = hidden[:, start : start + width].astype(F32).T
        for target, place in ((send, 1 - core), (keep, core)):
            for chip in range(chips):
                for i in range(parts):
                    start = ((chip * CORES + place) * parts + i) * shard_rows
                    start = pl.multiple_of(start, shard_rows)
                    to = i * side + chip * shard_rows
                    some[to : to + shard_rows, :] = turned[pl.ds(start, shard_rows), :]
            for i in range(parts):
                target[1 + parts + i] = jnp.dot(
                    some[i * side : (i + 1) * side, :].astype(BF16),
                    branch,
                    preferred_element_type=F32,
                ).astype(BF16)
    turned_a = placed_a[...].astype(F32).T.astype(BF16)
    turned_n = placed_n[...].astype(F32).T.astype(BF16)
    for target, start in ((send, side), (keep, 0)):
        target[0] = jnp.dot(
            turned_a[start : start + side], grad_out[...], preferred_element_type=F32
        ).astype(BF16)
        for q in range(parts):
            target[1 + q] = jnp.dot(
                turned_n[start : start + side],
                grad_pre[:, q * width : (q + 1) * width],
                preferred_element_type=F32,
            ).astype(BF16)


def weight_gradients(placed_a, placed_n, hidden, grad_pre, grad_out, cotangent, shard_rows):
    tokens, width = placed_a.shape
    parts = hidden.shape[1] // width
    kinds = 1 + parts * (1 if shard_rows % 8 else 2)
    shape = jax.ShapeDtypeStruct((kinds, width // CORES, width), BF16)
    return pl.pallas_call(
        functools.partial(gradient_kernel, shard_rows),
        out_shape=[shape, shape],
        in_specs=vmem_specs(6),
        out_specs=vmem_specs(2),
        scratch_shapes=[
            pltpu.VMEM((parts * width, tokens), F32),
            pltpu.VMEM((parts * width // CORES, tokens), F32),
        ],
        compiler_params=pltpu.CompilerParams(vmem_limit_bytes=50 * 2**20),
        cost_estimate=LIGHT,
    )(placed_a, placed_n, hidden, grad_pre, grad_out, cotangent)


def masked_scores(keys, queries, id_column, id_row, first):
    scores = lax.dot_general(keys, queries, (((1,), (1,)), ((), ())), preferred_element_type=F32)
    key_pos = lax.broadcasted_iota(jnp.int32, scores.shape, 0)
    query_pos = lax.broadcasted_iota(jnp.int32, scores.shape, 1) + first
    allowed = (key_pos <= query_pos) & (id_column == id_row)
    return jnp.where(allowed, scores, MASKED)


def column_of(id_row):
    length = id_row.shape[1]
    return jnp.broadcast_to(id_row, (LANES, length)).T[:, :1]


def forward_kernel(
    seq_count,
    heads,
    head_size,
    step_rows,
    block,
    rows_ref,
    weight,
    gain,
    bias,
    bqv,
    after,
    out,
    stats,
    whole,
    normed,
    ids,
    result,
    qkv_bias,
):
    length = whole.shape[0]
    group = heads * head_size
    width = weight.shape[0]
    index = lax.rem(lax.axis_index("seq"), lax.axis_size("seq") // seq_count)
    qkv_bias[...] = jnp.zeros_like(qkv_bias)
    for lo in range(0, width, group):
        here = index == lo // group
        for base, start in ((0, 0), (width, 2 * group)):
            piece = jnp.where(here, bqv[:, base + lo : base + lo + group], 0.0)
            qkv_bias[:, start : start + group] += piece
    for i in range(length // block):
        rows = norm_affine(rows_ref[i, :block, :].astype(F32), gain[...], bias[...])
        normed[i * block : (i + 1) * block, :] = rows.astype(BF16)
    id_rows = [rows_ref[i, block:, :block].astype(F32)[:1] for i in range(length // block)]
    id_row = jnp.concatenate(id_rows, 1)
    ids[...] = id_row
    id_column = column_of(id_row)
    for first in range(0, length, step_rows):
        last = first + step_rows
        product = jnp.dot(normed[first:last, :], weight[...], preferred_element_type=F32)
        whole[first:last, :] = (product + qkv_bias[...]).astype(BF16)
    values_t = whole[:, 2 * group : 3 * group].astype(F32).T.astype(BF16)
    for first in range(0, length, step_rows):
        last = first + step_rows
        tops = []
        for head in range(heads):
            lo = head * head_size
            queries = whole[first:last, lo : lo + head_size] * BF16(head_size**-0.5)
            keys = whole[:last, group + lo : group + lo + head_size]
            scores = masked_scores(keys, queries, id_column[:last], id_row[:, first:last], first)
            highest = jnp.max(scores, 0, keepdims=True)
            weights = jnp.exp(scores - highest)
            total = jnp.sum(weights, 0, keepdims=True)
            probs = (weights * (1.0 / total)).astype(BF16)
            tops.append(
                jnp.dot(
                    values_t[lo : lo + head_size, :last], probs, preferred_element_type=F32
                )
            )
            stats[head : head + 1, first:last] = highest + jnp.log(total)
        result[first:last, :] = jnp.concatenate(tops, 0).T.astype(BF16)
    half = block // 2
    for start in range(0, length, block):
        out[start // 2 : start // 2 + half, :group] = result[start : start + half, :]
        out[start // 2 : start // 2 + half, group:] = result[start + half : start + block, :]


def backward_kernel(
    heads,
    head_size,
    step_rows,
    block,
    whole,
    grads,
    stats,
    ids,
    after1,
    after2,
    out,
    grad_out,
    grad_query,
    grad_key,
    grad_value,
):
    length = whole.shape[0]
    group = heads * head_size
    half = block // 2
    for start in range(0, length, block):
        packed = grads[start // 2 : start // 2 + half, :]
        grad_out[start : start + half, :] = packed[:, :group]
        grad_out[start + half : start + block, :] = packed[:, group:]
    id_row = ids[...]
    id_column = column_of(id_row)
    keys_t = whole[:, group : 2 * group].astype(F32).T.astype(BF16)
    factor = head_size**-0.5
    grad_key[...] = jnp.zeros_like(grad_key)
    grad_value[...] = jnp.zeros_like(grad_value)
    for first in range(0, length, step_rows):
        last = first + step_rows
        tops = []
        for head in range(heads):
            lo = head * head_size
            queries = whole[first:last, lo : lo + head_size] * BF16(factor)
            keys = whole[:last, group + lo : group + lo + head_size]
            values = whole[:last, 2 * group + lo : 2 * group + lo + head_size]
            grad = grad_out[first:last, lo : lo + head_size]
            scores = masked_scores(keys, queries, id_column[:last], id_row[:, first:last], first)
            probs = jnp.exp(scores - stats[head : head + 1, first:last])
            grad_probs = lax.dot_general(
                values, grad, (((1,), (1,)), ((), ())), preferred_element_type=F32
            )
            delta = jnp.sum(probs * grad_probs, 0, keepdims=True)
            grad_scores = (probs * (grad_probs - delta)).astype(BF16)
            tops.append(
                jnp.dot(
                    keys_t[lo : lo + head_size, :last], grad_scores, preferred_element_type=F32
                )
                * factor
            )
            grad_key[head, :last, :] += jnp.dot(
                grad_scores, queries, preferred_element_type=F32
            )
            grad_value[head, :last, :] += jnp.dot(
                probs.astype(BF16), grad, preferred_element_type=F32
            )
        grad_query[first:last, :] = jnp.concatenate(tops, 0).T.astype(BF16)
    out[:, :group] = grad_query[...]
    for head in range(heads):
        lo = head * head_size
        out[:, group + lo : group + lo + head_size] = grad_key[head].astype(BF16)
        out[:, 2 * group + lo : 2 * group + lo + head_size] = grad_value[head].astype(BF16)


def attend_forward(rows, weight, gain, bias, bqv, after, seq_count, heads, head_size, block):
    length = rows.shape[0] * block
    width = rows.shape[2]
    group = heads * head_size
    return pl.pallas_call(
        functools.partial(forward_kernel, seq_count, heads, head_size, min(256, length), block),
        out_shape=[
            jax.ShapeDtypeStruct((length // 2, 2 * group), BF16),
            jax.ShapeDtypeStruct((heads, length), F32),
            jax.ShapeDtypeStruct((length, 3 * group), BF16),
            jax.ShapeDtypeStruct((length, width), BF16),
            jax.ShapeDtypeStruct((1, length), F32),
        ],
        in_specs=vmem_specs(5) + [ANYWHERE],
        out_specs=vmem_specs(5),
        scratch_shapes=[pltpu.VMEM((length, group), BF16), pltpu.VMEM((1, 3 * group), F32)],
        compiler_params=pltpu.CompilerParams(vmem_limit_bytes=48 * 2**20),
        cost_estimate=LIGHT,
    )(rows, weight, gain, bias, bqv, after)


def attend_backward(whole, grads, stats, ids, after, heads, head_size, block):
    length, width = whole.shape
    group = heads * head_size
    return pl.pallas_call(
        functools.partial(backward_kernel, heads, head_size, min(256, length), block),
        out_shape=jax.ShapeDtypeStruct((length, 3 * group), BF16),
        in_specs=vmem_specs(4) + [ANYWHERE] * 2,
        out_specs=vmem_specs(1)[0],
        scratch_shapes=[
            pltpu.VMEM((length, group), BF16),
            pltpu.VMEM((length, group), BF16),
            pltpu.VMEM((heads, length, head_size), F32),
            pltpu.VMEM((heads, length, head_size), F32),
        ],
        compiler_params=pltpu.CompilerParams(vmem_limit_bytes=48 * 2**20),
        cost_estimate=LIGHT,
    )(whole, grads, stats, ids, *after)


def on_device(
    inputs,
    segments,
    cotangent,
    ln1_gain,
    ln1_bias,
    w_qkv,
    b_qv,
    w_out,
    b_out,
    ln2_gain,
    ln2_bias,
    w_fc,
    b_fc,
    w_proj,
    b_proj,
):
    seq_count, block, width = inputs.shape
    head_size = width // HEADS
    tokens = seq_count * block
    count = lax.axis_size("seq")
    devices = count * lax.axis_size("dp")
    groups = count // seq_count
    heads = -(-HEADS // groups)
    spare = groups * heads - HEADS
    group = heads * head_size

    vectors = (ln1_gain, ln1_bias, b_qv, b_out, ln2_gain, ln2_bias, b_fc, b_proj)
    sizes = tuple(vector.shape[0] for vector in vectors)
    shard_rows = w_out.shape[0] // width
    parts = w_fc.shape[0] // w_out.shape[0]
    classes = groups // CORES
    chips = devices // CORES
    place = lax.axis_index("seq")
    core = place % CORES
    group_index = place % groups

    columns, blocks = first_blocks(
        w_qkv.reshape(shard_rows, 3 * width),
        inputs,
        segments,
        [vector.reshape(1, -1) for vector in vectors],
        classes,
        group,
    )
    tower_a = build_line(gather_columns(columns))
    lines, sequence = gather_sequence(blocks, tower_a)
    stacked = stack_weights(w_out.reshape(-1, width), w_fc.reshape(-1, parts * width), columns)
    low1, high1 = build_tower(z_pieces(stacked), 1, [tower_a])
    if lax.axis_size("dp") == 4:
        towers = [tower_a] + [swap_dp(tower_a, mask) for mask in range(1, 4)]
    else:
        towers = [lax.all_gather(tower_a, "dp", axis=0, tiled=True)]
    keep_a, send_a = split_halves(towers, [low1, lines])
    wqkv, gain1, bias1, bqv, bout, gain2, bias2, bfc, bproj = unpack_first(
        keep_a, swap_core(send_a), sizes
    )

    raw, stats, qkv, normed1, ids = attend_forward(
        sequence, wqkv, gain1, bias1, bqv, low1, seq_count, heads, head_size, block
    )
    pieces2 = z_pieces(gate(w_proj.reshape(-1, width), lines))
    low2, high2 = build_tower(pieces2, 0, [raw])
    attended = exchange(raw.reshape(count, block // 2, 2 * group))
    half1 = gather_plane(low1, high1, 1, raw, attended).reshape(1 + parts, -1, width)
    half2 = gather_plane(low2, high2, 0, attended)
    other1 = swap_core(half1)
    other2 = swap_core(half2)
    aligned = half2.shape[1] % 16 == 0
    if not aligned:
        half2 = ordered(core, half2, other2, 1).reshape(1, parts * width, width)

    spot = jnp.arange(width, dtype=jnp.int32)
    side = width // CORES
    own_core = (core + spot // side) % CORES
    order = (spot % side // shard_rows * CORES + own_core) * shard_rows + spot % shard_rows
    (
        outputs,
        grad_middle,
        grad_blocks,
        placed_a,
        placed_n,
        hidden,
        grad_pre,
        grad_out,
        grad_bout,
        grad_gain2,
        grad_bias2,
        grad_bfc,
        grad_bproj,
    ) = middle_block(
        half1,
        other1,
        half2,
        other2,
        attended,
        inputs,
        cotangent,
        order.reshape(1, width),
        (bout, gain2, bias2, bfc, bproj),
        groups,
    )
    grad_blocks = exchange(grad_blocks).reshape(-1, 2 * group)
    send_b, keep_b = weight_gradients(
        placed_a, placed_n, hidden, grad_pre, grad_out, cotangent, shard_rows
    )
    if send_b.shape[0] == 1 + parts:
        grad_wproj = lax.dot_general(
            hidden,
            cotangent.reshape(tokens, width),
            (((0,), (0,)), ((), ())),
            preferred_element_type=F32,
        )
        grad_wproj = grad_wproj.astype(BF16).reshape(chips, CORES, parts, shard_rows, width)
        grad_wproj = grad_wproj.transpose(1, 2, 0, 3, 4).reshape(CORES, parts, -1, width)
        send_b = jnp.concatenate([send_b, pick(grad_wproj, 1 - core, 0)], 0)
        keep_b = jnp.concatenate([keep_b, pick(grad_wproj, core, 0)], 0)
    sum_b = add(keep_b, swap_core(send_b)).reshape(-1, chips, shard_rows, width)
    steps = []

    def between(*after):
        if steps:
            steps.append(after[0])
        else:
            steps.append(
                attend_backward(qkv, grad_blocks, stats, ids, after, heads, head_size, block)
            )
        return steps[0]

    tower_b = scatter_plane(sum_b, 1, between)
    own_b = scatter_z(tower_b, 1)
    grad_qkv, first_sums = steps

    def blocks_of(value, rows):
        return value.astype(BF16).reshape(chips, CORES, rows, -1)

    rows = inputs.astype(F32).reshape(tokens, width)
    grad_normed1 = lax.dot_general(
        grad_qkv, wqkv, (((1,), (1,)), ((), ())), preferred_element_type=F32
    )
    own_normed1 = scatter_sequence(
        grad_normed1.astype(BF16).reshape(count, block, width), first_sums, tower_b
    )
    _, norm1_back = jax.vjp(lambda value: norm_affine(value, gain1, bias1), rows)
    (grad_in_part,) = norm1_back(own_normed1.astype(F32).reshape(tokens, width))
    grad_inputs = (grad_middle + grad_in_part).astype(BF16).reshape(inputs.shape)

    grad_qkv = gate(grad_qkv, first_sums)
    long_rows = sequence[:, :block].astype(F32).reshape(count * block, width)
    _, norm1_long_back = jax.vjp(lambda g, b: norm_affine(long_rows, g, b), gain1, bias1)
    grad_gain1, grad_bias1 = norm1_long_back(grad_normed1)
    grad_wqkv = lax.dot_general(
        normed1, grad_qkv, (((0,), (0,)), ((), ())), preferred_element_type=F32
    )
    sums = jnp.sum(grad_qkv, 0, dtype=F32).reshape(3, group)
    here = (jnp.arange(groups) == group_index)[None, :, None]
    grad_bqv = jnp.where(here, jnp.stack([sums[0], sums[2]])[:, None], 0.0)
    grad_bqv = grad_bqv.reshape(2, groups * heads, head_size)[:, :HEADS]
    grads = (
        grad_gain1,
        grad_bias1,
        grad_bqv,
        grad_bout,
        grad_gain2,
        grad_bias2,
        grad_bfc,
        grad_bproj,
    )
    small_grads = pack_small([grad.reshape(1, -1) for grad in grads], sizes, devices)
    small_grads = jnp.pad(small_grads, ((0, 0), (0, 0), (0, 3 * group - LANES)))
    block_a = jnp.concatenate(
        [blocks_of(grad_wqkv, shard_rows), small_grads.reshape(chips, CORES, ROWS, -1)], 2
    )
    send_a, keep_a = pick(block_a, 1 - core, 1), pick(block_a, core, 1)
    got_a = swap_core(send_a)
    pair_a = jnp.concatenate(
        [jnp.where(core == 0, keep_a, got_a), jnp.where(core == 0, got_a, keep_a)], -1
    )
    tower_a = scatter_plane_direct(pair_a, tower_b)
    own_a = scatter_columns(tower_a, own_b)
    own_small = jnp.sum(
        own_a[:, shard_rows:].reshape(classes, ROWS, CORES, 3 * group)[..., :LANES], (0, 2)
    )
    own = [own_small[i, :size] for i, size in enumerate(sizes)]
    own_qkv = own_a[:, :shard_rows].reshape(classes, shard_rows, CORES, 3, group)
    own_qkv = own_qkv.transpose(1, 3, 0, 2, 4).reshape(shard_rows, 3, groups * heads, head_size)
    own_qkv = own_qkv[:, :, :HEADS].reshape(-1)
    return (
        outputs,
        grad_inputs,
        own[0],
        own[1],
        own_qkv,
        own[2],
        own_b[0].reshape(-1),
        own[3],
        own[4],
        own[5],
        own_b[1 : 1 + parts].transpose(1, 0, 2).reshape(-1),
        own[6],
        own_b[1 + parts :].reshape(-1),
        own[7],
    )


def solution(mesh):
    token_spec = P("dp", "seq", None)
    flat_spec = P(("dp", "seq"))
    in_specs = (token_spec, P("dp", "seq"), token_spec) + (flat_spec,) * 12
    out_specs = (token_spec, token_spec) + (flat_spec,) * 12
    return jax.shard_map(
        on_device, mesh=mesh, in_specs=in_specs, out_specs=out_specs, check_vma=False
    )
```

```python
import functools
import math

import jax
import jax.numpy as jnp
from jax import lax
from jax.experimental import pallas as pl
from jax.experimental.pallas import tpu as pltpu
from jax.sharding import PartitionSpec as P

HEADS = 12
CORES = 2


EPSILON = 1e-05
MASKED = -1e30
F32 = jnp.float32
BF16 = jnp.bfloat16


def norm_affine(values, gain, bias):
    center = jnp.mean(values, -1, keepdims=True)
    centered = values - center
    variance = jnp.mean(centered * centered, -1, keepdims=True)
    return centered * lax.rsqrt(variance + EPSILON) * gain + bias


ANYWHERE = pl.BlockSpec(memory_space=pl.ANY)
LIGHT = pl.CostEstimate(flops=1, bytes_accessed=1, transcendentals=0)


def shift_z(value, step):
    size = lax.axis_size("seq")
    return lax.ppermute(value, "seq", [(i, (i + CORES * step) % size) for i in range(size)])


def swap_core(value):
    size = lax.axis_size("seq")
    return lax.ppermute(value, "seq", [(i, i ^ 1) for i in range(size)])


def swap_dp(value, bit):
    size = lax.axis_size("dp")
    return lax.ppermute(value, "dp", [(i, i ^ bit) for i in range(size)])


def ordered(flag, mine, other, axis):
    first = jnp.where(flag == 0, mine, other)
    second = jnp.where(flag == 0, other, mine)
    return jnp.stack([first, second], axis)


def roll_blocks(pieces, place):
    count = len(pieces)
    stacked = jnp.stack(pieces)
    twice = jnp.concatenate([stacked, stacked])
    return lax.dynamic_slice_in_dim(twice, lax.rem(count - place, count), count, 0)


def z_pieces(shard):
    heights = lax.axis_size("seq") // CORES
    return [shard] + [shift_z(shard, -step) for step in range(1, heights)]


def swap_z(value, bit):
    size = lax.axis_size("seq")
    return lax.ppermute(value, "seq", [(i, i ^ (CORES * bit)) for i in range(size)])


def gather_plane(low, high, axis, between, after):
    if lax.axis_size("dp") != 4:
        between(low)
        return lax.all_gather(jnp.concatenate([low, high], axis), "dp", axis=axis, tiled=True)
    plane = lax.axis_index("dp")
    y, x = plane // 2, plane % 2
    low_got, high_got = swap_dp(low, 1), swap_dp(high, 2)
    if after is not None:
        low_got, high_got = gate_both(low_got, high_got, after)
    low_x = ordered(x, low, low_got, axis)
    high_y = ordered(y, high, high_got, axis)
    second = between(low_x, high_y)
    low_got, high_got = gate_both(swap_dp(low_x, 2), swap_dp(high_y, 1), second)
    low_all = ordered(y, low_x, low_got, axis)
    high_all = ordered(x, high_y, high_got, axis + 1)
    half = jnp.concatenate([low_all, high_all], axis + 2)
    count = 4 * half.shape[axis + 2]
    return half.reshape(*low.shape[:axis], count, *low.shape[axis + 1 :])


def pick(value, index, axis):
    return lax.dynamic_index_in_dim(value, index, axis, keepdims=False)


def add(mine, other):
    return (mine.astype(F32) + other.astype(F32)).astype(mine.dtype)


def scatter_plane(split, axis, between=None):
    planes = lax.axis_size("dp")
    heights = lax.axis_size("seq") // CORES
    if planes != 4:
        if between is not None:
            between(split, split)
            between(split, split)
        return lax.psum_scatter(split, "dp", scatter_dimension=axis, tiled=True)
    plane = lax.axis_index("dp")
    y, x = plane // 2, plane % 2
    split = split.reshape(*split.shape[:axis], 2, 2, heights, *split.shape[axis + 1 :])
    low = lax.slice_in_dim(split, 0, heights // 2, axis=axis + 2)
    high = lax.slice_in_dim(split, heights // 2, heights, axis=axis + 2)
    low_send, high_send = pick(low, 1 - y, axis), pick(high, 1 - x, axis + 1)
    low_got, high_got = swap_dp(low_send, 2), swap_dp(high_send, 1)
    if between is not None:
        after = between(low_send, high_send)
        low_got, high_got = gate_both(low_got, high_got, after)
    low = add(pick(low, y, axis), low_got)
    high = add(pick(high, x, axis + 1), high_got)
    if between is not None:
        between(low, high)
    low = add(pick(low, x, axis), swap_dp(pick(low, 1 - x, axis), 1))
    high = add(pick(high, y, axis), swap_dp(pick(high, 1 - y, axis), 2))
    return jnp.concatenate([low, high], axis)


def scatter_z(tower, axis):
    heights = lax.axis_size("seq") // CORES
    level = lax.axis_index("seq") // CORES
    mine = pick(tower, level, axis).astype(F32)
    for step in range(1, heights):
        mine += shift_z(pick(tower, lax.rem(level + step, heights), axis), step).astype(F32)
    return mine


def z_bits():
    heights = lax.axis_size("seq") // CORES
    level = lax.axis_index("seq") // CORES
    top = heights // 2
    return level, top, level // top


def gather_sequence(blocks, after):
    level, top, half = z_bits()
    core = lax.axis_index("seq") % CORES
    got = gate(swap_z(pick(blocks, 1 - half, 0), top), after)
    held = ordered(half, pick(blocks, half, 0), got, 0)
    axis, bit = 1, top // 2
    while bit:
        held = ordered(level // bit % 2, held, swap_z(held, bit), axis)
        axis, bit = axis + 1, bit // 2
    return held, ordered(core, held, swap_core(held), axis).reshape(-1, *blocks.shape[1:])


def scatter_sequence(partial, first, second, third):
    level, top, half = z_bits()
    core = lax.axis_index("seq") % CORES
    shape = partial.shape[1:]
    count = top.bit_length()
    held = partial.reshape(*[2] * (count + 1), *shape)
    got = gate(swap_core(pick(held, 1 - core, count)), first)
    held = add(pick(held, core, count), got)
    axis, bit = count - 1, 1
    while bit < top:
        flag = level // bit % 2
        got = gate(swap_z(pick(held, 1 - flag, axis), bit), second)
        held = add(pick(held, flag, axis), got)
        axis, bit = axis - 1, bit * 2
    got = gate(swap_z(pick(held, 1 - half, 0), top), third)
    return ordered(half, pick(held, half, 0), got, 0)


def class_of(level):
    return level % (lax.axis_size("seq") // CORES // 2)


def gather_columns(blocks):
    heights = lax.axis_size("seq") // CORES
    level = lax.axis_index("seq") // CORES
    moved = [
        swap_z(pick(blocks, class_of(level ^ mask), 0), mask) for mask in range(1, heights)
    ]
    return [pick(blocks, class_of(level), 0)] + moved


def scatter_columns(tower):
    heights = tower.shape[0]
    level = lax.axis_index("seq") // CORES
    moved = [swap_z(pick(tower, level ^ mask, 0), mask) for mask in range(1, heights)]
    return [pick(tower, level, 0)] + moved


def scatter_plane_direct(split, after):
    planes = lax.axis_size("dp")
    if planes != 4:
        return lax.psum_scatter(split, "dp", scatter_dimension=0, tiled=True)
    plane = lax.axis_index("dp")
    split = split.reshape(planes, -1, *split.shape[1:])
    total = pick(split, plane, 0).astype(F32)
    for mask in range(1, planes):
        total += gate(swap_dp(pick(split, plane ^ mask, 0), mask), after).astype(F32)
    return total.astype(split.dtype)


def exchange(blocks):
    return lax.all_to_all(blocks, "seq", split_axis=0, concat_axis=0, tiled=True)


ROWS = 8
LANES = 128


def vmem_specs(count):
    return [pl.BlockSpec(memory_space=pltpu.VMEM) for _ in range(count)]


def place_lanes(size, total):
    source = lax.broadcasted_iota(jnp.int32, (LANES, total), 0)
    target = lax.rem(lax.broadcasted_iota(jnp.int32, (LANES, total), 1), size)
    return jnp.where(source == target, 1.0, 0.0).astype(BF16)


def owned_lanes(devices, size):
    device = lax.broadcasted_iota(jnp.int32, (devices, devices * size), 0)
    lane = lax.broadcasted_iota(jnp.int32, (devices, devices * size), 1)
    offset = lane - device * size
    return (offset >= 0) & (offset < size)


def line_kernel(*refs):
    pieces, tower = refs[:-1], refs[-1]
    level = lax.axis_index("seq") // CORES
    for mask, piece in enumerate(pieces):
        tower[level ^ mask] = piece[...]


def build_line(pieces):
    return pl.pallas_call(
        line_kernel,
        out_shape=jax.ShapeDtypeStruct((len(pieces), *pieces[0].shape), BF16),
        in_specs=vmem_specs(len(pieces)),
        out_specs=vmem_specs(1)[0],
        cost_estimate=LIGHT,
    )(*pieces)


def halves_kernel(count, *refs):
    towers, (keep, send) = refs[:count], refs[-2:]
    heights, _, columns = towers[0].shape
    half = columns // CORES
    core = lax.rem(lax.axis_index("seq"), CORES)
    plane = lax.axis_index("dp")
    for own in range(CORES):

        @pl.when(core == own)
        def _():
            for mask, tower in enumerate(towers):
                base = (plane ^ mask) * heights if count > 1 else 0
                for i in range(heights):
                    line = tower[i]
                    keep[base + i] = line[:, own * half : (own + 1) * half]
                    send[base + i] = line[:, (1 - own) * half : (2 - own) * half]


def split_halves(towers, after):
    heights, rows, columns = towers[0].shape
    shape = jax.ShapeDtypeStruct((len(towers) * heights, rows, columns // CORES), BF16)
    return pl.pallas_call(
        functools.partial(halves_kernel, len(towers)),
        out_shape=[shape, shape],
        in_specs=vmem_specs(len(towers)) + [ANYWHERE] * len(after),
        out_specs=vmem_specs(2),
        compiler_params=pltpu.CompilerParams(vmem_limit_bytes=40 * 2**20),
        cost_estimate=LIGHT,
    )(*towers, *after)


def finish_kernel(count, group, *refs):
    pieces, (weight, small) = refs[:count], refs[-2:]
    shard, width = weight.shape[0], weight.shape[1] // 3
    heights = count
    level = lax.axis_index("seq") // CORES
    terms = [piece[...].astype(F32) for piece in pieces]
    small_sum = jnp.zeros((ROWS, LANES), F32)
    for kind in range(heights // 2):
        total = jnp.zeros_like(terms[0])
        for mask, term in enumerate(terms):
            total += jnp.where(lax.rem(level ^ mask, heights // 2) == kind, term, 0.0)
        for core in range(CORES):
            start = core * 3 * group
            small_sum += total[shard:, start : start + LANES]
            lo = (kind * CORES + core) * group
            for part in range(3 if lo < width else 0):
                at = start + part * group
                weight[:, part * width + lo : part * width + lo + group] = total[
                    :shard, at : at + group
                ]
    small[...] = small_sum


def finish_columns(pieces, width, group, after):
    rows = pieces[0].shape[0]
    return pl.pallas_call(
        functools.partial(finish_kernel, len(pieces), group),
        out_shape=[
            jax.ShapeDtypeStruct((rows - ROWS, 3 * width), F32),
            jax.ShapeDtypeStruct((ROWS, LANES), F32),
        ],
        in_specs=vmem_specs(len(pieces)) + [ANYWHERE],
        out_specs=vmem_specs(2),
        cost_estimate=LIGHT,
    )(*pieces, after)


def unpack_kernel(sizes, keep, got, weight, *refs):
    outs, (lines, small) = refs[:-2], refs[-2:]
    chips, rows = keep.shape[:2]
    shard = rows - ROWS
    core = lax.rem(lax.axis_index("seq"), CORES)
    for own in range(CORES):

        @pl.when(core == own)
        def _():
            for source, place in ((keep, own), (got, 1 - own)):
                for chip in range(chips):
                    device = chip * CORES + place
                    line = source[chip].astype(F32)
                    lines[device * shard : (device + 1) * shard, :] = line[:shard]
                    small[device] = line[shard:, :LANES]

    weight[...] = lines[...].astype(BF16)
    devices = chips * CORES
    for i, (size, out) in enumerate(zip(sizes, outs)):
        spread = jnp.dot(
            small[:, i, :].astype(BF16),
            place_lanes(size, devices * size),
            preferred_element_type=F32,
        )
        out[...] = jnp.sum(jnp.where(owned_lanes(devices, size), spread, 0.0), 0, keepdims=True)


def unpack_first(keep, got, sizes):
    chips, rows, columns = keep.shape
    devices = chips * CORES
    width = devices * (rows - ROWS)
    return pl.pallas_call(
        functools.partial(unpack_kernel, sizes),
        out_shape=[jax.ShapeDtypeStruct((width, columns), BF16)]
        + [jax.ShapeDtypeStruct((1, devices * size), F32) for size in sizes],
        in_specs=vmem_specs(2),
        out_specs=vmem_specs(1 + len(sizes)),
        scratch_shapes=[
            pltpu.VMEM((width, columns), F32),
            pltpu.VMEM((devices, ROWS, LANES), F32),
        ],
        compiler_params=pltpu.CompilerParams(vmem_limit_bytes=40 * 2**20),
        cost_estimate=LIGHT,
    )(keep, got)


def pack_kernel(sizes, *refs):
    grads, packed, rows = refs[: len(sizes)], refs[len(sizes)], refs[len(sizes) + 1]
    devices = packed.shape[0]
    for i, (size, grad) in enumerate(zip(sizes, grads)):
        owned = jnp.where(owned_lanes(devices, size), grad[...], 0.0).astype(BF16)
        rows[:, i, :] = lax.dot_general(
            owned,
            place_lanes(size, devices * size),
            (((1,), (1,)), ((), ())),
            preferred_element_type=F32,
        )
    packed[...] = rows[...].astype(BF16)


def pack_small(grads, sizes, devices):
    return pl.pallas_call(
        functools.partial(pack_kernel, sizes),
        out_shape=jax.ShapeDtypeStruct((devices, ROWS, LANES), BF16),
        in_specs=vmem_specs(len(sizes)),
        out_specs=vmem_specs(1)[0],
        scratch_shapes=[pltpu.VMEM((devices, ROWS, LANES), F32)],
        compiler_params=pltpu.CompilerParams(vmem_limit_bytes=32 * 2**20),
        cost_estimate=LIGHT,
    )(*grads)


def gate(value, *after):
    def kernel(*refs):
        pass

    return pl.pallas_call(
        kernel,
        out_shape=jax.ShapeDtypeStruct(value.shape, value.dtype),
        in_specs=[ANYWHERE] * (1 + len(after)),
        out_specs=ANYWHERE,
        input_output_aliases={0: 0},
        cost_estimate=LIGHT,
    )(value, *after)


def gate_both(one, two, *after):
    def kernel(*refs):
        pass

    return pl.pallas_call(
        kernel,
        out_shape=[jax.ShapeDtypeStruct(value.shape, value.dtype) for value in (one, two)],
        in_specs=[ANYWHERE] * (2 + len(after)),
        out_specs=[ANYWHERE] * 2,
        input_output_aliases={0: 0, 1: 1},
        cost_estimate=LIGHT,
    )(one, two, *after)


def first_kernel(group, weight, rows, marks, *refs):
    vectors, (columns, blocks, lines, extra) = refs[:-4], refs[-4:]
    classes, _, width_pair = columns.shape
    shard_rows, width = weight.shape[0], weight.shape[1] // 3
    lines[...] = jnp.zeros_like(lines)
    for i, vector in enumerate(vectors):
        for start in range(0, width_pair, 3 * group):
            at = shard_rows + i
            lines[at : at + 1, start : start + vector.shape[1]] = vector[...].astype(F32)
    for kind in range(classes):
        for core in range(CORES):
            lo = (kind * CORES + core) * group
            for part in range(3):
                start = (core * 3 + part) * group
                if lo < width:
                    piece = weight[:, part * width + lo : part * width + lo + group].astype(F32)
                else:
                    piece = jnp.zeros((shard_rows, group), F32)
                lines[:shard_rows, start : start + group] = piece
        columns[kind] = lines[...].astype(BF16)
    block = rows.shape[1]
    extra[...] = jnp.zeros_like(extra)
    for i in range(rows.shape[0]):
        blocks[i, :block, :] = rows[i]
        extra[:1, :block] = marks[i : i + 1, :].astype(F32)
        blocks[i, block:, :] = extra[...].astype(BF16)


def first_blocks(weight, rows, marks, vectors, classes, group):
    shard_rows = weight.shape[0]
    count, block, width = rows.shape
    return pl.pallas_call(
        functools.partial(first_kernel, group),
        out_shape=[
            jax.ShapeDtypeStruct((classes, shard_rows + ROWS, CORES * 3 * group), BF16),
            jax.ShapeDtypeStruct((count, block + 16, width), BF16),
        ],
        in_specs=vmem_specs(3 + len(vectors)),
        out_specs=vmem_specs(2),
        scratch_shapes=[
            pltpu.VMEM((shard_rows + ROWS, CORES * 3 * group), F32),
            pltpu.VMEM((16, width), F32),
        ],
    )(weight, rows, marks, *vectors)


def stack_kernel(out_ref, fc_ref, after, stacked):
    width = out_ref.shape[1]
    stacked[0] = out_ref[...]
    for i in range(fc_ref.shape[1] // width):
        stacked[1 + i] = fc_ref[:, i * width : (i + 1) * width]


def stack_weights(w_out, w_fc, after):
    rows, width = w_out.shape
    return pl.pallas_call(
        stack_kernel,
        out_shape=jax.ShapeDtypeStruct((1 + w_fc.shape[1] // width, rows, width), BF16),
        in_specs=vmem_specs(2) + [ANYWHERE],
        out_specs=vmem_specs(1)[0],
        cost_estimate=LIGHT,
    )(w_out, w_fc, after)


def tower_kernel(axis, count, *refs):
    pieces, low, high = refs[:count], refs[-2], refs[-1]
    level = lax.axis_index("seq") // CORES
    for step, piece in enumerate(pieces):
        place = lax.rem(level + step, count)
        for half, start in ((low, 0), (high, count // 2)):

            @pl.when((place >= start) & (place < start + count // 2))
            def _():
                if axis == 1:
                    half[:, place - start] = piece[...]
                else:
                    half[place - start] = piece[...]


def build_tower(pieces, axis, after):
    count = len(pieces)
    shape = pieces[0].shape
    shape = (*shape[:axis], count // 2, *shape[axis:])
    return pl.pallas_call(
        functools.partial(tower_kernel, axis, count),
        out_shape=[jax.ShapeDtypeStruct(shape, BF16)] * 2,
        in_specs=vmem_specs(count) + [ANYWHERE] * len(after),
        out_specs=vmem_specs(2),
        compiler_params=pltpu.CompilerParams(vmem_limit_bytes=32 * 2**20),
        cost_estimate=LIGHT,
    )(*pieces, *after)


def one_hot_order(order_ref):
    width = order_ref.shape[1]
    features = lax.broadcasted_iota(jnp.int32, (width, width), 0)
    return jnp.where(features == order_ref[...], 1.0, 0.0).astype(BF16)


def contract_last(left, right):
    return lax.dot_general(left, right, (((1,), (1,)), ((), ())), preferred_element_type=F32)


def middle_kernel(
    groups,
    half1,
    other1,
    half2,
    other2,
    attended,
    inputs,
    cotangent,
    order_ref,
    bout,
    gain,
    bias,
    bfc,
    bproj,
    outputs,
    grad_middle,
    grad_blocks,
    placed_a,
    placed_n,
    hidden,
    grad_pre,
    grad_out,
    sum_out,
    sum_gain,
    sum_bias,
    sum_fc,
    sum_proj,
    weights1,
    weights2,
    attended_rows,
    slopes,
    permuted,
    sems,
):
    parts = weights1.shape[0] - 1
    width = weights1.shape[2]
    side = width // CORES
    seq_count, block, _ = inputs.shape
    tokens = seq_count * block
    core = lax.rem(lax.axis_index("seq"), CORES)
    chips, rows2 = half2.shape[:2]
    copies = []
    for kind in range(parts + 1):
        for index, source in enumerate((half1, other1)):
            copies.append(
                pltpu.make_async_copy(
                    source.at[kind],
                    weights1.at[kind, pl.ds(index * side, side)],
                    sems.at[len(copies)],
                )
            )
    ready1 = len(copies)
    if chips == 1:
        copies.append(pltpu.make_async_copy(half2.at[0], weights2, sems.at[len(copies)]))
    for index, source in enumerate((half2, other2) if chips > 1 else ()):
        place = core if index == 0 else 1 - core
        for chip in range(chips):
            start = pl.multiple_of((chip * CORES + place) * rows2, rows2)
            copies.append(
                pltpu.make_async_copy(
                    source.at[chip], weights2.at[pl.ds(start, rows2)], sems.at[len(copies)]
                )
            )
    for copy in copies:
        copy.start()
    order = one_hot_order(order_ref)

    half_block = block // 2
    group = attended.shape[2] // 2
    for i in range(seq_count):
        for g in range(groups):
            for part in range(2):
                start = i * block + part * half_block
                attended_rows[start : start + half_block, g * group : (g + 1) * group] = attended[
                    i * groups + g, :, part * group : (part + 1) * group
                ]
    placed = jnp.dot(attended_rows[:, :width], order, preferred_element_type=F32).astype(BF16)
    placed_a[...] = placed
    for copy in copies[:2]:
        copy.wait()
    rows = inputs[...].astype(F32).reshape(tokens, width)
    middle = rows + (jnp.dot(placed, weights1[0], preferred_element_type=F32) + bout[...])
    center = jnp.mean(middle, -1, keepdims=True)
    centered = middle - center
    scale = lax.rsqrt(jnp.mean(centered * centered, -1, keepdims=True) + EPSILON)
    unit = centered * scale
    normed = (unit * gain[...] + bias[...]).astype(BF16)
    placed = jnp.dot(normed, order, preferred_element_type=F32).astype(BF16)
    placed_n[...] = placed
    for copy in copies[2:ready1]:
        copy.wait()
    curve = math.sqrt(2.0 / math.pi)
    for q in range(parts):
        lo = q * width
        pre = jnp.dot(placed, weights1[1 + q], preferred_element_type=F32)
        pre = pre + bfc[:, lo : lo + width]
        square = pre * pre
        tanh = jnp.tanh(curve * (pre + 0.044715 * (pre * square)))
        hidden[:, lo : lo + width] = (0.5 * pre * (1.0 + tanh)).astype(BF16)
        slopes[:, lo : lo + width] = 0.5 * (1.0 + tanh) + 0.5 * pre * (1.0 - tanh * tanh) * (
            curve * (1.0 + 3 * 0.044715 * square)
        )
    for copy in copies[ready1:]:
        copy.wait()
    result = middle + bproj[...]
    for q in range(parts):
        lo = q * width
        result += jnp.dot(
            hidden[:, lo : lo + width], weights2[lo : lo + width], preferred_element_type=F32
        )
    outputs[...] = result.astype(BF16).reshape(seq_count, block, width)

    branch = cotangent[...].reshape(tokens, width)
    grad_rows = branch.astype(F32)
    sum_proj[...] = jnp.sum(grad_rows, 0, keepdims=True)
    grad_placed = jnp.zeros((tokens, width), F32)
    for q in range(parts):
        lo = q * width
        grad = contract_last(branch, weights2[lo : lo + width]) * slopes[:, lo : lo + width]
        grad = grad.astype(BF16)
        grad_pre[:, lo : lo + width] = grad
        sum_fc[:, lo : lo + width] = jnp.sum(grad.astype(F32), 0, keepdims=True)
        grad_placed += contract_last(grad, weights1[1 + q])
    high = grad_placed.astype(BF16)
    rest = grad_placed - high.astype(F32)
    mid = rest.astype(BF16)
    low = (rest - mid.astype(F32)).astype(BF16)
    grad_normed = contract_last(high, order) + (contract_last(mid, order) + contract_last(low, order))
    sum_bias[...] = jnp.sum(grad_normed, 0, keepdims=True)
    sum_gain[...] = jnp.sum(grad_normed * unit, 0, keepdims=True)
    grad_unit = grad_normed * gain[...]
    part = jnp.mean(grad_unit, -1, keepdims=True)
    cross = jnp.mean(grad_unit * unit, -1, keepdims=True)
    grad_mid = grad_rows + scale * (grad_unit - part - unit * cross)
    grad_middle[...] = grad_mid
    grad_attn = grad_mid.astype(BF16)
    grad_out[...] = grad_attn
    sum_out[...] = jnp.sum(grad_attn.astype(F32), 0, keepdims=True)
    back = contract_last(grad_attn, weights1[0]).astype(BF16)
    if permuted.shape[1] > width:
        permuted[...] = jnp.zeros_like(permuted)
    permuted[:, :width] = contract_last(back, order).astype(BF16)
    for i in range(seq_count):
        for g in range(groups):
            for part in range(2):
                start = i * block + part * half_block
                grad_blocks[i * groups + g, :, part * group : (part + 1) * group] = permuted[
                    start : start + half_block, g * group : (g + 1) * group
                ]


def middle_block(half1, other1, half2, other2, attended, inputs, cotangent, order, vectors, groups):
    kinds, side, width = half1.shape
    parts = kinds - 1
    chips = half2.shape[0]
    seq_count, block, _ = inputs.shape
    tokens = seq_count * block
    wide = groups * attended.shape[2] // 2

    def shape(*dims, kind=BF16):
        return jax.ShapeDtypeStruct(dims, kind)

    return pl.pallas_call(
        functools.partial(middle_kernel, groups),
        out_shape=[
            shape(seq_count, block, width),
            shape(tokens, width, kind=F32),
            shape(*attended.shape),
            shape(tokens, width),
            shape(tokens, width),
            shape(tokens, parts * width),
            shape(tokens, parts * width),
            shape(tokens, width),
            shape(1, width, kind=F32),
            shape(1, width, kind=F32),
            shape(1, width, kind=F32),
            shape(1, parts * width, kind=F32),
            shape(1, width, kind=F32),
        ],
        in_specs=[ANYWHERE] * 4 + vmem_specs(9),
        out_specs=vmem_specs(13),
        scratch_shapes=[
            pltpu.VMEM((kinds, width, width), BF16),
            pltpu.VMEM((parts * width, width), BF16),
            pltpu.VMEM((tokens, wide), BF16),
            pltpu.VMEM((tokens, parts * width), F32),
            pltpu.VMEM((tokens, wide), BF16),
            pltpu.SemaphoreType.DMA((2 * kinds + 2 * chips,)),
        ],
        compiler_params=pltpu.CompilerParams(vmem_limit_bytes=50 * 2**20),
        cost_estimate=LIGHT,
    )(half1, other1, half2, other2, attended, inputs, cotangent, order, *vectors)


def gradient_kernel(
    shard_rows, placed_a, placed_n, hidden, grad_pre, grad_out, cotangent, send, keep, turned, some
):
    width = placed_a.shape[1]
    side = width // CORES
    parts = hidden.shape[1] // width
    chips = side // shard_rows
    core = lax.rem(lax.axis_index("seq"), CORES)
    branch = cotangent[...].reshape(-1, width)
    if send.shape[0] > 1 + parts:
        for start in range(0, turned.shape[0], width):
            turned[start : start + width, :] = hidden[:, start : start + width].astype(F32).T
        for target, place in ((send, 1 - core), (keep, core)):
            for chip in range(chips):
                for i in range(parts):
                    start = ((chip * CORES + place) * parts + i) * shard_rows
                    start = pl.multiple_of(start, shard_rows)
                    to = i * side + chip * shard_rows
                    some[to : to + shard_rows, :] = turned[pl.ds(start, shard_rows), :]
            for i in range(parts):
                target[1 + parts + i] = jnp.dot(
                    some[i * side : (i + 1) * side, :].astype(BF16),
                    branch,
                    preferred_element_type=F32,
                ).astype(BF16)
    turned_a = placed_a[...].astype(F32).T.astype(BF16)
    turned_n = placed_n[...].astype(F32).T.astype(BF16)
    for target, start in ((send, side), (keep, 0)):
        target[0] = jnp.dot(
            turned_a[start : start + side], grad_out[...], preferred_element_type=F32
        ).astype(BF16)
        for q in range(parts):
            target[1 + q] = jnp.dot(
                turned_n[start : start + side],
                grad_pre[:, q * width : (q + 1) * width],
                preferred_element_type=F32,
            ).astype(BF16)


def weight_gradients(placed_a, placed_n, hidden, grad_pre, grad_out, cotangent, shard_rows):
    tokens, width = placed_a.shape
    parts = hidden.shape[1] // width
    kinds = 1 + parts * (1 if shard_rows % 8 else 2)
    shape = jax.ShapeDtypeStruct((kinds, width // CORES, width), BF16)
    return pl.pallas_call(
        functools.partial(gradient_kernel, shard_rows),
        out_shape=[shape, shape],
        in_specs=vmem_specs(6),
        out_specs=vmem_specs(2),
        scratch_shapes=[
            pltpu.VMEM((parts * width, tokens), F32),
            pltpu.VMEM((parts * width // CORES, tokens), F32),
        ],
        compiler_params=pltpu.CompilerParams(vmem_limit_bytes=50 * 2**20),
        cost_estimate=LIGHT,
    )(placed_a, placed_n, hidden, grad_pre, grad_out, cotangent)


def masked_scores(keys, queries, id_column, id_row, first):
    scores = lax.dot_general(keys, queries, (((1,), (1,)), ((), ())), preferred_element_type=F32)
    key_pos = lax.broadcasted_iota(jnp.int32, scores.shape, 0)
    query_pos = lax.broadcasted_iota(jnp.int32, scores.shape, 1) + first
    allowed = (key_pos <= query_pos) & (id_column == id_row)
    return jnp.where(allowed, scores, MASKED)


def column_of(id_row):
    length = id_row.shape[1]
    return jnp.broadcast_to(id_row, (LANES, length)).T[:, :1]


def forward_kernel(
    seq_count,
    heads,
    head_size,
    step_rows,
    block,
    rows_ref,
    weight,
    gain,
    bias,
    bqv,
    after,
    out,
    stats,
    whole,
    normed,
    ids,
    result,
    qkv_bias,
):
    length = whole.shape[0]
    group = heads * head_size
    width = weight.shape[0]
    index = lax.rem(lax.axis_index("seq"), lax.axis_size("seq") // seq_count)
    qkv_bias[...] = jnp.zeros_like(qkv_bias)
    for lo in range(0, width, group):
        here = index == lo // group
        for base, start in ((0, 0), (width, 2 * group)):
            piece = jnp.where(here, bqv[:, base + lo : base + lo + group], 0.0)
            qkv_bias[:, start : start + group] += piece
    for i in range(length // block):
        rows = norm_affine(rows_ref[i, :block, :].astype(F32), gain[...], bias[...])
        normed[i * block : (i + 1) * block, :] = rows.astype(BF16)
    id_rows = [rows_ref[i, block:, :block].astype(F32)[:1] for i in range(length // block)]
    id_row = jnp.concatenate(id_rows, 1)
    ids[...] = id_row
    id_column = column_of(id_row)
    for first in range(0, length, step_rows):
        last = first + step_rows
        product = jnp.dot(normed[first:last, :], weight[...], preferred_element_type=F32)
        whole[first:last, :] = (product + qkv_bias[...]).astype(BF16)
    values_t = whole[:, 2 * group : 3 * group].astype(F32).T.astype(BF16)
    for first in range(0, length, step_rows):
        last = first + step_rows
        tops = []
        for head in range(heads):
            lo = head * head_size
            queries = whole[first:last, lo : lo + head_size] * BF16(head_size**-0.5)
            keys = whole[:last, group + lo : group + lo + head_size]
            scores = masked_scores(keys, queries, id_column[:last], id_row[:, first:last], first)
            highest = jnp.max(scores, 0, keepdims=True)
            weights = jnp.exp(scores - highest)
            total = jnp.sum(weights, 0, keepdims=True)
            probs = (weights * (1.0 / total)).astype(BF16)
            tops.append(
                jnp.dot(
                    values_t[lo : lo + head_size, :last], probs, preferred_element_type=F32
                )
            )
            stats[head : head + 1, first:last] = highest + jnp.log(total)
        result[first:last, :] = jnp.concatenate(tops, 0).T.astype(BF16)
    half = block // 2
    for start in range(0, length, block):
        out[start // 2 : start // 2 + half, :group] = result[start : start + half, :]
        out[start // 2 : start // 2 + half, group:] = result[start + half : start + block, :]


def backward_kernel(
    heads,
    head_size,
    step_rows,
    block,
    whole,
    grads,
    stats,
    ids,
    after1,
    after2,
    out,
    grad_out,
    grad_query,
    grad_key,
    grad_value,
):
    length = whole.shape[0]
    group = heads * head_size
    half = block // 2
    for start in range(0, length, block):
        packed = grads[start // 2 : start // 2 + half, :]
        grad_out[start : start + half, :] = packed[:, :group]
        grad_out[start + half : start + block, :] = packed[:, group:]
    id_row = ids[...]
    id_column = column_of(id_row)
    keys_t = whole[:, group : 2 * group].astype(F32).T.astype(BF16)
    factor = head_size**-0.5
    grad_key[...] = jnp.zeros_like(grad_key)
    grad_value[...] = jnp.zeros_like(grad_value)
    for first in range(0, length, step_rows):
        last = first + step_rows
        tops = []
        for head in range(heads):
            lo = head * head_size
            queries = whole[first:last, lo : lo + head_size] * BF16(factor)
            keys = whole[:last, group + lo : group + lo + head_size]
            values = whole[:last, 2 * group + lo : 2 * group + lo + head_size]
            grad = grad_out[first:last, lo : lo + head_size]
            scores = masked_scores(keys, queries, id_column[:last], id_row[:, first:last], first)
            probs = jnp.exp(scores - stats[head : head + 1, first:last])
            grad_probs = lax.dot_general(
                values, grad, (((1,), (1,)), ((), ())), preferred_element_type=F32
            )
            delta = jnp.sum(probs * grad_probs, 0, keepdims=True)
            grad_scores = (probs * (grad_probs - delta)).astype(BF16)
            tops.append(
                jnp.dot(
                    keys_t[lo : lo + head_size, :last], grad_scores, preferred_element_type=F32
                )
                * factor
            )
            grad_key[head, :last, :] += jnp.dot(
                grad_scores, queries, preferred_element_type=F32
            )
            grad_value[head, :last, :] += jnp.dot(
                probs.astype(BF16), grad, preferred_element_type=F32
            )
        grad_query[first:last, :] = jnp.concatenate(tops, 0).T.astype(BF16)
    out[:, :group] = grad_query[...]
    for head in range(heads):
        lo = head * head_size
        out[:, group + lo : group + lo + head_size] = grad_key[head].astype(BF16)
        out[:, 2 * group + lo : 2 * group + lo + head_size] = grad_value[head].astype(BF16)


def attend_forward(rows, weight, gain, bias, bqv, after, seq_count, heads, head_size, block):
    length = rows.shape[0] * block
    width = rows.shape[2]
    group = heads * head_size
    return pl.pallas_call(
        functools.partial(forward_kernel, seq_count, heads, head_size, min(256, length), block),
        out_shape=[
            jax.ShapeDtypeStruct((length // 2, 2 * group), BF16),
            jax.ShapeDtypeStruct((heads, length), F32),
            jax.ShapeDtypeStruct((length, 3 * group), BF16),
            jax.ShapeDtypeStruct((length, width), BF16),
            jax.ShapeDtypeStruct((1, length), F32),
        ],
        in_specs=vmem_specs(5) + [ANYWHERE],
        out_specs=vmem_specs(5),
        scratch_shapes=[pltpu.VMEM((length, group), BF16), pltpu.VMEM((1, 3 * group), F32)],
        compiler_params=pltpu.CompilerParams(vmem_limit_bytes=48 * 2**20),
        cost_estimate=LIGHT,
    )(rows, weight, gain, bias, bqv, after)


def attend_backward(whole, grads, stats, ids, after, heads, head_size, block):
    length, width = whole.shape
    group = heads * head_size
    return pl.pallas_call(
        functools.partial(backward_kernel, heads, head_size, min(256, length), block),
        out_shape=jax.ShapeDtypeStruct((length, 3 * group), BF16),
        in_specs=vmem_specs(4) + [ANYWHERE] * 2,
        out_specs=vmem_specs(1)[0],
        scratch_shapes=[
            pltpu.VMEM((length, group), BF16),
            pltpu.VMEM((length, group), BF16),
            pltpu.VMEM((heads, length, head_size), F32),
            pltpu.VMEM((heads, length, head_size), F32),
        ],
        compiler_params=pltpu.CompilerParams(vmem_limit_bytes=48 * 2**20),
        cost_estimate=LIGHT,
    )(whole, grads, stats, ids, *after)


def on_device(
    inputs,
    segments,
    cotangent,
    ln1_gain,
    ln1_bias,
    w_qkv,
    b_qv,
    w_out,
    b_out,
    ln2_gain,
    ln2_bias,
    w_fc,
    b_fc,
    w_proj,
    b_proj,
):
    seq_count, block, width = inputs.shape
    head_size = width // HEADS
    tokens = seq_count * block
    count = lax.axis_size("seq")
    devices = count * lax.axis_size("dp")
    groups = count // seq_count
    heads = -(-HEADS // groups)
    spare = groups * heads - HEADS
    group = heads * head_size

    vectors = (ln1_gain, ln1_bias, b_qv, b_out, ln2_gain, ln2_bias, b_fc, b_proj)
    sizes = tuple(vector.shape[0] for vector in vectors)
    shard_rows = w_out.shape[0] // width
    parts = w_fc.shape[0] // w_out.shape[0]
    classes = groups // CORES
    chips = devices // CORES
    place = lax.axis_index("seq")
    core = place % CORES
    group_index = place % groups

    columns, blocks = first_blocks(
        w_qkv.reshape(shard_rows, 3 * width),
        inputs,
        segments,
        [vector.reshape(1, -1) for vector in vectors],
        classes,
        group,
    )
    tower_a = build_line(gather_columns(columns))
    stacked = stack_weights(w_out.reshape(-1, width), w_fc.reshape(-1, parts * width), columns)
    low1, high1 = build_tower(z_pieces(stacked), 1, [tower_a])
    lines, sequence = gather_sequence(gate(blocks, tower_a), low1)
    if lax.axis_size("dp") == 4:
        towers = [tower_a] + [swap_dp(tower_a, mask) for mask in range(1, 4)]
    else:
        towers = [lax.all_gather(tower_a, "dp", axis=0, tiled=True)]
    keep_a, send_a = split_halves(towers, [low1, lines])
    wqkv, gain1, bias1, bqv, bout, gain2, bias2, bfc, bproj = unpack_first(
        keep_a, swap_core(send_a), sizes
    )

    steps = []

    def attend(*after):
        raw, *rest = attend_forward(
            sequence, wqkv, gain1, bias1, bqv, after[0], seq_count, heads, head_size, block
        )
        steps.extend([raw, exchange(raw.reshape(count, block // 2, 2 * group)), rest])
        return steps[1]

    half1 = gather_plane(low1, high1, 1, attend, None).reshape(1 + parts, -1, width)
    raw, attended, (stats, qkv, normed1, ids) = steps
    pieces2 = z_pieces(gate(w_proj.reshape(-1, width), lines))
    low2, high2 = build_tower(pieces2, 0, [raw])
    half2 = gather_plane(low2, high2, 0, lambda *_: attended, attended)
    other1 = swap_core(half1)
    other2 = swap_core(half2)
    aligned = half2.shape[1] % 16 == 0
    if not aligned:
        half2 = ordered(core, half2, other2, 1).reshape(1, parts * width, width)

    spot = jnp.arange(width, dtype=jnp.int32)
    side = width // CORES
    own_core = (core + spot // side) % CORES
    order = (spot % side // shard_rows * CORES + own_core) * shard_rows + spot % shard_rows
    (
        outputs,
        grad_middle,
        grad_blocks,
        placed_a,
        placed_n,
        hidden,
        grad_pre,
        grad_out,
        grad_bout,
        grad_gain2,
        grad_bias2,
        grad_bfc,
        grad_bproj,
    ) = middle_block(
        half1,
        other1,
        half2,
        other2,
        attended,
        inputs,
        cotangent,
        order.reshape(1, width),
        (bout, gain2, bias2, bfc, bproj),
        groups,
    )
    grad_blocks = exchange(grad_blocks).reshape(-1, 2 * group)
    send_b, keep_b = weight_gradients(
        placed_a, placed_n, hidden, grad_pre, grad_out, cotangent, shard_rows
    )
    if send_b.shape[0] == 1 + parts:
        grad_wproj = lax.dot_general(
            hidden,
            cotangent.reshape(tokens, width),
            (((0,), (0,)), ((), ())),
            preferred_element_type=F32,
        )
        grad_wproj = grad_wproj.astype(BF16).reshape(chips, CORES, parts, shard_rows, width)
        grad_wproj = grad_wproj.transpose(1, 2, 0, 3, 4).reshape(CORES, parts, -1, width)
        send_b = jnp.concatenate([send_b, pick(grad_wproj, 1 - core, 0)], 0)
        keep_b = jnp.concatenate([keep_b, pick(grad_wproj, core, 0)], 0)
    sum_b = add(keep_b, swap_core(send_b)).reshape(-1, chips, shard_rows, width)
    steps = []

    def between(*after):
        if steps:
            steps.append(after)
        else:
            steps.append(
                attend_backward(qkv, grad_blocks, stats, ids, after, heads, head_size, block)
            )
        return steps[0]

    tower_b = scatter_plane(sum_b, 1, between)
    own_b = scatter_z(tower_b, 1)
    grad_qkv, first_sums = steps

    def blocks_of(value, rows):
        return value.astype(BF16).reshape(chips, CORES, rows, -1)

    rows = inputs.astype(F32).reshape(tokens, width)
    grad_normed1 = lax.dot_general(
        grad_qkv, wqkv, (((1,), (1,)), ((), ())), preferred_element_type=F32
    )
    own_normed1 = scatter_sequence(
        grad_normed1.astype(BF16).reshape(count, block, width), first_sums[0], tower_b, own_b
    )
    _, norm1_back = jax.vjp(lambda value: norm_affine(value, gain1, bias1), rows)
    (grad_in_part,) = norm1_back(own_normed1.astype(F32).reshape(tokens, width))
    grad_inputs = (grad_middle + grad_in_part).astype(BF16).reshape(inputs.shape)

    grad_qkv = gate(grad_qkv, *first_sums)
    long_rows = sequence[:, :block].astype(F32).reshape(count * block, width)
    _, norm1_long_back = jax.vjp(lambda g, b: norm_affine(long_rows, g, b), gain1, bias1)
    grad_gain1, grad_bias1 = norm1_long_back(grad_normed1)
    grad_wqkv = lax.dot_general(
        normed1, grad_qkv, (((0,), (0,)), ((), ())), preferred_element_type=F32
    )
    sums = jnp.sum(grad_qkv, 0, dtype=F32).reshape(3, group)
    here = (jnp.arange(groups) == group_index)[None, :, None]
    grad_bqv = jnp.where(here, jnp.stack([sums[0], sums[2]])[:, None], 0.0)
    grad_bqv = grad_bqv.reshape(2, groups * heads, head_size)[:, :HEADS]
    grads = (
        grad_gain1,
        grad_bias1,
        grad_bqv,
        grad_bout,
        grad_gain2,
        grad_bias2,
        grad_bfc,
        grad_bproj,
    )
    small_grads = pack_small([grad.reshape(1, -1) for grad in grads], sizes, devices)
    small_grads = jnp.pad(small_grads, ((0, 0), (0, 0), (0, 3 * group - LANES)))
    block_a = jnp.concatenate(
        [blocks_of(grad_wqkv, shard_rows), small_grads.reshape(chips, CORES, ROWS, -1)], 2
    )
    send_a, keep_a = pick(block_a, 1 - core, 1), pick(block_a, core, 1)
    got_a = swap_core(send_a)
    pair_a = jnp.concatenate(
        [jnp.where(core == 0, keep_a, got_a), jnp.where(core == 0, got_a, keep_a)], -1
    )
    tower_a = scatter_plane_direct(pair_a, tower_b)
    own_qkv, own_small = finish_columns(scatter_columns(tower_a), width, group, own_b)
    own = [own_small[i, :size] for i, size in enumerate(sizes)]
    own_qkv = own_qkv.reshape(-1)
    return (
        outputs,
        grad_inputs,
        own[0],
        own[1],
        own_qkv,
        own[2],
        own_b[0].reshape(-1),
        own[3],
        own[4],
        own[5],
        own_b[1 : 1 + parts].transpose(1, 0, 2).reshape(-1),
        own[6],
        own_b[1 + parts :].reshape(-1),
        own[7],
    )


def solution(mesh):
    token_spec = P("dp", "seq", None)
    flat_spec = P(("dp", "seq"))
    in_specs = (token_spec, P("dp", "seq"), token_spec) + (flat_spec,) * 12
    out_specs = (token_spec, token_spec) + (flat_spec,) * 12
    return jax.shard_map(
        on_device, mesh=mesh, in_specs=in_specs, out_specs=out_specs, check_vma=False
    )
```

```python
import functools
import math

import jax
import jax.numpy as jnp
from jax import lax
from jax.experimental import pallas as pl
from jax.experimental.pallas import tpu as pltpu
from jax.sharding import PartitionSpec as P

HEADS = 12
CORES = 2


EPSILON = 1e-05
MASKED = -1e30
F32 = jnp.float32
BF16 = jnp.bfloat16


def norm_affine(values, gain, bias):
    center = jnp.mean(values, -1, keepdims=True)
    centered = values - center
    variance = jnp.mean(centered * centered, -1, keepdims=True)
    return centered * lax.rsqrt(variance + EPSILON) * gain + bias


ANYWHERE = pl.BlockSpec(memory_space=pl.ANY)
LIGHT = pl.CostEstimate(flops=1, bytes_accessed=1, transcendentals=0)


def shift_z(value, step):
    size = lax.axis_size("seq")
    return lax.ppermute(value, "seq", [(i, (i + CORES * step) % size) for i in range(size)])


def swap_core(value):
    size = lax.axis_size("seq")
    return lax.ppermute(value, "seq", [(i, i ^ 1) for i in range(size)])


def swap_dp(value, bit):
    size = lax.axis_size("dp")
    return lax.ppermute(value, "dp", [(i, i ^ bit) for i in range(size)])


def ordered(flag, mine, other, axis):
    first = jnp.where(flag == 0, mine, other)
    second = jnp.where(flag == 0, other, mine)
    return jnp.stack([first, second], axis)


def roll_blocks(pieces, place):
    count = len(pieces)
    stacked = jnp.stack(pieces)
    twice = jnp.concatenate([stacked, stacked])
    return lax.dynamic_slice_in_dim(twice, lax.rem(count - place, count), count, 0)


def z_pieces(shard):
    heights = lax.axis_size("seq") // CORES
    return [shard] + [shift_z(shard, -step) for step in range(1, heights)]


def swap_z(value, bit):
    size = lax.axis_size("seq")
    return lax.ppermute(value, "seq", [(i, i ^ (CORES * bit)) for i in range(size)])


def gather_plane(low, high, axis, first=None, second=None):
    def move(value, bit, after):
        moved = swap_dp(value, bit)
        return moved if after is None else gate(moved, after)

    if lax.axis_size("dp") == 4:
        plane = lax.axis_index("dp")
        y, x = plane // 2, plane % 2
        low_x = ordered(x, low, move(low, 1, first), axis)
        high_y = ordered(y, high, move(high, 2, first), axis)
        low_all = ordered(y, low_x, move(low_x, 2, second), axis)
        high_all = ordered(x, high_y, move(high_y, 1, second), axis + 1)
        half = jnp.concatenate([low_all, high_all], axis + 2)
        count = 4 * half.shape[axis + 2]
    else:
        tower = jnp.concatenate([low, high], axis)
        half = lax.all_gather(tower, "dp", axis=axis, tiled=True)
        return half
    return half.reshape(*low.shape[:axis], count, *low.shape[axis + 1 :])


def pick(value, index, axis):
    return lax.dynamic_index_in_dim(value, index, axis, keepdims=False)


def add(mine, other):
    return (mine.astype(F32) + other.astype(F32)).astype(mine.dtype)


def scatter_plane(split, axis, between=None):
    planes = lax.axis_size("dp")
    heights = lax.axis_size("seq") // CORES
    if planes != 4:
        if between is not None:
            between(split, split)
            between(split, split)
        return lax.psum_scatter(split, "dp", scatter_dimension=axis, tiled=True)
    plane = lax.axis_index("dp")
    y, x = plane // 2, plane % 2
    split = split.reshape(*split.shape[:axis], 2, 2, heights, *split.shape[axis + 1 :])
    low = lax.slice_in_dim(split, 0, heights // 2, axis=axis + 2)
    high = lax.slice_in_dim(split, heights // 2, heights, axis=axis + 2)
    low_send, high_send = pick(low, 1 - y, axis), pick(high, 1 - x, axis + 1)
    low_got, high_got = swap_dp(low_send, 2), swap_dp(high_send, 1)
    if between is not None:
        after = between(low_send, high_send)
        low_got, high_got = gate_both(low_got, high_got, after)
    low = add(pick(low, y, axis), low_got)
    high = add(pick(high, x, axis + 1), high_got)
    if between is not None:
        between(low, high)
    low = add(pick(low, x, axis), swap_dp(pick(low, 1 - x, axis), 1))
    high = add(pick(high, y, axis), swap_dp(pick(high, 1 - y, axis), 2))
    return jnp.concatenate([low, high], axis)


def scatter_z(tower, axis):
    heights = lax.axis_size("seq") // CORES
    level = lax.axis_index("seq") // CORES
    mine = pick(tower, level, axis).astype(F32)
    for step in range(1, heights):
        mine += shift_z(pick(tower, lax.rem(level + step, heights), axis), step).astype(F32)
    return mine


def z_bits():
    heights = lax.axis_size("seq") // CORES
    level = lax.axis_index("seq") // CORES
    top = heights // 2
    return level, top, level // top


def gather_sequence(blocks, after):
    level, top, half = z_bits()
    core = lax.axis_index("seq") % CORES
    got = gate(swap_z(pick(blocks, 1 - half, 0), top), after)
    held = ordered(half, pick(blocks, half, 0), got, 0)
    axis, bit = 1, top // 2
    while bit:
        held = ordered(level // bit % 2, held, swap_z(held, bit), axis)
        axis, bit = axis + 1, bit // 2
    return held, ordered(core, held, swap_core(held), axis).reshape(-1, *blocks.shape[1:])


def scatter_sequence(partial, after):
    level, top, half = z_bits()
    core = lax.axis_index("seq") % CORES
    shape = partial.shape[1:]
    count = top.bit_length()
    held = partial.reshape(*[2] * (count + 1), *shape)
    got = gate(swap_core(pick(held, 1 - core, count)), after)
    held = add(pick(held, core, count), got)
    axis, bit = count - 1, 1
    while bit < top:
        flag = level // bit % 2
        got = swap_z(pick(held, 1 - flag, axis), bit)
        held = add(pick(held, flag, axis), got)
        axis, bit = axis - 1, bit * 2
    return ordered(half, pick(held, half, 0), swap_z(pick(held, 1 - half, 0), top), 0)


def class_of(level):
    return level % (lax.axis_size("seq") // CORES // 2)


def gather_columns(blocks):
    heights = lax.axis_size("seq") // CORES
    level = lax.axis_index("seq") // CORES
    moved = [
        swap_z(pick(blocks, class_of(level ^ mask), 0), mask) for mask in range(1, heights)
    ]
    return [pick(blocks, class_of(level), 0)] + moved


def scatter_columns(tower):
    heights = tower.shape[0]
    level = lax.axis_index("seq") // CORES
    moved = [swap_z(pick(tower, level ^ mask, 0), mask) for mask in range(1, heights)]
    return [pick(tower, level, 0)] + moved


def scatter_plane_direct(split, after):
    planes = lax.axis_size("dp")
    if planes != 4:
        return lax.psum_scatter(split, "dp", scatter_dimension=0, tiled=True)
    plane = lax.axis_index("dp")
    split = split.reshape(planes, -1, *split.shape[1:])
    total = pick(split, plane, 0).astype(F32)
    for mask in range(1, planes):
        total += gate(swap_dp(pick(split, plane ^ mask, 0), mask), after).astype(F32)
    return total.astype(split.dtype)


def exchange(blocks):
    return lax.all_to_all(blocks, "seq", split_axis=0, concat_axis=0, tiled=True)


ROWS = 8
LANES = 128


def vmem_specs(count):
    return [pl.BlockSpec(memory_space=pltpu.VMEM) for _ in range(count)]


def place_lanes(size, total):
    source = lax.broadcasted_iota(jnp.int32, (LANES, total), 0)
    target = lax.rem(lax.broadcasted_iota(jnp.int32, (LANES, total), 1), size)
    return jnp.where(source == target, 1.0, 0.0).astype(BF16)


def owned_lanes(devices, size):
    device = lax.broadcasted_iota(jnp.int32, (devices, devices * size), 0)
    lane = lax.broadcasted_iota(jnp.int32, (devices, devices * size), 1)
    offset = lane - device * size
    return (offset >= 0) & (offset < size)


def line_kernel(count, *refs):
    pieces, tower = refs[:count], refs[-1]
    level = lax.axis_index("seq") // CORES
    for mask, piece in enumerate(pieces):
        tower[level ^ mask] = piece[...]


def build_line(pieces, after):
    return pl.pallas_call(
        functools.partial(line_kernel, len(pieces)),
        out_shape=jax.ShapeDtypeStruct((len(pieces), *pieces[0].shape), BF16),
        in_specs=vmem_specs(len(pieces)) + [ANYWHERE],
        out_specs=vmem_specs(1)[0],
        cost_estimate=LIGHT,
    )(*pieces, after)


def halves_kernel(count, *refs):
    towers, (keep, send) = refs[:count], refs[-2:]
    heights, _, columns = towers[0].shape
    half = columns // CORES
    core = lax.rem(lax.axis_index("seq"), CORES)
    plane = lax.axis_index("dp")
    for own in range(CORES):

        @pl.when(core == own)
        def _():
            for mask, tower in enumerate(towers):
                base = (plane ^ mask) * heights if count > 1 else 0
                for i in range(heights):
                    line = tower[i]
                    keep[base + i] = line[:, own * half : (own + 1) * half]
                    send[base + i] = line[:, (1 - own) * half : (2 - own) * half]


def split_halves(towers, after):
    heights, rows, columns = towers[0].shape
    shape = jax.ShapeDtypeStruct((len(towers) * heights, rows, columns // CORES), BF16)
    return pl.pallas_call(
        functools.partial(halves_kernel, len(towers)),
        out_shape=[shape, shape],
        in_specs=vmem_specs(len(towers)) + [ANYWHERE] * len(after),
        out_specs=vmem_specs(2),
        compiler_params=pltpu.CompilerParams(vmem_limit_bytes=40 * 2**20),
        cost_estimate=LIGHT,
    )(*towers, *after)


def finish_kernel(count, group, *refs):
    pieces, (weight, small) = refs[:count], refs[-2:]
    shard, width = weight.shape[0], weight.shape[1] // 3
    heights = count
    level = lax.axis_index("seq") // CORES
    terms = [piece[...].astype(F32) for piece in pieces]
    small_sum = jnp.zeros((ROWS, LANES), F32)
    for kind in range(heights // 2):
        total = jnp.zeros_like(terms[0])
        for mask, term in enumerate(terms):
            total += jnp.where(lax.rem(level ^ mask, heights // 2) == kind, term, 0.0)
        for core in range(CORES):
            start = core * 3 * group
            small_sum += total[shard:, start : start + LANES]
            lo = (kind * CORES + core) * group
            for part in range(3 if lo < width else 0):
                at = start + part * group
                weight[:, part * width + lo : part * width + lo + group] = total[
                    :shard, at : at + group
                ]
    small[...] = small_sum


def finish_columns(pieces, width, group, after):
    rows = pieces[0].shape[0]
    return pl.pallas_call(
        functools.partial(finish_kernel, len(pieces), group),
        out_shape=[
            jax.ShapeDtypeStruct((rows - ROWS, 3 * width), F32),
            jax.ShapeDtypeStruct((ROWS, LANES), F32),
        ],
        in_specs=vmem_specs(len(pieces)) + [ANYWHERE],
        out_specs=vmem_specs(2),
        cost_estimate=LIGHT,
    )(*pieces, after)


def unpack_kernel(sizes, keep, got, weight, *refs):
    outs, (lines, small) = refs[:-2], refs[-2:]
    chips, rows = keep.shape[:2]
    shard = rows - ROWS
    core = lax.rem(lax.axis_index("seq"), CORES)
    for own in range(CORES):

        @pl.when(core == own)
        def _():
            for source, place in ((keep, own), (got, 1 - own)):
                for chip in range(chips):
                    device = chip * CORES + place
                    line = source[chip].astype(F32)
                    lines[device * shard : (device + 1) * shard, :] = line[:shard]
                    small[device] = line[shard:, :LANES]

    weight[...] = lines[...].astype(BF16)
    devices = chips * CORES
    for i, (size, out) in enumerate(zip(sizes, outs)):
        spread = jnp.dot(
            small[:, i, :].astype(BF16),
            place_lanes(size, devices * size),
            preferred_element_type=F32,
        )
        out[...] = jnp.sum(jnp.where(owned_lanes(devices, size), spread, 0.0), 0, keepdims=True)


def unpack_first(keep, got, sizes):
    chips, rows, columns = keep.shape
    devices = chips * CORES
    width = devices * (rows - ROWS)
    return pl.pallas_call(
        functools.partial(unpack_kernel, sizes),
        out_shape=[jax.ShapeDtypeStruct((width, columns), BF16)]
        + [jax.ShapeDtypeStruct((1, devices * size), F32) for size in sizes],
        in_specs=vmem_specs(2),
        out_specs=vmem_specs(1 + len(sizes)),
        scratch_shapes=[
            pltpu.VMEM((width, columns), F32),
            pltpu.VMEM((devices, ROWS, LANES), F32),
        ],
        compiler_params=pltpu.CompilerParams(vmem_limit_bytes=40 * 2**20),
        cost_estimate=LIGHT,
    )(keep, got)


def pack_kernel(sizes, *refs):
    grads, packed, rows = refs[: len(sizes)], refs[len(sizes)], refs[len(sizes) + 1]
    devices = packed.shape[0]
    for i, (size, grad) in enumerate(zip(sizes, grads)):
        owned = jnp.where(owned_lanes(devices, size), grad[...], 0.0).astype(BF16)
        rows[:, i, :] = lax.dot_general(
            owned,
            place_lanes(size, devices * size),
            (((1,), (1,)), ((), ())),
            preferred_element_type=F32,
        )
    packed[...] = rows[...].astype(BF16)


def pack_small(grads, sizes, devices):
    return pl.pallas_call(
        functools.partial(pack_kernel, sizes),
        out_shape=jax.ShapeDtypeStruct((devices, ROWS, LANES), BF16),
        in_specs=vmem_specs(len(sizes)),
        out_specs=vmem_specs(1)[0],
        scratch_shapes=[pltpu.VMEM((devices, ROWS, LANES), F32)],
        compiler_params=pltpu.CompilerParams(vmem_limit_bytes=32 * 2**20),
        cost_estimate=LIGHT,
    )(*grads)


def gate(value, *after):
    def kernel(*refs):
        pass

    return pl.pallas_call(
        kernel,
        out_shape=jax.ShapeDtypeStruct(value.shape, value.dtype),
        in_specs=[ANYWHERE] * (1 + len(after)),
        out_specs=ANYWHERE,
        input_output_aliases={0: 0},
        cost_estimate=LIGHT,
    )(value, *after)


def gate_both(one, two, *after):
    def kernel(*refs):
        pass

    return pl.pallas_call(
        kernel,
        out_shape=[jax.ShapeDtypeStruct(value.shape, value.dtype) for value in (one, two)],
        in_specs=[ANYWHERE] * (2 + len(after)),
        out_specs=[ANYWHERE] * 2,
        input_output_aliases={0: 0, 1: 1},
        cost_estimate=LIGHT,
    )(one, two, *after)


def first_kernel(group, weight, rows, marks, *refs):
    vectors, (columns, blocks, lines, extra) = refs[:-4], refs[-4:]
    classes, _, width_pair = columns.shape
    shard_rows, width = weight.shape[0], weight.shape[1] // 3
    lines[...] = jnp.zeros_like(lines)
    for i, vector in enumerate(vectors):
        for start in range(0, width_pair, 3 * group):
            at = shard_rows + i
            lines[at : at + 1, start : start + vector.shape[1]] = vector[...].astype(F32)
    for kind in range(classes):
        for core in range(CORES):
            lo = (kind * CORES + core) * group
            for part in range(3):
                start = (core * 3 + part) * group
                if lo < width:
                    piece = weight[:, part * width + lo : part * width + lo + group].astype(F32)
                else:
                    piece = jnp.zeros((shard_rows, group), F32)
                lines[:shard_rows, start : start + group] = piece
        columns[kind] = lines[...].astype(BF16)
    block = rows.shape[1]
    extra[...] = jnp.zeros_like(extra)
    for i in range(rows.shape[0]):
        blocks[i, :block, :] = rows[i]
        extra[:1, :block] = marks[i : i + 1, :].astype(F32)
        blocks[i, block:, :] = extra[...].astype(BF16)


def first_blocks(weight, rows, marks, vectors, classes, group):
    shard_rows = weight.shape[0]
    count, block, width = rows.shape
    return pl.pallas_call(
        functools.partial(first_kernel, group),
        out_shape=[
            jax.ShapeDtypeStruct((classes, shard_rows + ROWS, CORES * 3 * group), BF16),
            jax.ShapeDtypeStruct((count, block + 16, width), BF16),
        ],
        in_specs=vmem_specs(3 + len(vectors)),
        out_specs=vmem_specs(2),
        scratch_shapes=[
            pltpu.VMEM((shard_rows + ROWS, CORES * 3 * group), F32),
            pltpu.VMEM((16, width), F32),
        ],
    )(weight, rows, marks, *vectors)


def stack_kernel(out_ref, fc_ref, after, stacked):
    width = out_ref.shape[1]
    stacked[0] = out_ref[...]
    for i in range(fc_ref.shape[1] // width):
        stacked[1 + i] = fc_ref[:, i * width : (i + 1) * width]


def stack_weights(w_out, w_fc, after):
    rows, width = w_out.shape
    return pl.pallas_call(
        stack_kernel,
        out_shape=jax.ShapeDtypeStruct((1 + w_fc.shape[1] // width, rows, width), BF16),
        in_specs=vmem_specs(2) + [ANYWHERE],
        out_specs=vmem_specs(1)[0],
        cost_estimate=LIGHT,
    )(w_out, w_fc, after)


def tower_kernel(axis, count, *refs):
    pieces, low, high = refs[:count], refs[-2], refs[-1]
    level = lax.axis_index("seq") // CORES
    for step, piece in enumerate(pieces):
        place = lax.rem(level + step, count)
        for half, start in ((low, 0), (high, count // 2)):

            @pl.when((place >= start) & (place < start + count // 2))
            def _():
                if axis == 1:
                    half[:, place - start] = piece[...]
                else:
                    half[place - start] = piece[...]


def build_tower(pieces, axis, after):
    count = len(pieces)
    shape = pieces[0].shape
    shape = (*shape[:axis], count // 2, *shape[axis:])
    return pl.pallas_call(
        functools.partial(tower_kernel, axis, count),
        out_shape=[jax.ShapeDtypeStruct(shape, BF16)] * 2,
        in_specs=vmem_specs(count) + [ANYWHERE] * len(after),
        out_specs=vmem_specs(2),
        compiler_params=pltpu.CompilerParams(vmem_limit_bytes=32 * 2**20),
        cost_estimate=LIGHT,
    )(*pieces, *after)


def one_hot_order(order_ref):
    width = order_ref.shape[1]
    features = lax.broadcasted_iota(jnp.int32, (width, width), 0)
    return jnp.where(features == order_ref[...], 1.0, 0.0).astype(BF16)


def contract_last(left, right):
    return lax.dot_general(left, right, (((1,), (1,)), ((), ())), preferred_element_type=F32)


def middle_kernel(
    groups,
    half1,
    other1,
    half2,
    other2,
    attended,
    inputs,
    cotangent,
    order_ref,
    bout,
    gain,
    bias,
    bfc,
    bproj,
    outputs,
    grad_middle,
    grad_blocks,
    placed_a,
    placed_n,
    hidden,
    grad_pre,
    grad_out,
    sum_out,
    sum_gain,
    sum_bias,
    sum_fc,
    sum_proj,
    weights1,
    weights2,
    attended_rows,
    slopes,
    permuted,
    sems,
):
    parts = weights1.shape[0] - 1
    width = weights1.shape[2]
    side = width // CORES
    seq_count, block, _ = inputs.shape
    tokens = seq_count * block
    core = lax.rem(lax.axis_index("seq"), CORES)
    chips, rows2 = half2.shape[:2]
    copies = []
    for kind in range(parts + 1):
        for index, source in enumerate((half1, other1)):
            copies.append(
                pltpu.make_async_copy(
                    source.at[kind],
                    weights1.at[kind, pl.ds(index * side, side)],
                    sems.at[len(copies)],
                )
            )
    ready1 = len(copies)
    if chips == 1:
        copies.append(pltpu.make_async_copy(half2.at[0], weights2, sems.at[len(copies)]))
    for index, source in enumerate((half2, other2) if chips > 1 else ()):
        place = core if index == 0 else 1 - core
        for chip in range(chips):
            start = pl.multiple_of((chip * CORES + place) * rows2, rows2)
            copies.append(
                pltpu.make_async_copy(
                    source.at[chip], weights2.at[pl.ds(start, rows2)], sems.at[len(copies)]
                )
            )
    for copy in copies:
        copy.start()
    order = one_hot_order(order_ref)

    half_block = block // 2
    group = attended.shape[2] // 2
    for i in range(seq_count):
        for g in range(groups):
            for part in range(2):
                start = i * block + part * half_block
                attended_rows[start : start + half_block, g * group : (g + 1) * group] = attended[
                    i * groups + g, :, part * group : (part + 1) * group
                ]
    placed = jnp.dot(attended_rows[:, :width], order, preferred_element_type=F32).astype(BF16)
    placed_a[...] = placed
    for copy in copies[:2]:
        copy.wait()
    rows = inputs[...].astype(F32).reshape(tokens, width)
    middle = rows + (jnp.dot(placed, weights1[0], preferred_element_type=F32) + bout[...])
    center = jnp.mean(middle, -1, keepdims=True)
    centered = middle - center
    scale = lax.rsqrt(jnp.mean(centered * centered, -1, keepdims=True) + EPSILON)
    unit = centered * scale
    normed = (unit * gain[...] + bias[...]).astype(BF16)
    placed = jnp.dot(normed, order, preferred_element_type=F32).astype(BF16)
    placed_n[...] = placed
    for copy in copies[2:ready1]:
        copy.wait()
    curve = math.sqrt(2.0 / math.pi)
    for q in range(parts):
        lo = q * width
        pre = jnp.dot(placed, weights1[1 + q], preferred_element_type=F32)
        pre = pre + bfc[:, lo : lo + width]
        square = pre * pre
        tanh = jnp.tanh(curve * (pre + 0.044715 * (pre * square)))
        hidden[:, lo : lo + width] = (0.5 * pre * (1.0 + tanh)).astype(BF16)
        slopes[:, lo : lo + width] = 0.5 * (1.0 + tanh) + 0.5 * pre * (1.0 - tanh * tanh) * (
            curve * (1.0 + 3 * 0.044715 * square)
        )
    for copy in copies[ready1:]:
        copy.wait()
    result = middle + bproj[...]
    for q in range(parts):
        lo = q * width
        result += jnp.dot(
            hidden[:, lo : lo + width], weights2[lo : lo + width], preferred_element_type=F32
        )
    outputs[...] = result.astype(BF16).reshape(seq_count, block, width)

    branch = cotangent[...].reshape(tokens, width)
    grad_rows = branch.astype(F32)
    sum_proj[...] = jnp.sum(grad_rows, 0, keepdims=True)
    grad_placed = jnp.zeros((tokens, width), F32)
    for q in range(parts):
        lo = q * width
        grad = contract_last(branch, weights2[lo : lo + width]) * slopes[:, lo : lo + width]
        grad = grad.astype(BF16)
        grad_pre[:, lo : lo + width] = grad
        sum_fc[:, lo : lo + width] = jnp.sum(grad.astype(F32), 0, keepdims=True)
        grad_placed += contract_last(grad, weights1[1 + q])
    high = grad_placed.astype(BF16)
    rest = grad_placed - high.astype(F32)
    mid = rest.astype(BF16)
    low = (rest - mid.astype(F32)).astype(BF16)
    grad_normed = contract_last(high, order) + (contract_last(mid, order) + contract_last(low, order))
    sum_bias[...] = jnp.sum(grad_normed, 0, keepdims=True)
    sum_gain[...] = jnp.sum(grad_normed * unit, 0, keepdims=True)
    grad_unit = grad_normed * gain[...]
    part = jnp.mean(grad_unit, -1, keepdims=True)
    cross = jnp.mean(grad_unit * unit, -1, keepdims=True)
    grad_mid = grad_rows + scale * (grad_unit - part - unit * cross)
    grad_middle[...] = grad_mid
    grad_attn = grad_mid.astype(BF16)
    grad_out[...] = grad_attn
    sum_out[...] = jnp.sum(grad_attn.astype(F32), 0, keepdims=True)
    back = contract_last(grad_attn, weights1[0]).astype(BF16)
    if permuted.shape[1] > width:
        permuted[...] = jnp.zeros_like(permuted)
    permuted[:, :width] = contract_last(back, order).astype(BF16)
    for i in range(seq_count):
        for g in range(groups):
            for part in range(2):
                start = i * block + part * half_block
                grad_blocks[i * groups + g, :, part * group : (part + 1) * group] = permuted[
                    start : start + half_block, g * group : (g + 1) * group
                ]


def middle_block(half1, other1, half2, other2, attended, inputs, cotangent, order, vectors, groups):
    kinds, side, width = half1.shape
    parts = kinds - 1
    chips = half2.shape[0]
    seq_count, block, _ = inputs.shape
    tokens = seq_count * block
    wide = groups * attended.shape[2] // 2

    def shape(*dims, kind=BF16):
        return jax.ShapeDtypeStruct(dims, kind)

    return pl.pallas_call(
        functools.partial(middle_kernel, groups),
        out_shape=[
            shape(seq_count, block, width),
            shape(tokens, width, kind=F32),
            shape(*attended.shape),
            shape(tokens, width),
            shape(tokens, width),
            shape(tokens, parts * width),
            shape(tokens, parts * width),
            shape(tokens, width),
            shape(1, width, kind=F32),
            shape(1, width, kind=F32),
            shape(1, width, kind=F32),
            shape(1, parts * width, kind=F32),
            shape(1, width, kind=F32),
        ],
        in_specs=[ANYWHERE] * 4 + vmem_specs(9),
        out_specs=vmem_specs(13),
        scratch_shapes=[
            pltpu.VMEM((kinds, width, width), BF16),
            pltpu.VMEM((parts * width, width), BF16),
            pltpu.VMEM((tokens, wide), BF16),
            pltpu.VMEM((tokens, parts * width), F32),
            pltpu.VMEM((tokens, wide), BF16),
            pltpu.SemaphoreType.DMA((2 * kinds + 2 * chips,)),
        ],
        compiler_params=pltpu.CompilerParams(vmem_limit_bytes=50 * 2**20),
        cost_estimate=LIGHT,
    )(half1, other1, half2, other2, attended, inputs, cotangent, order, *vectors)


def gradient_kernel(
    shard_rows, placed_a, placed_n, hidden, grad_pre, grad_out, cotangent, send, keep, turned, some
):
    width = placed_a.shape[1]
    side = width // CORES
    parts = hidden.shape[1] // width
    chips = side // shard_rows
    core = lax.rem(lax.axis_index("seq"), CORES)
    branch = cotangent[...].reshape(-1, width)
    if send.shape[0] > 1 + parts:
        for start in range(0, turned.shape[0], width):
            turned[start : start + width, :] = hidden[:, start : start + width].astype(F32).T
        for target, place in ((send, 1 - core), (keep, core)):
            for chip in range(chips):
                for i in range(parts):
                    start = ((chip * CORES + place) * parts + i) * shard_rows
                    start = pl.multiple_of(start, shard_rows)
                    to = i * side + chip * shard_rows
                    some[to : to + shard_rows, :] = turned[pl.ds(start, shard_rows), :]
            for i in range(parts):
                target[1 + parts + i] = jnp.dot(
                    some[i * side : (i + 1) * side, :].astype(BF16),
                    branch,
                    preferred_element_type=F32,
                ).astype(BF16)
    turned_a = placed_a[...].astype(F32).T.astype(BF16)
    turned_n = placed_n[...].astype(F32).T.astype(BF16)
    for target, start in ((send, side), (keep, 0)):
        target[0] = jnp.dot(
            turned_a[start : start + side], grad_out[...], preferred_element_type=F32
        ).astype(BF16)
        for q in range(parts):
            target[1 + q] = jnp.dot(
                turned_n[start : start + side],
                grad_pre[:, q * width : (q + 1) * width],
                preferred_element_type=F32,
            ).astype(BF16)


def weight_gradients(placed_a, placed_n, hidden, grad_pre, grad_out, cotangent, shard_rows):
    tokens, width = placed_a.shape
    parts = hidden.shape[1] // width
    kinds = 1 + parts * (1 if shard_rows % 8 else 2)
    shape = jax.ShapeDtypeStruct((kinds, width // CORES, width), BF16)
    return pl.pallas_call(
        functools.partial(gradient_kernel, shard_rows),
        out_shape=[shape, shape],
        in_specs=vmem_specs(6),
        out_specs=vmem_specs(2),
        scratch_shapes=[
            pltpu.VMEM((parts * width, tokens), F32),
            pltpu.VMEM((parts * width // CORES, tokens), F32),
        ],
        compiler_params=pltpu.CompilerParams(vmem_limit_bytes=50 * 2**20),
        cost_estimate=LIGHT,
    )(placed_a, placed_n, hidden, grad_pre, grad_out, cotangent)


def masked_scores(keys, queries, id_column, id_row, first):
    scores = lax.dot_general(keys, queries, (((1,), (1,)), ((), ())), preferred_element_type=F32)
    key_pos = lax.broadcasted_iota(jnp.int32, scores.shape, 0)
    query_pos = lax.broadcasted_iota(jnp.int32, scores.shape, 1) + first
    allowed = (key_pos <= query_pos) & (id_column == id_row)
    return jnp.where(allowed, scores, MASKED)


def column_of(id_row):
    length = id_row.shape[1]
    return jnp.broadcast_to(id_row, (LANES, length)).T[:, :1]


def forward_kernel(
    seq_count,
    heads,
    head_size,
    step_rows,
    block,
    rows_ref,
    weight,
    gain,
    bias,
    bqv,
    after,
    out,
    stats,
    whole,
    normed,
    ids,
    result,
    qkv_bias,
):
    length = whole.shape[0]
    group = heads * head_size
    width = weight.shape[0]
    index = lax.rem(lax.axis_index("seq"), lax.axis_size("seq") // seq_count)
    qkv_bias[...] = jnp.zeros_like(qkv_bias)
    for lo in range(0, width, group):
        here = index == lo // group
        for base, start in ((0, 0), (width, 2 * group)):
            piece = jnp.where(here, bqv[:, base + lo : base + lo + group], 0.0)
            qkv_bias[:, start : start + group] += piece
    for i in range(length // block):
        rows = norm_affine(rows_ref[i, :block, :].astype(F32), gain[...], bias[...])
        normed[i * block : (i + 1) * block, :] = rows.astype(BF16)
    id_rows = [rows_ref[i, block:, :block].astype(F32)[:1] for i in range(length // block)]
    id_row = jnp.concatenate(id_rows, 1)
    ids[...] = id_row
    id_column = column_of(id_row)
    for first in range(0, length, step_rows):
        last = first + step_rows
        product = jnp.dot(normed[first:last, :], weight[...], preferred_element_type=F32)
        whole[first:last, :] = (product + qkv_bias[...]).astype(BF16)
    values_t = whole[:, 2 * group : 3 * group].astype(F32).T.astype(BF16)
    for first in range(0, length, step_rows):
        last = first + step_rows
        tops = []
        for head in range(heads):
            lo = head * head_size
            queries = whole[first:last, lo : lo + head_size] * BF16(head_size**-0.5)
            keys = whole[:last, group + lo : group + lo + head_size]
            scores = masked_scores(keys, queries, id_column[:last], id_row[:, first:last], first)
            highest = jnp.max(scores, 0, keepdims=True)
            weights = jnp.exp(scores - highest)
            total = jnp.sum(weights, 0, keepdims=True)
            probs = (weights * (1.0 / total)).astype(BF16)
            tops.append(
                jnp.dot(
                    values_t[lo : lo + head_size, :last], probs, preferred_element_type=F32
                )
            )
            stats[head : head + 1, first:last] = highest + jnp.log(total)
        result[first:last, :] = jnp.concatenate(tops, 0).T.astype(BF16)
    half = block // 2
    for start in range(0, length, block):
        out[start // 2 : start // 2 + half, :group] = result[start : start + half, :]
        out[start // 2 : start // 2 + half, group:] = result[start + half : start + block, :]


def backward_kernel(
    heads,
    head_size,
    step_rows,
    block,
    whole,
    grads,
    stats,
    ids,
    after1,
    after2,
    out,
    grad_out,
    grad_query,
    grad_key,
    grad_value,
):
    length = whole.shape[0]
    group = heads * head_size
    half = block // 2
    for start in range(0, length, block):
        packed = grads[start // 2 : start // 2 + half, :]
        grad_out[start : start + half, :] = packed[:, :group]
        grad_out[start + half : start + block, :] = packed[:, group:]
    id_row = ids[...]
    id_column = column_of(id_row)
    keys_t = whole[:, group : 2 * group].astype(F32).T.astype(BF16)
    factor = head_size**-0.5
    grad_key[...] = jnp.zeros_like(grad_key)
    grad_value[...] = jnp.zeros_like(grad_value)
    for first in range(0, length, step_rows):
        last = first + step_rows
        tops = []
        for head in range(heads):
            lo = head * head_size
            queries = whole[first:last, lo : lo + head_size] * BF16(factor)
            keys = whole[:last, group + lo : group + lo + head_size]
            values = whole[:last, 2 * group + lo : 2 * group + lo + head_size]
            grad = grad_out[first:last, lo : lo + head_size]
            scores = masked_scores(keys, queries, id_column[:last], id_row[:, first:last], first)
            probs = jnp.exp(scores - stats[head : head + 1, first:last])
            grad_probs = lax.dot_general(
                values, grad, (((1,), (1,)), ((), ())), preferred_element_type=F32
            )
            delta = jnp.sum(probs * grad_probs, 0, keepdims=True)
            grad_scores = (probs * (grad_probs - delta)).astype(BF16)
            tops.append(
                jnp.dot(
                    keys_t[lo : lo + head_size, :last], grad_scores, preferred_element_type=F32
                )
                * factor
            )
            grad_key[head, :last, :] += jnp.dot(
                grad_scores, queries, preferred_element_type=F32
            )
            grad_value[head, :last, :] += jnp.dot(
                probs.astype(BF16), grad, preferred_element_type=F32
            )
        grad_query[first:last, :] = jnp.concatenate(tops, 0).T.astype(BF16)
    out[:, :group] = grad_query[...]
    for head in range(heads):
        lo = head * head_size
        out[:, group + lo : group + lo + head_size] = grad_key[head].astype(BF16)
        out[:, 2 * group + lo : 2 * group + lo + head_size] = grad_value[head].astype(BF16)


def attend_forward(rows, weight, gain, bias, bqv, after, seq_count, heads, head_size, block):
    length = rows.shape[0] * block
    width = rows.shape[2]
    group = heads * head_size
    return pl.pallas_call(
        functools.partial(forward_kernel, seq_count, heads, head_size, min(256, length), block),
        out_shape=[
            jax.ShapeDtypeStruct((length // 2, 2 * group), BF16),
            jax.ShapeDtypeStruct((heads, length), F32),
            jax.ShapeDtypeStruct((length, 3 * group), BF16),
            jax.ShapeDtypeStruct((length, width), BF16),
            jax.ShapeDtypeStruct((1, length), F32),
        ],
        in_specs=vmem_specs(5) + [ANYWHERE],
        out_specs=vmem_specs(5),
        scratch_shapes=[pltpu.VMEM((length, group), BF16), pltpu.VMEM((1, 3 * group), F32)],
        compiler_params=pltpu.CompilerParams(vmem_limit_bytes=48 * 2**20),
        cost_estimate=LIGHT,
    )(rows, weight, gain, bias, bqv, after)


def attend_backward(whole, grads, stats, ids, after, heads, head_size, block):
    length, width = whole.shape
    group = heads * head_size
    return pl.pallas_call(
        functools.partial(backward_kernel, heads, head_size, min(256, length), block),
        out_shape=jax.ShapeDtypeStruct((length, 3 * group), BF16),
        in_specs=vmem_specs(4) + [ANYWHERE] * 2,
        out_specs=vmem_specs(1)[0],
        scratch_shapes=[
            pltpu.VMEM((length, group), BF16),
            pltpu.VMEM((length, group), BF16),
            pltpu.VMEM((heads, length, head_size), F32),
            pltpu.VMEM((heads, length, head_size), F32),
        ],
        compiler_params=pltpu.CompilerParams(vmem_limit_bytes=48 * 2**20),
        cost_estimate=LIGHT,
    )(whole, grads, stats, ids, *after)


def on_device(
    inputs,
    segments,
    cotangent,
    ln1_gain,
    ln1_bias,
    w_qkv,
    b_qv,
    w_out,
    b_out,
    ln2_gain,
    ln2_bias,
    w_fc,
    b_fc,
    w_proj,
    b_proj,
):
    seq_count, block, width = inputs.shape
    head_size = width // HEADS
    tokens = seq_count * block
    count = lax.axis_size("seq")
    devices = count * lax.axis_size("dp")
    groups = count // seq_count
    heads = -(-HEADS // groups)
    spare = groups * heads - HEADS
    group = heads * head_size

    vectors = (ln1_gain, ln1_bias, b_qv, b_out, ln2_gain, ln2_bias, b_fc, b_proj)
    sizes = tuple(vector.shape[0] for vector in vectors)
    shard_rows = w_out.shape[0] // width
    parts = w_fc.shape[0] // w_out.shape[0]
    classes = groups // CORES
    chips = devices // CORES
    place = lax.axis_index("seq")
    core = place % CORES
    group_index = place % groups

    columns, blocks = first_blocks(
        w_qkv.reshape(shard_rows, 3 * width),
        inputs,
        segments,
        [vector.reshape(1, -1) for vector in vectors],
        classes,
        group,
    )
    stacked = stack_weights(w_out.reshape(-1, width), w_fc.reshape(-1, parts * width), columns)
    tower_a = build_line(gather_columns(columns), stacked)
    lines, sequence = gather_sequence(blocks, tower_a)
    low1, high1 = build_tower(z_pieces(stacked), 1, [tower_a])
    if lax.axis_size("dp") == 4:
        towers = [tower_a] + [swap_dp(tower_a, mask) for mask in range(1, 4)]
    else:
        towers = [lax.all_gather(tower_a, "dp", axis=0, tiled=True)]
    keep_a, send_a = split_halves(towers, [low1, lines])
    wqkv, gain1, bias1, bqv, bout, gain2, bias2, bfc, bproj = unpack_first(
        keep_a, swap_core(send_a), sizes
    )

    raw, stats, qkv, normed1, ids = attend_forward(
        sequence, wqkv, gain1, bias1, bqv, low1, seq_count, heads, head_size, block
    )
    pieces2 = z_pieces(gate(w_proj.reshape(-1, width), lines))
    low2, high2 = build_tower(pieces2, 0, [raw])
    attended = exchange(raw.reshape(count, block // 2, 2 * group))
    half1 = gather_plane(low1, high1, 1, raw, attended).reshape(1 + parts, -1, width)
    half2 = gather_plane(low2, high2, 0, attended)
    other1 = swap_core(half1)
    other2 = swap_core(half2)
    aligned = half2.shape[1] % 16 == 0
    if not aligned:
        half2 = ordered(core, half2, other2, 1).reshape(1, parts * width, width)

    spot = jnp.arange(width, dtype=jnp.int32)
    side = width // CORES
    own_core = (core + spot // side) % CORES
    order = (spot % side // shard_rows * CORES + own_core) * shard_rows + spot % shard_rows
    (
        outputs,
        grad_middle,
        grad_blocks,
        placed_a,
        placed_n,
        hidden,
        grad_pre,
        grad_out,
        grad_bout,
        grad_gain2,
        grad_bias2,
        grad_bfc,
        grad_bproj,
    ) = middle_block(
        half1,
        other1,
        half2,
        other2,
        attended,
        inputs,
        cotangent,
        order.reshape(1, width),
        (bout, gain2, bias2, bfc, bproj),
        groups,
    )
    grad_blocks = exchange(grad_blocks).reshape(-1, 2 * group)
    send_b, keep_b = weight_gradients(
        placed_a, placed_n, hidden, grad_pre, grad_out, cotangent, shard_rows
    )
    if send_b.shape[0] == 1 + parts:
        grad_wproj = lax.dot_general(
            hidden,
            cotangent.reshape(tokens, width),
            (((0,), (0,)), ((), ())),
            preferred_element_type=F32,
        )
        grad_wproj = grad_wproj.astype(BF16).reshape(chips, CORES, parts, shard_rows, width)
        grad_wproj = grad_wproj.transpose(1, 2, 0, 3, 4).reshape(CORES, parts, -1, width)
        send_b = jnp.concatenate([send_b, pick(grad_wproj, 1 - core, 0)], 0)
        keep_b = jnp.concatenate([keep_b, pick(grad_wproj, core, 0)], 0)
    sum_b = add(keep_b, swap_core(send_b)).reshape(-1, chips, shard_rows, width)
    steps = []

    def between(*after):
        if steps:
            steps.append(after[0])
        else:
            steps.append(
                attend_backward(qkv, grad_blocks, stats, ids, after, heads, head_size, block)
            )
        return steps[0]

    tower_b = scatter_plane(sum_b, 1, between)
    own_b = scatter_z(tower_b, 1)
    grad_qkv, first_sums = steps

    def blocks_of(value, rows):
        return value.astype(BF16).reshape(chips, CORES, rows, -1)

    rows = inputs.astype(F32).reshape(tokens, width)
    grad_normed1 = lax.dot_general(
        grad_qkv, wqkv, (((1,), (1,)), ((), ())), preferred_element_type=F32
    )
    own_normed1 = scatter_sequence(
        grad_normed1.astype(BF16).reshape(count, block, width), first_sums
    )
    _, norm1_back = jax.vjp(lambda value: norm_affine(value, gain1, bias1), rows)
    (grad_in_part,) = norm1_back(own_normed1.astype(F32).reshape(tokens, width))
    grad_inputs = (grad_middle + grad_in_part).astype(BF16).reshape(inputs.shape)

    grad_qkv = gate(grad_qkv, tower_b)
    long_rows = sequence[:, :block].astype(F32).reshape(count * block, width)
    _, norm1_long_back = jax.vjp(lambda g, b: norm_affine(long_rows, g, b), gain1, bias1)
    grad_gain1, grad_bias1 = norm1_long_back(grad_normed1)
    grad_wqkv = lax.dot_general(
        normed1, grad_qkv, (((0,), (0,)), ((), ())), preferred_element_type=F32
    )
    sums = jnp.sum(grad_qkv, 0, dtype=F32).reshape(3, group)
    here = (jnp.arange(groups) == group_index)[None, :, None]
    grad_bqv = jnp.where(here, jnp.stack([sums[0], sums[2]])[:, None], 0.0)
    grad_bqv = grad_bqv.reshape(2, groups * heads, head_size)[:, :HEADS]
    grads = (
        grad_gain1,
        grad_bias1,
        grad_bqv,
        grad_bout,
        grad_gain2,
        grad_bias2,
        grad_bfc,
        grad_bproj,
    )
    small_grads = pack_small([grad.reshape(1, -1) for grad in grads], sizes, devices)
    small_grads = jnp.pad(small_grads, ((0, 0), (0, 0), (0, 3 * group - LANES)))
    block_a = jnp.concatenate(
        [blocks_of(grad_wqkv, shard_rows), small_grads.reshape(chips, CORES, ROWS, -1)], 2
    )
    send_a, keep_a = pick(block_a, 1 - core, 1), pick(block_a, core, 1)
    got_a = swap_core(send_a)
    pair_a = jnp.concatenate(
        [jnp.where(core == 0, keep_a, got_a), jnp.where(core == 0, got_a, keep_a)], -1
    )
    tower_a = scatter_plane_direct(pair_a, tower_b)
    own_qkv, own_small = finish_columns(scatter_columns(tower_a), width, group, own_b)
    own = [own_small[i, :size] for i, size in enumerate(sizes)]
    own_qkv = own_qkv.reshape(-1)
    return (
        outputs,
        grad_inputs,
        own[0],
        own[1],
        own_qkv,
        own[2],
        own_b[0].reshape(-1),
        own[3],
        own[4],
        own[5],
        own_b[1 : 1 + parts].transpose(1, 0, 2).reshape(-1),
        own[6],
        own_b[1 + parts :].reshape(-1),
        own[7],
    )


def solution(mesh):
    token_spec = P("dp", "seq", None)
    flat_spec = P(("dp", "seq"))
    in_specs = (token_spec, P("dp", "seq"), token_spec) + (flat_spec,) * 12
    out_specs = (token_spec, token_spec) + (flat_spec,) * 12
    return jax.shard_map(
        on_device, mesh=mesh, in_specs=in_specs, out_specs=out_specs, check_vma=False
    )
```

```python
import functools
import math

import jax
import jax.numpy as jnp
from jax import lax
from jax.experimental import pallas as pl
from jax.experimental.pallas import tpu as pltpu
from jax.sharding import PartitionSpec as P

HEADS = 12
CORES = 2


EPSILON = 1e-05
MASKED = -1e30
F32 = jnp.float32
BF16 = jnp.bfloat16


def norm_affine(values, gain, bias):
    center = jnp.mean(values, -1, keepdims=True)
    centered = values - center
    variance = jnp.mean(centered * centered, -1, keepdims=True)
    return centered * lax.rsqrt(variance + EPSILON) * gain + bias


ANYWHERE = pl.BlockSpec(memory_space=pl.ANY)
LIGHT = pl.CostEstimate(flops=1, bytes_accessed=1, transcendentals=0)


def shift_z(value, step):
    size = lax.axis_size("seq")
    return lax.ppermute(value, "seq", [(i, (i + CORES * step) % size) for i in range(size)])


def swap_core(value):
    size = lax.axis_size("seq")
    return lax.ppermute(value, "seq", [(i, i ^ 1) for i in range(size)])


def swap_dp(value, bit):
    size = lax.axis_size("dp")
    return lax.ppermute(value, "dp", [(i, i ^ bit) for i in range(size)])


def ordered(flag, mine, other, axis):
    first = jnp.where(flag == 0, mine, other)
    second = jnp.where(flag == 0, other, mine)
    return jnp.stack([first, second], axis)


def roll_blocks(pieces, place):
    count = len(pieces)
    stacked = jnp.stack(pieces)
    twice = jnp.concatenate([stacked, stacked])
    return lax.dynamic_slice_in_dim(twice, lax.rem(count - place, count), count, 0)


def z_pieces(shard):
    heights = lax.axis_size("seq") // CORES
    return [shard] + [shift_z(shard, -step) for step in range(1, heights)]


def swap_z(value, bit):
    size = lax.axis_size("seq")
    return lax.ppermute(value, "seq", [(i, i ^ (CORES * bit)) for i in range(size)])


def gather_plane(low, high, axis, first=None, second=None):
    def move(value, bit, after):
        moved = swap_dp(value, bit)
        return moved if after is None else gate(moved, after)

    if lax.axis_size("dp") == 4:
        plane = lax.axis_index("dp")
        y, x = plane // 2, plane % 2
        low_x = ordered(x, low, move(low, 1, first), axis)
        high_y = ordered(y, high, move(high, 2, first), axis)
        low_all = ordered(y, low_x, move(low_x, 2, second), axis)
        high_all = ordered(x, high_y, move(high_y, 1, second), axis + 1)
        half = jnp.concatenate([low_all, high_all], axis + 2)
        count = 4 * half.shape[axis + 2]
    else:
        tower = jnp.concatenate([low, high], axis)
        half = lax.all_gather(tower, "dp", axis=axis, tiled=True)
        return half
    return half.reshape(*low.shape[:axis], count, *low.shape[axis + 1 :])


def pick(value, index, axis):
    return lax.dynamic_index_in_dim(value, index, axis, keepdims=False)


def add(mine, other):
    return (mine.astype(F32) + other.astype(F32)).astype(mine.dtype)


def scatter_plane(split, axis, between=None):
    planes = lax.axis_size("dp")
    heights = lax.axis_size("seq") // CORES
    if planes != 4:
        if between is not None:
            between(split, split)
            between(split, split)
        return lax.psum_scatter(split, "dp", scatter_dimension=axis, tiled=True)
    plane = lax.axis_index("dp")
    y, x = plane // 2, plane % 2
    split = split.reshape(*split.shape[:axis], 2, 2, heights, *split.shape[axis + 1 :])
    low = lax.slice_in_dim(split, 0, heights // 2, axis=axis + 2)
    high = lax.slice_in_dim(split, heights // 2, heights, axis=axis + 2)
    low_send, high_send = pick(low, 1 - y, axis), pick(high, 1 - x, axis + 1)
    low_got, high_got = swap_dp(low_send, 2), swap_dp(high_send, 1)
    if between is not None:
        after = between(low_send, high_send)
        low_got, high_got = gate_both(low_got, high_got, after)
    low = add(pick(low, y, axis), low_got)
    high = add(pick(high, x, axis + 1), high_got)
    if between is not None:
        between(low, high)
    low = add(pick(low, x, axis), swap_dp(pick(low, 1 - x, axis), 1))
    high = add(pick(high, y, axis), swap_dp(pick(high, 1 - y, axis), 2))
    return jnp.concatenate([low, high], axis)


def scatter_z(tower, axis):
    heights = lax.axis_size("seq") // CORES
    level = lax.axis_index("seq") // CORES
    mine = pick(tower, level, axis).astype(F32)
    for step in range(1, heights):
        mine += shift_z(pick(tower, lax.rem(level + step, heights), axis), step).astype(F32)
    return mine


def z_bits():
    heights = lax.axis_size("seq") // CORES
    level = lax.axis_index("seq") // CORES
    top = heights // 2
    return level, top, level // top


def gather_sequence(blocks, after):
    level, top, half = z_bits()
    core = lax.axis_index("seq") % CORES
    got = gate(swap_z(pick(blocks, 1 - half, 0), top), after)
    held = ordered(half, pick(blocks, half, 0), got, 0)
    axis, bit = 1, top // 2
    while bit:
        held = ordered(level // bit % 2, held, swap_z(held, bit), axis)
        axis, bit = axis + 1, bit // 2
    return held, ordered(core, held, swap_core(held), axis).reshape(-1, *blocks.shape[1:])


def scatter_sequence(partial, after):
    level, top, half = z_bits()
    core = lax.axis_index("seq") % CORES
    shape = partial.shape[1:]
    count = top.bit_length()
    held = partial.reshape(*[2] * (count + 1), *shape)
    got = gate(swap_core(pick(held, 1 - core, count)), after)
    held = add(pick(held, core, count), got)
    axis, bit = count - 1, 1
    while bit < top:
        flag = level // bit % 2
        got = swap_z(pick(held, 1 - flag, axis), bit)
        held = add(pick(held, flag, axis), got)
        axis, bit = axis - 1, bit * 2
    return ordered(half, pick(held, half, 0), swap_z(pick(held, 1 - half, 0), top), 0)


def class_of(level):
    return level % (lax.axis_size("seq") // CORES // 2)


def gather_columns(blocks):
    heights = lax.axis_size("seq") // CORES
    level = lax.axis_index("seq") // CORES
    moved = [
        swap_z(pick(blocks, class_of(level ^ mask), 0), mask) for mask in range(1, heights)
    ]
    return [pick(blocks, class_of(level), 0)] + moved


def scatter_columns(tower):
    heights = tower.shape[0]
    level = lax.axis_index("seq") // CORES
    moved = [swap_z(pick(tower, level ^ mask, 0), mask) for mask in range(1, heights)]
    return [pick(tower, level, 0)] + moved


def scatter_plane_direct(split, after):
    planes = lax.axis_size("dp")
    if planes != 4:
        return lax.psum_scatter(split, "dp", scatter_dimension=0, tiled=True)
    plane = lax.axis_index("dp")
    split = split.reshape(planes, -1, *split.shape[1:])
    total = pick(split, plane, 0).astype(F32)
    for mask in range(1, planes):
        total += gate(swap_dp(pick(split, plane ^ mask, 0), mask), after).astype(F32)
    return total.astype(split.dtype)


def exchange(blocks):
    return lax.all_to_all(blocks, "seq", split_axis=0, concat_axis=0, tiled=True)


ROWS = 8
LANES = 128


def vmem_specs(count):
    return [pl.BlockSpec(memory_space=pltpu.VMEM) for _ in range(count)]


def place_lanes(size, total):
    source = lax.broadcasted_iota(jnp.int32, (LANES, total), 0)
    target = lax.rem(lax.broadcasted_iota(jnp.int32, (LANES, total), 1), size)
    return jnp.where(source == target, 1.0, 0.0).astype(BF16)


def owned_lanes(devices, size):
    device = lax.broadcasted_iota(jnp.int32, (devices, devices * size), 0)
    lane = lax.broadcasted_iota(jnp.int32, (devices, devices * size), 1)
    offset = lane - device * size
    return (offset >= 0) & (offset < size)


def line_kernel(count, *refs):
    pieces, tower = refs[:count], refs[-1]
    level = lax.axis_index("seq") // CORES
    for mask, piece in enumerate(pieces):
        tower[level ^ mask] = piece[...]


def build_line(pieces, after):
    return pl.pallas_call(
        functools.partial(line_kernel, len(pieces)),
        out_shape=jax.ShapeDtypeStruct((len(pieces), *pieces[0].shape), BF16),
        in_specs=vmem_specs(len(pieces)) + [ANYWHERE],
        out_specs=vmem_specs(1)[0],
        cost_estimate=LIGHT,
    )(*pieces, after)


def halves_kernel(count, *refs):
    towers, (keep, send) = refs[:count], refs[-2:]
    heights, _, columns = towers[0].shape
    half = columns // CORES
    core = lax.rem(lax.axis_index("seq"), CORES)
    plane = lax.axis_index("dp")
    for own in range(CORES):

        @pl.when(core == own)
        def _():
            for mask, tower in enumerate(towers):
                base = (plane ^ mask) * heights if count > 1 else 0
                for i in range(heights):
                    line = tower[i]
                    keep[base + i] = line[:, own * half : (own + 1) * half]
                    send[base + i] = line[:, (1 - own) * half : (2 - own) * half]


def split_halves(towers, after):
    heights, rows, columns = towers[0].shape
    shape = jax.ShapeDtypeStruct((len(towers) * heights, rows, columns // CORES), BF16)
    return pl.pallas_call(
        functools.partial(halves_kernel, len(towers)),
        out_shape=[shape, shape],
        in_specs=vmem_specs(len(towers)) + [ANYWHERE] * len(after),
        out_specs=vmem_specs(2),
        compiler_params=pltpu.CompilerParams(vmem_limit_bytes=40 * 2**20),
        cost_estimate=LIGHT,
    )(*towers, *after)


def finish_kernel(count, group, *refs):
    pieces, (weight, small) = refs[:count], refs[-2:]
    shard, width = weight.shape[0], weight.shape[1] // 3
    heights = count
    level = lax.axis_index("seq") // CORES
    terms = [piece[...].astype(F32) for piece in pieces]
    small_sum = jnp.zeros((ROWS, LANES), F32)
    for kind in range(heights // 2):
        total = jnp.zeros_like(terms[0])
        for mask, term in enumerate(terms):
            total += jnp.where(lax.rem(level ^ mask, heights // 2) == kind, term, 0.0)
        for core in range(CORES):
            start = core * 3 * group
            small_sum += total[shard:, start : start + LANES]
            lo = (kind * CORES + core) * group
            for part in range(3 if lo < width else 0):
                at = start + part * group
                weight[:, part * width + lo : part * width + lo + group] = total[
                    :shard, at : at + group
                ]
    small[...] = small_sum


def finish_columns(pieces, width, group, after):
    rows = pieces[0].shape[0]
    return pl.pallas_call(
        functools.partial(finish_kernel, len(pieces), group),
        out_shape=[
            jax.ShapeDtypeStruct((rows - ROWS, 3 * width), F32),
            jax.ShapeDtypeStruct((ROWS, LANES), F32),
        ],
        in_specs=vmem_specs(len(pieces)) + [ANYWHERE],
        out_specs=vmem_specs(2),
        cost_estimate=LIGHT,
    )(*pieces, after)


def unpack_kernel(sizes, keep, got, weight, *refs):
    outs, (lines, small) = refs[:-2], refs[-2:]
    chips, rows = keep.shape[:2]
    shard = rows - ROWS
    core = lax.rem(lax.axis_index("seq"), CORES)
    for own in range(CORES):

        @pl.when(core == own)
        def _():
            for source, place in ((keep, own), (got, 1 - own)):
                for chip in range(chips):
                    device = chip * CORES + place
                    line = source[chip].astype(F32)
                    lines[device * shard : (device + 1) * shard, :] = line[:shard]
                    small[device] = line[shard:, :LANES]

    weight[...] = lines[...].astype(BF16)
    devices = chips * CORES
    for i, (size, out) in enumerate(zip(sizes, outs)):
        spread = jnp.dot(
            small[:, i, :].astype(BF16),
            place_lanes(size, devices * size),
            preferred_element_type=F32,
        )
        out[...] = jnp.sum(jnp.where(owned_lanes(devices, size), spread, 0.0), 0, keepdims=True)


def unpack_first(keep, got, sizes):
    chips, rows, columns = keep.shape
    devices = chips * CORES
    width = devices * (rows - ROWS)
    return pl.pallas_call(
        functools.partial(unpack_kernel, sizes),
        out_shape=[jax.ShapeDtypeStruct((width, columns), BF16)]
        + [jax.ShapeDtypeStruct((1, devices * size), F32) for size in sizes],
        in_specs=vmem_specs(2),
        out_specs=vmem_specs(1 + len(sizes)),
        scratch_shapes=[
            pltpu.VMEM((width, columns), F32),
            pltpu.VMEM((devices, ROWS, LANES), F32),
        ],
        compiler_params=pltpu.CompilerParams(vmem_limit_bytes=40 * 2**20),
        cost_estimate=LIGHT,
    )(keep, got)


def pack_kernel(sizes, *refs):
    grads, packed, rows = refs[: len(sizes)], refs[len(sizes)], refs[len(sizes) + 1]
    devices = packed.shape[0]
    for i, (size, grad) in enumerate(zip(sizes, grads)):
        owned = jnp.where(owned_lanes(devices, size), grad[...], 0.0).astype(BF16)
        rows[:, i, :] = lax.dot_general(
            owned,
            place_lanes(size, devices * size),
            (((1,), (1,)), ((), ())),
            preferred_element_type=F32,
        )
    packed[...] = rows[...].astype(BF16)


def pack_small(grads, sizes, devices):
    return pl.pallas_call(
        functools.partial(pack_kernel, sizes),
        out_shape=jax.ShapeDtypeStruct((devices, ROWS, LANES), BF16),
        in_specs=vmem_specs(len(sizes)),
        out_specs=vmem_specs(1)[0],
        scratch_shapes=[pltpu.VMEM((devices, ROWS, LANES), F32)],
        compiler_params=pltpu.CompilerParams(vmem_limit_bytes=32 * 2**20),
        cost_estimate=LIGHT,
    )(*grads)


def gate(value, *after):
    def kernel(*refs):
        pass

    return pl.pallas_call(
        kernel,
        out_shape=jax.ShapeDtypeStruct(value.shape, value.dtype),
        in_specs=[ANYWHERE] * (1 + len(after)),
        out_specs=ANYWHERE,
        input_output_aliases={0: 0},
        cost_estimate=LIGHT,
    )(value, *after)


def gate_both(one, two, *after):
    def kernel(*refs):
        pass

    return pl.pallas_call(
        kernel,
        out_shape=[jax.ShapeDtypeStruct(value.shape, value.dtype) for value in (one, two)],
        in_specs=[ANYWHERE] * (2 + len(after)),
        out_specs=[ANYWHERE] * 2,
        input_output_aliases={0: 0, 1: 1},
        cost_estimate=LIGHT,
    )(one, two, *after)


def first_kernel(group, weight, rows, marks, *refs):
    vectors, (columns, blocks, lines, extra) = refs[:-4], refs[-4:]
    classes, _, width_pair = columns.shape
    shard_rows, width = weight.shape[0], weight.shape[1] // 3
    lines[...] = jnp.zeros_like(lines)
    for i, vector in enumerate(vectors):
        for start in range(0, width_pair, 3 * group):
            at = shard_rows + i
            lines[at : at + 1, start : start + vector.shape[1]] = vector[...].astype(F32)
    for kind in range(classes):
        for core in range(CORES):
            lo = (kind * CORES + core) * group
            for part in range(3):
                start = (core * 3 + part) * group
                if lo < width:
                    piece = weight[:, part * width + lo : part * width + lo + group].astype(F32)
                else:
                    piece = jnp.zeros((shard_rows, group), F32)
                lines[:shard_rows, start : start + group] = piece
        columns[kind] = lines[...].astype(BF16)
    block = rows.shape[1]
    extra[...] = jnp.zeros_like(extra)
    for i in range(rows.shape[0]):
        blocks[i, :block, :] = rows[i]
        extra[:1, :block] = marks[i : i + 1, :].astype(F32)
        blocks[i, block:, :] = extra[...].astype(BF16)


def first_blocks(weight, rows, marks, vectors, classes, group):
    shard_rows = weight.shape[0]
    count, block, width = rows.shape
    return pl.pallas_call(
        functools.partial(first_kernel, group),
        out_shape=[
            jax.ShapeDtypeStruct((classes, shard_rows + ROWS, CORES * 3 * group), BF16),
            jax.ShapeDtypeStruct((count, block + 16, width), BF16),
        ],
        in_specs=vmem_specs(3 + len(vectors)),
        out_specs=vmem_specs(2),
        scratch_shapes=[
            pltpu.VMEM((shard_rows + ROWS, CORES * 3 * group), F32),
            pltpu.VMEM((16, width), F32),
        ],
    )(weight, rows, marks, *vectors)


def stack_kernel(out_ref, fc_ref, after, stacked):
    width = out_ref.shape[1]
    stacked[0] = out_ref[...]
    for i in range(fc_ref.shape[1] // width):
        stacked[1 + i] = fc_ref[:, i * width : (i + 1) * width]


def stack_weights(w_out, w_fc, after):
    rows, width = w_out.shape
    return pl.pallas_call(
        stack_kernel,
        out_shape=jax.ShapeDtypeStruct((1 + w_fc.shape[1] // width, rows, width), BF16),
        in_specs=vmem_specs(2) + [ANYWHERE],
        out_specs=vmem_specs(1)[0],
        cost_estimate=LIGHT,
    )(w_out, w_fc, after)


def tower_kernel(axis, count, *refs):
    pieces, low, high = refs[:count], refs[-2], refs[-1]
    level = lax.axis_index("seq") // CORES
    for step, piece in enumerate(pieces):
        place = lax.rem(level + step, count)
        for half, start in ((low, 0), (high, count // 2)):

            @pl.when((place >= start) & (place < start + count // 2))
            def _():
                if axis == 1:
                    half[:, place - start] = piece[...]
                else:
                    half[place - start] = piece[...]


def build_tower(pieces, axis, after):
    count = len(pieces)
    shape = pieces[0].shape
    shape = (*shape[:axis], count // 2, *shape[axis:])
    return pl.pallas_call(
        functools.partial(tower_kernel, axis, count),
        out_shape=[jax.ShapeDtypeStruct(shape, BF16)] * 2,
        in_specs=vmem_specs(count) + [ANYWHERE] * len(after),
        out_specs=vmem_specs(2),
        compiler_params=pltpu.CompilerParams(vmem_limit_bytes=32 * 2**20),
        cost_estimate=LIGHT,
    )(*pieces, *after)


def one_hot_order(order_ref):
    width = order_ref.shape[1]
    features = lax.broadcasted_iota(jnp.int32, (width, width), 0)
    return jnp.where(features == order_ref[...], 1.0, 0.0).astype(BF16)


def contract_last(left, right):
    return lax.dot_general(left, right, (((1,), (1,)), ((), ())), preferred_element_type=F32)


def middle_kernel(
    groups,
    half1,
    other1,
    half2,
    other2,
    attended,
    inputs,
    cotangent,
    order_ref,
    bout,
    gain,
    bias,
    bfc,
    bproj,
    outputs,
    grad_middle,
    grad_blocks,
    placed_a,
    placed_n,
    hidden,
    grad_pre,
    grad_out,
    sum_out,
    sum_gain,
    sum_bias,
    sum_fc,
    sum_proj,
    weights1,
    weights2,
    attended_rows,
    slopes,
    permuted,
    sems,
):
    parts = weights1.shape[0] - 1
    width = weights1.shape[2]
    side = width // CORES
    seq_count, block, _ = inputs.shape
    tokens = seq_count * block
    core = lax.rem(lax.axis_index("seq"), CORES)
    chips, rows2 = half2.shape[:2]
    copies = []
    for kind in range(parts + 1):
        for index, source in enumerate((half1, other1)):
            copies.append(
                pltpu.make_async_copy(
                    source.at[kind],
                    weights1.at[kind, pl.ds(index * side, side)],
                    sems.at[len(copies)],
                )
            )
    ready1 = len(copies)
    if chips == 1:
        copies.append(pltpu.make_async_copy(half2.at[0], weights2, sems.at[len(copies)]))
    for index, source in enumerate((half2, other2) if chips > 1 else ()):
        place = core if index == 0 else 1 - core
        for chip in range(chips):
            start = pl.multiple_of((chip * CORES + place) * rows2, rows2)
            copies.append(
                pltpu.make_async_copy(
                    source.at[chip], weights2.at[pl.ds(start, rows2)], sems.at[len(copies)]
                )
            )
    for copy in copies:
        copy.start()
    order = one_hot_order(order_ref)

    half_block = block // 2
    group = attended.shape[2] // 2
    for i in range(seq_count):
        for g in range(groups):
            for part in range(2):
                start = i * block + part * half_block
                attended_rows[start : start + half_block, g * group : (g + 1) * group] = attended[
                    i * groups + g, :, part * group : (part + 1) * group
                ]
    placed = jnp.dot(attended_rows[:, :width], order, preferred_element_type=F32).astype(BF16)
    placed_a[...] = placed
    for copy in copies[:2]:
        copy.wait()
    rows = inputs[...].astype(F32).reshape(tokens, width)
    middle = rows + (jnp.dot(placed, weights1[0], preferred_element_type=F32) + bout[...])
    center = jnp.mean(middle, -1, keepdims=True)
    centered = middle - center
    scale = lax.rsqrt(jnp.mean(centered * centered, -1, keepdims=True) + EPSILON)
    unit = centered * scale
    normed = (unit * gain[...] + bias[...]).astype(BF16)
    placed = jnp.dot(normed, order, preferred_element_type=F32).astype(BF16)
    placed_n[...] = placed
    for copy in copies[2:ready1]:
        copy.wait()
    curve = math.sqrt(2.0 / math.pi)
    for q in range(parts):
        lo = q * width
        pre = jnp.dot(placed, weights1[1 + q], preferred_element_type=F32)
        pre = pre + bfc[:, lo : lo + width]
        square = pre * pre
        tanh = jnp.tanh(curve * (pre + 0.044715 * (pre * square)))
        hidden[:, lo : lo + width] = (0.5 * pre * (1.0 + tanh)).astype(BF16)
        slopes[:, lo : lo + width] = 0.5 * (1.0 + tanh) + 0.5 * pre * (1.0 - tanh * tanh) * (
            curve * (1.0 + 3 * 0.044715 * square)
        )
    for copy in copies[ready1:]:
        copy.wait()
    result = middle + bproj[...]
    for q in range(parts):
        lo = q * width
        result += jnp.dot(
            hidden[:, lo : lo + width], weights2[lo : lo + width], preferred_element_type=F32
        )
    outputs[...] = result.astype(BF16).reshape(seq_count, block, width)

    branch = cotangent[...].reshape(tokens, width)
    grad_rows = branch.astype(F32)
    sum_proj[...] = jnp.sum(grad_rows, 0, keepdims=True)
    grad_placed = jnp.zeros((tokens, width), F32)
    for q in range(parts):
        lo = q * width
        grad = contract_last(branch, weights2[lo : lo + width]) * slopes[:, lo : lo + width]
        grad = grad.astype(BF16)
        grad_pre[:, lo : lo + width] = grad
        sum_fc[:, lo : lo + width] = jnp.sum(grad.astype(F32), 0, keepdims=True)
        grad_placed += contract_last(grad, weights1[1 + q])
    high = grad_placed.astype(BF16)
    rest = grad_placed - high.astype(F32)
    mid = rest.astype(BF16)
    low = (rest - mid.astype(F32)).astype(BF16)
    grad_normed = contract_last(high, order) + (contract_last(mid, order) + contract_last(low, order))
    sum_bias[...] = jnp.sum(grad_normed, 0, keepdims=True)
    sum_gain[...] = jnp.sum(grad_normed * unit, 0, keepdims=True)
    grad_unit = grad_normed * gain[...]
    part = jnp.mean(grad_unit, -1, keepdims=True)
    cross = jnp.mean(grad_unit * unit, -1, keepdims=True)
    grad_mid = grad_rows + scale * (grad_unit - part - unit * cross)
    grad_middle[...] = grad_mid
    grad_attn = grad_mid.astype(BF16)
    grad_out[...] = grad_attn
    sum_out[...] = jnp.sum(grad_attn.astype(F32), 0, keepdims=True)
    back = contract_last(grad_attn, weights1[0]).astype(BF16)
    if permuted.shape[1] > width:
        permuted[...] = jnp.zeros_like(permuted)
    permuted[:, :width] = contract_last(back, order).astype(BF16)
    for i in range(seq_count):
        for g in range(groups):
            for part in range(2):
                start = i * block + part * half_block
                grad_blocks[i * groups + g, :, part * group : (part + 1) * group] = permuted[
                    start : start + half_block, g * group : (g + 1) * group
                ]


def middle_block(half1, other1, half2, other2, attended, inputs, cotangent, order, vectors, groups):
    kinds, side, width = half1.shape
    parts = kinds - 1
    chips = half2.shape[0]
    seq_count, block, _ = inputs.shape
    tokens = seq_count * block
    wide = groups * attended.shape[2] // 2

    def shape(*dims, kind=BF16):
        return jax.ShapeDtypeStruct(dims, kind)

    return pl.pallas_call(
        functools.partial(middle_kernel, groups),
        out_shape=[
            shape(seq_count, block, width),
            shape(tokens, width, kind=F32),
            shape(*attended.shape),
            shape(tokens, width),
            shape(tokens, width),
            shape(tokens, parts * width),
            shape(tokens, parts * width),
            shape(tokens, width),
            shape(1, width, kind=F32),
            shape(1, width, kind=F32),
            shape(1, width, kind=F32),
            shape(1, parts * width, kind=F32),
            shape(1, width, kind=F32),
        ],
        in_specs=[ANYWHERE] * 4 + vmem_specs(9),
        out_specs=vmem_specs(13),
        scratch_shapes=[
            pltpu.VMEM((kinds, width, width), BF16),
            pltpu.VMEM((parts * width, width), BF16),
            pltpu.VMEM((tokens, wide), BF16),
            pltpu.VMEM((tokens, parts * width), F32),
            pltpu.VMEM((tokens, wide), BF16),
            pltpu.SemaphoreType.DMA((2 * kinds + 2 * chips,)),
        ],
        compiler_params=pltpu.CompilerParams(vmem_limit_bytes=50 * 2**20),
        cost_estimate=LIGHT,
    )(half1, other1, half2, other2, attended, inputs, cotangent, order, *vectors)


def gradient_kernel(
    shard_rows, placed_a, placed_n, hidden, grad_pre, grad_out, cotangent, send, keep, turned, some
):
    width = placed_a.shape[1]
    side = width // CORES
    parts = hidden.shape[1] // width
    chips = side // shard_rows
    core = lax.rem(lax.axis_index("seq"), CORES)
    branch = cotangent[...].reshape(-1, width)
    if send.shape[0] > 1 + parts:
        for start in range(0, turned.shape[0], width):
            turned[start : start + width, :] = hidden[:, start : start + width].astype(F32).T
        for target, place in ((send, 1 - core), (keep, core)):
            for chip in range(chips):
                for i in range(parts):
                    start = ((chip * CORES + place) * parts + i) * shard_rows
                    start = pl.multiple_of(start, shard_rows)
                    to = i * side + chip * shard_rows
                    some[to : to + shard_rows, :] = turned[pl.ds(start, shard_rows), :]
            for i in range(parts):
                target[1 + parts + i] = jnp.dot(
                    some[i * side : (i + 1) * side, :].astype(BF16),
                    branch,
                    preferred_element_type=F32,
                ).astype(BF16)
    turned_a = placed_a[...].astype(F32).T.astype(BF16)
    turned_n = placed_n[...].astype(F32).T.astype(BF16)
    for target, start in ((send, side), (keep, 0)):
        target[0] = jnp.dot(
            turned_a[start : start + side], grad_out[...], preferred_element_type=F32
        ).astype(BF16)
        for q in range(parts):
            target[1 + q] = jnp.dot(
                turned_n[start : start + side],
                grad_pre[:, q * width : (q + 1) * width],
                preferred_element_type=F32,
            ).astype(BF16)


def weight_gradients(placed_a, placed_n, hidden, grad_pre, grad_out, cotangent, shard_rows):
    tokens, width = placed_a.shape
    parts = hidden.shape[1] // width
    kinds = 1 + parts * (1 if shard_rows % 8 else 2)
    shape = jax.ShapeDtypeStruct((kinds, width // CORES, width), BF16)
    return pl.pallas_call(
        functools.partial(gradient_kernel, shard_rows),
        out_shape=[shape, shape],
        in_specs=vmem_specs(6),
        out_specs=vmem_specs(2),
        scratch_shapes=[
            pltpu.VMEM((parts * width, tokens), F32),
            pltpu.VMEM((parts * width // CORES, tokens), F32),
        ],
        compiler_params=pltpu.CompilerParams(vmem_limit_bytes=50 * 2**20),
        cost_estimate=LIGHT,
    )(placed_a, placed_n, hidden, grad_pre, grad_out, cotangent)


def masked_scores(keys, queries, id_column, id_row, first):
    scores = lax.dot_general(keys, queries, (((1,), (1,)), ((), ())), preferred_element_type=F32)
    key_pos = lax.broadcasted_iota(jnp.int32, scores.shape, 0)
    query_pos = lax.broadcasted_iota(jnp.int32, scores.shape, 1) + first
    allowed = (key_pos <= query_pos) & (id_column == id_row)
    return jnp.where(allowed, scores, MASKED)


def column_of(id_row):
    length = id_row.shape[1]
    return jnp.broadcast_to(id_row, (LANES, length)).T[:, :1]


def forward_kernel(
    seq_count,
    heads,
    head_size,
    step_rows,
    block,
    rows_ref,
    weight,
    gain,
    bias,
    bqv,
    after,
    out,
    stats,
    whole,
    normed,
    ids,
    result,
    qkv_bias,
):
    length = whole.shape[0]
    group = heads * head_size
    width = weight.shape[0]
    index = lax.rem(lax.axis_index("seq"), lax.axis_size("seq") // seq_count)
    qkv_bias[...] = jnp.zeros_like(qkv_bias)
    for lo in range(0, width, group):
        here = index == lo // group
        for base, start in ((0, 0), (width, 2 * group)):
            piece = jnp.where(here, bqv[:, base + lo : base + lo + group], 0.0)
            qkv_bias[:, start : start + group] += piece
    for i in range(length // block):
        rows = norm_affine(rows_ref[i, :block, :].astype(F32), gain[...], bias[...])
        normed[i * block : (i + 1) * block, :] = rows.astype(BF16)
    id_rows = [rows_ref[i, block:, :block].astype(F32)[:1] for i in range(length // block)]
    id_row = jnp.concatenate(id_rows, 1)
    ids[...] = id_row
    id_column = column_of(id_row)
    for first in range(0, length, step_rows):
        last = first + step_rows
        product = jnp.dot(normed[first:last, :], weight[...], preferred_element_type=F32)
        whole[first:last, :] = (product + qkv_bias[...]).astype(BF16)
    values_t = whole[:, 2 * group : 3 * group].astype(F32).T.astype(BF16)
    for first in range(0, length, step_rows):
        last = first + step_rows
        tops = []
        for head in range(heads):
            lo = head * head_size
            queries = whole[first:last, lo : lo + head_size] * BF16(head_size**-0.5)
            keys = whole[:last, group + lo : group + lo + head_size]
            scores = masked_scores(keys, queries, id_column[:last], id_row[:, first:last], first)
            highest = jnp.max(scores, 0, keepdims=True)
            weights = jnp.exp(scores - highest)
            total = jnp.sum(weights, 0, keepdims=True)
            probs = (weights * (1.0 / total)).astype(BF16)
            tops.append(
                jnp.dot(
                    values_t[lo : lo + head_size, :last], probs, preferred_element_type=F32
                )
            )
            stats[head : head + 1, first:last] = highest + jnp.log(total)
        result[first:last, :] = jnp.concatenate(tops, 0).T.astype(BF16)
    half = block // 2
    for start in range(0, length, block):
        out[start // 2 : start // 2 + half, :group] = result[start : start + half, :]
        out[start // 2 : start // 2 + half, group:] = result[start + half : start + block, :]


def backward_kernel(
    heads,
    head_size,
    step_rows,
    block,
    whole,
    grads,
    stats,
    ids,
    after1,
    after2,
    out,
    grad_out,
    grad_query,
    grad_key,
    grad_value,
):
    length = whole.shape[0]
    group = heads * head_size
    half = block // 2
    for start in range(0, length, block):
        packed = grads[start // 2 : start // 2 + half, :]
        grad_out[start : start + half, :] = packed[:, :group]
        grad_out[start + half : start + block, :] = packed[:, group:]
    id_row = ids[...]
    id_column = column_of(id_row)
    keys_t = whole[:, group : 2 * group].astype(F32).T.astype(BF16)
    factor = head_size**-0.5
    grad_key[...] = jnp.zeros_like(grad_key)
    grad_value[...] = jnp.zeros_like(grad_value)
    for first in range(0, length, step_rows):
        last = first + step_rows
        tops = []
        for head in range(heads):
            lo = head * head_size
            queries = whole[first:last, lo : lo + head_size] * BF16(factor)
            keys = whole[:last, group + lo : group + lo + head_size]
            values = whole[:last, 2 * group + lo : 2 * group + lo + head_size]
            grad = grad_out[first:last, lo : lo + head_size]
            scores = masked_scores(keys, queries, id_column[:last], id_row[:, first:last], first)
            probs = jnp.exp(scores - stats[head : head + 1, first:last])
            grad_probs = lax.dot_general(
                values, grad, (((1,), (1,)), ((), ())), preferred_element_type=F32
            )
            delta = jnp.sum(probs * grad_probs, 0, keepdims=True)
            grad_scores = (probs * (grad_probs - delta)).astype(BF16)
            tops.append(
                jnp.dot(
                    keys_t[lo : lo + head_size, :last], grad_scores, preferred_element_type=F32
                )
                * factor
            )
            grad_key[head, :last, :] += jnp.dot(
                grad_scores, queries, preferred_element_type=F32
            )
            grad_value[head, :last, :] += jnp.dot(
                probs.astype(BF16), grad, preferred_element_type=F32
            )
        grad_query[first:last, :] = jnp.concatenate(tops, 0).T.astype(BF16)
    out[:, :group] = grad_query[...]
    for head in range(heads):
        lo = head * head_size
        out[:, group + lo : group + lo + head_size] = grad_key[head].astype(BF16)
        out[:, 2 * group + lo : 2 * group + lo + head_size] = grad_value[head].astype(BF16)


def attend_forward(rows, weight, gain, bias, bqv, after, seq_count, heads, head_size, block):
    length = rows.shape[0] * block
    width = rows.shape[2]
    group = heads * head_size
    return pl.pallas_call(
        functools.partial(forward_kernel, seq_count, heads, head_size, min(256, length), block),
        out_shape=[
            jax.ShapeDtypeStruct((length // 2, 2 * group), BF16),
            jax.ShapeDtypeStruct((heads, length), F32),
            jax.ShapeDtypeStruct((length, 3 * group), BF16),
            jax.ShapeDtypeStruct((length, width), BF16),
            jax.ShapeDtypeStruct((1, length), F32),
        ],
        in_specs=vmem_specs(5) + [ANYWHERE],
        out_specs=vmem_specs(5),
        scratch_shapes=[pltpu.VMEM((length, group), BF16), pltpu.VMEM((1, 3 * group), F32)],
        compiler_params=pltpu.CompilerParams(vmem_limit_bytes=48 * 2**20),
        cost_estimate=LIGHT,
    )(rows, weight, gain, bias, bqv, after)


def attend_backward(whole, grads, stats, ids, after, heads, head_size, block):
    length, width = whole.shape
    group = heads * head_size
    return pl.pallas_call(
        functools.partial(backward_kernel, heads, head_size, min(256, length), block),
        out_shape=jax.ShapeDtypeStruct((length, 3 * group), BF16),
        in_specs=vmem_specs(4) + [ANYWHERE] * 2,
        out_specs=vmem_specs(1)[0],
        scratch_shapes=[
            pltpu.VMEM((length, group), BF16),
            pltpu.VMEM((length, group), BF16),
            pltpu.VMEM((heads, length, head_size), F32),
            pltpu.VMEM((heads, length, head_size), F32),
        ],
        compiler_params=pltpu.CompilerParams(vmem_limit_bytes=48 * 2**20),
        cost_estimate=LIGHT,
    )(whole, grads, stats, ids, *after)


def on_device(
    inputs,
    segments,
    cotangent,
    ln1_gain,
    ln1_bias,
    w_qkv,
    b_qv,
    w_out,
    b_out,
    ln2_gain,
    ln2_bias,
    w_fc,
    b_fc,
    w_proj,
    b_proj,
):
    seq_count, block, width = inputs.shape
    head_size = width // HEADS
    tokens = seq_count * block
    count = lax.axis_size("seq")
    devices = count * lax.axis_size("dp")
    groups = count // seq_count
    heads = -(-HEADS // groups)
    spare = groups * heads - HEADS
    group = heads * head_size

    vectors = (ln1_gain, ln1_bias, b_qv, b_out, ln2_gain, ln2_bias, b_fc, b_proj)
    sizes = tuple(vector.shape[0] for vector in vectors)
    shard_rows = w_out.shape[0] // width
    parts = w_fc.shape[0] // w_out.shape[0]
    classes = groups // CORES
    chips = devices // CORES
    place = lax.axis_index("seq")
    core = place % CORES
    group_index = place % groups

    columns, blocks = first_blocks(
        w_qkv.reshape(shard_rows, 3 * width),
        inputs,
        segments,
        [vector.reshape(1, -1) for vector in vectors],
        classes,
        group,
    )
    stacked = stack_weights(w_out.reshape(-1, width), w_fc.reshape(-1, parts * width), columns)
    tower_a = build_line(gather_columns(columns), stacked)
    lines, sequence = gather_sequence(blocks, tower_a)
    low1, high1 = build_tower(z_pieces(stacked), 1, [tower_a])
    if lax.axis_size("dp") == 4:
        towers = [tower_a] + [swap_dp(tower_a, mask) for mask in range(1, 4)]
    else:
        towers = [lax.all_gather(tower_a, "dp", axis=0, tiled=True)]
    keep_a, send_a = split_halves(towers, [low1, lines])
    wqkv, gain1, bias1, bqv, bout, gain2, bias2, bfc, bproj = unpack_first(
        keep_a, swap_core(send_a), sizes
    )

    raw, stats, qkv, normed1, ids = attend_forward(
        sequence, wqkv, gain1, bias1, bqv, low1, seq_count, heads, head_size, block
    )
    pieces2 = z_pieces(gate(w_proj.reshape(-1, width), lines))
    low2, high2 = build_tower(pieces2, 0, [raw])
    attended = exchange(raw.reshape(count, block // 2, 2 * group))
    half1 = gather_plane(low1, high1, 1, raw, attended).reshape(1 + parts, -1, width)
    half2 = gather_plane(low2, high2, 0, attended)
    other1 = swap_core(half1)
    other2 = swap_core(half2)
    aligned = half2.shape[1] % 16 == 0
    if not aligned:
        half2 = ordered(core, half2, other2, 1).reshape(1, parts * width, width)

    spot = jnp.arange(width, dtype=jnp.int32)
    side = width // CORES
    own_core = (core + spot // side) % CORES
    order = (spot % side // shard_rows * CORES + own_core) * shard_rows + spot % shard_rows
    (
        outputs,
        grad_middle,
        grad_blocks,
        placed_a,
        placed_n,
        hidden,
        grad_pre,
        grad_out,
        grad_bout,
        grad_gain2,
        grad_bias2,
        grad_bfc,
        grad_bproj,
    ) = middle_block(
        half1,
        other1,
        half2,
        other2,
        attended,
        inputs,
        cotangent,
        order.reshape(1, width),
        (bout, gain2, bias2, bfc, bproj),
        groups,
    )
    grad_blocks = exchange(grad_blocks).reshape(-1, 2 * group)
    send_b, keep_b = weight_gradients(
        placed_a, placed_n, hidden, grad_pre, grad_out, cotangent, shard_rows
    )
    if send_b.shape[0] == 1 + parts:
        grad_wproj = lax.dot_general(
            hidden,
            cotangent.reshape(tokens, width),
            (((0,), (0,)), ((), ())),
            preferred_element_type=F32,
        )
        grad_wproj = grad_wproj.astype(BF16).reshape(chips, CORES, parts, shard_rows, width)
        grad_wproj = grad_wproj.transpose(1, 2, 0, 3, 4).reshape(CORES, parts, -1, width)
        send_b = jnp.concatenate([send_b, pick(grad_wproj, 1 - core, 0)], 0)
        keep_b = jnp.concatenate([keep_b, pick(grad_wproj, core, 0)], 0)
    sum_b = add(keep_b, swap_core(send_b)).reshape(-1, chips, shard_rows, width)
    steps = []

    def between(*after):
        if steps:
            steps.append(after[0])
        else:
            steps.append(
                attend_backward(qkv, grad_blocks, stats, ids, after, heads, head_size, block)
            )
        return steps[0]

    tower_b = scatter_plane(sum_b, 1, between)
    own_b = scatter_z(tower_b, 1)
    grad_qkv, first_sums = steps

    def blocks_of(value, rows):
        return value.astype(BF16).reshape(chips, CORES, rows, -1)

    rows = inputs.astype(F32).reshape(tokens, width)
    grad_normed1 = lax.dot_general(
        grad_qkv, wqkv, (((1,), (1,)), ((), ())), preferred_element_type=F32
    )
    own_normed1 = scatter_sequence(
        grad_normed1.astype(BF16).reshape(count, block, width), first_sums
    )
    _, norm1_back = jax.vjp(lambda value: norm_affine(value, gain1, bias1), rows)
    (grad_in_part,) = norm1_back(own_normed1.astype(F32).reshape(tokens, width))
    grad_inputs = (grad_middle + grad_in_part).astype(BF16).reshape(inputs.shape)

    grad_qkv = gate(grad_qkv, first_sums)
    long_rows = sequence[:, :block].astype(F32).reshape(count * block, width)
    _, norm1_long_back = jax.vjp(lambda g, b: norm_affine(long_rows, g, b), gain1, bias1)
    grad_gain1, grad_bias1 = norm1_long_back(grad_normed1)
    grad_wqkv = lax.dot_general(
        normed1, grad_qkv, (((0,), (0,)), ((), ())), preferred_element_type=F32
    )
    sums = jnp.sum(grad_qkv, 0, dtype=F32).reshape(3, group)
    here = (jnp.arange(groups) == group_index)[None, :, None]
    grad_bqv = jnp.where(here, jnp.stack([sums[0], sums[2]])[:, None], 0.0)
    grad_bqv = grad_bqv.reshape(2, groups * heads, head_size)[:, :HEADS]
    grads = (
        grad_gain1,
        grad_bias1,
        grad_bqv,
        grad_bout,
        grad_gain2,
        grad_bias2,
        grad_bfc,
        grad_bproj,
    )
    small_grads = pack_small([grad.reshape(1, -1) for grad in grads], sizes, devices)
    small_grads = jnp.pad(small_grads, ((0, 0), (0, 0), (0, 3 * group - LANES)))
    block_a = jnp.concatenate(
        [blocks_of(grad_wqkv, shard_rows), small_grads.reshape(chips, CORES, ROWS, -1)], 2
    )
    send_a, keep_a = pick(block_a, 1 - core, 1), pick(block_a, core, 1)
    got_a = swap_core(send_a)
    pair_a = jnp.concatenate(
        [jnp.where(core == 0, keep_a, got_a), jnp.where(core == 0, got_a, keep_a)], -1
    )
    tower_a = scatter_plane_direct(pair_a, tower_b)
    own_qkv, own_small = finish_columns(scatter_columns(tower_a), width, group, own_b)
    own = [own_small[i, :size] for i, size in enumerate(sizes)]
    own_qkv = own_qkv.reshape(-1)
    return (
        outputs,
        grad_inputs,
        own[0],
        own[1],
        own_qkv,
        own[2],
        own_b[0].reshape(-1),
        own[3],
        own[4],
        own[5],
        own_b[1 : 1 + parts].transpose(1, 0, 2).reshape(-1),
        own[6],
        own_b[1 + parts :].reshape(-1),
        own[7],
    )


def solution(mesh):
    token_spec = P("dp", "seq", None)
    flat_spec = P(("dp", "seq"))
    in_specs = (token_spec, P("dp", "seq"), token_spec) + (flat_spec,) * 12
    out_specs = (token_spec, token_spec) + (flat_spec,) * 12
    return jax.shard_map(
        on_device, mesh=mesh, in_specs=in_specs, out_specs=out_specs, check_vma=False
    )
```
